32 devices in a mesh: stream: 4 (over y, x), tok: 8 (over z, core).
Axes of the slice: x: 2, y: 2, z: 4, core: 2. Of those that a mesh axis runs over, the one named last changes fastest.
Arguments:
- latents: bfloat16 [32, 128, 768], P('stream'), may hold values from -6 to 6
- tokens: bfloat16 [32768, 768], P(('stream', 'tok')), may hold values from -6 to 6
- token_sample: int32 [32768], P(('stream', 'tok')), may hold values from 0 to 31, as said below
- token_mask: int32 [32768], P(('stream', 'tok')), may hold values from 0 to 1, as said below
- drop_mask: int32 [32], replicated, may hold values from 0 to 1, as said below
- gain_query: float32 [768], replicated, may hold values from 0.25 to 1.75
- w_query: bfloat16 [768, 768], replicated, may hold values from -0.21875 to 0.21875
- gain_token: float32 [768], replicated, may hold values from 0.25 to 1.75
- w_key: bfloat16 [768, 768], replicated, may hold values from -0.21875 to 0.21875
- w_value: bfloat16 [768, 768], replicated, may hold values from -0.21875 to 0.21875
- w_out: bfloat16 [768, 768], replicated, may hold values from -6 to 6
- gain_mlp: float32 [768], replicated, may hold values from 0.25 to 1.75
- w_up: bfloat16 [768, 3072], replicated, may hold values from -0.21875 to 0.21875
- b_up: float32 [3072], replicated, may hold values from -3 to 3
- w_down: bfloat16 [3072, 768], replicated, may hold values from -0.109375 to 0.109375
- b_down: float32 [768], replicated, may hold values from -3 to 3
- cotangent: bfloat16 [32, 128, 768], P('stream'), may hold values from -6 to 6
Outputs:
- result: bfloat16 [32, 128, 768], P('stream')
- d_latents: float32 [32, 128, 768], P('stream')
- d_tokens: float32 [32768, 768], P(('stream', 'tok'))
- d_gain_query: float32 [768], P('stream')
- d_w_query: float32 [768, 768], P(None, 'stream')
- d_gain_token: float32 [768], replicated
- d_w_key: float32 [768, 768], replicated
- d_w_value: float32 [768, 768], replicated
- d_w_out: float32 [768, 768], P(None, 'stream')
- d_gain_mlp: float32 [768], P('stream')
- d_w_up: float32 [768, 3072], P(None, 'stream')
- d_b_up: float32 [3072], P('stream')
- d_w_down: float32 [3072, 768], P('stream')
- d_b_down: float32 [768], P('stream')
The draws below stay inside these ranges and needn't reach their ends.
Inputs may be any that keep to these rules, and one draw needn't show every extreme that they name: `token_sample`: tokens on devices of stream index s name only samples s * 8 to s * 8 + 7, and every sample has real tokens on some device of its group. `token_mask`: on each device the real tokens come first; the last stream index holds text and is mostly padding, the first device of each group is full. `drop_mask`: at least one sample applies the block.
All inputs are finite; a program needn't handle non-finite values.
Results may differ from the reference program's by a relative error of at most 0.015.
Values sent between devices are 32-bit elements; how exact they have to be, the bound alone decides.
A program may use at most 192 MiB of HBM per device.

```python
import jax
import jax.numpy as jnp
from jax import lax

D = 768
HEADS = 12
HEAD_DIM = 64
FF = 3072
LATENTS = 128
TOK_DEV = 1024
BG = 8
B = 32
TOKENS = 32768
N_STREAM = 4
N_TOK = 8


def group_layout():
    place = jnp.arange(TOKENS, dtype=jnp.int32)
    device = place // TOK_DEV
    return (device // N_TOK, device % N_TOK, place % TOK_DEV)


def draw_token_sample(key, part):
    key = jax.random.fold_in(key, 11)
    group, member, within = group_layout()
    longest = jax.random.randint(jax.random.fold_in(key, 1), (N_STREAM,), 0, BG, dtype=jnp.int32)
    start = jax.random.randint(jax.random.fold_in(key, 2), (N_STREAM, BG), 0, N_TOK // 2 + 1, dtype=jnp.int32)
    reach = jax.random.randint(jax.random.fold_in(key, 3), (N_STREAM, BG), 0, 1 << 20, dtype=jnp.int32) % (N_TOK - 1 - start)
    finish = start + reach
    members = jnp.arange(N_TOK, dtype=jnp.int32)
    sample_ids = jnp.arange(BG, dtype=jnp.int32)
    present = (members[None, None, :] >= start[..., None]) & (members[None, None, :] <= finish[..., None])
    is_long = sample_ids[None, :] == longest[:, None]
    present = present | is_long[..., None]
    order = (sample_ids[None, :] - longest[:, None]) % BG
    before = order[:, :, None] > order[:, None, :]
    rank = jnp.sum((before[..., None] & present[:, None, :, :]).astype(jnp.int32), axis=2)
    present_dev = jnp.transpose(present, (0, 2, 1))
    rank_dev = jnp.transpose(rank, (0, 2, 1))
    count_dev = jnp.sum(present_dev.astype(jnp.int32), axis=2)
    present_tok = present_dev[group, member]
    rank_tok = rank_dev[group, member]
    count_tok = count_dev[group, member]
    drawn = jax.random.randint(jax.random.fold_in(key, 4), (TOKENS,), 0, 1 << 20, dtype=jnp.int32) % count_tok
    pick = jnp.where(within < count_tok, within, drawn)
    hit = present_tok & (rank_tok == pick[:, None])
    chosen = jnp.sum(jnp.where(hit, sample_ids[None, :], 0), axis=1)
    return (group * BG + chosen).astype(jnp.int32)


def draw_token_mask(key, part):
    key = jax.random.fold_in(key, 23)
    group, member, within = group_layout()
    devices = N_STREAM * N_TOK
    video = jax.random.randint(key, (devices,), TOK_DEV // 2, TOK_DEV + 1, dtype=jnp.int32)
    text = jax.random.randint(jax.random.fold_in(key, 1), (devices,), max(BG, TOK_DEV // 8), TOK_DEV // 2 + 1, dtype=jnp.int32)
    device_ids = jnp.arange(devices, dtype=jnp.int32)
    counts = jnp.where(device_ids // N_TOK == N_STREAM - 1, text, video)
    counts = jnp.where(device_ids % N_TOK == 0, TOK_DEV, counts)
    return (within < counts[group * N_TOK + member]).astype(jnp.int32)


def draw_drop_mask(key, part):
    key = jax.random.fold_in(key, 37)
    count = BG * N_STREAM
    coins = jax.random.randint(key, (count,), 0, 2, dtype=jnp.int32)
    chosen = jax.random.randint(jax.random.fold_in(key, 1), (), 0, count, dtype=jnp.int32)
    return jnp.where(jnp.arange(count, dtype=jnp.int32) == chosen, 1, coins).astype(jnp.int32)


def shard_levels(rng, dims, split, low, largest):
    def one(axis_at, shards_of):
        heights = jax.random.uniform(jax.random.fold_in(jax.random.fold_in(rng, 6), axis_at), (shards_of,), jnp.float32, low / len(split), largest / len(split))
        return jnp.repeat(jnp.exp(heights), dims[axis_at] // shards_of).reshape((-1,) + (1,) * (len(dims) - axis_at - 1))

    loudness = one(*split[0])
    for cut in split[1:]:
        loudness = loudness * one(*cut)
    return loudness


def centred(rng, dims, scale, bound, cuts=(), held_as=jnp.bfloat16):
    array = scale * jax.random.normal(rng, dims, jnp.float32)
    if cuts:
        array = array * shard_levels(rng, dims, cuts, -0.22, 0.18)
    return jnp.clip(array, -bound, bound).astype(held_as)


def setup_inputs(seed: int = 0) -> dict:
    streams_of = jax.random.split(jax.random.key(seed), 18)
    return {
        "latents": centred(streams_of[0], (B, LATENTS, D), 1.0, 6.0, ((0, 4),)),
        "tokens": centred(streams_of[1], (TOKENS, D), 1.0, 6.0, ((0, 32),)),
        "token_sample": draw_token_sample(jax.random.fold_in(streams_of[17], 71), 0),
        "token_mask": draw_token_mask(jax.random.fold_in(streams_of[17], 71), 0),
        "drop_mask": draw_drop_mask(jax.random.fold_in(streams_of[17], 71), 0),
        "gain_query": jnp.clip(1.0 + 0.15 * jax.random.normal(streams_of[5], (D,), jnp.float32), 0.25, 1.75),
        "w_query": centred(streams_of[6], (D, D), D ** -0.5, 0.21875),
        "gain_token": jnp.clip(1.0 + 0.15 * jax.random.normal(streams_of[7], (D,), jnp.float32), 0.25, 1.75),
        "w_key": centred(streams_of[8], (D, D), D ** -0.5, 0.21875),
        "w_value": centred(streams_of[9], (D, D), D ** -0.5, 0.21875),
        "w_out": centred(streams_of[10], (D, D), (max(1, D * BG // (N_TOK * TOK_DEV))) ** -0.5, 6.0),
        "gain_mlp": jnp.clip(1.0 + 0.15 * jax.random.normal(streams_of[11], (D,), jnp.float32), 0.25, 1.75),
        "w_up": centred(streams_of[12], (D, FF), D ** -0.5, 0.21875),
        "b_up": centred(streams_of[13], (FF,), 0.5, 3.0, (), jnp.float32),
        "w_down": centred(streams_of[14], (FF, D), FF ** -0.5, 0.109375),
        "b_down": centred(streams_of[15], (D,), 0.5, 3.0, (), jnp.float32),
        "cotangent": centred(streams_of[16], (B, LATENTS, D), 1.0, 6.0, ((0, 4),)),
    }


@jax.custom_vjp
def low(v):
    return lax.optimization_barrier(v.astype(jnp.bfloat16)).astype(jnp.float32)

@jax.custom_vjp
def low_back(v):
    return v

def low_keep(v):
    return (low(v), None)

def low_pass(kept, grad):
    return (grad,)

def back_keep(v):
    return (v, None)

def back_low(kept, grad):
    return (low(grad),)
low.defvjp(low_keep, low_pass)
low_back.defvjp(back_keep, back_low)
HIGH = lax.Precision.HIGHEST

def layer_norm(values, gain):
    center = values - lax.optimization_barrier(jnp.mean(values, -1, keepdims=True))
    spread = lax.optimization_barrier(jnp.mean(center * center, -1, keepdims=True))
    return center * lax.rsqrt(spread + 1e-05) * gain

def reference(latents, tokens, token_sample, token_mask, drop_mask, gain_query, w_query, gain_token, w_key, w_value, w_out, gain_mlp, w_up, b_up, w_down, b_down, cotangent):
    samples_all = BG * N_STREAM
    group_tokens = N_TOK * TOK_DEV
    applied = jnp.sum(drop_mask).astype(jnp.float32)
    scale_all = drop_mask.astype(jnp.float32) * samples_all / applied

    def forward(lat_f, tok_f, g_query, wq, g_token, wk, wv, wo, g_mlp, wup, bup, wdown, bdown):
        pieces = []
        for group in range(N_STREAM):
            lat_g = lat_f[group * BG:(group + 1) * BG]
            tok_g = tok_f[group * group_tokens:(group + 1) * group_tokens]
            ids = token_sample[group * group_tokens:(group + 1) * group_tokens] - group * BG
            real = token_mask[group * group_tokens:(group + 1) * group_tokens]
            valid = (ids.reshape(N_TOK, 1, TOK_DEV) == jnp.arange(BG, dtype=jnp.int32).reshape(1, BG, 1)) & (real.reshape(N_TOK, 1, TOK_DEV) == 1)
            normed = low(layer_norm(lat_g, g_query))
            query = low_back(low(jnp.einsum('bld,de->ble', normed, wq, precision=HIGH))).reshape(BG, LATENTS, HEADS, HEAD_DIM)
            tnorm = low(layer_norm(tok_g, g_token))
            keys = low_back(low(jnp.dot(tnorm, wk, precision=HIGH))).reshape(N_TOK, TOK_DEV, HEADS, HEAD_DIM)
            values = low_back(low(jnp.dot(tnorm, wv, precision=HIGH))).reshape(N_TOK, TOK_DEV, HEADS, HEAD_DIM)

            def block_scores(key_block, valid_block):
                raw = low_back(jnp.einsum('blhd,thd->bhlt', query, key_block, precision=HIGH))
                return jnp.where(valid_block[:, None, None, :], 0.125 * raw, -1e+30)

            def max_step(carry, item):
                key_block, valid_block = item
                return (jnp.maximum(carry, lax.optimization_barrier(jnp.max(block_scores(key_block, valid_block), -1))), None)
            top, _ = lax.scan(jax.checkpoint(max_step), jnp.full((BG, HEADS, LATENTS), -1e+30, jnp.float32), (keys, valid))

            def sum_step(carry, item):
                key_block, value_block, valid_block = item
                scores = block_scores(key_block, valid_block)
                weight = jnp.where(valid_block[:, None, None, :], jnp.exp(scores - top[..., None]), 0.0)
                numer = carry[0] + low_back(jnp.einsum('bhlt,thd->blhd', low(weight), value_block, precision=HIGH))
                return ((numer, carry[1] + lax.optimization_barrier(jnp.sum(weight, -1))), None)
            start = (jnp.zeros((BG, LATENTS, HEADS, HEAD_DIM), jnp.float32), jnp.zeros((BG, HEADS, LATENTS), jnp.float32))
            (numer, denom), _ = lax.scan(jax.checkpoint(sum_step), start, (keys, values, valid))
            attended = numer / jnp.transpose(denom, (0, 2, 1))[..., None]
            attended = low_back(low(attended.reshape(BG, LATENTS, D)))
            branch = low_back(jnp.einsum('ble,ed->bld', attended, wo, precision=HIGH))
            factor = scale_all[group * BG:(group + 1) * BG][:, None, None]
            middle = lat_g + factor * branch
            hnorm = low(layer_norm(middle, g_mlp))
            pre = low_back(jnp.einsum('bld,df->blf', hnorm, wup, precision=HIGH) + bup)
            hidden = low(jax.nn.gelu(pre))
            mlp_out = low_back(jnp.einsum('blf,fd->bld', hidden, wdown, precision=HIGH) + bdown)
            pieces.append(middle + factor * mlp_out)
        return jnp.concatenate(pieces, 0)
    floats = (latents.astype(jnp.float32), tokens.astype(jnp.float32), gain_query, w_query.astype(jnp.float32), gain_token, w_key.astype(jnp.float32), w_value.astype(jnp.float32), w_out.astype(jnp.float32), gain_mlp, w_up.astype(jnp.float32), b_up, w_down.astype(jnp.float32), b_down)
    output, pullback = jax.vjp(forward, *floats)
    grads = pullback(cotangent.astype(jnp.float32))
    return (output.astype(jnp.bfloat16), grads[0], grads[1], grads[2], grads[3], grads[4], grads[5], grads[6], grads[7], grads[8], grads[9], grads[10], grads[11], grads[12])
```

```python
import functools

import jax
import jax.numpy as jnp
from jax import lax
from jax.experimental import pallas as pl
from jax.experimental.pallas import tpu as pltpu
from jax.sharding import PartitionSpec as P

HEADS = 12
HEAD_DIM = 64
PAIRS = HEADS // 2
PIECES = 4
PIECE_HEADS = HEADS // PIECES
NUM_ROWS = PIECE_HEADS * HEAD_DIM
PIECE_ROWS = NUM_ROWS + 8
BLOCK = 256
NEG = -1e30
F32 = jnp.float32
BF16 = jnp.bfloat16
VMEM_BYTES = 56 * 1024 * 1024


def norm_parts(values):
    center = values - jnp.mean(values, -1, keepdims=True)
    spread = jnp.mean(center * center, -1, keepdims=True)
    inv = lax.rsqrt(spread + 1e-05)
    return center * inv, inv


def norm_back(unit, inv, gain, grad):
    scaled = grad * gain
    inner = scaled - jnp.mean(scaled, -1, keepdims=True)
    return inv * (inner - unit * jnp.mean(scaled * unit, -1, keepdims=True))


def dot(a, b, contract=(1, 0)):
    return lax.dot_general(
        a, b, (((contract[0],), (contract[1],)), ((), ())), preferred_element_type=F32
    )


def piece_of(head):
    return head // PIECE_HEADS, head % PIECE_HEADS


def forward_kernel(
    ids_ref,
    tok_ref,
    lat_ref,
    gain_q_ref,
    wq_ref,
    gain_t_ref,
    wk_ref,
    wv_ref,
    part_ref,
    key_ref,
    val_ref,
    tsort_ref,
    query_ref,
    normed_ref,
    place_ref,
    bounds_ref,
    tnorm_ref,
    pos_ref,
    top_ref,
    den_ref,
    num_ref,
):
    samples = part_ref.shape[0]
    rows = tok_ref.shape[0]
    width = tok_ref.shape[1]
    lat_rows = 128
    step = 256

    ids = ids_ref[...]
    lane = lax.broadcasted_iota(jnp.int32, (samples, rows), 1)
    member = ids == lax.broadcasted_iota(jnp.int32, (samples, rows), 0)
    ones = jnp.where(member, 1.0, 0.0)
    count = ones
    shift = 1
    while shift < rows:
        count = count + jnp.where(lane >= shift, pltpu.roll(count, shift, 1), 0.0)
        shift *= 2
    rank = count - ones
    begin = jnp.int32(0)
    pos = jnp.full((1, rows), -1.0, F32)
    for s in range(samples):
        total = jnp.sum(ones[s : s + 1]).astype(jnp.int32)
        bounds_ref[s] = begin
        bounds_ref[samples + s] = total
        pos = jnp.where(member[s : s + 1], rank[s : s + 1] + begin.astype(F32), pos)
        begin = begin + total
    pos_ref[...] = jnp.broadcast_to(pos, (8, rows))
    place_ref[...] = jnp.broadcast_to(pos, (128, rows)).T

    def token_norm(i, carry):
        at = pl.ds(pl.multiple_of(i * step, step), step)
        unit, _ = norm_parts(tok_ref[at, :].astype(F32))
        tnorm_ref[at, :] = (unit * gain_t_ref[...]).astype(BF16)
        return carry

    lax.fori_loop(0, rows // step, token_norm, 0)

    def token_sort(i, carry):
        at = pl.ds(pl.multiple_of(i * step, step), step)
        target = lax.broadcasted_iota(jnp.int32, (step, rows), 0) + i * step
        chosen = target.astype(F32) == pos_ref[0:1, :]
        pick = jnp.where(chosen, 1.0, 0.0).astype(BF16)
        tsort = dot(pick, tnorm_ref[...]).astype(BF16)
        tsort_ref[at, :] = tsort
        key_ref[at, :] = dot(tsort, wk_ref[...]).astype(BF16)
        val_ref[at, :] = dot(tsort, wv_ref[...]).astype(BF16)
        return carry

    lax.fori_loop(0, rows // step, token_sort, 0)
    key_ref[rows:, :] = jnp.zeros((BLOCK, width), BF16)
    val_ref[rows:, :] = jnp.zeros((BLOCK, width), BF16)

    def sample_step(s, carry):
        at = pl.ds(pl.multiple_of(s * lat_rows, lat_rows), lat_rows)
        unit, _ = norm_parts(lat_ref[at, :].astype(F32))
        normed = (unit * gain_q_ref[...]).astype(BF16)
        normed_ref[at, :] = normed
        query = dot(normed, wq_ref[...]) * 0.125
        turned = query.T.astype(BF16)
        blank = jnp.zeros((HEAD_DIM, lat_rows), BF16)
        for p in range(PAIRS):
            lo = 2 * p * HEAD_DIM
            query_ref[s, p, :HEAD_DIM, :lat_rows] = turned[lo : lo + HEAD_DIM]
            query_ref[s, p, :HEAD_DIM, lat_rows:] = blank
            query_ref[s, p, HEAD_DIM:, :lat_rows] = blank
            query_ref[s, p, HEAD_DIM:, lat_rows:] = turned[lo + HEAD_DIM : lo + 2 * HEAD_DIM]
        start = bounds_ref[s]
        total = bounds_ref[samples + s]
        base = lax.div(start, 16) * 16
        blocks = jnp.where(total > 0, lax.div(start + total - base + BLOCK - 1, BLOCK), 0)
        num_ref[...] = jnp.zeros_like(num_ref)
        top_ref[...] = jnp.full_like(top_ref, NEG)
        den_ref[...] = jnp.zeros_like(den_ref)

        def block_step(b, carry):
            row = pl.multiple_of(base + b * BLOCK, 16)
            index = lax.broadcasted_iota(jnp.int32, (BLOCK, 2 * lat_rows), 0) + row
            inside = (index >= start) & (index < start + total)
            for p in range(PAIRS):
                cols = slice(p * 128, (p + 1) * 128)
                score = dot(key_ref[pl.ds(row, BLOCK), cols], query_ref[s, p])
                score = jnp.where(inside, score, NEG)
                old = top_ref[p : p + 1, :]
                new = jnp.maximum(old, jnp.max(score, 0, keepdims=True))
                fade = jnp.exp(old - new)
                weight = jnp.exp(score - new)
                top_ref[p : p + 1, :] = new
                den_ref[p : p + 1, :] = den_ref[p : p + 1, :] * fade + jnp.sum(
                    weight, 0, keepdims=True
                )
                both = dot(val_ref[pl.ds(row, BLOCK), cols], weight.astype(BF16), (0, 0))
                for half in range(2):
                    at_rows = slice(p * 128 + half * HEAD_DIM, p * 128 + (half + 1) * HEAD_DIM)
                    at_cols = slice(half * lat_rows, (half + 1) * lat_rows)
                    num_ref[at_rows, :] = (
                        num_ref[at_rows, :] * fade[:, at_cols]
                        + both[half * HEAD_DIM : (half + 1) * HEAD_DIM, at_cols]
                    )
            return carry

        lax.fori_loop(0, blocks, block_step, 0)
        for h in range(HEADS):
            piece, i = piece_of(h)
            p, half = h // 2, h % 2
            at_cols = slice(half * lat_rows, (half + 1) * lat_rows)
            part_ref[s, piece, i * HEAD_DIM : (i + 1) * HEAD_DIM, :] = num_ref[
                h * HEAD_DIM : (h + 1) * HEAD_DIM, :
            ]
            part_ref[s, piece, NUM_ROWS + i : NUM_ROWS + i + 1, :] = top_ref[p : p + 1, at_cols]
            part_ref[
                s, piece, NUM_ROWS + PIECE_HEADS + i : NUM_ROWS + PIECE_HEADS + i + 1, :
            ] = den_ref[p : p + 1, at_cols]
        for piece in range(PIECES):
            part_ref[s, piece, NUM_ROWS + 2 * PIECE_HEADS :, :] = jnp.zeros(
                (8 - 2 * PIECE_HEADS, lat_rows), F32
            )
        return carry

    lax.fori_loop(0, samples, sample_step, 0)


def vmem():
    return pl.BlockSpec(memory_space=pltpu.VMEM)


def smem():
    return pl.BlockSpec(memory_space=pltpu.SMEM)


def attend_forward(ids, tokens, latents, gain_q, wq, gain_t, wk, wv):
    samples, lat_rows, width = latents.shape
    rows = tokens.shape[0]
    sds = jax.ShapeDtypeStruct
    return pl.pallas_call(
        forward_kernel,
        name="attend_forward",
        out_shape=(
            sds((samples, PIECES, PIECE_ROWS, lat_rows), F32),
            sds((rows + BLOCK, width), BF16),
            sds((rows + BLOCK, width), BF16),
            sds((rows, width), BF16),
            sds((samples, PAIRS, 128, 2 * lat_rows), BF16),
            sds((samples * lat_rows, width), BF16),
            sds((rows, 128), F32),
            sds((2 * samples,), jnp.int32),
        ),
        in_specs=[vmem()] * 8,
        out_specs=(vmem(),) * 7 + (smem(),),
        scratch_shapes=[
            pltpu.VMEM((rows, width), BF16),
            pltpu.VMEM((8, rows), F32),
            pltpu.VMEM((8, 2 * lat_rows), F32),
            pltpu.VMEM((8, 2 * lat_rows), F32),
            pltpu.VMEM((width, lat_rows), F32),
        ],
        compiler_params=pltpu.CompilerParams(vmem_limit_bytes=VMEM_BYTES),
    )(
        ids.reshape(1, rows),
        tokens,
        latents.reshape(samples * lat_rows, width),
        gain_q.reshape(1, width),
        wq,
        gain_t.reshape(1, width),
        wk,
        wv,
    )


def backward_kernel(
    bounds_ref,
    lat_ref,
    key_ref,
    val_ref,
    query_ref,
    normed_ref,
    dnum_ref,
    stat_ref,
    gain_q_ref,
    wq_ref,
    dkey_ref,
    dval_ref,
    dlat_ref,
    dgain_ref,
    dwq_ref,
    dk_ref,
    dv_ref,
    grad_ref,
    dquery_ref,
    turn_ref,
):
    samples = query_ref.shape[0]
    rows = dkey_ref.shape[0]
    lat_rows = 128
    step = 256
    for r in range(0, rows + BLOCK, step):
        dk_ref[r : r + step, :] = jnp.zeros((step, dk_ref.shape[1]), F32)
        dv_ref[r : r + step, :] = jnp.zeros((step, dv_ref.shape[1]), F32)
    grad_ref[...] = jnp.zeros_like(grad_ref)
    dgain_ref[...] = jnp.zeros_like(dgain_ref)

    def sample_step(s, carry):
        start = bounds_ref[s]
        total = bounds_ref[samples + s]
        base = lax.div(start, 16) * 16
        blocks = jnp.where(total > 0, lax.div(start + total - base + BLOCK - 1, BLOCK), 0)
        turn_ref[...] = jnp.zeros_like(turn_ref)
        for h in range(HEADS):
            p, half = h // 2, h % 2
            grad_ref[
                p,
                half * HEAD_DIM : (half + 1) * HEAD_DIM,
                half * lat_rows : (half + 1) * lat_rows,
            ] = dnum_ref[s, h * HEAD_DIM : (h + 1) * HEAD_DIM, :].astype(BF16)

        def block_step(b, carry):
            row = pl.multiple_of(base + b * BLOCK, 16)
            index = lax.broadcasted_iota(jnp.int32, (BLOCK, 2 * lat_rows), 0) + row
            inside = (index >= start) & (index < start + total)
            at = pl.ds(row, BLOCK)
            for p in range(PAIRS):
                cols = slice(p * 128, (p + 1) * 128)
                key = key_ref[at, cols]
                query = query_ref[s, p]
                grad = grad_ref[p]
                score = dot(key, query)
                weight = jnp.where(inside, jnp.exp(score - stat_ref[s, p : p + 1, :]), 0.0)
                dprob = dot(val_ref[at, cols], grad)
                dscore = (weight * (dprob - stat_ref[s, 8 + p : 9 + p, :])).astype(BF16)
                dv_ref[at, cols] += dot(weight.astype(BF16), grad, (1, 1))
                dk_ref[at, cols] += dot(dscore, query, (1, 1))
                both = dot(key, dscore, (0, 0))
                for half in range(2):
                    turn_ref[
                        p * 128 + half * HEAD_DIM : p * 128 + (half + 1) * HEAD_DIM, :
                    ] += both[
                        half * HEAD_DIM : (half + 1) * HEAD_DIM,
                        half * lat_rows : (half + 1) * lat_rows,
                    ]
            return carry

        lax.fori_loop(0, blocks, block_step, 0)
        at = pl.ds(pl.multiple_of(s * lat_rows, lat_rows), lat_rows)
        dquery = (turn_ref[...].T * 0.125).astype(BF16)
        dquery_ref[at, :] = dquery
        unit, inv = norm_parts(lat_ref[at, :].astype(F32))
        dnormed = dot(dquery, wq_ref[...], (1, 1))
        dgain_ref[0:1, :] += jnp.sum(dnormed * unit, 0, keepdims=True)
        dlat_ref[at, :] = norm_back(unit, inv, gain_q_ref[...], dnormed)
        return carry

    lax.fori_loop(0, samples, sample_step, 0)
    for r in range(0, rows, step):
        dkey_ref[r : r + step, :] = dk_ref[r : r + step, :].astype(BF16)
        dval_ref[r : r + step, :] = dv_ref[r : r + step, :].astype(BF16)
    width = dwq_ref.shape[0]
    for c in range(0, width, 256):
        dwq_ref[c : c + 256, :] = dot(normed_ref[:, c : c + 256], dquery_ref[...], (0, 0))


def attend_backward(bounds, latents, keys, values, query, normed, dnum, stat, gain_q, wq):
    samples, lat_rows, width = latents.shape
    rows = keys.shape[0] - BLOCK
    sds = jax.ShapeDtypeStruct
    return pl.pallas_call(
        backward_kernel,
        name="attend_backward",
        out_shape=(
            sds((rows, width), BF16),
            sds((rows, width), BF16),
            sds((samples * lat_rows, width), F32),
            sds((8, width), F32),
            sds((width, width), F32),
        ),
        in_specs=[smem()] + [vmem()] * 9,
        out_specs=(vmem(),) * 5,
        scratch_shapes=[
            pltpu.VMEM((rows + BLOCK, width), F32),
            pltpu.VMEM((rows + BLOCK, width), F32),
            pltpu.VMEM((PAIRS, 128, 2 * lat_rows), BF16),
            pltpu.VMEM((samples * lat_rows, width), BF16),
            pltpu.VMEM((width, lat_rows), F32),
        ],
        compiler_params=pltpu.CompilerParams(vmem_limit_bytes=VMEM_BYTES),
    )(
        bounds,
        latents.reshape(samples * lat_rows, width),
        keys,
        values,
        query,
        normed,
        dnum,
        stat,
        gain_q.reshape(1, width),
        wq,
    )


def token_kernel(
    place_ref,
    tok_ref,
    tsort_ref,
    dkey_ref,
    dval_ref,
    gain_t_ref,
    wk_ref,
    wv_ref,
    dtok_ref,
    dgain_ref,
    dwk_ref,
    dwv_ref,
):
    rows = tok_ref.shape[0]
    width = tok_ref.shape[1]
    step = 256
    for c in range(0, width, 256):
        dwk_ref[c : c + 256, :] = dot(tsort_ref[:, c : c + 256], dkey_ref[...], (0, 0))
        dwv_ref[c : c + 256, :] = dot(tsort_ref[:, c : c + 256], dval_ref[...], (0, 0))
    dgain_ref[...] = jnp.zeros_like(dgain_ref)

    def token_step(i, carry):
        at = pl.ds(pl.multiple_of(i * step, step), step)
        target = lax.broadcasted_iota(jnp.int32, (step, rows), 1).astype(F32)
        chosen = target == place_ref[at, 0:1]
        pick = jnp.where(chosen, 1.0, 0.0).astype(BF16)
        dkey = dot(pick, dkey_ref[...]).astype(BF16)
        dval = dot(pick, dval_ref[...]).astype(BF16)
        dnormed = dot(dkey, wk_ref[...], (1, 1)) + dot(dval, wv_ref[...], (1, 1))
        unit, inv = norm_parts(tok_ref[at, :].astype(F32))
        dgain_ref[0:1, :] += jnp.sum(dnormed * unit, 0, keepdims=True)
        dtok_ref[at, :] = norm_back(unit, inv, gain_t_ref[...], dnormed)
        return carry

    lax.fori_loop(0, rows // step, token_step, 0)


def token_backward(place, tokens, tsort, dkey, dval, gain_t, wk, wv):
    rows, width = tokens.shape
    sds = jax.ShapeDtypeStruct
    return pl.pallas_call(
        token_kernel,
        name="token_backward",
        out_shape=(
            sds((rows, width), F32),
            sds((8, width), F32),
            sds((width, width), F32),
            sds((width, width), F32),
        ),
        in_specs=[vmem()] * 8,
        out_specs=(vmem(),) * 4,
        compiler_params=pltpu.CompilerParams(vmem_limit_bytes=VMEM_BYTES),
    )(place, tokens, tsort, dkey, dval, gain_t.reshape(1, width), wk, wv)


def layer_norm(values, gain):
    center = values - jnp.mean(values, -1, keepdims=True)
    spread = jnp.mean(center * center, -1, keepdims=True)
    return center * lax.rsqrt(spread + 1e-05) * gain


def local(
    latents,
    tokens,
    token_sample,
    token_mask,
    drop_mask,
    gain_query,
    w_query,
    gain_token,
    w_key,
    w_value,
    w_out,
    gain_mlp,
    w_up,
    b_up,
    w_down,
    b_down,
    cotangent,
):
    samples, lat_rows, width = latents.shape
    group_index = lax.axis_index("stream")
    tok_index = lax.axis_index("tok")
    streams = lax.axis_size("stream")
    members = lax.axis_size("tok")
    samples_all = drop_mask.shape[0]
    scale_all = drop_mask.astype(F32) * samples_all / jnp.sum(drop_mask).astype(F32)
    factor = lax.dynamic_slice_in_dim(scale_all, group_index * samples, samples)[:, None, None]
    ids = jnp.where(token_mask == 1, token_sample - group_index * samples, -1)
    part, keys, values, tsort, query, normed, place, bounds = attend_forward(
        ids, tokens, latents, gain_query, w_query, gain_token, w_key, w_value
    )
    top_part = part[:, :, NUM_ROWS : NUM_ROWS + PIECE_HEADS]
    den_part = part[:, :, NUM_ROWS + PIECE_HEADS : NUM_ROWS + 2 * PIECE_HEADS]
    num_part = part[:, :, :NUM_ROWS].reshape(samples, PIECES, PIECE_HEADS, HEAD_DIM, lat_rows)
    top = lax.pmax(top_part, "tok")
    fade = jnp.exp(top_part - top)
    numer, denom = lax.psum((num_part * fade[:, :, :, None], den_part * fade), "tok")
    att_t = (numer / denom[:, :, :, None]).reshape(samples, width, lat_rows)
    attended = jnp.transpose(att_t, (0, 2, 1))
    attended_low = attended.astype(BF16).reshape(samples * lat_rows, width)
    lat_f = latents.astype(F32)
    branch = jnp.dot(attended_low, w_out, preferred_element_type=F32).reshape(
        samples, lat_rows, width
    )
    middle = lat_f + factor * branch
    hnorm, mlp_norm_back = jax.vjp(layer_norm, middle, gain_mlp)
    hnorm_low = hnorm.astype(BF16).reshape(samples * lat_rows, width)
    pre = jnp.dot(hnorm_low, w_up, preferred_element_type=F32) + b_up
    activated, gelu_back = jax.vjp(jax.nn.gelu, pre)
    hidden_low = activated.astype(BF16)
    mlp_out = (jnp.dot(hidden_low, w_down, preferred_element_type=F32) + b_down).reshape(
        samples, lat_rows, width
    )
    result = (middle + factor * mlp_out).astype(BF16)
    d_result = cotangent.astype(F32)
    d_mlp = (factor * d_result).astype(BF16).reshape(samples * lat_rows, width)
    grad_bdown = jnp.sum(d_mlp.astype(F32), 0)
    d_hidden = jnp.einsum("rd,fd->rf", d_mlp, w_down, preferred_element_type=F32)
    d_pre = gelu_back(d_hidden)[0].astype(BF16)
    grad_bup = jnp.sum(d_pre.astype(F32), 0)
    d_hnorm = jnp.einsum("rf,df->rd", d_pre, w_up, preferred_element_type=F32).reshape(
        samples, lat_rows, width
    )
    d_middle_part, grad_gmlp = mlp_norm_back(d_hnorm)
    d_middle = d_result + d_middle_part
    d_branch = (factor * d_middle).astype(BF16).reshape(samples * lat_rows, width)
    d_att = jnp.einsum("ed,brd->ber", w_out, d_branch.reshape(samples, lat_rows, width),
                       preferred_element_type=F32).astype(BF16).astype(F32)
    d_att = d_att.reshape(samples, HEADS, HEAD_DIM, lat_rows)
    den_h = denom.reshape(samples, HEADS, lat_rows)
    top_h = top.reshape(samples, HEADS, lat_rows)
    dnum = (d_att / den_h[:, :, None]).reshape(samples, width, lat_rows)
    delta = jnp.sum(d_att * att_t.reshape(d_att.shape), 2) / den_h
    blank = jnp.zeros((samples, 8 - PAIRS, 2 * lat_rows), F32)
    stat = jnp.concatenate(
        (
            top_h.reshape(samples, PAIRS, 2 * lat_rows),
            blank,
            delta.reshape(samples, PAIRS, 2 * lat_rows),
            blank,
        ),
        1,
    )

    shares = 8
    share = lax.rem(tok_index, shares)
    depth = width // shares
    hid_dim = w_up.shape[1]
    mine = lambda x: lax.dynamic_slice_in_dim(x, share * depth, depth, 1)
    grad_up = jnp.einsum("rd,rf->df", mine(hnorm_low), d_pre, preferred_element_type=F32)
    grad_down = jnp.einsum("rf,rd->df", hidden_low, mine(d_mlp), preferred_element_type=F32)
    grad_out = jnp.einsum("re,rd->ed", mine(attended_low), d_branch, preferred_element_type=F32)
    both = jnp.concatenate((grad_up, grad_down), 0)
    both = lax.psum_scatter(both, "stream", scatter_dimension=1, tiled=True)
    grad_out = lax.psum_scatter(grad_out, "stream", scatter_dimension=1, tiled=True)
    groups = [list(range(g, g + shares)) for g in range(0, members, shares)]
    both = lax.all_gather(both, "tok", axis_index_groups=groups)
    grad_up = both[:, :depth].reshape(width, -1)
    grad_down = both[:, depth:].reshape(width, -1).T
    grad_out = lax.all_gather(grad_out, "tok", axis_index_groups=groups, tiled=True)

    dkey, dval, dlat, dgain_q, grad_query = attend_backward(
        bounds, latents, keys, values, query, normed, dnum, stat, gain_query, w_query
    )
    d_tokens, dgain_t, grad_key, grad_value = token_backward(
        place, tokens, tsort, dkey, dval, gain_token, w_key, w_value
    )
    d_latents = d_middle + lax.psum(dlat, "tok").reshape(d_middle.shape)
    grad_key, grad_value, grad_query, grad_gtoken, grad_gquery = lax.psum(
        (grad_key, grad_value, grad_query, dgain_t[0], dgain_q[0]), ("stream", "tok")
    )
    grad_bup, grad_bdown, grad_gmlp = lax.psum((grad_bup, grad_bdown, grad_gmlp), "stream")

    def own(x, axis):
        size = x.shape[axis] // streams
        return lax.dynamic_slice_in_dim(x, group_index * size, size, axis)

    return (
        result,
        d_latents,
        d_tokens,
        own(grad_gquery, 0),
        own(grad_query, 1),
        grad_gtoken,
        grad_key,
        grad_value,
        grad_out,
        own(grad_gmlp, 0),
        grad_up,
        own(grad_bup, 0),
        grad_down,
        own(grad_bdown, 0),
    )


def solution(mesh):
    return jax.shard_map(
        local,
        mesh=mesh,
        in_specs=(
            P("stream", None, None),
            P(("stream", "tok"), None),
            P(("stream", "tok")),
            P(("stream", "tok")),
            P(),
            P(),
            P(),
            P(),
            P(),
            P(),
            P(),
            P(),
            P(),
            P(),
            P(),
            P(),
            P("stream", None, None),
        ),
        out_specs=(
            P("stream", None, None),
            P("stream", None, None),
            P(("stream", "tok"), None),
            P("stream"),
            P(None, "stream"),
            P(),
            P(),
            P(),
            P(None, "stream"),
            P("stream"),
            P(None, "stream"),
            P("stream"),
            P("stream", None),
            P("stream"),
        ),
        check_vma=False,
    )
```

```python
import functools

import jax
import jax.numpy as jnp
from jax import lax
from jax.experimental import pallas as pl
from jax.experimental.pallas import tpu as pltpu
from jax.sharding import PartitionSpec as P

HEADS = 12
HEAD_DIM = 64
PAIRS = HEADS // 2
PIECES = 4
PIECE_HEADS = HEADS // PIECES
NUM_ROWS = PIECE_HEADS * HEAD_DIM
PIECE_ROWS = NUM_ROWS + 16
MSG_ROWS = HEADS * HEAD_DIM + 32
BLOCK = 256
NEG = -1e30
F32 = jnp.float32
BF16 = jnp.bfloat16
VMEM_BYTES = 56 * 1024 * 1024


def norm_parts(values):
    center = values - jnp.mean(values, -1, keepdims=True)
    spread = jnp.mean(center * center, -1, keepdims=True)
    inv = lax.rsqrt(spread + 1e-05)
    return center * inv, inv


def norm_back(unit, inv, gain, grad):
    scaled = grad * gain
    inner = scaled - jnp.mean(scaled, -1, keepdims=True)
    return inv * (inner - unit * jnp.mean(scaled * unit, -1, keepdims=True))


def dot(a, b, contract=(1, 0)):
    return lax.dot_general(
        a, b, (((contract[0],), (contract[1],)), ((), ())), preferred_element_type=F32
    )


def piece_of(head):
    return head // PIECE_HEADS, head % PIECE_HEADS


def forward_kernel(
    ids_ref,
    tok_ref,
    lat_ref,
    gain_q_ref,
    wq_ref,
    gain_t_ref,
    wk_ref,
    wv_ref,
    part_ref,
    key_ref,
    val_ref,
    tsort_ref,
    query_ref,
    normed_ref,
    place_ref,
    bounds_ref,
    tnorm_ref,
    pos_ref,
    top_ref,
    den_ref,
    num_ref,
):
    samples = part_ref.shape[0]
    rows = tok_ref.shape[0]
    width = tok_ref.shape[1]
    lat_rows = 128
    step = 256

    ids = ids_ref[...]
    lane = lax.broadcasted_iota(jnp.int32, (samples, rows), 1)
    member = ids == lax.broadcasted_iota(jnp.int32, (samples, rows), 0)
    ones = jnp.where(member, 1.0, 0.0)
    count = ones
    shift = 1
    while shift < rows:
        count = count + jnp.where(lane >= shift, pltpu.roll(count, shift, 1), 0.0)
        shift *= 2
    rank = count - ones
    begin = jnp.int32(0)
    pos = jnp.full((1, rows), -1.0, F32)
    for s in range(samples):
        total = jnp.sum(ones[s : s + 1]).astype(jnp.int32)
        bounds_ref[s] = begin
        bounds_ref[samples + s] = total
        pos = jnp.where(member[s : s + 1], rank[s : s + 1] + begin.astype(F32), pos)
        begin = begin + total
    pos_ref[...] = jnp.broadcast_to(pos, (8, rows))
    place_ref[...] = jnp.broadcast_to(pos, (128, rows)).T

    def token_norm(i, carry):
        at = pl.ds(pl.multiple_of(i * step, step), step)
        unit, _ = norm_parts(tok_ref[at, :].astype(F32))
        tnorm_ref[at, :] = (unit * gain_t_ref[...]).astype(BF16)
        return carry

    lax.fori_loop(0, rows // step, token_norm, 0)

    def token_sort(i, carry):
        at = pl.ds(pl.multiple_of(i * step, step), step)
        target = lax.broadcasted_iota(jnp.int32, (step, rows), 0) + i * step
        chosen = target.astype(F32) == pos_ref[0:1, :]
        pick = jnp.where(chosen, 1.0, 0.0).astype(BF16)
        tsort = dot(pick, tnorm_ref[...]).astype(BF16)
        tsort_ref[at, :] = tsort
        key_ref[at, :] = dot(tsort, wk_ref[...]).astype(BF16)
        val_ref[at, :] = dot(tsort, wv_ref[...]).astype(BF16)
        return carry

    lax.fori_loop(0, rows // step, token_sort, 0)
    key_ref[rows:, :] = jnp.zeros((BLOCK, width), BF16)
    val_ref[rows:, :] = jnp.zeros((BLOCK, width), BF16)

    def sample_step(s, carry):
        at = pl.ds(pl.multiple_of(s * lat_rows, lat_rows), lat_rows)
        unit, _ = norm_parts(lat_ref[at, :].astype(F32))
        normed = (unit * gain_q_ref[...]).astype(BF16)
        normed_ref[at, :] = normed
        query = dot(normed, wq_ref[...]) * 0.125
        turned = query.T.astype(BF16)
        blank = jnp.zeros((HEAD_DIM, lat_rows), BF16)
        for p in range(PAIRS):
            lo = 2 * p * HEAD_DIM
            query_ref[s, p, :HEAD_DIM, :lat_rows] = turned[lo : lo + HEAD_DIM]
            query_ref[s, p, :HEAD_DIM, lat_rows:] = blank
            query_ref[s, p, HEAD_DIM:, :lat_rows] = blank
            query_ref[s, p, HEAD_DIM:, lat_rows:] = turned[lo + HEAD_DIM : lo + 2 * HEAD_DIM]
        start = bounds_ref[s]
        total = bounds_ref[samples + s]
        base = lax.div(start, 16) * 16
        blocks = jnp.where(total > 0, lax.div(start + total - base + BLOCK - 1, BLOCK), 0)
        for piece in range(PIECES):
            part_ref[s, piece, NUM_ROWS:, :] = jnp.zeros((16, lat_rows), F32)
        num_ref[...] = jnp.zeros_like(num_ref)
        top_ref[...] = jnp.full_like(top_ref, NEG)
        den_ref[...] = jnp.zeros_like(den_ref)

        def block_step(b, carry):
            row = pl.multiple_of(base + b * BLOCK, 16)
            index = lax.broadcasted_iota(jnp.int32, (BLOCK, 2 * lat_rows), 0) + row
            inside = (index >= start) & (index < start + total)
            for p in range(PAIRS):
                cols = slice(p * 128, (p + 1) * 128)
                score = dot(key_ref[pl.ds(row, BLOCK), cols], query_ref[s, p])
                score = jnp.where(inside, score, NEG)
                old = top_ref[p : p + 1, :]
                new = jnp.maximum(old, jnp.max(score, 0, keepdims=True))
                fade = jnp.exp(old - new)
                weight = jnp.exp(score - new)
                top_ref[p : p + 1, :] = new
                den_ref[p : p + 1, :] = den_ref[p : p + 1, :] * fade + jnp.sum(
                    weight, 0, keepdims=True
                )
                both = dot(val_ref[pl.ds(row, BLOCK), cols], weight.astype(BF16), (0, 0))
                for half in range(2):
                    at_rows = slice(p * 128 + half * HEAD_DIM, p * 128 + (half + 1) * HEAD_DIM)
                    at_cols = slice(half * lat_rows, (half + 1) * lat_rows)
                    num_ref[at_rows, :] = (
                        num_ref[at_rows, :] * fade[:, at_cols]
                        + both[half * HEAD_DIM : (half + 1) * HEAD_DIM, at_cols]
                    )
            return carry

        lax.fori_loop(0, blocks, block_step, 0)
        for h in range(HEADS):
            piece, i = piece_of(h)
            p, half = h // 2, h % 2
            at_cols = slice(half * lat_rows, (half + 1) * lat_rows)
            part_ref[s, piece, i * HEAD_DIM : (i + 1) * HEAD_DIM, :] = num_ref[
                h * HEAD_DIM : (h + 1) * HEAD_DIM, :
            ]
            part_ref[s, piece, NUM_ROWS + i : NUM_ROWS + i + 1, :] = top_ref[p : p + 1, at_cols]
            part_ref[s, piece, NUM_ROWS + 8 + i : NUM_ROWS + 9 + i, :] = den_ref[
                p : p + 1, at_cols
            ]
        return carry

    lax.fori_loop(0, samples, sample_step, 0)


def vmem():
    return pl.BlockSpec(memory_space=pltpu.VMEM)


def smem():
    return pl.BlockSpec(memory_space=pltpu.SMEM)


def attend_forward(ids, tokens, latents, gain_q, wq, gain_t, wk, wv):
    samples, lat_rows, width = latents.shape
    rows = tokens.shape[0]
    sds = jax.ShapeDtypeStruct
    return pl.pallas_call(
        forward_kernel,
        name="attend_forward",
        out_shape=(
            sds((samples, PIECES, PIECE_ROWS, lat_rows), F32),
            sds((rows + BLOCK, width), BF16),
            sds((rows + BLOCK, width), BF16),
            sds((rows, width), BF16),
            sds((samples, PAIRS, 128, 2 * lat_rows), BF16),
            sds((samples * lat_rows, width), BF16),
            sds((rows, 128), F32),
            sds((2 * samples,), jnp.int32),
        ),
        in_specs=[vmem()] * 8,
        out_specs=(vmem(),) * 7 + (smem(),),
        scratch_shapes=[
            pltpu.VMEM((rows, width), BF16),
            pltpu.VMEM((8, rows), F32),
            pltpu.VMEM((8, 2 * lat_rows), F32),
            pltpu.VMEM((8, 2 * lat_rows), F32),
            pltpu.VMEM((width, lat_rows), F32),
        ],
        compiler_params=pltpu.CompilerParams(vmem_limit_bytes=VMEM_BYTES),
    )(
        ids.reshape(1, rows),
        tokens,
        latents.reshape(samples * lat_rows, width),
        gain_q.reshape(1, width),
        wq,
        gain_t.reshape(1, width),
        wk,
        wv,
    )


def backward_kernel(
    bounds_ref,
    lat_ref,
    key_ref,
    val_ref,
    query_ref,
    normed_ref,
    msg_ref,
    gain_q_ref,
    wq_ref,
    dkey_ref,
    dval_ref,
    dlat_ref,
    dgain_ref,
    dwq_ref,
    dk_ref,
    dv_ref,
    grad_ref,
    dquery_ref,
    turn_ref,
    stat_ref,
):
    samples = query_ref.shape[0]
    rows = dkey_ref.shape[0]
    lat_rows = 128
    step = 256
    width = dwq_ref.shape[0]
    for r in range(0, rows + BLOCK, step):
        dk_ref[r : r + step, :] = jnp.zeros((step, dk_ref.shape[1]), F32)
        dv_ref[r : r + step, :] = jnp.zeros((step, dv_ref.shape[1]), F32)
    grad_ref[...] = jnp.zeros_like(grad_ref)
    dgain_ref[...] = jnp.zeros_like(dgain_ref)

    def sample_step(s, carry):
        start = bounds_ref[s]
        total = bounds_ref[samples + s]
        base = lax.div(start, 16) * 16
        blocks = jnp.where(total > 0, lax.div(start + total - base + BLOCK - 1, BLOCK), 0)
        turn_ref[...] = jnp.zeros_like(turn_ref)
        for h in range(HEADS):
            p, half = h // 2, h % 2
            grad_ref[
                p,
                half * HEAD_DIM : (half + 1) * HEAD_DIM,
                half * lat_rows : (half + 1) * lat_rows,
            ] = msg_ref[s, h * HEAD_DIM : (h + 1) * HEAD_DIM, :].astype(BF16)

            stat_ref[p : p + 1, half * lat_rows : (half + 1) * lat_rows] = msg_ref[
                s, width + h : width + h + 1, :
            ]
            stat_ref[8 + p : 9 + p, half * lat_rows : (half + 1) * lat_rows] = msg_ref[
                s, width + 16 + h : width + 17 + h, :
            ]

        def block_step(b, carry):
            row = pl.multiple_of(base + b * BLOCK, 16)
            index = lax.broadcasted_iota(jnp.int32, (BLOCK, 2 * lat_rows), 0) + row
            inside = (index >= start) & (index < start + total)
            at = pl.ds(row, BLOCK)
            for p in range(PAIRS):
                cols = slice(p * 128, (p + 1) * 128)
                key = key_ref[at, cols]
                query = query_ref[s, p]
                grad = grad_ref[p]
                score = dot(key, query)
                weight = jnp.where(inside, jnp.exp(score - stat_ref[p : p + 1, :]), 0.0)
                dprob = dot(val_ref[at, cols], grad)
                dscore = (weight * (dprob - stat_ref[8 + p : 9 + p, :])).astype(BF16)
                dv_ref[at, cols] += dot(weight.astype(BF16), grad, (1, 1))
                dk_ref[at, cols] += dot(dscore, query, (1, 1))
                both = dot(key, dscore, (0, 0))
                for half in range(2):
                    turn_ref[
                        p * 128 + half * HEAD_DIM : p * 128 + (half + 1) * HEAD_DIM, :
                    ] += both[
                        half * HEAD_DIM : (half + 1) * HEAD_DIM,
                        half * lat_rows : (half + 1) * lat_rows,
                    ]
            return carry

        lax.fori_loop(0, blocks, block_step, 0)
        at = pl.ds(pl.multiple_of(s * lat_rows, lat_rows), lat_rows)
        dquery = (turn_ref[...].T * 0.125).astype(BF16)
        dquery_ref[at, :] = dquery
        unit, inv = norm_parts(lat_ref[at, :].astype(F32))
        dnormed = dot(dquery, wq_ref[...], (1, 1))
        dgain_ref[0:1, :] += jnp.sum(dnormed * unit, 0, keepdims=True)
        dlat_ref[at, :] = norm_back(unit, inv, gain_q_ref[...], dnormed)
        return carry

    lax.fori_loop(0, samples, sample_step, 0)
    for r in range(0, rows, step):
        dkey_ref[r : r + step, :] = dk_ref[r : r + step, :].astype(BF16)
        dval_ref[r : r + step, :] = dv_ref[r : r + step, :].astype(BF16)
    for c in range(0, width, 256):
        dwq_ref[c : c + 256, :] = dot(normed_ref[:, c : c + 256], dquery_ref[...], (0, 0))


def attend_backward(bounds, latents, keys, values, query, normed, msg, gain_q, wq):
    samples, lat_rows, width = latents.shape
    rows = keys.shape[0] - BLOCK
    sds = jax.ShapeDtypeStruct
    return pl.pallas_call(
        backward_kernel,
        name="attend_backward",
        out_shape=(
            sds((rows, width), BF16),
            sds((rows, width), BF16),
            sds((samples * lat_rows, width), F32),
            sds((8, width), F32),
            sds((width, width), F32),
        ),
        in_specs=[smem()] + [vmem()] * 8,
        out_specs=(vmem(),) * 5,
        scratch_shapes=[
            pltpu.VMEM((rows + BLOCK, width), F32),
            pltpu.VMEM((rows + BLOCK, width), F32),
            pltpu.VMEM((PAIRS, 128, 2 * lat_rows), BF16),
            pltpu.VMEM((samples * lat_rows, width), BF16),
            pltpu.VMEM((width, lat_rows), F32),
            pltpu.VMEM((16, 2 * lat_rows), F32),
        ],
        compiler_params=pltpu.CompilerParams(vmem_limit_bytes=VMEM_BYTES),
    )(
        bounds,
        latents.reshape(samples * lat_rows, width),
        keys,
        values,
        query,
        normed,
        msg,
        gain_q.reshape(1, width),
        wq,
    )


def token_kernel(
    place_ref,
    tok_ref,
    tsort_ref,
    dkey_ref,
    dval_ref,
    gain_t_ref,
    wk_ref,
    wv_ref,
    dtok_ref,
    dgain_ref,
    dwk_ref,
    dwv_ref,
):
    rows = tok_ref.shape[0]
    width = tok_ref.shape[1]
    step = 256
    for c in range(0, width, 256):
        dwk_ref[c : c + 256, :] = dot(tsort_ref[:, c : c + 256], dkey_ref[...], (0, 0))
        dwv_ref[c : c + 256, :] = dot(tsort_ref[:, c : c + 256], dval_ref[...], (0, 0))
    dgain_ref[...] = jnp.zeros_like(dgain_ref)

    def token_step(i, carry):
        at = pl.ds(pl.multiple_of(i * step, step), step)
        target = lax.broadcasted_iota(jnp.int32, (step, rows), 1).astype(F32)
        chosen = target == place_ref[at, 0:1]
        pick = jnp.where(chosen, 1.0, 0.0).astype(BF16)
        dkey = dot(pick, dkey_ref[...]).astype(BF16)
        dval = dot(pick, dval_ref[...]).astype(BF16)
        dnormed = dot(dkey, wk_ref[...], (1, 1)) + dot(dval, wv_ref[...], (1, 1))
        unit, inv = norm_parts(tok_ref[at, :].astype(F32))
        dgain_ref[0:1, :] += jnp.sum(dnormed * unit, 0, keepdims=True)
        dtok_ref[at, :] = norm_back(unit, inv, gain_t_ref[...], dnormed)
        return carry

    lax.fori_loop(0, rows // step, token_step, 0)


def token_backward(place, tokens, tsort, dkey, dval, gain_t, wk, wv):
    rows, width = tokens.shape
    sds = jax.ShapeDtypeStruct
    return pl.pallas_call(
        token_kernel,
        name="token_backward",
        out_shape=(
            sds((rows, width), F32),
            sds((8, width), F32),
            sds((width, width), F32),
            sds((width, width), F32),
        ),
        in_specs=[vmem()] * 8,
        out_specs=(vmem(),) * 4,
        compiler_params=pltpu.CompilerParams(vmem_limit_bytes=VMEM_BYTES),
    )(place, tokens, tsort, dkey, dval, gain_t.reshape(1, width), wk, wv)


MESH = pl.DeviceIdType.MESH


def merge(a_ref, b_ref, out_ref):
    a_tail, b_tail = a_ref[NUM_ROWS : NUM_ROWS + 8, :], b_ref[NUM_ROWS : NUM_ROWS + 8, :]
    top = jnp.maximum(a_tail, b_tail)
    a_fade, b_fade = jnp.exp(a_tail - top), jnp.exp(b_tail - top)
    den = a_ref[NUM_ROWS + 8 :, :] * a_fade + b_ref[NUM_ROWS + 8 :, :] * b_fade
    for i in range(PIECE_HEADS):
        at = slice(i * HEAD_DIM, (i + 1) * HEAD_DIM)
        out_ref[at, :] = (
            a_ref[at, :] * a_fade[i : i + 1, :] + b_ref[at, :] * b_fade[i : i + 1, :]
        )
    out_ref[NUM_ROWS : NUM_ROWS + 8, :] = top
    out_ref[NUM_ROWS + 8 :, :] = den


def gelu_parts(x):
    c = 0.7978845608028654
    square = x * x
    t = jnp.tanh(c * x * (1.0 + 0.044715 * square))
    half = 0.5 * (1.0 + t)
    slope = half + (0.5 * c) * x * (1.0 - t * t) * (1.0 + (3 * 0.044715) * square)
    return x * half, slope


def latent_kernel(
    part_ref,
    drop_ref,
    lat_ref,
    cot_ref,
    wo_hbm,
    gain_ref,
    wup_hbm,
    bup_ref,
    wdn_hbm,
    bdn_ref,
    msg_ref,
    res_ref,
    dmid_ref,
    a_ref,
    b_ref,
    att_ref,
    vec_ref,
    wo_ref,
    wup_ref,
    wdn_ref,
    pair_ref,
    own_ref,
    right_in,
    right_out,
    left_in,
    left_out,
    res_out,
    res_in,
    att_t_ref,
    mid_ref,
    acc_ref,
    dacc_ref,
    weight_sem,
    pair_send,
    pair_recv,
    right_send,
    right_recv,
    left_send,
    left_recv,
    msg_send,
    msg_recv,
    res_send,
    res_recv,
):
    samples = part_ref.shape[0]
    half = samples // 2
    lat_rows = 128
    width = lat_ref.shape[1]
    chunks = half * PIECES
    stream = lax.axis_index("stream")
    tok = lax.axis_index("tok")
    chips = lax.axis_size("tok") // 2
    core = lax.rem(tok, 2)
    chip = lax.div(tok, 2)
    partner = (stream, tok + 1 - 2 * core)
    right = (stream, tok + 2)
    left = (stream, tok - 2)
    has_right = chip < chips - 1
    has_left = chip > 0

    barrier = pltpu.get_barrier_semaphore()
    pl.semaphore_signal(barrier, inc=1, device_id=partner, device_id_type=MESH)

    @pl.when(has_right)
    def _():
        pl.semaphore_signal(barrier, inc=1, device_id=right, device_id_type=MESH)

    @pl.when(has_left)
    def _():
        pl.semaphore_signal(barrier, inc=1, device_id=left, device_id_type=MESH)

    weights = [
        pltpu.make_async_copy(src, dst, weight_sem.at[i])
        for i, (src, dst) in enumerate(((wo_hbm, wo_ref), (wup_hbm, wup_ref), (wdn_hbm, wdn_ref)))
    ]
    for copy in weights:
        copy.start()
    pl.semaphore_wait(
        barrier, 1 + has_right.astype(jnp.int32) + has_left.astype(jnp.int32)
    )

    def pair_copy(i):
        j, q = lax.div(i, PIECES), lax.rem(i, PIECES)
        return pltpu.make_async_remote_copy(
            src_ref=part_ref.at[(1 - core) * half + j, q],
            dst_ref=pair_ref.at[i],
            send_sem=pair_send.at[i],
            recv_sem=pair_recv.at[i],
            device_id=partner,
            device_id_type=MESH,
        )

    def right_copy(i):
        return pltpu.make_async_remote_copy(
            src_ref=right_out.at[i],
            dst_ref=right_in.at[i],
            send_sem=right_send.at[i],
            recv_sem=right_recv.at[i],
            device_id=right,
            device_id_type=MESH,
        )

    def left_copy(i):
        return pltpu.make_async_remote_copy(
            src_ref=left_out.at[i],
            dst_ref=left_in.at[i],
            send_sem=left_send.at[i],
            recv_sem=left_recv.at[i],
            device_id=left,
            device_id_type=MESH,
        )

    def msg_copy(j):
        at = core * half + j
        return pltpu.make_async_remote_copy(
            src_ref=msg_ref.at[at],
            dst_ref=msg_ref.at[at],
            send_sem=msg_send.at[j],
            recv_sem=msg_recv.at[j],
            device_id=partner,
            device_id_type=MESH,
        )

    def msg_arrival(j):
        at = (1 - core) * half + j
        return pltpu.make_async_remote_copy(
            src_ref=msg_ref.at[at],
            dst_ref=msg_ref.at[at],
            send_sem=msg_send.at[j],
            recv_sem=msg_recv.at[j],
            device_id=partner,
            device_id_type=MESH,
        )

    def res_copy(j):
        return pltpu.make_async_remote_copy(
            src_ref=res_out.at[j],
            dst_ref=res_in.at[j],
            send_sem=res_send.at[j],
            recv_sem=res_recv.at[j],
            device_id=partner,
            device_id_type=MESH,
        )

    def start_pair(i, carry):
        pair_copy(i).start()
        return carry

    lax.fori_loop(0, chunks, start_pair, 0)

    drop = drop_ref[...].astype(F32)
    scale_all = drop * drop.shape[1] / jnp.sum(drop, 1, keepdims=True)
    drop_lane = lax.broadcasted_iota(jnp.int32, drop.shape, 1)
    vec_ref[...] = jnp.zeros_like(vec_ref)

    def mlp(j, q):
        sample = core * half + j
        rows = pl.ds(pl.multiple_of(sample * lat_rows, lat_rows), lat_rows)
        mine = pl.ds(pl.multiple_of(j * lat_rows, lat_rows), lat_rows)
        scale = jnp.sum(
            jnp.where(drop_lane == stream * samples + sample, scale_all, 0.0), 1, keepdims=True
        )

        @pl.when(q == 0)
        def _():
            for h in range(HEADS):
                piece, i = piece_of(h)
                at = j * PIECES + piece
                den = own_ref[at, NUM_ROWS + 8 + i : NUM_ROWS + 9 + i, :]
                att_t_ref[h * HEAD_DIM : (h + 1) * HEAD_DIM, :] = own_ref[
                    at, i * HEAD_DIM : (i + 1) * HEAD_DIM, :
                ] * (1.0 / den)
            att = att_t_ref[...].T.astype(BF16)
            att_ref[mine, :] = att
            mid = lat_ref[rows, :].astype(F32) + scale * dot(att, wo_ref[...])
            mid_ref[...] = mid
            unit, _ = norm_parts(mid)
            a_ref[0, mine, :] = (unit * gain_ref[...]).astype(BF16)
            dm = (scale * cot_ref[rows, :].astype(F32)).astype(BF16)
            a_ref[1, mine, :] = dm
            vec_ref[1:2, :width] += jnp.sum(dm.astype(F32), 0, keepdims=True)
            acc_ref[...] = jnp.broadcast_to(bdn_ref[...], acc_ref.shape)
            dacc_ref[...] = jnp.zeros_like(dacc_ref)

        span = wup_ref.shape[1] // PIECES
        cols = pl.ds(pl.multiple_of(q * span, 128), span)
        pre = dot(a_ref[0, mine, :], wup_ref[:, cols]) + bup_ref[:, cols]
        active, slope = gelu_parts(pre)
        hidden = active.astype(BF16)
        b_ref[1, mine, cols] = hidden
        acc_ref[...] += dot(hidden, wdn_ref[cols, :])
        dpre = (slope * dot(a_ref[1, mine, :], wdn_ref[cols, :], (1, 1))).astype(BF16)
        b_ref[0, mine, cols] = dpre
        vec_ref[0:1, cols] += jnp.sum(dpre.astype(F32), 0, keepdims=True)
        dacc_ref[...] += dot(dpre, wup_ref[:, cols], (1, 1))

        @pl.when(q == PIECES - 1)
        def _():
            mid = mid_ref[...]
            res = (mid + scale * acc_ref[...]).astype(BF16)
            res_ref[rows, :] = res
            res_out[j] = res.astype(F32)
            res_copy(j).start()
            unit, inv = norm_parts(mid)
            dhn = dacc_ref[...]
            vec_ref[2:3, :width] += jnp.sum(dhn * unit, 0, keepdims=True)
            dmid = cot_ref[rows, :].astype(F32) + norm_back(unit, inv, gain_ref[...], dhn)
            dmid_ref[mine, :] = dmid
            da = (scale * dmid).astype(BF16)
            a_ref[2, mine, :] = da
            datt_t = dot(wo_ref[...], da, (1, 1)).astype(BF16).astype(F32)
            msg_ref[sample, width:, :] = jnp.zeros((MSG_ROWS - width, lat_rows), F32)
            for h in range(HEADS):
                piece, i = piece_of(h)
                at = j * PIECES + piece
                inverse = 1.0 / own_ref[at, NUM_ROWS + 8 + i : NUM_ROWS + 9 + i, :]
                span_h = slice(h * HEAD_DIM, (h + 1) * HEAD_DIM)
                one = datt_t[span_h]
                msg_ref[sample, span_h, :] = (one * inverse).astype(BF16).astype(F32)
                delta = jnp.sum(one * att_t_ref[span_h, :], 0, keepdims=True) * inverse
                msg_ref[sample, width + h : width + h + 1, :] = own_ref[
                    at, NUM_ROWS + i : NUM_ROWS + i + 1, :
                ]
                msg_ref[sample, width + 16 + h : width + 17 + h, :] = delta
            msg_copy(j).start()

    def step(t, carry):
        @pl.when(t < chunks)
        def _():
            pair_copy(t).wait_recv()
            j, q = lax.div(t, PIECES), lax.rem(t, PIECES)
            merge(part_ref.at[core * half + j, q], pair_ref.at[t], own_ref.at[t])

        r = t - chip

        @pl.when((r >= 0) & (r < chunks))
        def _():
            @pl.when(has_left)
            def _():
                right_copy(r).wait_recv()
                merge(own_ref.at[r], right_in.at[r], right_out.at[r])

            @pl.when(jnp.logical_not(has_left))
            def _():
                right_out[r] = own_ref[r]

            @pl.when(has_right)
            def _():
                right_copy(r).start()

        u = t - (chips - 1 - chip)

        @pl.when((u >= 0) & (u < chunks))
        def _():
            @pl.when(has_right)
            def _():
                left_copy(u).wait_recv()

            @pl.when(has_left)
            def _():
                @pl.when(has_right)
                def _():
                    merge(own_ref.at[u], left_in.at[u], left_out.at[u])

                @pl.when(jnp.logical_not(has_right))
                def _():
                    left_out[u] = own_ref[u]

                left_copy(u).start()

        w = t - (chips - 1)

        @pl.when((w >= 0) & (w < chunks))
        def _():
            @pl.when(has_right)
            def _():
                merge(right_out.at[w], left_in.at[w], own_ref.at[w])

            @pl.when(jnp.logical_not(has_right))
            def _():
                own_ref[w] = right_out[w]

        m = w - (PIECES - 1)

        @pl.when(m == 0)
        def _():
            for copy in weights:
                copy.wait()

        @pl.when(m >= 0)
        def _():
            mlp(lax.div(m, PIECES), lax.rem(m, PIECES))

        return carry

    lax.fori_loop(0, chunks + chips - 1 + PIECES - 1, step, 0)

    def finish_chunk(i, carry):
        pair_copy(i).wait_send()

        @pl.when(has_right)
        def _():
            right_copy(i).wait_send()

        @pl.when(has_left)
        def _():
            left_copy(i).wait_send()

        return carry

    lax.fori_loop(0, chunks, finish_chunk, 0)

    def finish_sample(j, carry):
        res_copy(j).wait_recv()
        other = (1 - core) * half + j
        rows = pl.ds(pl.multiple_of(other * lat_rows, lat_rows), lat_rows)
        res_ref[rows, :] = res_in[j].astype(BF16)
        res_copy(j).wait_send()
        msg_copy(j).wait_send()
        msg_arrival(j).wait_recv()
        return carry

    lax.fori_loop(0, half, finish_sample, 0)


def anywhere():
    return pl.BlockSpec(memory_space=pl.ANY)


def latent_block(part, drop_mask, latents, cotangent, wo, gain, wup, bup, wdn, bdn):
    samples, lat_rows, width = latents.shape
    half = samples // 2
    chunks = half * PIECES
    hidden = wup.shape[1]
    sds = jax.ShapeDtypeStruct
    chunk = lambda: pltpu.VMEM((chunks, PIECE_ROWS, lat_rows), F32)
    dma = pltpu.SemaphoreType.DMA
    return pl.pallas_call(
        latent_kernel,
        name="latent_block",
        out_shape=(
            sds((samples, MSG_ROWS, lat_rows), F32),
            sds((samples * lat_rows, width), BF16),
            sds((half * lat_rows, width), F32),
            sds((3, half * lat_rows, width), BF16),
            sds((2, half * lat_rows, hidden), BF16),
            sds((half * lat_rows, width), BF16),
            sds((8, hidden), F32),
        ),
        in_specs=[
            vmem(),
            vmem(),
            vmem(),
            vmem(),
            anywhere(),
            vmem(),
            anywhere(),
            vmem(),
            anywhere(),
            vmem(),
        ],
        out_specs=(vmem(),) * 7,
        scratch_shapes=[
            pltpu.VMEM(wo.shape, BF16),
            pltpu.VMEM(wup.shape, BF16),
            pltpu.VMEM(wdn.shape, BF16),
            chunk(),
            chunk(),
            chunk(),
            chunk(),
            chunk(),
            chunk(),
            pltpu.VMEM((half, lat_rows, width), F32),
            pltpu.VMEM((half, lat_rows, width), F32),
            pltpu.VMEM((width, lat_rows), F32),
            pltpu.VMEM((lat_rows, width), F32),
            pltpu.VMEM((lat_rows, width), F32),
            pltpu.VMEM((lat_rows, width), F32),
            dma((3,)),
            dma((chunks,)),
            dma((chunks,)),
            dma((chunks,)),
            dma((chunks,)),
            dma((chunks,)),
            dma((chunks,)),
            dma((half,)),
            dma((half,)),
            dma((half,)),
            dma((half,)),
        ],
        compiler_params=pltpu.CompilerParams(
            vmem_limit_bytes=VMEM_BYTES, collective_id=1, has_side_effects=True
        ),
    )(
        part,
        drop_mask.reshape(1, -1),
        latents.reshape(samples * lat_rows, width),
        cotangent.reshape(samples * lat_rows, width),
        wo,
        gain.reshape(1, width),
        wup,
        bup.reshape(1, hidden),
        wdn,
        bdn.reshape(1, width),
    )


def local(
    latents,
    tokens,
    token_sample,
    token_mask,
    drop_mask,
    gain_query,
    w_query,
    gain_token,
    w_key,
    w_value,
    w_out,
    gain_mlp,
    w_up,
    b_up,
    w_down,
    b_down,
    cotangent,
):
    samples, lat_rows, width = latents.shape
    group_index = lax.axis_index("stream")
    tok_index = lax.axis_index("tok")
    streams = lax.axis_size("stream")
    members = lax.axis_size("tok")
    ids = jnp.where(token_mask == 1, token_sample - group_index * samples, -1)
    part, keys, values, tsort, query, normed, place, bounds = attend_forward(
        ids, tokens, latents, gain_query, w_query, gain_token, w_key, w_value
    )
    msg, result, dmid, lefts, rights, attended, vec = latent_block(
        part, drop_mask, latents, cotangent, w_out, gain_mlp, w_up, b_up, w_down, b_down
    )
    result = result.reshape(latents.shape)

    core = lax.rem(tok_index, 2)
    shares = 4
    share = lax.rem(tok_index // 2, shares)
    depth = width // shares
    mine = lambda x: lax.dynamic_slice_in_dim(x, share * depth, depth, 1)
    grad_up = jnp.einsum("rd,rf->df", mine(lefts[0]), rights[0], preferred_element_type=F32)
    grad_down = jnp.einsum("rf,rd->df", rights[1], mine(lefts[1]), preferred_element_type=F32)
    grad_out = jnp.einsum("re,rd->ed", mine(attended), lefts[2], preferred_element_type=F32)
    both = jnp.concatenate((grad_up, grad_down), 0)
    both = lax.psum_scatter(both, "stream", scatter_dimension=1, tiled=True)
    grad_out = lax.psum_scatter(grad_out, "stream", scatter_dimension=1, tiled=True)
    size = 2 * shares
    groups = [list(range(g, g + size)) for g in range(0, members, size)]
    both = lax.all_gather(both, "tok", axis_index_groups=groups)
    both = both.reshape(shares, 2, 2 * depth, -1).sum(1)
    grad_up = both[:, :depth].reshape(width, -1)
    grad_down = both[:, depth:].reshape(width, -1).T
    grad_out = lax.all_gather(grad_out, "tok", axis_index_groups=groups)
    grad_out = grad_out.reshape(shares, 2, depth, -1).sum(1).reshape(width, -1)

    dkey, dval, dlat, dgain_q, grad_query = attend_backward(
        bounds, latents, keys, values, query, normed, msg, gain_query, w_query
    )
    d_tokens, dgain_t, grad_key, grad_value = token_backward(
        place, tokens, tsort, dkey, dval, gain_token, w_key, w_value
    )
    dlat = dlat.reshape(2, -1, width)
    dlat = dlat.at[core].add(jnp.where(tok_index < 2, dmid, 0.0))
    d_latents = lax.psum(dlat, "tok").reshape(latents.shape)
    pairs = [[g, g + 1] for g in range(0, members, 2)]
    vec = lax.psum(vec, "tok", axis_index_groups=pairs)
    grad_bup, grad_bdown, grad_gmlp = vec[0], vec[1, :width], vec[2, :width]
    grad_key, grad_value, grad_query, grad_gtoken, grad_gquery = lax.psum(
        (grad_key, grad_value, grad_query, dgain_t[0], dgain_q[0]), ("stream", "tok")
    )
    grad_bup, grad_bdown, grad_gmlp = lax.psum((grad_bup, grad_bdown, grad_gmlp), "stream")

    def own(x, axis):
        size = x.shape[axis] // streams
        return lax.dynamic_slice_in_dim(x, group_index * size, size, axis)

    return (
        result,
        d_latents,
        d_tokens,
        own(grad_gquery, 0),
        own(grad_query, 1),
        grad_gtoken,
        grad_key,
        grad_value,
        grad_out,
        own(grad_gmlp, 0),
        grad_up,
        own(grad_bup, 0),
        grad_down,
        own(grad_bdown, 0),
    )


def solution(mesh):
    return jax.shard_map(
        local,
        mesh=mesh,
        in_specs=(
            P("stream", None, None),
            P(("stream", "tok"), None),
            P(("stream", "tok")),
            P(("stream", "tok")),
            P(),
            P(),
            P(),
            P(),
            P(),
            P(),
            P(),
            P(),
            P(),
            P(),
            P(),
            P(),
            P("stream", None, None),
        ),
        out_specs=(
            P("stream", None, None),
            P("stream", None, None),
            P(("stream", "tok"), None),
            P("stream"),
            P(None, "stream"),
            P(),
            P(),
            P(),
            P(None, "stream"),
            P("stream"),
            P(None, "stream"),
            P("stream"),
            P("stream", None),
            P("stream"),
        ),
        check_vma=False,
    )
```

```python
import functools

import jax
import jax.numpy as jnp
from jax import lax
from jax.experimental import pallas as pl
from jax.experimental.pallas import tpu as pltpu
from jax.sharding import PartitionSpec as P

HEADS = 12
HEAD_DIM = 64
PAIRS = HEADS // 2
PIECES = 4
PIECE_HEADS = HEADS // PIECES
NUM_ROWS = PIECE_HEADS * HEAD_DIM
PIECE_ROWS = NUM_ROWS + 16
MSG_ROWS = HEADS * HEAD_DIM + 32
BLOCK = 256
LAG = 2
TOKEN_TICKS = (1, 2, 3, 4, 5, 6, 7, 8)
SMALL_TICK = 8
PAIR_TICK = 9
ONE_TICK = 12
TWO_TICK = 15
WIDE_ONE_TICKS = (7, 13)
WIDE_TWO_TICKS = (11, 17)
NEG = -1e30
F32 = jnp.float32
BF16 = jnp.bfloat16
VMEM_BYTES = 56 * 1024 * 1024


def norm_parts(values):
    center = values - jnp.mean(values, -1, keepdims=True)
    spread = jnp.mean(center * center, -1, keepdims=True)
    inv = lax.rsqrt(spread + 1e-05)
    return center * inv, inv


def norm_back(unit, inv, gain, grad):
    scaled = grad * gain
    inner = scaled - jnp.mean(scaled, -1, keepdims=True)
    return inv * (inner - unit * jnp.mean(scaled * unit, -1, keepdims=True))


def dot(a, b, contract=(1, 0)):
    return lax.dot_general(
        a, b, (((contract[0],), (contract[1],)), ((), ())), preferred_element_type=F32
    )


def piece_of(head):
    return head // PIECE_HEADS, head % PIECE_HEADS


def forward_kernel(
    ids_ref,
    tok_ref,
    lat_ref,
    gain_q_ref,
    wq_ref,
    gain_t_ref,
    wk_ref,
    wv_ref,
    part_ref,
    key_ref,
    val_ref,
    tsort_ref,
    query_ref,
    normed_ref,
    place_ref,
    bounds_ref,
    tnorm_ref,
    pos_ref,
    top_ref,
    den_ref,
    num_ref,
):
    samples = part_ref.shape[0]
    rows = tok_ref.shape[0]
    width = tok_ref.shape[1]
    lat_rows = 128
    step = 256

    ids = ids_ref[...]
    lane = lax.broadcasted_iota(jnp.int32, (samples, rows), 1)
    member = ids == lax.broadcasted_iota(jnp.int32, (samples, rows), 0)
    ones = jnp.where(member, 1.0, 0.0)
    count = ones
    shift = 1
    while shift < rows:
        count = count + jnp.where(lane >= shift, pltpu.roll(count, shift, 1), 0.0)
        shift *= 2
    rank = count - ones
    begin = jnp.int32(0)
    pos = jnp.full((1, rows), -1.0, F32)
    for s in range(samples):
        total = jnp.sum(ones[s : s + 1]).astype(jnp.int32)
        bounds_ref[s] = begin
        bounds_ref[samples + s] = total
        pos = jnp.where(member[s : s + 1], rank[s : s + 1] + begin.astype(F32), pos)
        begin = begin + total
    pos_ref[...] = jnp.broadcast_to(pos, (8, rows))
    place_ref[...] = jnp.broadcast_to(pos, (128, rows)).T

    def token_norm(i, carry):
        at = pl.ds(pl.multiple_of(i * step, step), step)
        unit, _ = norm_parts(tok_ref[at, :].astype(F32))
        tnorm_ref[at, :] = (unit * gain_t_ref[...]).astype(BF16)
        return carry

    lax.fori_loop(0, rows // step, token_norm, 0)

    def token_sort(i, carry):
        at = pl.ds(pl.multiple_of(i * step, step), step)
        target = lax.broadcasted_iota(jnp.int32, (step, rows), 0) + i * step
        chosen = target.astype(F32) == pos_ref[0:1, :]
        pick = jnp.where(chosen, 1.0, 0.0).astype(BF16)
        tsort = dot(pick, tnorm_ref[...]).astype(BF16)
        tsort_ref[at, :] = tsort
        key_ref[at, :] = dot(tsort, wk_ref[...]).astype(BF16)
        val_ref[at, :] = dot(tsort, wv_ref[...]).astype(BF16)
        return carry

    lax.fori_loop(0, rows // step, token_sort, 0)
    key_ref[rows:, :] = jnp.zeros((BLOCK, width), BF16)
    val_ref[rows:, :] = jnp.zeros((BLOCK, width), BF16)

    def sample_step(s, carry):
        at = pl.ds(pl.multiple_of(s * lat_rows, lat_rows), lat_rows)
        unit, _ = norm_parts(lat_ref[at, :].astype(F32))
        normed = (unit * gain_q_ref[...]).astype(BF16)
        normed_ref[at, :] = normed
        query = dot(normed, wq_ref[...]) * 0.125
        turned = query.T.astype(BF16)
        blank = jnp.zeros((HEAD_DIM, lat_rows), BF16)
        for p in range(PAIRS):
            lo = 2 * p * HEAD_DIM
            query_ref[s, p, :HEAD_DIM, :lat_rows] = turned[lo : lo + HEAD_DIM]
            query_ref[s, p, :HEAD_DIM, lat_rows:] = blank
            query_ref[s, p, HEAD_DIM:, :lat_rows] = blank
            query_ref[s, p, HEAD_DIM:, lat_rows:] = turned[lo + HEAD_DIM : lo + 2 * HEAD_DIM]
        start = bounds_ref[s]
        total = bounds_ref[samples + s]
        base = lax.div(start, 16) * 16
        blocks = jnp.where(total > 0, lax.div(start + total - base + BLOCK - 1, BLOCK), 0)
        for piece in range(PIECES):
            part_ref[s, piece, NUM_ROWS:, :] = jnp.zeros((16, lat_rows), F32)
        num_ref[...] = jnp.zeros_like(num_ref)
        top_ref[...] = jnp.full_like(top_ref, NEG)
        den_ref[...] = jnp.zeros_like(den_ref)

        def block_step(b, carry):
            row = pl.multiple_of(base + b * BLOCK, 16)
            index = lax.broadcasted_iota(jnp.int32, (BLOCK, 2 * lat_rows), 0) + row
            inside = (index >= start) & (index < start + total)
            for p in range(PAIRS):
                cols = slice(p * 128, (p + 1) * 128)
                score = dot(key_ref[pl.ds(row, BLOCK), cols], query_ref[s, p])
                score = jnp.where(inside, score, NEG)
                old = top_ref[p : p + 1, :]
                new = jnp.maximum(old, jnp.max(score, 0, keepdims=True))
                fade = jnp.exp(old - new)
                weight = jnp.exp(score - new)
                top_ref[p : p + 1, :] = new
                den_ref[p : p + 1, :] = den_ref[p : p + 1, :] * fade + jnp.sum(
                    weight, 0, keepdims=True
                )
                both = dot(val_ref[pl.ds(row, BLOCK), cols], weight.astype(BF16), (0, 0))
                for half in range(2):
                    at_rows = slice(p * 128 + half * HEAD_DIM, p * 128 + (half + 1) * HEAD_DIM)
                    at_cols = slice(half * lat_rows, (half + 1) * lat_rows)
                    num_ref[at_rows, :] = (
                        num_ref[at_rows, :] * fade[:, at_cols]
                        + both[half * HEAD_DIM : (half + 1) * HEAD_DIM, at_cols]
                    )
            return carry

        lax.fori_loop(0, blocks, block_step, 0)
        for h in range(HEADS):
            piece, i = piece_of(h)
            p, half = h // 2, h % 2
            at_cols = slice(half * lat_rows, (half + 1) * lat_rows)
            part_ref[s, piece, i * HEAD_DIM : (i + 1) * HEAD_DIM, :] = num_ref[
                h * HEAD_DIM : (h + 1) * HEAD_DIM, :
            ]
            part_ref[s, piece, NUM_ROWS + i : NUM_ROWS + i + 1, :] = top_ref[p : p + 1, at_cols]
            part_ref[s, piece, NUM_ROWS + 8 + i : NUM_ROWS + 9 + i, :] = den_ref[
                p : p + 1, at_cols
            ]
        return carry

    lax.fori_loop(0, samples, sample_step, 0)


def vmem():
    return pl.BlockSpec(memory_space=pltpu.VMEM)


def smem():
    return pl.BlockSpec(memory_space=pltpu.SMEM)


def attend_forward(ids, tokens, latents, gain_q, wq, gain_t, wk, wv):
    samples, lat_rows, width = latents.shape
    rows = tokens.shape[0]
    sds = jax.ShapeDtypeStruct
    return pl.pallas_call(
        forward_kernel,
        name="attend_forward",
        out_shape=(
            sds((samples, PIECES, PIECE_ROWS, lat_rows), F32),
            sds((rows + BLOCK, width), BF16),
            sds((rows + BLOCK, width), BF16),
            sds((rows, width), BF16),
            sds((samples, PAIRS, 128, 2 * lat_rows), BF16),
            sds((samples * lat_rows, width), BF16),
            sds((rows, 128), F32),
            sds((2 * samples,), jnp.int32),
        ),
        in_specs=[vmem()] * 8,
        out_specs=(vmem(),) * 7 + (smem(),),
        scratch_shapes=[
            pltpu.VMEM((rows, width), BF16),
            pltpu.VMEM((8, rows), F32),
            pltpu.VMEM((8, 2 * lat_rows), F32),
            pltpu.VMEM((8, 2 * lat_rows), F32),
            pltpu.VMEM((width, lat_rows), F32),
        ],
        compiler_params=pltpu.CompilerParams(vmem_limit_bytes=VMEM_BYTES),
    )(
        ids.reshape(1, rows),
        tokens,
        latents.reshape(samples * lat_rows, width),
        gain_q.reshape(1, width),
        wq,
        gain_t.reshape(1, width),
        wk,
        wv,
    )


def backward_kernel(
    bounds_ref,
    lat_ref,
    key_ref,
    val_ref,
    query_ref,
    normed_ref,
    msg_ref,
    gain_q_ref,
    wq_ref,
    dkv_ref,
    dlat_ref,
    dgain_ref,
    dwq_ref,
    dk_ref,
    dv_ref,
    grad_ref,
    dquery_ref,
    turn_ref,
    stat_ref,
):
    samples = query_ref.shape[0]
    rows = dkv_ref.shape[1]
    lat_rows = 128
    step = 256
    width = dwq_ref.shape[0]
    for r in range(0, rows + BLOCK, step):
        dk_ref[r : r + step, :] = jnp.zeros((step, dk_ref.shape[1]), F32)
        dv_ref[r : r + step, :] = jnp.zeros((step, dv_ref.shape[1]), F32)
    grad_ref[...] = jnp.zeros_like(grad_ref)
    dgain_ref[...] = jnp.zeros_like(dgain_ref)

    def sample_step(s, carry):
        start = bounds_ref[s]
        total = bounds_ref[samples + s]
        base = lax.div(start, 16) * 16
        blocks = jnp.where(total > 0, lax.div(start + total - base + BLOCK - 1, BLOCK), 0)
        turn_ref[...] = jnp.zeros_like(turn_ref)
        for h in range(HEADS):
            p, half = h // 2, h % 2
            grad_ref[
                p,
                half * HEAD_DIM : (half + 1) * HEAD_DIM,
                half * lat_rows : (half + 1) * lat_rows,
            ] = msg_ref[s, h * HEAD_DIM : (h + 1) * HEAD_DIM, :].astype(BF16)

            stat_ref[p : p + 1, half * lat_rows : (half + 1) * lat_rows] = msg_ref[
                s, width + h : width + h + 1, :
            ]
            stat_ref[8 + p : 9 + p, half * lat_rows : (half + 1) * lat_rows] = msg_ref[
                s, width + 16 + h : width + 17 + h, :
            ]

        def block_step(b, carry):
            row = pl.multiple_of(base + b * BLOCK, 16)
            index = lax.broadcasted_iota(jnp.int32, (BLOCK, 2 * lat_rows), 0) + row
            inside = (index >= start) & (index < start + total)
            at = pl.ds(row, BLOCK)
            for p in range(PAIRS):
                cols = slice(p * 128, (p + 1) * 128)
                key = key_ref[at, cols]
                query = query_ref[s, p]
                grad = grad_ref[p]
                score = dot(key, query)
                weight = jnp.where(inside, jnp.exp(score - stat_ref[p : p + 1, :]), 0.0)
                dprob = dot(val_ref[at, cols], grad)
                dscore = (weight * (dprob - stat_ref[8 + p : 9 + p, :])).astype(BF16)
                dv_ref[at, cols] += dot(weight.astype(BF16), grad, (1, 1))
                dk_ref[at, cols] += dot(dscore, query, (1, 1))
                both = dot(key, dscore, (0, 0))
                for half in range(2):
                    turn_ref[
                        p * 128 + half * HEAD_DIM : p * 128 + (half + 1) * HEAD_DIM, :
                    ] += both[
                        half * HEAD_DIM : (half + 1) * HEAD_DIM,
                        half * lat_rows : (half + 1) * lat_rows,
                    ]
            return carry

        lax.fori_loop(0, blocks, block_step, 0)
        at = pl.ds(pl.multiple_of(s * lat_rows, lat_rows), lat_rows)
        dquery = (turn_ref[...].T * 0.125).astype(BF16)
        dquery_ref[at, :] = dquery
        unit, inv = norm_parts(lat_ref[at, :].astype(F32))
        dnormed = dot(dquery, wq_ref[...], (1, 1))
        dgain_ref[0:1, :] += jnp.sum(dnormed * unit, 0, keepdims=True)
        dlat_ref[at, :] = norm_back(unit, inv, gain_q_ref[...], dnormed)
        return carry

    lax.fori_loop(0, samples, sample_step, 0)
    for r in range(0, rows, step):
        dkv_ref[0, r : r + step, :] = dk_ref[r : r + step, :].astype(BF16)
        dkv_ref[1, r : r + step, :] = dv_ref[r : r + step, :].astype(BF16)
    for c in range(0, width, 256):
        dwq_ref[c : c + 256, :] = dot(dquery_ref[:, c : c + 256], normed_ref[...], (0, 0))


def attend_backward(bounds, latents, keys, values, query, normed, msg, gain_q, wq):
    samples, lat_rows, width = latents.shape
    rows = keys.shape[0] - BLOCK
    sds = jax.ShapeDtypeStruct
    return pl.pallas_call(
        backward_kernel,
        name="attend_backward",
        out_shape=(
            sds((2, rows, width), BF16),
            sds((samples * lat_rows, width), F32),
            sds((8, width), F32),
            sds((width, width), F32),
        ),
        in_specs=[smem()] + [vmem()] * 8,
        out_specs=(vmem(),) * 4,
        scratch_shapes=[
            pltpu.VMEM((rows + BLOCK, width), F32),
            pltpu.VMEM((rows + BLOCK, width), F32),
            pltpu.VMEM((PAIRS, 128, 2 * lat_rows), BF16),
            pltpu.VMEM((samples * lat_rows, width), BF16),
            pltpu.VMEM((width, lat_rows), F32),
            pltpu.VMEM((16, 2 * lat_rows), F32),
        ],
        compiler_params=pltpu.CompilerParams(vmem_limit_bytes=VMEM_BYTES),
    )(
        bounds,
        latents.reshape(samples * lat_rows, width),
        keys,
        values,
        query,
        normed,
        msg,
        gain_q.reshape(1, width),
        wq,
    )


MESH = pl.DeviceIdType.MESH


def merge(a_ref, b_ref, out_ref):
    a_tail, b_tail = a_ref[NUM_ROWS : NUM_ROWS + 8, :], b_ref[NUM_ROWS : NUM_ROWS + 8, :]
    top = jnp.maximum(a_tail, b_tail)
    a_fade, b_fade = jnp.exp(a_tail - top), jnp.exp(b_tail - top)
    den = a_ref[NUM_ROWS + 8 :, :] * a_fade + b_ref[NUM_ROWS + 8 :, :] * b_fade
    for i in range(PIECE_HEADS):
        at = slice(i * HEAD_DIM, (i + 1) * HEAD_DIM)
        out_ref[at, :] = (
            a_ref[at, :] * a_fade[i : i + 1, :] + b_ref[at, :] * b_fade[i : i + 1, :]
        )
    out_ref[NUM_ROWS : NUM_ROWS + 8, :] = top
    out_ref[NUM_ROWS + 8 :, :] = den


def gelu_parts(x):
    c = 0.7978845608028654
    square = x * x
    t = jnp.tanh(c * x * (1.0 + 0.044715 * square))
    half = 0.5 * (1.0 + t)
    slope = half + (0.5 * c) * x * (1.0 - t * t) * (1.0 + (3 * 0.044715) * square)
    return x * half, slope


def latent_kernel(
    part_ref,
    drop_ref,
    lat_ref,
    cot_ref,
    wo_hbm,
    gain_ref,
    wup_hbm,
    bup_ref,
    wdn_hbm,
    bdn_ref,
    msg_ref,
    res_ref,
    dmid_ref,
    a_ref,
    b_ref,
    att_ref,
    vec_ref,
    wo_ref,
    wup_ref,
    wdn_ref,
    pair_ref,
    own_ref,
    right_in,
    right_out,
    left_in,
    left_out,
    res_out,
    res_in,
    att_t_ref,
    mid_ref,
    acc_ref,
    dacc_ref,
    weight_sem,
    pair_send,
    pair_recv,
    right_send,
    right_recv,
    left_send,
    left_recv,
    msg_send,
    msg_recv,
    res_send,
    res_recv,
):
    samples = part_ref.shape[0]
    half = samples // 2
    lat_rows = 128
    width = lat_ref.shape[1]
    chunks = half * PIECES
    stream = lax.axis_index("stream")
    tok = lax.axis_index("tok")
    chips = lax.axis_size("tok") // 2
    core = lax.rem(tok, 2)
    chip = lax.div(tok, 2)
    partner = (stream, tok + 1 - 2 * core)
    right = (stream, tok + 2)
    left = (stream, tok - 2)
    has_right = chip < chips - 1
    has_left = chip > 0

    barrier = pltpu.get_barrier_semaphore()
    pl.semaphore_signal(barrier, inc=1, device_id=partner, device_id_type=MESH)

    @pl.when(has_right)
    def _():
        pl.semaphore_signal(barrier, inc=1, device_id=right, device_id_type=MESH)

    @pl.when(has_left)
    def _():
        pl.semaphore_signal(barrier, inc=1, device_id=left, device_id_type=MESH)

    weights = [
        pltpu.make_async_copy(src, dst, weight_sem.at[i])
        for i, (src, dst) in enumerate(((wo_hbm, wo_ref), (wup_hbm, wup_ref), (wdn_hbm, wdn_ref)))
    ]
    for copy in weights:
        copy.start()
    pl.semaphore_wait(
        barrier, 1 + has_right.astype(jnp.int32) + has_left.astype(jnp.int32)
    )

    def pair_copy(i):
        j, q = lax.div(i, PIECES), lax.rem(i, PIECES)
        return pltpu.make_async_remote_copy(
            src_ref=part_ref.at[(1 - core) * half + j, q],
            dst_ref=pair_ref.at[i],
            send_sem=pair_send.at[i],
            recv_sem=pair_recv.at[i],
            device_id=partner,
            device_id_type=MESH,
        )

    def right_copy(i):
        return pltpu.make_async_remote_copy(
            src_ref=right_out.at[i],
            dst_ref=right_in.at[i],
            send_sem=right_send.at[i],
            recv_sem=right_recv.at[i],
            device_id=right,
            device_id_type=MESH,
        )

    def left_copy(i):
        return pltpu.make_async_remote_copy(
            src_ref=left_out.at[i],
            dst_ref=left_in.at[i],
            send_sem=left_send.at[i],
            recv_sem=left_recv.at[i],
            device_id=left,
            device_id_type=MESH,
        )

    def msg_copy(j):
        at = core * half + j
        return pltpu.make_async_remote_copy(
            src_ref=msg_ref.at[at],
            dst_ref=msg_ref.at[at],
            send_sem=msg_send.at[j],
            recv_sem=msg_recv.at[j],
            device_id=partner,
            device_id_type=MESH,
        )

    def msg_arrival(j):
        at = (1 - core) * half + j
        return pltpu.make_async_remote_copy(
            src_ref=msg_ref.at[at],
            dst_ref=msg_ref.at[at],
            send_sem=msg_send.at[j],
            recv_sem=msg_recv.at[j],
            device_id=partner,
            device_id_type=MESH,
        )

    def res_copy(j):
        return pltpu.make_async_remote_copy(
            src_ref=res_out.at[j],
            dst_ref=res_in.at[j],
            send_sem=res_send.at[j],
            recv_sem=res_recv.at[j],
            device_id=partner,
            device_id_type=MESH,
        )

    def start_pair(i, carry):
        pair_copy(i).start()
        return carry

    lax.fori_loop(0, chunks, start_pair, 0)

    drop = drop_ref[...].astype(F32)
    scale_all = drop * drop.shape[1] / jnp.sum(drop, 1, keepdims=True)
    drop_lane = lax.broadcasted_iota(jnp.int32, drop.shape, 1)
    vec_ref[...] = jnp.zeros_like(vec_ref)

    def mlp(j, q):
        sample = core * half + j
        rows = pl.ds(pl.multiple_of(sample * lat_rows, lat_rows), lat_rows)
        mine = pl.ds(pl.multiple_of(j * lat_rows, lat_rows), lat_rows)
        scale = jnp.sum(
            jnp.where(drop_lane == stream * samples + sample, scale_all, 0.0), 1, keepdims=True
        )

        @pl.when(q == 0)
        def _():
            for h in range(HEADS):
                piece, i = piece_of(h)
                at = j * PIECES + piece
                den = own_ref[at, NUM_ROWS + 8 + i : NUM_ROWS + 9 + i, :]
                att_t_ref[h * HEAD_DIM : (h + 1) * HEAD_DIM, :] = own_ref[
                    at, i * HEAD_DIM : (i + 1) * HEAD_DIM, :
                ] * (1.0 / den)
            att = att_t_ref[...].T.astype(BF16)
            att_ref[mine, :] = att
            mid = lat_ref[rows, :].astype(F32) + scale * dot(att, wo_ref[...])
            mid_ref[...] = mid
            unit, _ = norm_parts(mid)
            a_ref[0, mine, :] = (unit * gain_ref[...]).astype(BF16)
            dm = (scale * cot_ref[rows, :].astype(F32)).astype(BF16)
            a_ref[1, mine, :] = dm
            vec_ref[1:2, :width] += jnp.sum(dm.astype(F32), 0, keepdims=True)
            acc_ref[...] = jnp.broadcast_to(bdn_ref[...], acc_ref.shape)
            dacc_ref[...] = jnp.zeros_like(dacc_ref)

        span = wup_ref.shape[1] // PIECES
        cols = pl.ds(pl.multiple_of(q * span, 128), span)
        pre = dot(a_ref[0, mine, :], wup_ref[:, cols]) + bup_ref[:, cols]
        active, slope = gelu_parts(pre)
        hidden = active.astype(BF16)
        b_ref[1, mine, cols] = hidden
        acc_ref[...] += dot(hidden, wdn_ref[cols, :])
        dpre = (slope * dot(a_ref[1, mine, :], wdn_ref[cols, :], (1, 1))).astype(BF16)
        b_ref[0, mine, cols] = dpre
        vec_ref[0:1, cols] += jnp.sum(dpre.astype(F32), 0, keepdims=True)
        dacc_ref[...] += dot(dpre, wup_ref[:, cols], (1, 1))

        @pl.when(q == PIECES - 1)
        def _():
            mid = mid_ref[...]
            res = (mid + scale * acc_ref[...]).astype(BF16)
            res_ref[rows, :] = res
            res_out[j] = res.astype(F32)
            res_copy(j).start()
            unit, inv = norm_parts(mid)
            dhn = dacc_ref[...]
            vec_ref[2:3, :width] += jnp.sum(dhn * unit, 0, keepdims=True)
            dmid = cot_ref[rows, :].astype(F32) + norm_back(unit, inv, gain_ref[...], dhn)
            dmid_ref[mine, :] = dmid
            da = (scale * dmid).astype(BF16)
            a_ref[2, mine, :] = da
            datt_t = dot(wo_ref[...], da, (1, 1)).astype(BF16).astype(F32)
            msg_ref[sample, width:, :] = jnp.zeros((MSG_ROWS - width, lat_rows), F32)
            for h in range(HEADS):
                piece, i = piece_of(h)
                at = j * PIECES + piece
                inverse = 1.0 / own_ref[at, NUM_ROWS + 8 + i : NUM_ROWS + 9 + i, :]
                span_h = slice(h * HEAD_DIM, (h + 1) * HEAD_DIM)
                one = datt_t[span_h]
                msg_ref[sample, span_h, :] = (one * inverse).astype(BF16).astype(F32)
                delta = jnp.sum(one * att_t_ref[span_h, :], 0, keepdims=True) * inverse
                msg_ref[sample, width + h : width + h + 1, :] = own_ref[
                    at, NUM_ROWS + i : NUM_ROWS + i + 1, :
                ]
                msg_ref[sample, width + 16 + h : width + 17 + h, :] = delta
            msg_copy(j).start()

    def step(t, carry):
        @pl.when(t < chunks)
        def _():
            pair_copy(t).wait_recv()
            j, q = lax.div(t, PIECES), lax.rem(t, PIECES)
            merge(part_ref.at[core * half + j, q], pair_ref.at[t], own_ref.at[t])

        r = t - LAG * chip

        @pl.when((r >= 0) & (r < chunks))
        def _():
            @pl.when(has_left)
            def _():
                right_copy(r).wait_recv()
                merge(own_ref.at[r], right_in.at[r], right_out.at[r])

            @pl.when(jnp.logical_not(has_left))
            def _():
                right_out[r] = own_ref[r]

            @pl.when(has_right)
            def _():
                right_copy(r).start()

        u = t - LAG * (chips - 1 - chip)

        @pl.when((u >= 0) & (u < chunks))
        def _():
            @pl.when(has_right)
            def _():
                left_copy(u).wait_recv()

            @pl.when(has_left)
            def _():
                @pl.when(has_right)
                def _():
                    merge(own_ref.at[u], left_in.at[u], left_out.at[u])

                @pl.when(jnp.logical_not(has_right))
                def _():
                    left_out[u] = own_ref[u]

                left_copy(u).start()

        w = t - LAG * jnp.maximum(chip, chips - 1 - chip)

        @pl.when((w >= 0) & (w < chunks))
        def _():
            @pl.when(has_right)
            def _():
                merge(right_out.at[w], left_in.at[w], own_ref.at[w])

            @pl.when(jnp.logical_not(has_right))
            def _():
                own_ref[w] = right_out[w]

        m = w - (PIECES - 1)

        @pl.when(m == 0)
        def _():
            for copy in weights:
                copy.wait()

        @pl.when((m >= 0) & (m < chunks))
        def _():
            mlp(lax.div(m, PIECES), lax.rem(m, PIECES))

        return carry

    lax.fori_loop(0, chunks + LAG * (chips - 1) + PIECES - 1, step, 0)

    def finish_chunk(i, carry):
        pair_copy(i).wait_send()

        @pl.when(has_right)
        def _():
            right_copy(i).wait_send()

        @pl.when(has_left)
        def _():
            left_copy(i).wait_send()

        return carry

    lax.fori_loop(0, chunks, finish_chunk, 0)

    def finish_sample(j, carry):
        res_copy(j).wait_recv()
        other = (1 - core) * half + j
        rows = pl.ds(pl.multiple_of(other * lat_rows, lat_rows), lat_rows)
        res_ref[rows, :] = res_in[j].astype(BF16)
        res_copy(j).wait_send()
        msg_copy(j).wait_send()
        msg_arrival(j).wait_recv()
        return carry

    lax.fori_loop(0, half, finish_sample, 0)


def anywhere():
    return pl.BlockSpec(memory_space=pl.ANY)


def latent_block(part, drop_mask, latents, cotangent, wo, gain, wup, bup, wdn, bdn):
    samples, lat_rows, width = latents.shape
    half = samples // 2
    chunks = half * PIECES
    hidden = wup.shape[1]
    sds = jax.ShapeDtypeStruct
    chunk = lambda: pltpu.VMEM((chunks, PIECE_ROWS, lat_rows), F32)
    dma = pltpu.SemaphoreType.DMA
    return pl.pallas_call(
        latent_kernel,
        name="latent_block",
        out_shape=(
            sds((samples, MSG_ROWS, lat_rows), F32),
            sds((samples * lat_rows, width), BF16),
            sds((half * lat_rows, width), F32),
            sds((3, half * lat_rows, width), BF16),
            sds((2, half * lat_rows, hidden), BF16),
            sds((half * lat_rows, width), BF16),
            sds((8, hidden), F32),
        ),
        in_specs=[
            vmem(),
            vmem(),
            vmem(),
            vmem(),
            anywhere(),
            vmem(),
            anywhere(),
            vmem(),
            anywhere(),
            vmem(),
        ],
        out_specs=(vmem(),) * 7,
        scratch_shapes=[
            pltpu.VMEM(wo.shape, BF16),
            pltpu.VMEM(wup.shape, BF16),
            pltpu.VMEM(wdn.shape, BF16),
            chunk(),
            chunk(),
            chunk(),
            chunk(),
            chunk(),
            chunk(),
            pltpu.VMEM((half, lat_rows, width), F32),
            pltpu.VMEM((half, lat_rows, width), F32),
            pltpu.VMEM((width, lat_rows), F32),
            pltpu.VMEM((lat_rows, width), F32),
            pltpu.VMEM((lat_rows, width), F32),
            pltpu.VMEM((lat_rows, width), F32),
            dma((3,)),
            dma((chunks,)),
            dma((chunks,)),
            dma((chunks,)),
            dma((chunks,)),
            dma((chunks,)),
            dma((chunks,)),
            dma((half,)),
            dma((half,)),
            dma((half,)),
            dma((half,)),
        ],
        compiler_params=pltpu.CompilerParams(
            vmem_limit_bytes=VMEM_BYTES, collective_id=1, has_side_effects=True
        ),
    )(
        part,
        drop_mask.reshape(1, -1),
        latents.reshape(samples * lat_rows, width),
        cotangent.reshape(samples * lat_rows, width),
        wo,
        gain.reshape(1, width),
        wup,
        bup.reshape(1, hidden),
        wdn,
        bdn.reshape(1, width),
    )


ZROWS = 32
SUBS = 2


def gradient_kernel(
    dlat_hbm,
    dmid_ref,
    latent_hbm,
    dwq_ref,
    vec_ref,
    dgain_q_ref,
    place_ref,
    tok_ref,
    tsort_ref,
    dkv_ref,
    gain_t_ref,
    wk_ref,
    wv_ref,
    dlat_out,
    gather_out,
    kv_out,
    query_out,
    small_out,
    dtok_ref,
    line_ref,
    right_ref,
    left_ref,
    dmine_ref,
    wide_ref,
    wide_one,
    wide_two,
    send_ref,
    mine_ref,
    pair_ref,
    one_ref,
    two_ref,
    small_ref,
    load_sem,
    wide_load_sem,
    dpair_send,
    dpair_recv,
    right_send,
    right_recv,
    left_send,
    left_recv,
    back_send,
    back_recv,
    back_local,
    wide_one_send,
    wide_one_recv,
    wide_two_send,
    wide_two_recv,
    wide_z_send,
    wide_z_recv,
    wide_core_send,
    wide_core_recv,
    wide_local,
    pair_send,
    pair_recv,
    one_send,
    one_recv,
    two_send,
    two_recv,
    spread_send,
    spread_recv,
    share_send,
    share_recv,
    query_send,
    query_recv,
    keep_local,
):
    width = tok_ref.shape[1]
    rows = tok_ref.shape[0]
    lat_chunks = dmine_ref.shape[0]
    all_chunks = line_ref.shape[0]
    kv_rows = send_ref.shape[2]
    q_rows = query_out.shape[2]
    mix = kv_rows + q_rows
    half_chunks = (all_chunks - lat_chunks) // 2
    kv_chunks = kv_rows // ZROWS
    wide_half = wide_ref.shape[2]
    sub_rows = wide_half // SUBS

    stream = lax.axis_index("stream")
    tok = lax.axis_index("tok")
    chips = lax.axis_size("tok") // 2
    core = lax.rem(tok, 2)
    chip = lax.div(tok, 2)
    other = 1 - core
    parity = lax.rem(chip, 2)
    flip_x = stream + 1 - 2 * lax.rem(stream, 2)
    flip_y = lax.rem(stream + 2, 4)
    flip_xy = 3 - stream
    partner = (stream, tok + 1 - 2 * core)
    right = (stream, tok + 2)
    left = (stream, tok - 2)
    beside = (stream, tok + 2 - 4 * parity)
    near = ((flip_x, tok), (flip_y, tok))
    first = (flip_x, flip_y)
    has_right = chip < chips - 1
    has_left = chip > 0

    barrier = pltpu.get_barrier_semaphore()
    for target in (partner,) + near:
        pl.semaphore_signal(barrier, inc=1, device_id=target, device_id_type=MESH)

    @pl.when(has_right)
    def _():
        pl.semaphore_signal(barrier, inc=1, device_id=right, device_id_type=MESH)

    @pl.when(has_left)
    def _():
        pl.semaphore_signal(barrier, inc=1, device_id=left, device_id_type=MESH)

    def remote(src, dst, send, recv, target):
        return pltpu.make_async_remote_copy(
            src_ref=src,
            dst_ref=dst,
            send_sem=send,
            recv_sem=recv,
            device_id=target,
            device_id_type=MESH,
        )

    load = pltpu.make_async_copy(dlat_hbm.at[core], dmine_ref, load_sem)
    load.start()
    wide_loads = []
    for h in range(2):
        for n, block in enumerate((stream, first[1 - h])):
            copy = pltpu.make_async_copy(
                latent_hbm.at[block, pl.ds(h * wide_half, wide_half)],
                wide_ref.at[h, n],
                wide_load_sem.at[2 * h + n],
            )
            copy.start()
            wide_loads.append(copy)
    pl.semaphore_wait(barrier, 3 + has_right.astype(jnp.int32) + has_left.astype(jnp.int32))

    def dpair_copy(i):
        return remote(
            dlat_hbm.at[other, i], line_ref.at[i], dpair_send.at[i], dpair_recv.at[i], partner
        )

    def start_dpair(i, carry):
        dpair_copy(i).start()
        return carry

    lax.fori_loop(0, lat_chunks, start_dpair, 0)

    def wide_one_copy(h, n, sub):
        block = (first[h], flip_xy)[n]
        at = pl.ds(h * wide_half + sub * sub_rows, sub_rows)
        return remote(
            latent_hbm.at[block, at],
            wide_one.at[h, n, pl.ds(sub * sub_rows, sub_rows)],
            wide_one_send.at[h, n, sub],
            wide_one_recv.at[h, n, sub],
            near[h],
        )

    def wide_two_copy(h, sub):
        at = pl.ds(sub * sub_rows, sub_rows)
        return remote(
            wide_ref.at[h, 1, at],
            wide_two.at[h, at],
            wide_two_send.at[h, sub],
            wide_two_recv.at[h, sub],
            near[1 - h],
        )

    def gather_at(c, e, h, sub):
        return gather_out.at[c, e, pl.ds(h * wide_half + sub * sub_rows, sub_rows)]

    def wide_z_copy(h, sub):
        return remote(
            wide_ref.at[h, 0, pl.ds(sub * sub_rows, sub_rows)],
            gather_at(core, parity, h, sub),
            wide_z_send.at[h, sub],
            wide_z_recv.at[h, sub],
            beside,
        )

    def wide_z_arrival(h, sub):
        return remote(
            wide_ref.at[h, 0, pl.ds(sub * sub_rows, sub_rows)],
            gather_at(core, 1 - parity, h, sub),
            wide_z_send.at[h, sub],
            wide_z_recv.at[h, sub],
            beside,
        )

    def wide_core_copy(far, h, sub):
        if far:
            src = gather_at(core, 1 - parity, h, sub)
            dst = gather_at(core, 1 - parity, h, sub)
        else:
            src = wide_ref.at[h, 0, pl.ds(sub * sub_rows, sub_rows)]
            dst = gather_at(core, parity, h, sub)
        return remote(
            src, dst, wide_core_send.at[far, h, sub], wide_core_recv.at[far, h, sub], partner
        )

    def wide_core_arrival(far, h, sub):
        place = gather_at(other, 1 - parity if far else parity, h, sub)
        return remote(
            place, place, wide_core_send.at[far, h, sub], wide_core_recv.at[far, h, sub], partner
        )

    def wide_keep(h, sub):
        return pltpu.make_async_copy(
            wide_ref.at[h, 0, pl.ds(sub * sub_rows, sub_rows)],
            gather_at(core, parity, h, sub),
            wide_local.at[h, sub],
        )

    for sub in range(SUBS):
        for h in range(2):
            for n in range(2):
                wide_one_copy(h, n, sub).start()

    def wide_event_one(sub):
        at = slice(sub * sub_rows, (sub + 1) * sub_rows)
        for h in range(2):
            for n in range(2):
                wide_one_copy(h, n, sub).wait_recv()
            wide_ref[h, 1, at, :] += wide_one[h, 1, at, :]
            wide_two_copy(h, sub).start()
            wide_ref[h, 0, at, :] += wide_one[h, 0, at, :]

    def wide_event_two(sub):
        at = slice(sub * sub_rows, (sub + 1) * sub_rows)
        for h in range(2):
            wide_two_copy(h, sub).wait_recv()
            wide_ref[h, 0, at, :] += wide_two[h, at, :]
            wide_z_copy(h, sub).start()
            wide_core_copy(0, h, sub).start()
            wide_keep(h, sub).start()

    def wide_event_three(sub):
        for h in range(2):
            wide_z_arrival(h, sub).wait_recv()
            wide_core_copy(1, h, sub).start()

    turned = tsort_ref[...].T
    share = width // 4
    for block in range(4):
        at = slice(block * share, (block + 1) * share)
        product = dot(turned[at], dkv_ref[other])
        for h in range(2):
            send_ref[h, block] = product[h * kv_rows : (h + 1) * kv_rows]

    def pair_copies():
        out = []
        for h in range(2):
            out.append(
                remote(
                    send_ref.at[h],
                    pair_ref.at[h, :, pl.ds(0, kv_rows)],
                    pair_send.at[h],
                    pair_recv.at[h],
                    partner,
                )
            )
            out.append(
                remote(
                    dwq_ref.at[:, other, h],
                    pair_ref.at[h, :, pl.ds(kv_rows, q_rows)],
                    pair_send.at[2 + h],
                    pair_recv.at[2 + h],
                    partner,
                )
            )
        out.append(
            remote(
                small_ref,
                pair_ref.at[0, :, pl.ds(mix, 16)],
                pair_send.at[4],
                pair_recv.at[4],
                partner,
            )
        )
        return out

    pairs = pair_copies()
    for copy in pairs[:4]:
        copy.start()

    for block in range(4):
        at = slice(block * share, (block + 1) * share)
        product = dot(turned[at], dkv_ref[core])
        for h in range(2):
            piece = product[h * kv_rows : (h + 1) * kv_rows]
            mine_ref[h, block, :kv_rows, :] = piece
            mine_ref[h, block, kv_rows:mix, :] = dwq_ref[block, core, h]
    mine_ref[1, :, mix:, :] = jnp.zeros((4, 16, width), F32)

    here = (chip == 0).astype(F32)

    token_step = 128
    small_ref[...] = jnp.zeros_like(small_ref)

    def token_part(i):
        at = pl.ds(pl.multiple_of(i * token_step, token_step), token_step)
        target = lax.broadcasted_iota(jnp.int32, (token_step, rows), 1).astype(F32)
        pick = jnp.where(target == place_ref[at, 0:1], 1.0, 0.0).astype(BF16)
        dkey = dot(pick, dkv_ref[0]).astype(BF16)
        dval = dot(pick, dkv_ref[1]).astype(BF16)
        dnormed = dot(dkey, wk_ref[...], (1, 1)) + dot(dval, wv_ref[...], (1, 1))
        unit, inv = norm_parts(tok_ref[at, :].astype(F32))
        small_ref[0, 4:5, :] += jnp.sum(dnormed * unit, 0, keepdims=True)
        dtok_ref[at, :] = norm_back(unit, inv, gain_t_ref[...], dnormed)

    def small_start():
        for block in range(4):
            small_ref[block, 0:1, :] = vec_ref[0:1, block * width : (block + 1) * width] * here
            small_ref[block, 1:2, :] = dgain_q_ref[0:1, :]
            small_ref[block, 2:3, :] = vec_ref[2:3, :width] * here
            small_ref[block, 3:4, :] = vec_ref[1:2, :width] * here
            if block:
                small_ref[block, 4:5, :] = small_ref[0, 4:5, :]
        pairs[4].start()

    def one_copy(h, n):
        block = (first[h], flip_xy)[n]
        return remote(
            mine_ref.at[h, block], one_ref.at[h, n], one_send.at[h, n], one_recv.at[h, n], near[h]
        )

    def two_copy(h):
        return remote(
            mine_ref.at[h, first[1 - h]], two_ref.at[h], two_send.at[h], two_recv.at[h], near[1 - h]
        )

    def pair_event():
        for copy in pairs:
            copy.wait_recv()
        for h in range(2):
            for block in range(4):
                mine_ref[h, block, :mix, :] += pair_ref[h, block, :mix, :]
                if h == 0:
                    mine_ref[h, block, mix:, :] = small_ref[block] + pair_ref[h, block, mix:, :]
        for h in range(2):
            for n in range(2):
                one_copy(h, n).start()

    def one_event():
        for h in range(2):
            for n in range(2):
                one_copy(h, n).wait_recv()
            mine_ref[h, first[1 - h]] += one_ref[h, 1]
            two_copy(h).start()

    def two_event():
        for h in range(2):
            two_copy(h).wait_recv()
            total = mine_ref[h, stream] + one_ref[h, 0] + two_ref[h]
            for k in range(half_chunks):
                line_ref[lat_chunks + h * half_chunks + k] = total[k * ZROWS : (k + 1) * ZROWS]

    def right_copy(i):
        return remote(right_ref.at[i], right_ref.at[i], right_send.at[i], right_recv.at[i], right)

    def left_copy(i):
        return remote(left_ref.at[i], left_ref.at[i], left_send.at[i], left_recv.at[i], left)

    def back_copy(i):
        return remote(
            line_ref.at[i], dlat_out.at[core, i], back_send.at[i], back_recv.at[i], partner
        )

    def back_arrival(i):
        return remote(
            line_ref.at[i], dlat_out.at[other, i], back_send.at[i], back_recv.at[i], partner
        )

    def back_keep(i):
        return pltpu.make_async_copy(line_ref.at[i], dlat_out.at[core, i], back_local.at[i])

    def line_step(t):
        @pl.when(t < lat_chunks)
        def _():
            dpair_copy(t).wait_recv()
            line_ref[t] += dmine_ref[t] + dmid_ref[t] * here

        r = t - LAG * chip

        @pl.when((r >= 0) & (r < all_chunks))
        def _():
            @pl.when(has_left)
            def _():
                right_copy(r).wait_recv()
                right_ref[r] += line_ref[r]

            @pl.when(jnp.logical_not(has_left))
            def _():
                right_ref[r] = line_ref[r]

            @pl.when(has_right)
            def _():
                right_copy(r).start()

        u = t - LAG * (chips - 1 - chip)

        @pl.when((u >= 0) & (u < all_chunks))
        def _():
            @pl.when(has_right)
            def _():
                left_copy(u).wait_recv()
                left_ref[u] += line_ref[u]

            @pl.when(jnp.logical_not(has_right))
            def _():
                left_ref[u] = line_ref[u]

            @pl.when(has_left)
            def _():
                left_copy(u).start()

        w = t - LAG * jnp.maximum(chip, chips - 1 - chip)

        @pl.when((w >= 0) & (w < all_chunks))
        def _():
            line_ref[w] = right_ref[w] + left_ref[w] - line_ref[w]

            @pl.when(w < lat_chunks)
            def _():
                back_copy(w).start()
                back_keep(w).start()

    def own_piece(h):
        return line_ref.at[pl.ds(lat_chunks + h * half_chunks, kv_chunks)]

    def spread_one(h):
        return remote(
            own_piece(h),
            kv_out.at[core, stream, h],
            spread_send.at[0, h],
            spread_recv.at[0, h],
            near[1 - h],
        )

    def spread_two(h, n):
        block = (stream, first[1 - h])[n]
        src = own_piece(h) if n == 0 else kv_out.at[core, block, h]
        return remote(
            src,
            kv_out.at[core, block, h],
            spread_send.at[1 + n, h],
            spread_recv.at[1 + n, h],
            near[h],
        )

    def spread_one_arrival(h):
        place = kv_out.at[core, first[1 - h], h]
        return remote(
            place, place, spread_send.at[0, h], spread_recv.at[0, h], near[1 - h]
        )

    def spread_two_arrival(h, n):
        place = kv_out.at[core, (first[h], flip_xy)[n], h]
        return remote(place, place, spread_send.at[1 + n, h], spread_recv.at[1 + n, h], near[h])

    def block_of(h, k):
        return (stream, first[1 - h], first[h], flip_xy)[k]

    def share_copy(h, k):
        block = block_of(h, k)
        src = own_piece(h) if k == 0 else kv_out.at[core, block, h]
        return remote(
            src, kv_out.at[core, block, h], share_send.at[h, k], share_recv.at[h, k], partner
        )

    def share_arrival(h, k):
        place = kv_out.at[other, block_of(h, k), h]
        return remote(place, place, share_send.at[h, k], share_recv.at[h, k], partner)

    def kv_keep(h):
        return pltpu.make_async_copy(own_piece(h), kv_out.at[core, stream, h], keep_local.at[h])

    def query_piece(h):
        return mine_ref.at[h, stream, pl.ds(kv_rows, q_rows)]

    def query_copy(h):
        return remote(
            query_piece(h),
            query_out.at[core, h],
            query_send.at[h],
            query_recv.at[h],
            partner,
        )

    def query_arrival(h):
        return remote(
            query_piece(h),
            query_out.at[other, h],
            query_send.at[h],
            query_recv.at[h],
            partner,
        )

    def query_keep(h):
        return pltpu.make_async_copy(query_piece(h), query_out.at[core, h], keep_local.at[2 + h])

    def spread_event(h):
        spread_one(h).start()
        spread_two(h, 0).start()
        share_copy(h, 0).start()
        kv_keep(h).start()
        flat = lat_chunks + h * half_chunks + kv_chunks
        for k in range(0, q_rows, 16):
            at = flat * ZROWS + kv_rows * 0 + k
            chunk, row = at // ZROWS, at % ZROWS
            mine_ref[h, stream, kv_rows + k : kv_rows + k + 16, :] = line_ref[
                chunk, row : row + 16, :
            ]
        query_copy(h).start()
        query_keep(h).start()
        if h == 0:
            at = flat * ZROWS + q_rows
            chunk, row = at // ZROWS, at % ZROWS
            small_out[...] = line_ref[chunk, row : row + 16, :]

    tail = LAG * (chips - 1)
    ready = lambda h: lat_chunks + (h + 1) * half_chunks - 1 + tail
    events = {}

    def at_tick(tick, run):
        events.setdefault(tick, []).append(run)

    parts = rows // token_step
    for i in range(parts):
        at_tick(TOKEN_TICKS[i % len(TOKEN_TICKS)], functools.partial(token_part, i))
    at_tick(SMALL_TICK, small_start)
    at_tick(PAIR_TICK, pair_event)
    at_tick(ONE_TICK, one_event)
    at_tick(TWO_TICK, two_event)
    for sub in range(SUBS):
        at_tick(WIDE_ONE_TICKS[sub], functools.partial(wide_event_one, sub))
        at_tick(WIDE_TWO_TICKS[sub], functools.partial(wide_event_two, sub))
    load.wait()
    for copy in wide_loads:
        copy.wait()

    def step(t, carry):
        line_step(t)
        for tick in sorted(events):

            @pl.when(t == tick)
            def _(tick=tick):
                for run in events[tick]:
                    run()

        return carry

    lax.fori_loop(0, ready(0) + 1, step, 0)
    spread_event(0)
    lax.fori_loop(ready(0) + 1, ready(1) + 1, step, 0)
    spread_event(1)
    for sub in range(SUBS):
        wide_event_three(sub)
    for h in range(2):
        spread_one_arrival(h).wait_recv()
        spread_two(h, 1).start()
        share_copy(h, 1).start()
    for h in range(2):
        for n in range(2):
            spread_two_arrival(h, n).wait_recv()
            share_copy(h, 2 + n).start()

    def finish_lat(i, carry):
        dpair_copy(i).wait_send()
        back_copy(i).wait_send()
        back_arrival(i).wait_recv()
        back_keep(i).wait()
        return carry

    lax.fori_loop(0, lat_chunks, finish_lat, 0)

    def finish_line(i, carry):
        @pl.when(has_right)
        def _():
            right_copy(i).wait_send()

        @pl.when(has_left)
        def _():
            left_copy(i).wait_send()

        return carry

    lax.fori_loop(0, all_chunks, finish_line, 0)
    for copy in pairs:
        copy.wait_send()
    for h in range(2):
        for n in range(2):
            one_copy(h, n).wait_send()
            spread_two(h, n).wait_send()
        two_copy(h).wait_send()
        spread_one(h).wait_send()
        kv_keep(h).wait()
        query_copy(h).wait_send()
        query_arrival(h).wait_recv()
        query_keep(h).wait()
        for k in range(4):
            share_copy(h, k).wait_send()
            share_arrival(h, k).wait_recv()
        for sub in range(SUBS):
            for n in range(2):
                wide_one_copy(h, n, sub).wait_send()
                wide_core_copy(n, h, sub).wait_send()
                wide_core_arrival(n, h, sub).wait_recv()
            wide_two_copy(h, sub).wait_send()
            wide_z_copy(h, sub).wait_send()
            wide_keep(h, sub).wait()


def gradients(dlat, dmid, latent, dwq, vec, dgain_q, place, tokens, tsort, dkv, gain_t, wk, wv):
    rows, width = tokens.shape
    half = dlat.shape[0] // 2
    lat_chunks = half // ZROWS
    wide_rows, wide_cols = latent.shape[1:]
    share = width // 4
    kv_rows, q_rows = share // 2, share // 4
    block = kv_rows + q_rows + 16
    all_chunks = lat_chunks + 2 * block // ZROWS
    sds = jax.ShapeDtypeStruct
    dma = pltpu.SemaphoreType.DMA
    buf = lambda *shape: pltpu.VMEM(shape, F32)
    both = lambda *shape: [dma(shape), dma(shape)]
    return pl.pallas_call(
        gradient_kernel,
        name="gradients",
        out_shape=(
            sds((2, lat_chunks, ZROWS, width), F32),
            sds((2, 2, wide_rows, wide_cols), F32),
            sds((2, 4, 2, kv_rows // ZROWS, ZROWS, width), F32),
            sds((2, 2, q_rows, width), F32),
            sds((16, width), F32),
            sds((rows, width), F32),
        ),
        in_specs=[anywhere(), vmem(), anywhere()] + [vmem()] * 10,
        out_specs=(anywhere(),) * 4 + (vmem(),) * 2,
        scratch_shapes=[
            buf(all_chunks, ZROWS, width),
            buf(all_chunks, ZROWS, width),
            buf(all_chunks, ZROWS, width),
            buf(lat_chunks, ZROWS, width),
            buf(2, 2, wide_rows // 2, wide_cols),
            buf(2, 2, wide_rows // 2, wide_cols),
            buf(2, wide_rows // 2, wide_cols),
            buf(2, 4, kv_rows, width),
            buf(2, 4, block, width),
            buf(2, 4, block, width),
            buf(2, 2, block, width),
            buf(2, block, width),
            buf(4, 16, width),
            dma,
            dma((4,)),
        ]
        + both(lat_chunks)
        + both(all_chunks)
        + both(all_chunks)
        + both(lat_chunks)
        + [dma((lat_chunks,))]
        + both(2, 2, SUBS)
        + both(2, SUBS)
        + both(2, SUBS)
        + both(2, 2, SUBS)
        + [dma((2, SUBS))]
        + both(5)
        + both(2, 2)
        + both(2)
        + both(3, 2)
        + both(2, 4)
        + both(2)
        + [dma((4,))],
        compiler_params=pltpu.CompilerParams(
            vmem_limit_bytes=VMEM_BYTES, collective_id=2, has_side_effects=True
        ),
    )(
        dlat.reshape(2, lat_chunks, ZROWS, width),
        dmid.reshape(lat_chunks, ZROWS, width),
        latent,
        dwq.reshape(4, 2, 2, q_rows, width),
        vec,
        dgain_q,
        place,
        tokens,
        tsort,
        dkv,
        gain_t.reshape(1, width),
        wk,
        wv,
    )


def local(
    latents,
    tokens,
    token_sample,
    token_mask,
    drop_mask,
    gain_query,
    w_query,
    gain_token,
    w_key,
    w_value,
    w_out,
    gain_mlp,
    w_up,
    b_up,
    w_down,
    b_down,
    cotangent,
):
    samples, lat_rows, width = latents.shape
    group_index = lax.axis_index("stream")
    tok_index = lax.axis_index("tok")
    streams = lax.axis_size("stream")
    members = lax.axis_size("tok")
    ids = jnp.where(token_mask == 1, token_sample - group_index * samples, -1)
    part, keys, values, tsort, query, normed, place, bounds = attend_forward(
        ids, tokens, latents, gain_query, w_query, gain_token, w_key, w_value
    )
    msg, result, dmid, lefts, rights, attended, vec = latent_block(
        part, drop_mask, latents, cotangent, w_out, gain_mlp, w_up, b_up, w_down, b_down
    )
    result = result.reshape(latents.shape)

    core = lax.rem(tok_index, 2)
    parity = lax.rem(tok_index // 2, 2)
    half_rows = lefts.shape[1]
    cols = w_up.shape[1] // streams // 2
    rights = rights.reshape(2, half_rows, streams, 2, cols)
    rights = lax.dynamic_index_in_dim(rights, parity, 3, keepdims=False)
    attended = lax.dynamic_slice_in_dim(attended, parity * cols, cols, 1)
    grad_out = jnp.einsum("rd,re->de", lefts[2], attended, preferred_element_type=F32)
    grad_out = grad_out.reshape(streams, 2, -1, cols)

    def part(which):
        pick = lambda x: lax.dynamic_index_in_dim(x, which, 0, keepdims=False)
        wide = jnp.einsum(
            "rd,rsf->sdf", pick(lefts), pick(rights), preferred_element_type=F32
        )
        return jnp.concatenate(
            (wide, lax.dynamic_index_in_dim(grad_out, which, 1, keepdims=False)), 1
        )

    swap = [(i, i ^ 1) for i in range(members)]
    latent = part(core) + lax.ppermute(part(1 - core), "tok", swap)

    dkv, dlat, dgain_q, dwq = attend_backward(
        bounds, latents, keys, values, query, normed, msg, gain_query, w_query
    )
    d_latents, gather, kv, grad_query, small, d_tokens = gradients(
        dlat, dmid, latent, dwq, vec, dgain_q, place, tokens, tsort, dkv, gain_token, w_key, w_value
    )
    kv = kv.reshape(2, width, width)
    grad_up = jnp.transpose(gather[0, :, :width], (1, 0, 2)).reshape(width, 2 * cols)
    grad_down = jnp.transpose(gather[1, :, :width], (0, 2, 1)).reshape(2 * cols, width)
    grad_out = jnp.transpose(gather[:, :, width:], (1, 3, 0, 2)).reshape(width, -1)

    def own(x):
        size = x.shape[0] // streams
        return lax.dynamic_slice_in_dim(x, group_index * size, size, 0)

    return (
        result,
        d_latents.reshape(latents.shape),
        d_tokens,
        own(small[1]),
        grad_query.reshape(-1, width).T,
        small[4],
        kv[0],
        kv[1],
        grad_out,
        own(small[2]),
        grad_up,
        small[0],
        grad_down,
        own(small[3]),
    )


def solution(mesh):
    return jax.shard_map(
        local,
        mesh=mesh,
        in_specs=(
            P("stream", None, None),
            P(("stream", "tok"), None),
            P(("stream", "tok")),
            P(("stream", "tok")),
            P(),
            P(),
            P(),
            P(),
            P(),
            P(),
            P(),
            P(),
            P(),
            P(),
            P(),
            P(),
            P("stream", None, None),
        ),
        out_specs=(
            P("stream", None, None),
            P("stream", None, None),
            P(("stream", "tok"), None),
            P("stream"),
            P(None, "stream"),
            P(),
            P(),
            P(),
            P(None, "stream"),
            P("stream"),
            P(None, "stream"),
            P("stream"),
            P("stream", None),
            P("stream"),
        ),
        check_vma=False,
    )
```

```python
import functools

import jax
import jax.numpy as jnp
from jax import lax
from jax.experimental import pallas as pl
from jax.experimental.pallas import tpu as pltpu
from jax.sharding import PartitionSpec as P

HEADS = 12
HEAD_DIM = 64
PAIRS = HEADS // 2
PIECES = 4
PIECE_HEADS = HEADS // PIECES
NUM_ROWS = PIECE_HEADS * HEAD_DIM
PIECE_ROWS = NUM_ROWS + 16
MSG_ROWS = HEADS * HEAD_DIM + 32
BLOCK = 256
LAG = 2
WIDE_START_TICKS = (0, 0, 0, 1)
KV_TICKS = (2, 3)
PAIR_TICK = 5
ONE_TICK = 9
TWO_TICK = 14
WIDE_ONE_TICKS = (7, 12)
WIDE_TWO_TICKS = (10, 17)
TOKEN_TICKS = (4, 6, 6, 8, 8, 11, 11, 13)
NEG = -1e30
F32 = jnp.float32
BF16 = jnp.bfloat16
VMEM_BYTES = 56 * 1024 * 1024


def norm_parts(values):
    center = values - jnp.mean(values, -1, keepdims=True)
    spread = jnp.mean(center * center, -1, keepdims=True)
    inv = lax.rsqrt(spread + 1e-05)
    return center * inv, inv


def norm_back(unit, inv, gain, grad):
    scaled = grad * gain
    inner = scaled - jnp.mean(scaled, -1, keepdims=True)
    return inv * (inner - unit * jnp.mean(scaled * unit, -1, keepdims=True))


def dot(a, b, contract=(1, 0)):
    return lax.dot_general(
        a, b, (((contract[0],), (contract[1],)), ((), ())), preferred_element_type=F32
    )


def row(ref):
    return ref[...].reshape(1, ref.shape[0])


def piece_of(head):
    return head // PIECE_HEADS, head % PIECE_HEADS


def forward_kernel(
    sample_ref,
    mask_ref,
    tok_ref,
    lat_ref,
    gain_q_ref,
    wq_ref,
    gain_t_ref,
    wk_ref,
    wv_ref,
    part_ref,
    key_ref,
    val_ref,
    tsort_ref,
    query_ref,
    normed_ref,
    place_ref,
    bounds_ref,
    tnorm_ref,
    pos_ref,
    top_ref,
    den_ref,
    num_ref,
):
    samples = part_ref.shape[0]
    rows = tok_ref.shape[0]
    width = tok_ref.shape[1]
    lat_rows = 128
    step = 256

    named = row(sample_ref) - lax.axis_index("stream") * samples
    ids = jnp.where(row(mask_ref) == 1, named, -1)
    lane = lax.broadcasted_iota(jnp.int32, (samples, rows), 1)
    member = ids == lax.broadcasted_iota(jnp.int32, (samples, rows), 0)
    ones = jnp.where(member, 1.0, 0.0)
    count = ones
    shift = 1
    while shift < rows:
        count = count + jnp.where(lane >= shift, pltpu.roll(count, shift, 1), 0.0)
        shift *= 2
    rank = count - ones
    begin = jnp.int32(0)
    pos = jnp.full((1, rows), -1.0, F32)
    for s in range(samples):
        total = jnp.sum(ones[s : s + 1]).astype(jnp.int32)
        bounds_ref[s] = begin
        bounds_ref[samples + s] = total
        pos = jnp.where(member[s : s + 1], rank[s : s + 1] + begin.astype(F32), pos)
        begin = begin + total
    pos_ref[...] = jnp.broadcast_to(pos, (8, rows))
    place_ref[...] = jnp.broadcast_to(pos, (128, rows)).T

    def token_norm(i, carry):
        at = pl.ds(pl.multiple_of(i * step, step), step)
        unit, _ = norm_parts(tok_ref[at, :].astype(F32))
        tnorm_ref[at, :] = (unit * row(gain_t_ref)).astype(BF16)
        return carry

    lax.fori_loop(0, rows // step, token_norm, 0)

    def token_sort(i, carry):
        at = pl.ds(pl.multiple_of(i * step, step), step)
        target = lax.broadcasted_iota(jnp.int32, (step, rows), 0) + i * step
        chosen = target.astype(F32) == pos_ref[0:1, :]
        pick = jnp.where(chosen, 1.0, 0.0).astype(BF16)
        tsort = dot(pick, tnorm_ref[...]).astype(BF16)
        tsort_ref[at, :] = tsort
        key_ref[at, :] = dot(tsort, wk_ref[...]).astype(BF16)
        val_ref[at, :] = dot(tsort, wv_ref[...]).astype(BF16)
        return carry

    lax.fori_loop(0, rows // step, token_sort, 0)
    key_ref[rows:, :] = jnp.zeros((BLOCK, width), BF16)
    val_ref[rows:, :] = jnp.zeros((BLOCK, width), BF16)

    def sample_step(s, carry):
        at = pl.ds(pl.multiple_of(s * lat_rows, lat_rows), lat_rows)
        unit, _ = norm_parts(lat_ref[at, :].astype(F32))
        normed = (unit * row(gain_q_ref)).astype(BF16)
        normed_ref[at, :] = normed
        query = dot(normed, wq_ref[...]) * 0.125
        turned = query.T.astype(BF16)
        blank = jnp.zeros((HEAD_DIM, lat_rows), BF16)
        for p in range(PAIRS):
            lo = 2 * p * HEAD_DIM
            query_ref[s, p, :HEAD_DIM, :lat_rows] = turned[lo : lo + HEAD_DIM]
            query_ref[s, p, :HEAD_DIM, lat_rows:] = blank
            query_ref[s, p, HEAD_DIM:, :lat_rows] = blank
            query_ref[s, p, HEAD_DIM:, lat_rows:] = turned[lo + HEAD_DIM : lo + 2 * HEAD_DIM]
        start = bounds_ref[s]
        total = bounds_ref[samples + s]
        base = lax.div(start, 16) * 16
        blocks = jnp.where(total > 0, lax.div(start + total - base + BLOCK - 1, BLOCK), 0)
        for piece in range(PIECES):
            part_ref[s, piece, NUM_ROWS:, :] = jnp.zeros((16, lat_rows), F32)
        num_ref[...] = jnp.zeros_like(num_ref)
        top_ref[...] = jnp.full_like(top_ref, NEG)
        den_ref[...] = jnp.zeros_like(den_ref)

        def block_step(b, carry):
            row = pl.multiple_of(base + b * BLOCK, 16)
            index = lax.broadcasted_iota(jnp.int32, (BLOCK, 2 * lat_rows), 0) + row
            inside = (index >= start) & (index < start + total)
            for p in range(PAIRS):
                cols = slice(p * 128, (p + 1) * 128)
                score = dot(key_ref[pl.ds(row, BLOCK), cols], query_ref[s, p])
                score = jnp.where(inside, score, NEG)
                old = top_ref[p : p + 1, :]
                new = jnp.maximum(old, jnp.max(score, 0, keepdims=True))
                fade = jnp.exp(old - new)
                weight = jnp.exp(score - new)
                top_ref[p : p + 1, :] = new
                den_ref[p : p + 1, :] = den_ref[p : p + 1, :] * fade + jnp.sum(
                    weight, 0, keepdims=True
                )
                both = dot(val_ref[pl.ds(row, BLOCK), cols], weight.astype(BF16), (0, 0))
                for half in range(2):
                    at_rows = slice(p * 128 + half * HEAD_DIM, p * 128 + (half + 1) * HEAD_DIM)
                    at_cols = slice(half * lat_rows, (half + 1) * lat_rows)
                    num_ref[at_rows, :] = (
                        num_ref[at_rows, :] * fade[:, at_cols]
                        + both[half * HEAD_DIM : (half + 1) * HEAD_DIM, at_cols]
                    )
            return carry

        lax.fori_loop(0, blocks, block_step, 0)
        for h in range(HEADS):
            piece, i = piece_of(h)
            p, half = h // 2, h % 2
            at_cols = slice(half * lat_rows, (half + 1) * lat_rows)
            part_ref[s, piece, i * HEAD_DIM : (i + 1) * HEAD_DIM, :] = num_ref[
                h * HEAD_DIM : (h + 1) * HEAD_DIM, :
            ]
            part_ref[s, piece, NUM_ROWS + i : NUM_ROWS + i + 1, :] = top_ref[p : p + 1, at_cols]
            part_ref[s, piece, NUM_ROWS + 8 + i : NUM_ROWS + 9 + i, :] = den_ref[
                p : p + 1, at_cols
            ]
        return carry

    lax.fori_loop(0, samples, sample_step, 0)


def vmem():
    return pl.BlockSpec(memory_space=pltpu.VMEM)


def smem():
    return pl.BlockSpec(memory_space=pltpu.SMEM)


def attend_forward(sample, mask, tokens, latents, gain_q, wq, gain_t, wk, wv):
    samples, lat_rows, width = latents.shape
    rows = tokens.shape[0]
    sds = jax.ShapeDtypeStruct
    return pl.pallas_call(
        forward_kernel,
        name="attend_forward",
        out_shape=(
            sds((samples, PIECES, PIECE_ROWS, lat_rows), F32),
            sds((rows + BLOCK, width), BF16),
            sds((rows + BLOCK, width), BF16),
            sds((rows, width), BF16),
            sds((samples, PAIRS, 128, 2 * lat_rows), BF16),
            sds((samples * lat_rows, width), BF16),
            sds((rows, 128), F32),
            sds((2 * samples,), jnp.int32),
        ),
        in_specs=[vmem()] * 9,
        out_specs=(vmem(),) * 7 + (smem(),),
        scratch_shapes=[
            pltpu.VMEM((rows, width), BF16),
            pltpu.VMEM((8, rows), F32),
            pltpu.VMEM((8, 2 * lat_rows), F32),
            pltpu.VMEM((8, 2 * lat_rows), F32),
            pltpu.VMEM((width, lat_rows), F32),
        ],
        compiler_params=pltpu.CompilerParams(vmem_limit_bytes=VMEM_BYTES),
    )(
        sample,
        mask,
        tokens,
        latents.reshape(samples * lat_rows, width),
        gain_q,
        wq,
        gain_t,
        wk,
        wv,
    )


def backward_kernel(
    bounds_ref,
    lat_ref,
    key_ref,
    val_ref,
    query_ref,
    normed_ref,
    msg_ref,
    gain_q_ref,
    wq_ref,
    dkv_ref,
    dlat_ref,
    dgain_ref,
    dwq_ref,
    dk_ref,
    dv_ref,
    grad_ref,
    dquery_ref,
    turn_ref,
    stat_ref,
):
    samples = query_ref.shape[0]
    rows = dkv_ref.shape[1]
    lat_rows = 128
    step = 256
    width = dwq_ref.shape[0]
    for r in range(0, rows + BLOCK, step):
        dk_ref[r : r + step, :] = jnp.zeros((step, dk_ref.shape[1]), F32)
        dv_ref[r : r + step, :] = jnp.zeros((step, dv_ref.shape[1]), F32)
    grad_ref[...] = jnp.zeros_like(grad_ref)
    dgain_ref[...] = jnp.zeros_like(dgain_ref)

    def sample_step(s, carry):
        start = bounds_ref[s]
        total = bounds_ref[samples + s]
        base = lax.div(start, 16) * 16
        blocks = jnp.where(total > 0, lax.div(start + total - base + BLOCK - 1, BLOCK), 0)
        turn_ref[...] = jnp.zeros_like(turn_ref)
        for h in range(HEADS):
            p, half = h // 2, h % 2
            grad_ref[
                p,
                half * HEAD_DIM : (half + 1) * HEAD_DIM,
                half * lat_rows : (half + 1) * lat_rows,
            ] = msg_ref[s, h * HEAD_DIM : (h + 1) * HEAD_DIM, :].astype(BF16)

            stat_ref[p : p + 1, half * lat_rows : (half + 1) * lat_rows] = msg_ref[
                s, width + h : width + h + 1, :
            ]
            stat_ref[8 + p : 9 + p, half * lat_rows : (half + 1) * lat_rows] = msg_ref[
                s, width + 16 + h : width + 17 + h, :
            ]

        def block_step(b, carry):
            row = pl.multiple_of(base + b * BLOCK, 16)
            index = lax.broadcasted_iota(jnp.int32, (BLOCK, 2 * lat_rows), 0) + row
            inside = (index >= start) & (index < start + total)
            at = pl.ds(row, BLOCK)
            for p in range(PAIRS):
                cols = slice(p * 128, (p + 1) * 128)
                key = key_ref[at, cols]
                query = query_ref[s, p]
                grad = grad_ref[p]
                score = dot(key, query)
                weight = jnp.where(inside, jnp.exp(score - stat_ref[p : p + 1, :]), 0.0)
                dprob = dot(val_ref[at, cols], grad)
                dscore = (weight * (dprob - stat_ref[8 + p : 9 + p, :])).astype(BF16)
                dv_ref[at, cols] += dot(weight.astype(BF16), grad, (1, 1))
                dk_ref[at, cols] += dot(dscore, query, (1, 1))
                both = dot(key, dscore, (0, 0))
                for half in range(2):
                    turn_ref[
                        p * 128 + half * HEAD_DIM : p * 128 + (half + 1) * HEAD_DIM, :
                    ] += both[
                        half * HEAD_DIM : (half + 1) * HEAD_DIM,
                        half * lat_rows : (half + 1) * lat_rows,
                    ]
            return carry

        lax.fori_loop(0, blocks, block_step, 0)
        at = pl.ds(pl.multiple_of(s * lat_rows, lat_rows), lat_rows)
        dquery = (turn_ref[...].T * 0.125).astype(BF16)
        dquery_ref[at, :] = dquery
        unit, inv = norm_parts(lat_ref[at, :].astype(F32))
        dnormed = dot(dquery, wq_ref[...], (1, 1))
        dgain_ref[0:1, :] += jnp.sum(dnormed * unit, 0, keepdims=True)
        dlat_ref[at, :] = norm_back(unit, inv, row(gain_q_ref), dnormed)
        return carry

    lax.fori_loop(0, samples, sample_step, 0)
    for r in range(0, rows, step):
        dkv_ref[0, r : r + step, :] = dk_ref[r : r + step, :].astype(BF16)
        dkv_ref[1, r : r + step, :] = dv_ref[r : r + step, :].astype(BF16)
    for c in range(0, width, 256):
        dwq_ref[c : c + 256, :] = dot(dquery_ref[:, c : c + 256], normed_ref[...], (0, 0))


def attend_backward(bounds, latents, keys, values, query, normed, msg, gain_q, wq):
    samples, lat_rows, width = latents.shape
    rows = keys.shape[0] - BLOCK
    sds = jax.ShapeDtypeStruct
    return pl.pallas_call(
        backward_kernel,
        name="attend_backward",
        out_shape=(
            sds((2, rows, width), BF16),
            sds((samples * lat_rows, width), F32),
            sds((8, width), F32),
            sds((width, width), F32),
        ),
        in_specs=[smem()] + [vmem()] * 8,
        out_specs=(vmem(),) * 4,
        scratch_shapes=[
            pltpu.VMEM((rows + BLOCK, width), F32),
            pltpu.VMEM((rows + BLOCK, width), F32),
            pltpu.VMEM((PAIRS, 128, 2 * lat_rows), BF16),
            pltpu.VMEM((samples * lat_rows, width), BF16),
            pltpu.VMEM((width, lat_rows), F32),
            pltpu.VMEM((16, 2 * lat_rows), F32),
        ],
        compiler_params=pltpu.CompilerParams(vmem_limit_bytes=VMEM_BYTES),
    )(
        bounds,
        latents.reshape(samples * lat_rows, width),
        keys,
        values,
        query,
        normed,
        msg,
        gain_q,
        wq,
    )


MESH = pl.DeviceIdType.MESH


def merge(a_ref, b_ref, out_ref):
    a_tail, b_tail = a_ref[NUM_ROWS : NUM_ROWS + 8, :], b_ref[NUM_ROWS : NUM_ROWS + 8, :]
    top = jnp.maximum(a_tail, b_tail)
    a_fade, b_fade = jnp.exp(a_tail - top), jnp.exp(b_tail - top)
    den = a_ref[NUM_ROWS + 8 :, :] * a_fade + b_ref[NUM_ROWS + 8 :, :] * b_fade
    for i in range(PIECE_HEADS):
        at = slice(i * HEAD_DIM, (i + 1) * HEAD_DIM)
        out_ref[at, :] = (
            a_ref[at, :] * a_fade[i : i + 1, :] + b_ref[at, :] * b_fade[i : i + 1, :]
        )
    out_ref[NUM_ROWS : NUM_ROWS + 8, :] = top
    out_ref[NUM_ROWS + 8 :, :] = den


def gelu_parts(x):
    c = 0.7978845608028654
    square = x * x
    t = jnp.tanh(c * x * (1.0 + 0.044715 * square))
    half = 0.5 * (1.0 + t)
    slope = half + (0.5 * c) * x * (1.0 - t * t) * (1.0 + (3 * 0.044715) * square)
    return x * half, slope


def latent_kernel(
    part_hbm,
    drop_ref,
    lat_ref,
    cot_ref,
    wo_hbm,
    gain_ref,
    wup_hbm,
    bup_ref,
    wdn_hbm,
    bdn_ref,
    msg_ref,
    res_ref,
    dmid_ref,
    a_ref,
    b_ref,
    side_ref,
    vec_ref,
    wo_ref,
    wup_ref,
    wdn_ref,
    pair_ref,
    own_ref,
    right_in,
    right_out,
    left_in,
    left_out,
    res_out,
    res_in,
    att_t_ref,
    mid_ref,
    acc_ref,
    dacc_ref,
    hn_ref,
    dm_ref,
    da_ref,
    att_ref,
    hn_out,
    hn_in,
    half_out,
    half_in,
    side_all,
    side_in,
    hn_send,
    hn_recv,
    half_send,
    half_recv,
    side_send,
    side_recv,
    own_sem,
    weight_sem,
    pair_send,
    pair_recv,
    right_send,
    right_recv,
    left_send,
    left_recv,
    msg_send,
    msg_recv,
    res_send,
    res_recv,
):
    samples = msg_ref.shape[0]
    half = samples // 2
    lat_rows = 128
    width = lat_ref.shape[1]
    chunks = half * PIECES
    stream = lax.axis_index("stream")
    tok = lax.axis_index("tok")
    chips = lax.axis_size("tok") // 2
    core = lax.rem(tok, 2)
    chip = lax.div(tok, 2)
    parity = lax.rem(chip, 2)
    partner = (stream, tok + 1 - 2 * core)
    right = (stream, tok + 2)
    left = (stream, tok - 2)
    has_right = chip < chips - 1
    has_left = chip > 0
    on_first = core == 0

    barrier = pltpu.get_barrier_semaphore()
    pl.semaphore_signal(barrier, inc=1, device_id=partner, device_id_type=MESH)

    @pl.when(has_right)
    def _():
        pl.semaphore_signal(barrier, inc=1, device_id=right, device_id_type=MESH)

    @pl.when(has_left)
    def _():
        pl.semaphore_signal(barrier, inc=1, device_id=left, device_id_type=MESH)

    own_load = pltpu.make_async_copy(
        part_hbm.at[pl.ds(core * chunks, chunks)], own_ref, own_sem
    )
    own_load.start()
    weights = [
        pltpu.make_async_copy(src, dst, weight_sem.at[i])
        for i, (src, dst) in enumerate(((wo_hbm, wo_ref), (wup_hbm, wup_ref), (wdn_hbm, wdn_ref)))
    ]
    for copy in weights:
        copy.start()
    pl.semaphore_wait(
        barrier, 1 + has_right.astype(jnp.int32) + has_left.astype(jnp.int32)
    )

    def pair_copy(i):
        return pltpu.make_async_remote_copy(
            src_ref=part_hbm.at[(1 - core) * chunks + i],
            dst_ref=pair_ref.at[i],
            send_sem=pair_send.at[i],
            recv_sem=pair_recv.at[i],
            device_id=partner,
            device_id_type=MESH,
        )

    def right_copy(i):
        return pltpu.make_async_remote_copy(
            src_ref=right_out.at[i],
            dst_ref=right_in.at[i],
            send_sem=right_send.at[i],
            recv_sem=right_recv.at[i],
            device_id=right,
            device_id_type=MESH,
        )

    def left_copy(i):
        return pltpu.make_async_remote_copy(
            src_ref=left_out.at[i],
            dst_ref=left_in.at[i],
            send_sem=left_send.at[i],
            recv_sem=left_recv.at[i],
            device_id=left,
            device_id_type=MESH,
        )

    def msg_copy(j):
        at = core * half + j
        return pltpu.make_async_remote_copy(
            src_ref=msg_ref.at[at],
            dst_ref=msg_ref.at[at],
            send_sem=msg_send.at[j],
            recv_sem=msg_recv.at[j],
            device_id=partner,
            device_id_type=MESH,
        )

    def msg_arrival(j):
        at = (1 - core) * half + j
        return pltpu.make_async_remote_copy(
            src_ref=msg_ref.at[at],
            dst_ref=msg_ref.at[at],
            send_sem=msg_send.at[j],
            recv_sem=msg_recv.at[j],
            device_id=partner,
            device_id_type=MESH,
        )

    def res_copy(j):
        return pltpu.make_async_remote_copy(
            src_ref=res_out.at[j],
            dst_ref=res_in.at[j],
            send_sem=res_send.at[j],
            recv_sem=res_recv.at[j],
            device_id=partner,
            device_id_type=MESH,
        )

    def hn_copy(j):
        return pltpu.make_async_remote_copy(
            src_ref=hn_out.at[j],
            dst_ref=hn_in.at[j],
            send_sem=hn_send.at[j],
            recv_sem=hn_recv.at[j],
            device_id=partner,
            device_id_type=MESH,
        )

    def half_copy(i):
        return pltpu.make_async_remote_copy(
            src_ref=half_out.at[i],
            dst_ref=half_in.at[i],
            send_sem=half_send.at[i],
            recv_sem=half_recv.at[i],
            device_id=partner,
            device_id_type=MESH,
        )

    side_copy = pltpu.make_async_remote_copy(
        src_ref=side_all.at[:, 1 - core],
        dst_ref=side_in,
        send_sem=side_send,
        recv_sem=side_recv,
        device_id=partner,
        device_id_type=MESH,
    )

    def start_pair(i, carry):
        pair_copy(i).start()
        return carry

    lax.fori_loop(0, chunks, start_pair, 0)
    own_load.wait()

    drop = row(drop_ref).astype(F32)
    scale_all = drop * drop.shape[1] / jnp.sum(drop, 1, keepdims=True)
    drop_lane = lax.broadcasted_iota(jnp.int32, drop.shape, 1)
    vec_ref[...] = jnp.zeros_like(vec_ref)

    def mlp(j, q):
        sample = core * half + j
        rows = pl.ds(pl.multiple_of(sample * lat_rows, lat_rows), lat_rows)
        mine = pl.ds(pl.multiple_of(j * lat_rows, lat_rows), lat_rows)
        scale = jnp.sum(
            jnp.where(drop_lane == stream * samples + sample, scale_all, 0.0), 1, keepdims=True
        )

        @pl.when(q == 0)
        def _():
            for h in range(HEADS):
                piece, i = piece_of(h)
                at = j * PIECES + piece
                den = own_ref[at, NUM_ROWS + 8 + i : NUM_ROWS + 9 + i, :]
                att_t_ref[h * HEAD_DIM : (h + 1) * HEAD_DIM, :] = own_ref[
                    at, i * HEAD_DIM : (i + 1) * HEAD_DIM, :
                ] * (1.0 / den)
            att = att_t_ref[...].T.astype(BF16)
            att_ref[mine, :] = jnp.where(parity == 0, att[:, : width // 2], att[:, width // 2 :])
            mid = lat_ref[rows, :].astype(F32) + scale * dot(att, wo_ref[...])
            mid_ref[...] = mid
            unit, _ = norm_parts(mid)
            hn = (unit * row(gain_ref)).astype(BF16)
            dm = (scale * cot_ref[rows, :].astype(F32)).astype(BF16)
            hn_ref[...] = hn
            dm_ref[...] = dm
            a_ref[rows, :] = jnp.where(on_first, hn, dm)

            @pl.when(jnp.logical_not(on_first))
            def _():
                hn_out[j] = hn.astype(F32)
                hn_copy(j).start()

            vec_ref[1:2, :width] += jnp.sum(dm.astype(F32), 0, keepdims=True)
            acc_ref[...] = jnp.broadcast_to(row(bdn_ref), acc_ref.shape)
            dacc_ref[...] = jnp.zeros_like(dacc_ref)

        span = wup_ref.shape[1] // PIECES
        cols = pl.ds(pl.multiple_of(q * span, 128), span)
        pre = dot(hn_ref[...], wup_ref[:, cols]) + bup_ref[cols].reshape(1, span)
        active, slope = gelu_parts(pre)
        hidden = active.astype(BF16)
        acc_ref[...] += dot(hidden, wdn_ref[cols, :])
        dpre = (slope * dot(dm_ref[...], wdn_ref[cols, :], (1, 1))).astype(BF16)
        piece = j * PIECES + q
        near_half = lambda x: jnp.where(parity == 0, x[:, : span // 2], x[:, span // 2 :])
        hidden_half, dpre_half = near_half(hidden), near_half(dpre)
        b_ref[q, rows, :] = jnp.where(on_first, dpre_half, hidden_half)
        half_out[piece] = jnp.where(on_first, hidden_half, dpre_half).astype(F32)
        half_copy(piece).start()
        vec_ref[0:1, cols] += jnp.sum(dpre.astype(F32), 0, keepdims=True)
        dacc_ref[...] += dot(dpre, wup_ref[:, cols], (1, 1))

        @pl.when(q == PIECES - 1)
        def _():
            mid = mid_ref[...]
            res = (mid + scale * acc_ref[...]).astype(BF16)
            res_ref[rows, :] = res
            res_out[j] = res.astype(F32)
            res_copy(j).start()
            unit, inv = norm_parts(mid)
            dhn = dacc_ref[...]
            vec_ref[2:3, :width] += jnp.sum(dhn * unit, 0, keepdims=True)
            dmid = cot_ref[rows, :].astype(F32) + norm_back(unit, inv, row(gain_ref), dhn)
            dmid_ref[mine, :] = dmid
            da = (scale * dmid).astype(BF16)
            da_ref[mine, :] = da
            datt_t = dot(wo_ref[...], da, (1, 1)).astype(BF16).astype(F32)
            msg_ref[sample, width:, :] = jnp.zeros((MSG_ROWS - width, lat_rows), F32)
            for h in range(HEADS):
                piece, i = piece_of(h)
                at = j * PIECES + piece
                inverse = 1.0 / own_ref[at, NUM_ROWS + 8 + i : NUM_ROWS + 9 + i, :]
                span_h = slice(h * HEAD_DIM, (h + 1) * HEAD_DIM)
                one = datt_t[span_h]
                msg_ref[sample, span_h, :] = (one * inverse).astype(BF16).astype(F32)
                delta = jnp.sum(one * att_t_ref[span_h, :], 0, keepdims=True) * inverse
                msg_ref[sample, width + h : width + h + 1, :] = own_ref[
                    at, NUM_ROWS + i : NUM_ROWS + i + 1, :
                ]
                msg_ref[sample, width + 16 + h : width + 17 + h, :] = delta
            msg_copy(j).start()

    def step(t, carry):
        @pl.when(t < chunks)
        def _():
            pair_copy(t).wait_recv()
            merge(own_ref.at[t], pair_ref.at[t], own_ref.at[t])

        r = t - LAG * chip

        @pl.when((r >= 0) & (r < chunks))
        def _():
            @pl.when(has_left)
            def _():
                right_copy(r).wait_recv()
                merge(own_ref.at[r], right_in.at[r], right_out.at[r])

            @pl.when(jnp.logical_not(has_left))
            def _():
                right_out[r] = own_ref[r]

            @pl.when(has_right)
            def _():
                right_copy(r).start()

        u = t - LAG * (chips - 1 - chip)

        @pl.when((u >= 0) & (u < chunks))
        def _():
            @pl.when(has_right)
            def _():
                left_copy(u).wait_recv()

            @pl.when(has_left)
            def _():
                @pl.when(has_right)
                def _():
                    merge(own_ref.at[u], left_in.at[u], left_out.at[u])

                @pl.when(jnp.logical_not(has_right))
                def _():
                    left_out[u] = own_ref[u]

                left_copy(u).start()

        w = t - LAG * jnp.maximum(chip, chips - 1 - chip)

        @pl.when((w >= 0) & (w < chunks))
        def _():
            @pl.when(has_right)
            def _():
                merge(right_out.at[w], left_in.at[w], own_ref.at[w])

            @pl.when(jnp.logical_not(has_right))
            def _():
                own_ref[w] = right_out[w]

        m = w - (PIECES - 1)

        @pl.when(m == 0)
        def _():
            for copy in weights:
                copy.wait()

        @pl.when((m >= 0) & (m < chunks))
        def _():
            mlp(lax.div(m, PIECES), lax.rem(m, PIECES))

        return carry

    lax.fori_loop(0, chunks + LAG * (chips - 1) + PIECES - 1, step, 0)

    share = width // 8
    for block in range(4):
        at = slice(block * 2 * share, (block + 1) * 2 * share)
        product = dot(da_ref[:, at], att_ref[...], (0, 0))
        side_all[block, 0] = product[:share]
        side_all[block, 1] = product[share:]
    side_copy.start()

    def finish_chunk(i, carry):
        pair_copy(i).wait_send()
        half_copy(i).wait_send()
        half_copy(i).wait_recv()
        at = ((1 - core) * half + lax.div(i, PIECES)) * lat_rows
        rows = pl.ds(pl.multiple_of(at, lat_rows), lat_rows)
        b_ref[lax.rem(i, PIECES), rows, :] = half_in[i].astype(BF16)

        @pl.when(has_right)
        def _():
            right_copy(i).wait_send()

        @pl.when(has_left)
        def _():
            left_copy(i).wait_send()

        return carry

    lax.fori_loop(0, chunks, finish_chunk, 0)

    def finish_sample(j, carry):
        res_copy(j).wait_recv()
        other = (1 - core) * half + j
        rows = pl.ds(pl.multiple_of(other * lat_rows, lat_rows), lat_rows)
        res_ref[rows, :] = res_in[j].astype(BF16)

        @pl.when(on_first)
        def _():
            hn_copy(j).wait_recv()
            a_ref[rows, :] = hn_in[j].astype(BF16)

        @pl.when(jnp.logical_not(on_first))
        def _():
            hn_copy(j).wait_send()
            scale = jnp.sum(
                jnp.where(drop_lane == stream * samples + other, scale_all, 0.0), 1, keepdims=True
            )
            a_ref[rows, :] = (scale * cot_ref[rows, :].astype(F32)).astype(BF16)

        res_copy(j).wait_send()
        msg_copy(j).wait_send()
        msg_arrival(j).wait_recv()
        return carry

    lax.fori_loop(0, half, finish_sample, 0)
    side_copy.wait()
    side_ref[...] = side_all[:, core] + side_in[...]


def anywhere():
    return pl.BlockSpec(memory_space=pl.ANY)


def latent_block(part, drop_mask, latents, cotangent, wo, gain, wup, bup, wdn, bdn):
    samples, lat_rows, width = latents.shape
    half = samples // 2
    chunks = half * PIECES
    hidden = wup.shape[1]
    sds = jax.ShapeDtypeStruct
    chunk = lambda: pltpu.VMEM((chunks, PIECE_ROWS, lat_rows), F32)
    dma = pltpu.SemaphoreType.DMA
    return pl.pallas_call(
        latent_kernel,
        name="latent_block",
        out_shape=(
            sds((samples, MSG_ROWS, lat_rows), F32),
            sds((samples * lat_rows, width), BF16),
            sds((half * lat_rows, width), F32),
            sds((samples * lat_rows, width), BF16),
            sds((PIECES, samples * lat_rows, hidden // PIECES // 2), BF16),
            sds((4, width // 8, width // 2), F32),
            sds((8, hidden), F32),
        ),
        in_specs=[
            anywhere(),
            vmem(),
            vmem(),
            vmem(),
            anywhere(),
            vmem(),
            anywhere(),
            vmem(),
            anywhere(),
            vmem(),
        ],
        out_specs=(vmem(),) * 7,
        scratch_shapes=[
            pltpu.VMEM(wo.shape, BF16),
            pltpu.VMEM(wup.shape, BF16),
            pltpu.VMEM(wdn.shape, BF16),
            chunk(),
            chunk(),
            chunk(),
            chunk(),
            chunk(),
            chunk(),
            pltpu.VMEM((half, lat_rows, width), F32),
            pltpu.VMEM((half, lat_rows, width), F32),
            pltpu.VMEM((width, lat_rows), F32),
            pltpu.VMEM((lat_rows, width), F32),
            pltpu.VMEM((lat_rows, width), F32),
            pltpu.VMEM((lat_rows, width), F32),
            pltpu.VMEM((lat_rows, width), BF16),
            pltpu.VMEM((lat_rows, width), BF16),
            pltpu.VMEM((half * lat_rows, width), BF16),
            pltpu.VMEM((half * lat_rows, width // 2), BF16),
            pltpu.VMEM((half, lat_rows, width), F32),
            pltpu.VMEM((half, lat_rows, width), F32),
            pltpu.VMEM((chunks, lat_rows, hidden // PIECES // 2), F32),
            pltpu.VMEM((chunks, lat_rows, hidden // PIECES // 2), F32),
            pltpu.VMEM((4, 2, width // 8, width // 2), F32),
            pltpu.VMEM((4, width // 8, width // 2), F32),
            dma((half,)),
            dma((half,)),
            dma((chunks,)),
            dma((chunks,)),
            dma,
            dma,
            dma,
            dma((3,)),
            dma((chunks,)),
            dma((chunks,)),
            dma((chunks,)),
            dma((chunks,)),
            dma((chunks,)),
            dma((chunks,)),
            dma((half,)),
            dma((half,)),
            dma((half,)),
            dma((half,)),
        ],
        compiler_params=pltpu.CompilerParams(
            vmem_limit_bytes=VMEM_BYTES, collective_id=1, has_side_effects=True
        ),
    )(
        part.reshape(samples * PIECES, PIECE_ROWS, lat_rows),
        drop_mask,
        latents.reshape(samples * lat_rows, width),
        cotangent.reshape(samples * lat_rows, width),
        wo,
        gain,
        wup,
        bup,
        wdn,
        bdn,
    )


ZROWS = 32
SUBS = 2


def gradient_kernel(
    dlat_hbm,
    dmid_ref,
    a_ref,
    b_ref,
    side_ref,
    dwq_ref,
    vec_ref,
    dgain_q_ref,
    place_ref,
    tok_ref,
    tsort_ref,
    dkv_ref,
    gain_t_ref,
    wk_ref,
    wv_ref,
    dlat_out,
    gather_out,
    kv_out,
    query_out,
    small_out,
    dtok_ref,
    line_ref,
    right_ref,
    left_ref,
    dmine_ref,
    wide_ref,
    wide_one,
    wide_two,
    send_ref,
    mine_ref,
    pair_ref,
    one_ref,
    two_ref,
    small_ref,
    gain_ref,
    load_sem,
    dpair_send,
    dpair_recv,
    right_send,
    right_recv,
    left_send,
    left_recv,
    back_send,
    back_recv,
    back_local,
    wide_one_send,
    wide_one_recv,
    wide_two_send,
    wide_two_recv,
    wide_z_send,
    wide_z_recv,
    wide_core_send,
    wide_core_recv,
    wide_local,
    pair_send,
    pair_recv,
    one_send,
    one_recv,
    two_send,
    two_recv,
    spread_send,
    spread_recv,
    share_send,
    share_recv,
    query_send,
    query_recv,
    keep_local,
):
    width = tok_ref.shape[1]
    rows = tok_ref.shape[0]
    lat_chunks = dmine_ref.shape[0]
    all_chunks = line_ref.shape[0]
    kv_rows = send_ref.shape[2]
    q_rows = query_out.shape[2]
    mix = kv_rows + q_rows
    half_chunks = (all_chunks - lat_chunks) // 2
    kv_chunks = kv_rows // ZROWS
    wide_half = wide_ref.shape[1] // 2
    sub_rows = wide_half // SUBS

    stream = lax.axis_index("stream")
    tok = lax.axis_index("tok")
    chips = lax.axis_size("tok") // 2
    core = lax.rem(tok, 2)
    chip = lax.div(tok, 2)
    other = 1 - core
    parity = lax.rem(chip, 2)
    flip_x = stream + 1 - 2 * lax.rem(stream, 2)
    flip_y = lax.rem(stream + 2, 4)
    flip_xy = 3 - stream
    partner = (stream, tok + 1 - 2 * core)
    right = (stream, tok + 2)
    left = (stream, tok - 2)
    beside = (stream, tok + 2 - 4 * parity)
    near = ((flip_x, tok), (flip_y, tok))
    first = (flip_x, flip_y)
    has_right = chip < chips - 1
    has_left = chip > 0

    barrier = pltpu.get_barrier_semaphore()
    for target in (partner,) + near:
        pl.semaphore_signal(barrier, inc=1, device_id=target, device_id_type=MESH)

    @pl.when(has_right)
    def _():
        pl.semaphore_signal(barrier, inc=1, device_id=right, device_id_type=MESH)

    @pl.when(has_left)
    def _():
        pl.semaphore_signal(barrier, inc=1, device_id=left, device_id_type=MESH)

    def remote(src, dst, send, recv, target):
        return pltpu.make_async_remote_copy(
            src_ref=src,
            dst_ref=dst,
            send_sem=send,
            recv_sem=recv,
            device_id=target,
            device_id_type=MESH,
        )

    load = pltpu.make_async_copy(dlat_hbm.at[core], dmine_ref, load_sem)
    load.start()
    pl.semaphore_wait(barrier, 3 + has_right.astype(jnp.int32) + has_left.astype(jnp.int32))

    def dpair_copy(i):
        return remote(
            dlat_hbm.at[other, i], line_ref.at[i], dpair_send.at[i], dpair_recv.at[i], partner
        )

    def start_dpair(i, carry):
        dpair_copy(i).start()
        return carry

    lax.fori_loop(0, lat_chunks, start_dpair, 0)

    def wide_one_copy(h, n, sub):
        block = (first[h], flip_xy)[n]
        at = pl.ds(h * wide_half + sub * sub_rows, sub_rows)
        return remote(
            wide_ref.at[block, at],
            wide_one.at[h, n, pl.ds(sub * sub_rows, sub_rows)],
            wide_one_send.at[h, n, sub],
            wide_one_recv.at[h, n, sub],
            near[h],
        )

    def wide_at(block, h, sub):
        return wide_ref.at[block, pl.ds(h * wide_half + sub * sub_rows, sub_rows)]

    def wide_two_copy(h, sub):
        at = pl.ds(sub * sub_rows, sub_rows)
        return remote(
            wide_at(first[1 - h], h, sub),
            wide_two.at[h, at],
            wide_two_send.at[h, sub],
            wide_two_recv.at[h, sub],
            near[1 - h],
        )

    def gather_at(c, e, h, sub):
        return gather_out.at[c, e, pl.ds(h * wide_half + sub * sub_rows, sub_rows)]

    def wide_z_copy(h, sub):
        return remote(
            wide_at(stream, h, sub),
            gather_at(core, parity, h, sub),
            wide_z_send.at[h, sub],
            wide_z_recv.at[h, sub],
            beside,
        )

    def wide_z_arrival(h, sub):
        return remote(
            wide_at(stream, h, sub),
            gather_at(core, 1 - parity, h, sub),
            wide_z_send.at[h, sub],
            wide_z_recv.at[h, sub],
            beside,
        )

    def wide_core_copy(far, h, sub):
        if far:
            src = gather_at(core, 1 - parity, h, sub)
            dst = gather_at(core, 1 - parity, h, sub)
        else:
            src = wide_at(stream, h, sub)
            dst = gather_at(core, parity, h, sub)
        return remote(
            src, dst, wide_core_send.at[far, h, sub], wide_core_recv.at[far, h, sub], partner
        )

    def wide_core_arrival(far, h, sub):
        place = gather_at(other, 1 - parity if far else parity, h, sub)
        return remote(
            place, place, wide_core_send.at[far, h, sub], wide_core_recv.at[far, h, sub], partner
        )

    def wide_keep(h, sub):
        return pltpu.make_async_copy(
            wide_at(stream, h, sub),
            gather_at(core, parity, h, sub),
            wide_local.at[h, sub],
        )

    def wide_product(block):
        wide_ref[block, :width, :] = dot(a_ref[...], b_ref[block], (0, 0))
        wide_ref[block, width:, :] = side_ref[block]

    def wide_start(k):
        wide_product((flip_xy, first[0], first[1], stream)[k])
        if k < 3:
            for sub in range(SUBS):
                for h in range(2):
                    if k == 0:
                        wide_one_copy(h, 1, sub).start()
                    elif k == 1 + h:
                        wide_one_copy(h, 0, sub).start()

    def wide_event_one(sub):
        at = slice(sub * sub_rows, (sub + 1) * sub_rows)
        for h in range(2):
            for n in range(2):
                wide_one_copy(h, n, sub).wait_recv()
            span = pl.ds(h * wide_half + sub * sub_rows, sub_rows)
            wide_ref[first[1 - h], span, :] += wide_one[h, 1, at, :]
            wide_two_copy(h, sub).start()
            wide_ref[stream, span, :] += wide_one[h, 0, at, :]

    def wide_event_two(sub):
        at = slice(sub * sub_rows, (sub + 1) * sub_rows)
        for h in range(2):
            wide_two_copy(h, sub).wait_recv()
            span = pl.ds(h * wide_half + sub * sub_rows, sub_rows)
            wide_ref[stream, span, :] += wide_two[h, at, :]
            wide_z_copy(h, sub).start()
            wide_core_copy(0, h, sub).start()
            wide_keep(h, sub).start()

    def wide_event_three(sub):
        for h in range(2):
            wide_z_arrival(h, sub).wait_recv()
            wide_core_copy(1, h, sub).start()

    share = width // 4

    def gain_part(which, block, product):
        at = slice(block * share, (block + 1) * share)
        weight = jnp.where(which == 0, wk_ref[at, :], wv_ref[at, :]).astype(F32)
        gain_ref[at, 0:1] += jnp.sum(product * weight, 1, keepdims=True)

    def token_product(block, which):
        at = slice(block * share, (block + 1) * share)
        return dot(tsort_ref[:, at], dkv_ref[which], (0, 0))

    def token_other():
        gain_ref[...] = jnp.zeros_like(gain_ref)
        for block in range(4):
            product = token_product(block, other)
            for h in range(2):
                send_ref[h, block] = product[h * kv_rows : (h + 1) * kv_rows]
            gain_part(other, block, product)
        for copy in pairs[:4]:
            copy.start()

    def pair_copies():
        out = []
        for h in range(2):
            out.append(
                remote(
                    send_ref.at[h],
                    pair_ref.at[h, :, pl.ds(0, kv_rows)],
                    pair_send.at[h],
                    pair_recv.at[h],
                    partner,
                )
            )
            out.append(
                remote(
                    dwq_ref.at[:, other, h],
                    pair_ref.at[h, :, pl.ds(kv_rows, q_rows)],
                    pair_send.at[2 + h],
                    pair_recv.at[2 + h],
                    partner,
                )
            )
        out.append(
            remote(
                small_ref,
                pair_ref.at[0, :, pl.ds(mix, 16)],
                pair_send.at[4],
                pair_recv.at[4],
                partner,
            )
        )
        return out

    pairs = pair_copies()

    def token_own():
        for block in range(4):
            product = token_product(block, core)
            for h in range(2):
                piece = product[h * kv_rows : (h + 1) * kv_rows]
                mine_ref[h, block, :kv_rows, :] = piece
                mine_ref[h, block, kv_rows:mix, :] = dwq_ref[block, core, h]
            gain_part(core, block, product)
        mine_ref[1, :, mix:, :] = jnp.zeros((4, 16, width), F32)
        small_ref[...] = jnp.zeros_like(small_ref)
        gain = jnp.broadcast_to(gain_ref[:, 0:1], gain_ref.shape).T[0:1, :] / row(gain_t_ref)
        for block in range(4):
            small_ref[block, 0:1, :] = vec_ref[0:1, block * width : (block + 1) * width] * here
            small_ref[block, 1:2, :] = dgain_q_ref[0:1, :]
            small_ref[block, 2:3, :] = vec_ref[2:3, :width] * here
            small_ref[block, 3:4, :] = vec_ref[1:2, :width] * here
            small_ref[block, 4:5, :] = gain
        pairs[4].start()

    here = (chip == 0).astype(F32)

    token_step = 128

    def token_part(i):
        at = pl.ds(pl.multiple_of(i * token_step, token_step), token_step)
        target = lax.broadcasted_iota(jnp.int32, (token_step, rows), 1).astype(F32)
        pick = jnp.where(target == place_ref[at, 0:1], 1.0, 0.0).astype(BF16)
        dkey = dot(pick, dkv_ref[0]).astype(BF16)
        dval = dot(pick, dkv_ref[1]).astype(BF16)
        dnormed = dot(dkey, wk_ref[...], (1, 1)) + dot(dval, wv_ref[...], (1, 1))
        unit, inv = norm_parts(tok_ref[at, :].astype(F32))
        dtok_ref[at, :] = norm_back(unit, inv, row(gain_t_ref), dnormed)

    def one_copy(h, n):
        block = (first[h], flip_xy)[n]
        return remote(
            mine_ref.at[h, block], one_ref.at[h, n], one_send.at[h, n], one_recv.at[h, n], near[h]
        )

    def two_copy(h):
        return remote(
            mine_ref.at[h, first[1 - h]], two_ref.at[h], two_send.at[h], two_recv.at[h], near[1 - h]
        )

    def pair_event():
        for copy in pairs:
            copy.wait_recv()
        for h in range(2):
            for block in range(4):
                mine_ref[h, block, :mix, :] += pair_ref[h, block, :mix, :]
                if h == 0:
                    mine_ref[h, block, mix:, :] = small_ref[block] + pair_ref[h, block, mix:, :]
        for h in range(2):
            for n in range(2):
                one_copy(h, n).start()

    def one_event():
        for h in range(2):
            for n in range(2):
                one_copy(h, n).wait_recv()
            mine_ref[h, first[1 - h]] += one_ref[h, 1]
            two_copy(h).start()

    def two_event():
        for h in range(2):
            two_copy(h).wait_recv()
            total = mine_ref[h, stream] + one_ref[h, 0] + two_ref[h]
            for k in range(half_chunks):
                line_ref[lat_chunks + h * half_chunks + k] = total[k * ZROWS : (k + 1) * ZROWS]

    def right_copy(i):
        return remote(right_ref.at[i], right_ref.at[i], right_send.at[i], right_recv.at[i], right)

    def left_copy(i):
        return remote(left_ref.at[i], left_ref.at[i], left_send.at[i], left_recv.at[i], left)

    def back_copy(i):
        return remote(
            line_ref.at[i], dlat_out.at[core, i], back_send.at[i], back_recv.at[i], partner
        )

    def back_arrival(i):
        return remote(
            line_ref.at[i], dlat_out.at[other, i], back_send.at[i], back_recv.at[i], partner
        )

    def back_keep(i):
        return pltpu.make_async_copy(line_ref.at[i], dlat_out.at[core, i], back_local.at[i])

    def line_step(t):
        @pl.when(t < lat_chunks)
        def _():
            dpair_copy(t).wait_recv()
            line_ref[t] += dmine_ref[t] + dmid_ref[t] * here

        r = t - LAG * chip

        @pl.when((r >= 0) & (r < all_chunks))
        def _():
            @pl.when(has_left)
            def _():
                right_copy(r).wait_recv()
                right_ref[r] += line_ref[r]

            @pl.when(jnp.logical_not(has_left))
            def _():
                right_ref[r] = line_ref[r]

            @pl.when(has_right)
            def _():
                right_copy(r).start()

        u = t - LAG * (chips - 1 - chip)

        @pl.when((u >= 0) & (u < all_chunks))
        def _():
            @pl.when(has_right)
            def _():
                left_copy(u).wait_recv()
                left_ref[u] += line_ref[u]

            @pl.when(jnp.logical_not(has_right))
            def _():
                left_ref[u] = line_ref[u]

            @pl.when(has_left)
            def _():
                left_copy(u).start()

        w = t - LAG * jnp.maximum(chip, chips - 1 - chip)

        @pl.when((w >= 0) & (w < all_chunks))
        def _():
            line_ref[w] = right_ref[w] + left_ref[w] - line_ref[w]

            @pl.when(w < lat_chunks)
            def _():
                back_copy(w).start()
                back_keep(w).start()

    def own_piece(h):
        return line_ref.at[pl.ds(lat_chunks + h * half_chunks, kv_chunks)]

    def spread_one(h):
        return remote(
            own_piece(h),
            kv_out.at[core, stream, h],
            spread_send.at[0, h],
            spread_recv.at[0, h],
            near[1 - h],
        )

    def spread_two(h, n):
        block = (stream, first[1 - h])[n]
        src = own_piece(h) if n == 0 else kv_out.at[core, block, h]
        return remote(
            src,
            kv_out.at[core, block, h],
            spread_send.at[1 + n, h],
            spread_recv.at[1 + n, h],
            near[h],
        )

    def spread_one_arrival(h):
        place = kv_out.at[core, first[1 - h], h]
        return remote(
            place, place, spread_send.at[0, h], spread_recv.at[0, h], near[1 - h]
        )

    def spread_two_arrival(h, n):
        place = kv_out.at[core, (first[h], flip_xy)[n], h]
        return remote(place, place, spread_send.at[1 + n, h], spread_recv.at[1 + n, h], near[h])

    def block_of(h, k):
        return (stream, first[1 - h], first[h], flip_xy)[k]

    def share_copy(h, k):
        block = block_of(h, k)
        src = own_piece(h) if k == 0 else kv_out.at[core, block, h]
        return remote(
            src, kv_out.at[core, block, h], share_send.at[h, k], share_recv.at[h, k], partner
        )

    def share_arrival(h, k):
        place = kv_out.at[other, block_of(h, k), h]
        return remote(place, place, share_send.at[h, k], share_recv.at[h, k], partner)

    def kv_keep(h):
        return pltpu.make_async_copy(own_piece(h), kv_out.at[core, stream, h], keep_local.at[h])

    def query_piece(h):
        return mine_ref.at[h, stream, pl.ds(kv_rows, q_rows)]

    def query_copy(h):
        return remote(
            query_piece(h),
            query_out.at[core, h],
            query_send.at[h],
            query_recv.at[h],
            partner,
        )

    def query_arrival(h):
        return remote(
            query_piece(h),
            query_out.at[other, h],
            query_send.at[h],
            query_recv.at[h],
            partner,
        )

    def query_keep(h):
        return pltpu.make_async_copy(query_piece(h), query_out.at[core, h], keep_local.at[2 + h])

    def spread_event(h):
        spread_one(h).start()
        spread_two(h, 0).start()
        share_copy(h, 0).start()
        kv_keep(h).start()
        flat = lat_chunks + h * half_chunks + kv_chunks
        for k in range(0, q_rows, 16):
            at = flat * ZROWS + kv_rows * 0 + k
            chunk, row = at // ZROWS, at % ZROWS
            mine_ref[h, stream, kv_rows + k : kv_rows + k + 16, :] = line_ref[
                chunk, row : row + 16, :
            ]
        query_copy(h).start()
        query_keep(h).start()
        if h == 0:
            at = flat * ZROWS + q_rows
            chunk, row = at // ZROWS, at % ZROWS
            small_out[...] = line_ref[chunk, row : row + 16, :]

    tail = LAG * (chips - 1)
    ready = lambda h: lat_chunks + (h + 1) * half_chunks - 1 + tail
    events = {}

    def at_tick(tick, run):
        events.setdefault(tick, []).append(run)

    parts = rows // token_step
    for i in range(parts):
        at_tick(TOKEN_TICKS[i % len(TOKEN_TICKS)], functools.partial(token_part, i))
    for k in range(4):
        at_tick(WIDE_START_TICKS[k], functools.partial(wide_start, k))
    at_tick(KV_TICKS[0], token_other)
    at_tick(KV_TICKS[1], token_own)
    at_tick(PAIR_TICK, pair_event)
    at_tick(ONE_TICK, one_event)
    at_tick(TWO_TICK, two_event)
    for sub in range(SUBS):
        at_tick(WIDE_ONE_TICKS[sub], functools.partial(wide_event_one, sub))
        at_tick(WIDE_TWO_TICKS[sub], functools.partial(wide_event_two, sub))
    load.wait()

    def step(t, carry):
        line_step(t)
        for tick in sorted(events):

            @pl.when(t == tick)
            def _(tick=tick):
                for run in events[tick]:
                    run()

        return carry

    lax.fori_loop(0, ready(0) + 1, step, 0)
    spread_event(0)
    lax.fori_loop(ready(0) + 1, ready(1) + 1, step, 0)
    spread_event(1)
    for sub in range(SUBS):
        wide_event_three(sub)
    for h in range(2):
        spread_one_arrival(h).wait_recv()
        spread_two(h, 1).start()
        share_copy(h, 1).start()
    for h in range(2):
        for n in range(2):
            spread_two_arrival(h, n).wait_recv()
            share_copy(h, 2 + n).start()

    def finish_lat(i, carry):
        dpair_copy(i).wait_send()
        back_copy(i).wait_send()
        back_arrival(i).wait_recv()
        back_keep(i).wait()
        return carry

    lax.fori_loop(0, lat_chunks, finish_lat, 0)

    def finish_line(i, carry):
        @pl.when(has_right)
        def _():
            right_copy(i).wait_send()

        @pl.when(has_left)
        def _():
            left_copy(i).wait_send()

        return carry

    lax.fori_loop(0, all_chunks, finish_line, 0)
    for copy in pairs:
        copy.wait_send()
    for h in range(2):
        for n in range(2):
            one_copy(h, n).wait_send()
            spread_two(h, n).wait_send()
        two_copy(h).wait_send()
        spread_one(h).wait_send()
        kv_keep(h).wait()
        query_copy(h).wait_send()
        query_arrival(h).wait_recv()
        query_keep(h).wait()
        for k in range(4):
            share_copy(h, k).wait_send()
            share_arrival(h, k).wait_recv()
        for sub in range(SUBS):
            for n in range(2):
                wide_one_copy(h, n, sub).wait_send()
                wide_core_copy(n, h, sub).wait_send()
                wide_core_arrival(n, h, sub).wait_recv()
            wide_two_copy(h, sub).wait_send()
            wide_z_copy(h, sub).wait_send()
            wide_keep(h, sub).wait()


def gradients(
    dlat, dmid, a, b, side, dwq, vec, dgain_q, place, tokens, tsort, dkv, gain_t, wk, wv
):
    rows, width = tokens.shape
    half = dlat.shape[0] // 2
    lat_chunks = half // ZROWS
    wide_rows, wide_cols = a.shape[1] + side.shape[1], b.shape[2]
    share = width // 4
    kv_rows, q_rows = share // 2, share // 4
    block = kv_rows + q_rows + 16
    all_chunks = lat_chunks + 2 * block // ZROWS
    sds = jax.ShapeDtypeStruct
    dma = pltpu.SemaphoreType.DMA
    buf = lambda *shape: pltpu.VMEM(shape, F32)
    both = lambda *shape: [dma(shape), dma(shape)]
    return pl.pallas_call(
        gradient_kernel,
        name="gradients",
        out_shape=(
            sds((2, lat_chunks, ZROWS, width), F32),
            sds((2, 2, wide_rows, wide_cols), F32),
            sds((2, 4, 2, kv_rows // ZROWS, ZROWS, width), F32),
            sds((2, 2, q_rows, width), F32),
            sds((16, width), F32),
            sds((rows, width), F32),
        ),
        in_specs=[anywhere()] + [vmem()] * 14,
        out_specs=(anywhere(),) * 4 + (vmem(),) * 2,
        scratch_shapes=[
            buf(all_chunks, ZROWS, width),
            buf(all_chunks, ZROWS, width),
            buf(all_chunks, ZROWS, width),
            buf(lat_chunks, ZROWS, width),
            buf(4, wide_rows, wide_cols),
            buf(2, 2, wide_rows // 2, wide_cols),
            buf(2, wide_rows // 2, wide_cols),
            buf(2, 4, kv_rows, width),
            buf(2, 4, block, width),
            buf(2, 4, block, width),
            buf(2, 2, block, width),
            buf(2, block, width),
            buf(4, 16, width),
            buf(width, 128),
            dma,
        ]
        + both(lat_chunks)
        + both(all_chunks)
        + both(all_chunks)
        + both(lat_chunks)
        + [dma((lat_chunks,))]
        + both(2, 2, SUBS)
        + both(2, SUBS)
        + both(2, SUBS)
        + both(2, 2, SUBS)
        + [dma((2, SUBS))]
        + both(5)
        + both(2, 2)
        + both(2)
        + both(3, 2)
        + both(2, 4)
        + both(2)
        + [dma((4,))],
        compiler_params=pltpu.CompilerParams(
            vmem_limit_bytes=VMEM_BYTES, collective_id=2, has_side_effects=True
        ),
    )(
        dlat.reshape(2, lat_chunks, ZROWS, width),
        dmid.reshape(lat_chunks, ZROWS, width),
        a,
        b,
        side,
        dwq.reshape(4, 2, 2, q_rows, width),
        vec,
        dgain_q,
        place,
        tokens,
        tsort,
        dkv,
        gain_t,
        wk,
        wv,
    )


def closing_kernel(
    dlat_hbm,
    gather_hbm,
    kv_hbm,
    query_ref,
    small_ref,
    dtok_hbm,
    dlat_out,
    dtok_out,
    up_out,
    key_out,
    val_out,
    down_ref,
    out_ref,
    wq_ref,
    gain_q_ref,
    gain_t_ref,
    gain_mlp_ref,
    bup_ref,
    bdn_ref,
    wide_ref,
    side_ref,
    sems,
):
    width = small_ref.shape[1]
    cols = wide_ref.shape[2]
    moves = [
        (gather_hbm.at[1], wide_ref),
        (gather_hbm.at[0, :, pl.ds(width, side_ref.shape[1])], side_ref),
        (kv_hbm.at[0], key_out),
        (kv_hbm.at[1], val_out),
        (dlat_hbm, dlat_out),
        (dtok_hbm, dtok_out),
    ]
    for e in range(2):
        moves.append((gather_hbm.at[0, e, pl.ds(0, width)], up_out.at[:, pl.ds(e * cols, cols)]))
    copies = [pltpu.make_async_copy(a, b, sems.at[i]) for i, (a, b) in enumerate(moves)]
    for copy in copies:
        copy.start()
    stream = lax.axis_index("stream")
    gain_t_ref[...] = small_ref[4]
    bup_ref[...] = small_ref[0]
    size = gain_q_ref.shape[0]
    for i, ref in ((1, gain_q_ref), (2, gain_mlp_ref), (3, bdn_ref)):
        line = small_ref[i : i + 1, :]
        piece = line[:, :size]
        for k in range(1, width // size):
            piece = jnp.where(stream == k, line[:, k * size : (k + 1) * size], piece)
        ref[...] = piece[0]
    wq_ref[...] = query_ref[...].T
    copies[0].wait()
    copies[1].wait()
    for e in range(2):
        span = slice(e * cols, (e + 1) * cols)
        down_ref[span, :] = wide_ref[e, :width, :].T
        out_ref[span, :] = jnp.concatenate((side_ref[e], wide_ref[e, width:, :]), 0).T
    for copy in copies[2:]:
        copy.wait()


def closing(dlat, gather, kv, query, small, dtok):
    width = small.shape[1]
    wide_rows, cols = gather.shape[2:]
    share = query.shape[0]
    rows = dtok.shape[0]
    sds = lambda *shape: jax.ShapeDtypeStruct(shape, F32)
    return pl.pallas_call(
        closing_kernel,
        name="closing",
        out_shape=(
            sds(*dlat.shape),
            sds(rows, width),
            sds(width, 2 * cols),
            sds(width, width),
            sds(width, width),
            sds(2 * cols, width),
            sds(width, share),
            sds(width, share),
            sds(share),
            sds(width),
            sds(share),
            sds(2 * cols),
            sds(share),
        ),
        in_specs=[anywhere()] * 3 + [vmem()] * 2 + [anywhere()],
        out_specs=(anywhere(),) * 5 + (vmem(),) * 8,
        scratch_shapes=[
            pltpu.VMEM((2, wide_rows, cols), F32),
            pltpu.VMEM((2, wide_rows - width, cols), F32),
            pltpu.SemaphoreType.DMA((8,)),
        ],
        compiler_params=pltpu.CompilerParams(vmem_limit_bytes=VMEM_BYTES),
    )(dlat, gather, kv, query, small, dtok)


def local(
    latents,
    tokens,
    token_sample,
    token_mask,
    drop_mask,
    gain_query,
    w_query,
    gain_token,
    w_key,
    w_value,
    w_out,
    gain_mlp,
    w_up,
    b_up,
    w_down,
    b_down,
    cotangent,
):
    samples, lat_rows, width = latents.shape
    part, keys, values, tsort, query, normed, place, bounds = attend_forward(
        token_sample, token_mask, tokens, latents, gain_query, w_query, gain_token, w_key, w_value
    )
    msg, result, dmid, a, b, side, vec = latent_block(
        part, drop_mask, latents, cotangent, w_out, gain_mlp, w_up, b_up, w_down, b_down
    )
    dkv, dlat, dgain_q, dwq = attend_backward(
        bounds, latents, keys, values, query, normed, msg, gain_query, w_query
    )
    dlat, gather, kv, dwq, small, d_tokens = gradients(
        dlat, dmid, a, b, side, dwq, vec, dgain_q, place, tokens, tsort, dkv, gain_token,
        w_key, w_value,
    )
    (
        d_latents,
        d_tokens,
        grad_up,
        grad_key,
        grad_value,
        grad_down,
        grad_out,
        grad_query,
        grad_gquery,
        grad_gtoken,
        grad_gmlp,
        grad_bup,
        grad_bdown,
    ) = closing(
        dlat.reshape(samples * lat_rows, width),
        gather,
        kv.reshape(2, width, width),
        dwq.reshape(-1, width),
        small,
        d_tokens,
    )
    return (
        result.reshape(latents.shape),
        d_latents.reshape(latents.shape),
        d_tokens,
        grad_gquery,
        grad_query,
        grad_gtoken,
        grad_key,
        grad_value,
        grad_out,
        grad_gmlp,
        grad_up,
        grad_bup,
        grad_down,
        grad_bdown,
    )


def solution(mesh):
    return jax.shard_map(
        local,
        mesh=mesh,
        in_specs=(
            P("stream", None, None),
            P(("stream", "tok"), None),
            P(("stream", "tok")),
            P(("stream", "tok")),
            P(),
            P(),
            P(),
            P(),
            P(),
            P(),
            P(),
            P(),
            P(),
            P(),
            P(),
            P(),
            P("stream", None, None),
        ),
        out_specs=(
            P("stream", None, None),
            P("stream", None, None),
            P(("stream", "tok"), None),
            P("stream"),
            P(None, "stream"),
            P(),
            P(),
            P(),
            P(None, "stream"),
            P("stream"),
            P(None, "stream"),
            P("stream"),
            P("stream", None),
            P("stream"),
        ),
        check_vma=False,
    )
```

```python
import functools

import jax
import jax.numpy as jnp
from jax import lax
from jax.experimental import pallas as pl
from jax.experimental.pallas import tpu as pltpu
from jax.sharding import PartitionSpec as P

HEADS = 12
HEAD_DIM = 64
PAIRS = HEADS // 2
PIECES = 4
PIECE_HEADS = HEADS // PIECES
NUM_ROWS = PIECE_HEADS * HEAD_DIM
PIECE_ROWS = NUM_ROWS + 16
MSG_ROWS = HEADS * HEAD_DIM + 32
BLOCK = 256
LAG = 2
GAP = 6
SUBS = 3
EARLY_SUBS = 1
SPREAD_LAG = 3
WIDE_START_TICKS = (1, 2, 2, 4)
KV_TICKS = (0, 3)
PAIR_TICK = 5
MORE_TICK = 21
ONE_TICK = 15
TWO_TICK = 20
WIDE_ONE_TICKS = (10, 27, 30)
WIDE_TWO_TICKS = (16, 32, 35)
WIDE_THREE_TICKS = (25, -1, -1)
TOKEN_TICKS = (6, 7, 8, 9, 11, 12, 13, 16)
NEG = -1e30
F32 = jnp.float32
BF16 = jnp.bfloat16
VMEM_BYTES = 56 * 1024 * 1024


def norm_parts(values):
    center = values - jnp.mean(values, -1, keepdims=True)
    spread = jnp.mean(center * center, -1, keepdims=True)
    inv = lax.rsqrt(spread + 1e-05)
    return center * inv, inv


def norm_back(unit, inv, gain, grad):
    scaled = grad * gain
    inner = scaled - jnp.mean(scaled, -1, keepdims=True)
    return inv * (inner - unit * jnp.mean(scaled * unit, -1, keepdims=True))


def dot(a, b, contract=(1, 0)):
    return lax.dot_general(
        a, b, (((contract[0],), (contract[1],)), ((), ())), preferred_element_type=F32
    )


def row(ref):
    return ref[...].reshape(1, ref.shape[0])


def piece_of(head):
    return head // PIECE_HEADS, head % PIECE_HEADS


def forward_kernel(
    sample_ref,
    mask_ref,
    tok_ref,
    lat_ref,
    gain_q_ref,
    wq_ref,
    gain_t_ref,
    wk_ref,
    wv_ref,
    part_ref,
    key_ref,
    val_ref,
    tsort_ref,
    query_ref,
    normed_ref,
    place_ref,
    bounds_ref,
    tnorm_ref,
    pos_ref,
    top_ref,
    den_ref,
    num_ref,
):
    samples = part_ref.shape[0]
    rows = tok_ref.shape[0]
    width = tok_ref.shape[1]
    lat_rows = 128
    step = 256

    named = row(sample_ref) - lax.axis_index("stream") * samples
    ids = jnp.where(row(mask_ref) == 1, named, -1)
    lane = lax.broadcasted_iota(jnp.int32, (samples, rows), 1)
    member = ids == lax.broadcasted_iota(jnp.int32, (samples, rows), 0)
    ones = jnp.where(member, 1.0, 0.0)
    count = ones
    shift = 1
    while shift < rows:
        count = count + jnp.where(lane >= shift, pltpu.roll(count, shift, 1), 0.0)
        shift *= 2
    rank = count - ones
    begin = jnp.int32(0)
    pos = jnp.full((1, rows), -1.0, F32)
    for s in range(samples):
        total = jnp.sum(ones[s : s + 1]).astype(jnp.int32)
        bounds_ref[s] = begin
        bounds_ref[samples + s] = total
        pos = jnp.where(member[s : s + 1], rank[s : s + 1] + begin.astype(F32), pos)
        begin = begin + total
    pos_ref[...] = jnp.broadcast_to(pos, (8, rows))
    place_ref[...] = jnp.broadcast_to(pos, (128, rows)).T

    def token_norm(i, carry):
        at = pl.ds(pl.multiple_of(i * step, step), step)
        unit, _ = norm_parts(tok_ref[at, :].astype(F32))
        tnorm_ref[at, :] = (unit * row(gain_t_ref)).astype(BF16)
        return carry

    lax.fori_loop(0, rows // step, token_norm, 0)

    def token_sort(i, carry):
        at = pl.ds(pl.multiple_of(i * step, step), step)
        target = lax.broadcasted_iota(jnp.int32, (step, rows), 0) + i * step
        chosen = target.astype(F32) == pos_ref[0:1, :]
        pick = jnp.where(chosen, 1.0, 0.0).astype(BF16)
        tsort = dot(pick, tnorm_ref[...]).astype(BF16)
        tsort_ref[at, :] = tsort
        key_ref[at, :] = dot(tsort, wk_ref[...]).astype(BF16)
        val_ref[at, :] = dot(tsort, wv_ref[...]).astype(BF16)
        return carry

    lax.fori_loop(0, rows // step, token_sort, 0)
    key_ref[rows:, :] = jnp.zeros((BLOCK, width), BF16)
    val_ref[rows:, :] = jnp.zeros((BLOCK, width), BF16)

    def sample_step(s, carry):
        at = pl.ds(pl.multiple_of(s * lat_rows, lat_rows), lat_rows)
        unit, _ = norm_parts(lat_ref[at, :].astype(F32))
        normed = (unit * row(gain_q_ref)).astype(BF16)
        normed_ref[at, :] = normed
        query = dot(normed, wq_ref[...]) * 0.125
        turned = query.T.astype(BF16)
        blank = jnp.zeros((HEAD_DIM, lat_rows), BF16)
        for p in range(PAIRS):
            lo = 2 * p * HEAD_DIM
            query_ref[s, p, :HEAD_DIM, :lat_rows] = turned[lo : lo + HEAD_DIM]
            query_ref[s, p, :HEAD_DIM, lat_rows:] = blank
            query_ref[s, p, HEAD_DIM:, :lat_rows] = blank
            query_ref[s, p, HEAD_DIM:, lat_rows:] = turned[lo + HEAD_DIM : lo + 2 * HEAD_DIM]
        start = bounds_ref[s]
        total = bounds_ref[samples + s]
        base = lax.div(start, 16) * 16
        blocks = jnp.where(total > 0, lax.div(start + total - base + BLOCK - 1, BLOCK), 0)
        for piece in range(PIECES):
            part_ref[s, piece, NUM_ROWS:, :] = jnp.zeros((16, lat_rows), F32)
        num_ref[...] = jnp.zeros_like(num_ref)
        top_ref[...] = jnp.full_like(top_ref, NEG)
        den_ref[...] = jnp.zeros_like(den_ref)

        def block_step(b, carry):
            row = pl.multiple_of(base + b * BLOCK, 16)
            index = lax.broadcasted_iota(jnp.int32, (BLOCK, 2 * lat_rows), 0) + row
            inside = (index >= start) & (index < start + total)
            for p in range(PAIRS):
                cols = slice(p * 128, (p + 1) * 128)
                score = dot(key_ref[pl.ds(row, BLOCK), cols], query_ref[s, p])
                score = jnp.where(inside, score, NEG)
                old = top_ref[p : p + 1, :]
                new = jnp.maximum(old, jnp.max(score, 0, keepdims=True))
                fade = jnp.exp(old - new)
                weight = jnp.exp(score - new)
                top_ref[p : p + 1, :] = new
                den_ref[p : p + 1, :] = den_ref[p : p + 1, :] * fade + jnp.sum(
                    weight, 0, keepdims=True
                )
                both = dot(val_ref[pl.ds(row, BLOCK), cols], weight.astype(BF16), (0, 0))
                for half in range(2):
                    at_rows = slice(p * 128 + half * HEAD_DIM, p * 128 + (half + 1) * HEAD_DIM)
                    at_cols = slice(half * lat_rows, (half + 1) * lat_rows)
                    num_ref[at_rows, :] = (
                        num_ref[at_rows, :] * fade[:, at_cols]
                        + both[half * HEAD_DIM : (half + 1) * HEAD_DIM, at_cols]
                    )
            return carry

        lax.fori_loop(0, blocks, block_step, 0)
        for h in range(HEADS):
            piece, i = piece_of(h)
            p, half = h // 2, h % 2
            at_cols = slice(half * lat_rows, (half + 1) * lat_rows)
            part_ref[s, piece, i * HEAD_DIM : (i + 1) * HEAD_DIM, :] = num_ref[
                h * HEAD_DIM : (h + 1) * HEAD_DIM, :
            ]
            part_ref[s, piece, NUM_ROWS + i : NUM_ROWS + i + 1, :] = top_ref[p : p + 1, at_cols]
            part_ref[s, piece, NUM_ROWS + 8 + i : NUM_ROWS + 9 + i, :] = den_ref[
                p : p + 1, at_cols
            ]
        return carry

    lax.fori_loop(0, samples, sample_step, 0)


def vmem():
    return pl.BlockSpec(memory_space=pltpu.VMEM)


def smem():
    return pl.BlockSpec(memory_space=pltpu.SMEM)


def attend_forward(sample, mask, tokens, latents, gain_q, wq, gain_t, wk, wv):
    samples, lat_rows, width = latents.shape
    rows = tokens.shape[0]
    sds = jax.ShapeDtypeStruct
    return pl.pallas_call(
        forward_kernel,
        name="attend_forward",
        out_shape=(
            sds((samples, PIECES, PIECE_ROWS, lat_rows), F32),
            sds((rows + BLOCK, width), BF16),
            sds((rows + BLOCK, width), BF16),
            sds((rows, width), BF16),
            sds((samples, PAIRS, 128, 2 * lat_rows), BF16),
            sds((samples * lat_rows, width), BF16),
            sds((rows, 128), F32),
            sds((2 * samples,), jnp.int32),
        ),
        in_specs=[vmem()] * 9,
        out_specs=(vmem(),) * 7 + (smem(),),
        scratch_shapes=[
            pltpu.VMEM((rows, width), BF16),
            pltpu.VMEM((8, rows), F32),
            pltpu.VMEM((8, 2 * lat_rows), F32),
            pltpu.VMEM((8, 2 * lat_rows), F32),
            pltpu.VMEM((width, lat_rows), F32),
        ],
        compiler_params=pltpu.CompilerParams(vmem_limit_bytes=VMEM_BYTES),
    )(
        sample,
        mask,
        tokens,
        latents.reshape(samples * lat_rows, width),
        gain_q,
        wq,
        gain_t,
        wk,
        wv,
    )


def backward_kernel(
    bounds_ref,
    lat_ref,
    key_ref,
    val_ref,
    query_ref,
    normed_ref,
    msg_ref,
    dmid_ref,
    gain_q_ref,
    wq_ref,
    res_hbm,
    dkv_ref,
    dlat_ref,
    dgain_ref,
    dwq_ref,
    res_out,
    dk_ref,
    dv_ref,
    grad_ref,
    dquery_ref,
    turn_ref,
    stat_ref,
    res_ref,
    res_sems,
):
    samples = query_ref.shape[0]
    rows = dkv_ref.shape[1]
    lat_rows = 128
    step = 256
    width = dwq_ref.shape[0]
    for r in range(0, rows + BLOCK, step):
        dk_ref[r : r + step, :] = jnp.zeros((step, dk_ref.shape[1]), F32)
        dv_ref[r : r + step, :] = jnp.zeros((step, dv_ref.shape[1]), F32)
    res_load = pltpu.make_async_copy(res_hbm, res_ref, res_sems.at[0])
    res_store = pltpu.make_async_copy(res_ref, res_out, res_sems.at[1])
    res_load.start()
    member = lax.axis_index("tok")
    grad_ref[...] = jnp.zeros_like(grad_ref)
    dgain_ref[...] = jnp.zeros_like(dgain_ref)

    def sample_step(s, carry):
        start = bounds_ref[s]
        total = bounds_ref[samples + s]
        base = lax.div(start, 16) * 16
        blocks = jnp.where(total > 0, lax.div(start + total - base + BLOCK - 1, BLOCK), 0)
        turn_ref[...] = jnp.zeros_like(turn_ref)
        for h in range(HEADS):
            p, half = h // 2, h % 2
            grad_ref[
                p,
                half * HEAD_DIM : (half + 1) * HEAD_DIM,
                half * lat_rows : (half + 1) * lat_rows,
            ] = msg_ref[s, h * HEAD_DIM : (h + 1) * HEAD_DIM, :].astype(BF16)

            stat_ref[p : p + 1, half * lat_rows : (half + 1) * lat_rows] = msg_ref[
                s, width + h : width + h + 1, :
            ]
            stat_ref[8 + p : 9 + p, half * lat_rows : (half + 1) * lat_rows] = msg_ref[
                s, width + 16 + h : width + 17 + h, :
            ]

        def block_step(b, carry):
            row = pl.multiple_of(base + b * BLOCK, 16)
            index = lax.broadcasted_iota(jnp.int32, (BLOCK, 2 * lat_rows), 0) + row
            inside = (index >= start) & (index < start + total)
            at = pl.ds(row, BLOCK)
            for p in range(PAIRS):
                cols = slice(p * 128, (p + 1) * 128)
                key = key_ref[at, cols]
                query = query_ref[s, p]
                grad = grad_ref[p]
                score = dot(key, query)
                weight = jnp.where(inside, jnp.exp(score - stat_ref[p : p + 1, :]), 0.0)
                dprob = dot(val_ref[at, cols], grad)
                dscore = (weight * (dprob - stat_ref[8 + p : 9 + p, :])).astype(BF16)
                dv_ref[at, cols] += dot(weight.astype(BF16), grad, (1, 1))
                dk_ref[at, cols] += dot(dscore, query, (1, 1))
                both = dot(key, dscore, (0, 0))
                for half in range(2):
                    turn_ref[
                        p * 128 + half * HEAD_DIM : p * 128 + (half + 1) * HEAD_DIM, :
                    ] += both[
                        half * HEAD_DIM : (half + 1) * HEAD_DIM,
                        half * lat_rows : (half + 1) * lat_rows,
                    ]
            return carry

        lax.fori_loop(0, blocks, block_step, 0)
        at = pl.ds(pl.multiple_of(s * lat_rows, lat_rows), lat_rows)
        dquery = (turn_ref[...].T * 0.125).astype(BF16)
        dquery_ref[at, :] = dquery
        unit, inv = norm_parts(lat_ref[at, :].astype(F32))
        dnormed = dot(dquery, wq_ref[...], (1, 1))
        dgain_ref[0:1, :] += jnp.sum(dnormed * unit, 0, keepdims=True)
        dlat = norm_back(unit, inv, row(gain_q_ref), dnormed)
        dlat_ref[at, :] = dlat
        j = s - lax.rem(member, 2) * (samples // 2)

        @pl.when((member < 2) & (j >= 0) & (j < samples // 2))
        def _():
            mine = pl.ds(pl.multiple_of(j * lat_rows, lat_rows), lat_rows)
            dlat_ref[at, :] = dlat + dmid_ref[mine, :]

        return carry

    lax.fori_loop(0, samples, sample_step, 0)
    res_load.wait()
    res_store.start()
    for r in range(0, rows, step):
        dkv_ref[0, r : r + step, :] = dk_ref[r : r + step, :].astype(BF16)
        dkv_ref[1, r : r + step, :] = dv_ref[r : r + step, :].astype(BF16)
    for c in range(0, width, 256):
        dwq_ref[c : c + 256, :] = dot(dquery_ref[:, c : c + 256], normed_ref[...], (0, 0))
    res_store.wait()


def attend_backward(bounds, latents, keys, values, query, normed, msg, dmid, gain_q, wq, result):
    samples, lat_rows, width = latents.shape
    rows = keys.shape[0] - BLOCK
    sds = jax.ShapeDtypeStruct
    return pl.pallas_call(
        backward_kernel,
        name="attend_backward",
        out_shape=(
            sds((2, rows, width), BF16),
            sds((samples * lat_rows, width), F32),
            sds((8, width), F32),
            sds((width, width), F32),
            sds(result.shape, BF16),
        ),
        in_specs=[smem()] + [vmem()] * 9 + [anywhere()],
        out_specs=(vmem(),) * 4 + (anywhere(),),
        scratch_shapes=[
            pltpu.VMEM((rows + BLOCK, width), F32),
            pltpu.VMEM((rows + BLOCK, width), F32),
            pltpu.VMEM((PAIRS, 128, 2 * lat_rows), BF16),
            pltpu.VMEM((samples * lat_rows, width), BF16),
            pltpu.VMEM((width, lat_rows), F32),
            pltpu.VMEM((16, 2 * lat_rows), F32),
            pltpu.VMEM(result.shape, BF16),
            pltpu.SemaphoreType.DMA((2,)),
        ],
        compiler_params=pltpu.CompilerParams(vmem_limit_bytes=VMEM_BYTES),
    )(
        bounds,
        latents.reshape(samples * lat_rows, width),
        keys,
        values,
        query,
        normed,
        msg,
        dmid,
        gain_q,
        wq,
        result,
    )


MESH = pl.DeviceIdType.MESH


def merge(a_ref, b_ref, out_ref):
    a_tail, b_tail = a_ref[NUM_ROWS : NUM_ROWS + 8, :], b_ref[NUM_ROWS : NUM_ROWS + 8, :]
    top = jnp.maximum(a_tail, b_tail)
    a_fade, b_fade = jnp.exp(a_tail - top), jnp.exp(b_tail - top)
    den = a_ref[NUM_ROWS + 8 :, :] * a_fade + b_ref[NUM_ROWS + 8 :, :] * b_fade
    for i in range(PIECE_HEADS):
        at = slice(i * HEAD_DIM, (i + 1) * HEAD_DIM)
        out_ref[at, :] = (
            a_ref[at, :] * a_fade[i : i + 1, :] + b_ref[at, :] * b_fade[i : i + 1, :]
        )
    out_ref[NUM_ROWS : NUM_ROWS + 8, :] = top
    out_ref[NUM_ROWS + 8 :, :] = den


def gelu_parts(x):
    c = 0.7978845608028654
    square = x * x
    t = jnp.tanh(c * x * (1.0 + 0.044715 * square))
    half = 0.5 * (1.0 + t)
    slope = half + (0.5 * c) * x * (1.0 - t * t) * (1.0 + (3 * 0.044715) * square)
    return x * half, slope


def latent_kernel(
    part_hbm,
    drop_ref,
    lat_ref,
    cot_ref,
    wo_hbm,
    gain_ref,
    wup_hbm,
    bup_ref,
    wdn_hbm,
    bdn_ref,
    msg_ref,
    res_ref,
    dmid_ref,
    a_ref,
    b_ref,
    side_ref,
    vec_ref,
    wo_ref,
    wup_ref,
    wdn_ref,
    pair_ref,
    own_ref,
    right_in,
    right_out,
    left_in,
    left_out,
    res_out,
    res_in,
    att_t_ref,
    mid_ref,
    acc_ref,
    dacc_ref,
    hn_ref,
    dm_ref,
    da_ref,
    att_ref,
    hn_out,
    hn_in,
    half_out,
    half_in,
    side_all,
    side_in,
    hn_send,
    hn_recv,
    half_send,
    half_recv,
    side_send,
    side_recv,
    own_sem,
    weight_sem,
    pair_send,
    pair_recv,
    right_send,
    right_recv,
    left_send,
    left_recv,
    msg_send,
    msg_recv,
    res_send,
    res_recv,
):
    samples = msg_ref.shape[0]
    half = samples // 2
    lat_rows = 128
    width = lat_ref.shape[1]
    chunks = half * PIECES
    stream = lax.axis_index("stream")
    tok = lax.axis_index("tok")
    chips = lax.axis_size("tok") // 2
    core = lax.rem(tok, 2)
    chip = lax.div(tok, 2)
    parity = lax.rem(chip, 2)
    partner = (stream, tok + 1 - 2 * core)
    right = (stream, tok + 2)
    left = (stream, tok - 2)
    has_right = chip < chips - 1
    has_left = chip > 0
    on_first = core == 0

    barrier = pltpu.get_barrier_semaphore()
    pl.semaphore_signal(barrier, inc=1, device_id=partner, device_id_type=MESH)

    @pl.when(has_right)
    def _():
        pl.semaphore_signal(barrier, inc=1, device_id=right, device_id_type=MESH)

    @pl.when(has_left)
    def _():
        pl.semaphore_signal(barrier, inc=1, device_id=left, device_id_type=MESH)

    own_load = pltpu.make_async_copy(
        part_hbm.at[pl.ds(core * chunks, chunks)], own_ref, own_sem
    )
    own_load.start()
    weights = [
        pltpu.make_async_copy(src, dst, weight_sem.at[i])
        for i, (src, dst) in enumerate(((wo_hbm, wo_ref), (wup_hbm, wup_ref), (wdn_hbm, wdn_ref)))
    ]
    for copy in weights:
        copy.start()
    pl.semaphore_wait(
        barrier, 1 + has_right.astype(jnp.int32) + has_left.astype(jnp.int32)
    )

    def pair_copy(i):
        return pltpu.make_async_remote_copy(
            src_ref=part_hbm.at[(1 - core) * chunks + i],
            dst_ref=pair_ref.at[i],
            send_sem=pair_send.at[i],
            recv_sem=pair_recv.at[i],
            device_id=partner,
            device_id_type=MESH,
        )

    def right_copy(i):
        return pltpu.make_async_remote_copy(
            src_ref=right_out.at[i],
            dst_ref=right_in.at[i],
            send_sem=right_send.at[i],
            recv_sem=right_recv.at[i],
            device_id=right,
            device_id_type=MESH,
        )

    def left_copy(i):
        return pltpu.make_async_remote_copy(
            src_ref=left_out.at[i],
            dst_ref=left_in.at[i],
            send_sem=left_send.at[i],
            recv_sem=left_recv.at[i],
            device_id=left,
            device_id_type=MESH,
        )

    def msg_copy(j):
        at = core * half + j
        return pltpu.make_async_remote_copy(
            src_ref=msg_ref.at[at],
            dst_ref=msg_ref.at[at],
            send_sem=msg_send.at[j],
            recv_sem=msg_recv.at[j],
            device_id=partner,
            device_id_type=MESH,
        )

    def msg_arrival(j):
        at = (1 - core) * half + j
        return pltpu.make_async_remote_copy(
            src_ref=msg_ref.at[at],
            dst_ref=msg_ref.at[at],
            send_sem=msg_send.at[j],
            recv_sem=msg_recv.at[j],
            device_id=partner,
            device_id_type=MESH,
        )

    def res_copy(j):
        return pltpu.make_async_remote_copy(
            src_ref=res_out.at[j],
            dst_ref=res_in.at[j],
            send_sem=res_send.at[j],
            recv_sem=res_recv.at[j],
            device_id=partner,
            device_id_type=MESH,
        )

    def hn_copy(j):
        return pltpu.make_async_remote_copy(
            src_ref=hn_out.at[j],
            dst_ref=hn_in.at[j],
            send_sem=hn_send.at[j],
            recv_sem=hn_recv.at[j],
            device_id=partner,
            device_id_type=MESH,
        )

    def half_copy(i):
        return pltpu.make_async_remote_copy(
            src_ref=half_out.at[i],
            dst_ref=half_in.at[i],
            send_sem=half_send.at[i],
            recv_sem=half_recv.at[i],
            device_id=partner,
            device_id_type=MESH,
        )

    side_copy = pltpu.make_async_remote_copy(
        src_ref=side_all.at[:, 1 - core],
        dst_ref=side_in,
        send_sem=side_send,
        recv_sem=side_recv,
        device_id=partner,
        device_id_type=MESH,
    )

    def start_pair(i, carry):
        pair_copy(i).start()
        return carry

    lax.fori_loop(0, chunks, start_pair, 0)
    own_load.wait()

    drop = row(drop_ref).astype(F32)
    scale_all = drop * drop.shape[1] / jnp.sum(drop, 1, keepdims=True)
    drop_lane = lax.broadcasted_iota(jnp.int32, drop.shape, 1)
    vec_ref[...] = jnp.zeros_like(vec_ref)

    def mlp(j, q):
        sample = core * half + j
        rows = pl.ds(pl.multiple_of(sample * lat_rows, lat_rows), lat_rows)
        mine = pl.ds(pl.multiple_of(j * lat_rows, lat_rows), lat_rows)
        scale = jnp.sum(
            jnp.where(drop_lane == stream * samples + sample, scale_all, 0.0), 1, keepdims=True
        )

        @pl.when(q == 0)
        def _():
            for h in range(HEADS):
                piece, i = piece_of(h)
                at = j * PIECES + piece
                den = own_ref[at, NUM_ROWS + 8 + i : NUM_ROWS + 9 + i, :]
                att_t_ref[h * HEAD_DIM : (h + 1) * HEAD_DIM, :] = own_ref[
                    at, i * HEAD_DIM : (i + 1) * HEAD_DIM, :
                ] * (1.0 / den)
            att = att_t_ref[...].T.astype(BF16)
            att_ref[mine, :] = jnp.where(parity == 0, att[:, : width // 2], att[:, width // 2 :])
            mid = lat_ref[rows, :].astype(F32) + scale * dot(att, wo_ref[...])
            mid_ref[...] = mid
            unit, _ = norm_parts(mid)
            hn = (unit * row(gain_ref)).astype(BF16)
            dm = (scale * cot_ref[rows, :].astype(F32)).astype(BF16)
            hn_ref[...] = hn
            dm_ref[...] = dm
            a_ref[rows, :] = jnp.where(on_first, hn, dm)

            @pl.when(jnp.logical_not(on_first))
            def _():
                hn_out[j] = hn.astype(F32)
                hn_copy(j).start()

            vec_ref[1:2, :width] += jnp.sum(dm.astype(F32), 0, keepdims=True)
            acc_ref[...] = jnp.broadcast_to(row(bdn_ref), acc_ref.shape)
            dacc_ref[...] = jnp.zeros_like(dacc_ref)

        span = wup_ref.shape[1] // PIECES
        cols = pl.ds(pl.multiple_of(q * span, 128), span)
        pre = dot(hn_ref[...], wup_ref[:, cols]) + bup_ref[cols].reshape(1, span)
        active, slope = gelu_parts(pre)
        hidden = active.astype(BF16)
        acc_ref[...] += dot(hidden, wdn_ref[cols, :])
        dpre = (slope * dot(dm_ref[...], wdn_ref[cols, :], (1, 1))).astype(BF16)
        piece = j * PIECES + q
        near_half = lambda x: jnp.where(parity == 0, x[:, : span // 2], x[:, span // 2 :])
        hidden_half, dpre_half = near_half(hidden), near_half(dpre)
        b_ref[q, rows, :] = jnp.where(on_first, dpre_half, hidden_half)
        half_out[piece] = jnp.where(on_first, hidden_half, dpre_half).astype(F32)
        half_copy(piece).start()
        vec_ref[0:1, cols] += jnp.sum(dpre.astype(F32), 0, keepdims=True)
        dacc_ref[...] += dot(dpre, wup_ref[:, cols], (1, 1))

        @pl.when(q == PIECES - 1)
        def _():
            mid = mid_ref[...]
            res = (mid + scale * acc_ref[...]).astype(BF16)
            res_ref[rows, :] = res
            res_out[j] = res.astype(F32)
            res_copy(j).start()
            unit, inv = norm_parts(mid)
            dhn = dacc_ref[...]
            vec_ref[2:3, :width] += jnp.sum(dhn * unit, 0, keepdims=True)
            dmid = cot_ref[rows, :].astype(F32) + norm_back(unit, inv, row(gain_ref), dhn)
            dmid_ref[mine, :] = dmid
            da = (scale * dmid).astype(BF16)
            da_ref[mine, :] = da
            datt_t = dot(wo_ref[...], da, (1, 1)).astype(BF16).astype(F32)
            msg_ref[sample, width:, :] = jnp.zeros((MSG_ROWS - width, lat_rows), F32)
            for h in range(HEADS):
                piece, i = piece_of(h)
                at = j * PIECES + piece
                inverse = 1.0 / own_ref[at, NUM_ROWS + 8 + i : NUM_ROWS + 9 + i, :]
                span_h = slice(h * HEAD_DIM, (h + 1) * HEAD_DIM)
                one = datt_t[span_h]
                msg_ref[sample, span_h, :] = (one * inverse).astype(BF16).astype(F32)
                delta = jnp.sum(one * att_t_ref[span_h, :], 0, keepdims=True) * inverse
                msg_ref[sample, width + h : width + h + 1, :] = own_ref[
                    at, NUM_ROWS + i : NUM_ROWS + i + 1, :
                ]
                msg_ref[sample, width + 16 + h : width + 17 + h, :] = delta
            msg_copy(j).start()

    def step(t, carry):
        @pl.when(t < chunks)
        def _():
            pair_copy(t).wait_recv()
            merge(own_ref.at[t], pair_ref.at[t], own_ref.at[t])

        r = t - LAG * chip

        @pl.when((r >= 0) & (r < chunks))
        def _():
            @pl.when(has_left)
            def _():
                right_copy(r).wait_recv()
                merge(own_ref.at[r], right_in.at[r], right_out.at[r])

            @pl.when(jnp.logical_not(has_left))
            def _():
                right_out[r] = own_ref[r]

            @pl.when(has_right)
            def _():
                right_copy(r).start()

        u = t - LAG * (chips - 1 - chip)

        @pl.when((u >= 0) & (u < chunks))
        def _():
            @pl.when(has_right)
            def _():
                left_copy(u).wait_recv()

            @pl.when(has_left)
            def _():
                @pl.when(has_right)
                def _():
                    merge(own_ref.at[u], left_in.at[u], left_out.at[u])

                @pl.when(jnp.logical_not(has_right))
                def _():
                    left_out[u] = own_ref[u]

                left_copy(u).start()

        w = t - LAG * jnp.maximum(chip, chips - 1 - chip)

        @pl.when((w >= 0) & (w < chunks))
        def _():
            @pl.when(has_right)
            def _():
                merge(right_out.at[w], left_in.at[w], own_ref.at[w])

            @pl.when(jnp.logical_not(has_right))
            def _():
                own_ref[w] = right_out[w]

        m = w - (PIECES - 1)

        @pl.when(m == 0)
        def _():
            for copy in weights:
                copy.wait()

        @pl.when((m >= 0) & (m < chunks))
        def _():
            mlp(lax.div(m, PIECES), lax.rem(m, PIECES))

        return carry

    lax.fori_loop(0, chunks + LAG * (chips - 1) + PIECES - 1, step, 0)

    share = width // 8
    for block in range(4):
        at = slice(block * 2 * share, (block + 1) * 2 * share)
        product = dot(da_ref[:, at], att_ref[...], (0, 0))
        side_all[block, 0] = product[:share]
        side_all[block, 1] = product[share:]
    side_copy.start()

    def finish_chunk(i, carry):
        pair_copy(i).wait_send()
        half_copy(i).wait_send()
        half_copy(i).wait_recv()
        at = ((1 - core) * half + lax.div(i, PIECES)) * lat_rows
        rows = pl.ds(pl.multiple_of(at, lat_rows), lat_rows)
        b_ref[lax.rem(i, PIECES), rows, :] = half_in[i].astype(BF16)

        @pl.when(has_right)
        def _():
            right_copy(i).wait_send()

        @pl.when(has_left)
        def _():
            left_copy(i).wait_send()

        return carry

    lax.fori_loop(0, chunks, finish_chunk, 0)

    def finish_sample(j, carry):
        res_copy(j).wait_recv()
        other = (1 - core) * half + j
        rows = pl.ds(pl.multiple_of(other * lat_rows, lat_rows), lat_rows)
        res_ref[rows, :] = res_in[j].astype(BF16)

        @pl.when(on_first)
        def _():
            hn_copy(j).wait_recv()
            a_ref[rows, :] = hn_in[j].astype(BF16)

        @pl.when(jnp.logical_not(on_first))
        def _():
            hn_copy(j).wait_send()
            scale = jnp.sum(
                jnp.where(drop_lane == stream * samples + other, scale_all, 0.0), 1, keepdims=True
            )
            a_ref[rows, :] = (scale * cot_ref[rows, :].astype(F32)).astype(BF16)

        res_copy(j).wait_send()
        msg_copy(j).wait_send()
        msg_arrival(j).wait_recv()
        return carry

    lax.fori_loop(0, half, finish_sample, 0)
    side_copy.wait()
    side_ref[...] = side_all[:, core] + side_in[...]


def anywhere():
    return pl.BlockSpec(memory_space=pl.ANY)


def latent_block(part, drop_mask, latents, cotangent, wo, gain, wup, bup, wdn, bdn):
    samples, lat_rows, width = latents.shape
    half = samples // 2
    chunks = half * PIECES
    hidden = wup.shape[1]
    sds = jax.ShapeDtypeStruct
    chunk = lambda: pltpu.VMEM((chunks, PIECE_ROWS, lat_rows), F32)
    dma = pltpu.SemaphoreType.DMA
    return pl.pallas_call(
        latent_kernel,
        name="latent_block",
        out_shape=(
            sds((samples, MSG_ROWS, lat_rows), F32),
            sds((samples * lat_rows, width), BF16),
            sds((half * lat_rows, width), F32),
            sds((samples * lat_rows, width), BF16),
            sds((PIECES, samples * lat_rows, hidden // PIECES // 2), BF16),
            sds((4, width // 8, width // 2), F32),
            sds((8, hidden), F32),
        ),
        in_specs=[
            anywhere(),
            vmem(),
            vmem(),
            vmem(),
            anywhere(),
            vmem(),
            anywhere(),
            vmem(),
            anywhere(),
            vmem(),
        ],
        out_specs=(vmem(),) * 7,
        scratch_shapes=[
            pltpu.VMEM(wo.shape, BF16),
            pltpu.VMEM(wup.shape, BF16),
            pltpu.VMEM(wdn.shape, BF16),
            chunk(),
            chunk(),
            chunk(),
            chunk(),
            chunk(),
            chunk(),
            pltpu.VMEM((half, lat_rows, width), F32),
            pltpu.VMEM((half, lat_rows, width), F32),
            pltpu.VMEM((width, lat_rows), F32),
            pltpu.VMEM((lat_rows, width), F32),
            pltpu.VMEM((lat_rows, width), F32),
            pltpu.VMEM((lat_rows, width), F32),
            pltpu.VMEM((lat_rows, width), BF16),
            pltpu.VMEM((lat_rows, width), BF16),
            pltpu.VMEM((half * lat_rows, width), BF16),
            pltpu.VMEM((half * lat_rows, width // 2), BF16),
            pltpu.VMEM((half, lat_rows, width), F32),
            pltpu.VMEM((half, lat_rows, width), F32),
            pltpu.VMEM((chunks, lat_rows, hidden // PIECES // 2), F32),
            pltpu.VMEM((chunks, lat_rows, hidden // PIECES // 2), F32),
            pltpu.VMEM((4, 2, width // 8, width // 2), F32),
            pltpu.VMEM((4, width // 8, width // 2), F32),
            dma((half,)),
            dma((half,)),
            dma((chunks,)),
            dma((chunks,)),
            dma,
            dma,
            dma,
            dma((3,)),
            dma((chunks,)),
            dma((chunks,)),
            dma((chunks,)),
            dma((chunks,)),
            dma((chunks,)),
            dma((chunks,)),
            dma((half,)),
            dma((half,)),
            dma((half,)),
            dma((half,)),
        ],
        compiler_params=pltpu.CompilerParams(
            vmem_limit_bytes=VMEM_BYTES, collective_id=1, has_side_effects=True
        ),
    )(
        part.reshape(samples * PIECES, PIECE_ROWS, lat_rows),
        drop_mask,
        latents.reshape(samples * lat_rows, width),
        cotangent.reshape(samples * lat_rows, width),
        wo,
        gain,
        wup,
        bup,
        wdn,
        bdn,
    )


ZROWS = 32


def gradient_kernel(
    dlat_hbm,
    a_hbm,
    b_hbm,
    side_ref,
    dwq_hbm,
    vec_ref,
    dgain_q_ref,
    place_ref,
    tok_hbm,
    tsort_hbm,
    dkv_hbm,
    gain_t_ref,
    wk_ref,
    wv_ref,
    dlat_out,
    gather_out,
    kv_out,
    query_out,
    small_out,
    dtok_out,
    line_ref,
    right_ref,
    left_ref,
    dmine_ref,
    wide_ref,
    wide_one,
    wide_two,
    send_ref,
    mine_ref,
    pair_ref,
    one_ref,
    two_ref,
    small_ref,
    gain_ref,
    wide_far,
    spread_ref,
    stage_ref,
    stage_sem,
    a_ref,
    b_ref,
    dwq_ref,
    tok_ref,
    tsort_ref,
    dkv_ref,
    load_sem,
    dpair_send,
    dpair_recv,
    right_send,
    right_recv,
    left_send,
    left_recv,
    back_send,
    back_recv,
    back_local,
    wide_one_send,
    wide_one_recv,
    wide_two_send,
    wide_two_recv,
    wide_z_send,
    wide_z_recv,
    wide_core_send,
    wide_core_recv,
    wide_local,
    pair_send,
    pair_recv,
    one_send,
    one_recv,
    two_send,
    two_recv,
    spread_send,
    spread_recv,
    share_send,
    share_recv,
    query_send,
    query_recv,
    query_local,
    keep_local,
):
    rows, width = tok_ref.shape
    lat_chunks = dmine_ref.shape[0]
    all_chunks = line_ref.shape[0]
    kv_rows = send_ref.shape[2]
    q_rows = query_out.shape[2]
    mix = kv_rows + q_rows
    half_chunks = (all_chunks - lat_chunks) // 2
    kv_chunks = kv_rows // ZROWS
    wide_half = wide_ref.shape[1] // 2
    sub_rows = wide_half // SUBS

    stream = lax.axis_index("stream")
    tok = lax.axis_index("tok")
    chips = lax.axis_size("tok") // 2
    core = lax.rem(tok, 2)
    chip = lax.div(tok, 2)
    other = 1 - core
    parity = lax.rem(chip, 2)
    flip_x = stream + 1 - 2 * lax.rem(stream, 2)
    flip_y = lax.rem(stream + 2, 4)
    flip_xy = 3 - stream
    partner = (stream, tok + 1 - 2 * core)
    right = (stream, tok + 2)
    left = (stream, tok - 2)
    beside = (stream, tok + 2 - 4 * parity)
    near = ((flip_x, tok), (flip_y, tok))
    first = (flip_x, flip_y)
    has_right = chip < chips - 1
    has_left = chip > 0

    barrier = pltpu.get_barrier_semaphore()
    for target in (partner,) + near:
        pl.semaphore_signal(barrier, inc=1, device_id=target, device_id_type=MESH)

    @pl.when(has_right)
    def _():
        pl.semaphore_signal(barrier, inc=1, device_id=right, device_id_type=MESH)

    @pl.when(has_left)
    def _():
        pl.semaphore_signal(barrier, inc=1, device_id=left, device_id_type=MESH)

    def remote(src, dst, send, recv, target):
        return pltpu.make_async_remote_copy(
            src_ref=src,
            dst_ref=dst,
            send_sem=send,
            recv_sem=recv,
            device_id=target,
            device_id_type=MESH,
        )

    pulls = [
        pltpu.make_async_copy(src, dst, load_sem.at[i])
        for i, (src, dst) in enumerate(
            (
                (tsort_hbm, tsort_ref),
                (dkv_hbm, dkv_ref),
                (dlat_hbm.at[core], dmine_ref),
                (a_hbm, a_ref),
                (b_hbm, b_ref),
                (dwq_hbm, dwq_ref),
                (tok_hbm, tok_ref),
            )
        )
    ]
    for copy in pulls:
        copy.start()
    pl.semaphore_wait(barrier, 3 + has_right.astype(jnp.int32) + has_left.astype(jnp.int32))

    def dpair_copy(i):
        return remote(
            dlat_hbm.at[other, i], line_ref.at[i], dpair_send.at[i], dpair_recv.at[i], partner
        )

    def start_dpair(i, carry):
        dpair_copy(i).start()
        return carry

    lax.fori_loop(0, lat_chunks, start_dpair, 0)

    def wide_one_copy(h, n, sub):
        block = (first[h], flip_xy)[n]
        at = pl.ds(h * wide_half + sub * sub_rows, sub_rows)
        return remote(
            wide_ref.at[block, at],
            wide_one.at[h, n, pl.ds(sub * sub_rows, sub_rows)],
            wide_one_send.at[h, n, sub],
            wide_one_recv.at[h, n, sub],
            near[h],
        )

    def wide_at(block, h, sub):
        return wide_ref.at[block, pl.ds(h * wide_half + sub * sub_rows, sub_rows)]

    def wide_two_copy(h, sub):
        at = pl.ds(sub * sub_rows, sub_rows)
        return remote(
            wide_at(first[1 - h], h, sub),
            wide_two.at[h, at],
            wide_two_send.at[h, sub],
            wide_two_recv.at[h, sub],
            near[1 - h],
        )

    def gather_at(c, e, h, sub):
        return gather_out.at[c, e, pl.ds(h * wide_half + sub * sub_rows, sub_rows)]

    def far_at(h, sub):
        return wide_far.at[pl.ds(h * wide_half + sub * sub_rows, sub_rows)]

    def wide_z_copy(h, sub):
        return remote(
            wide_at(stream, h, sub),
            far_at(h, sub),
            wide_z_send.at[h, sub],
            wide_z_recv.at[h, sub],
            beside,
        )

    def wide_core_copy(far, h, sub):
        if far:
            src = far_at(h, sub)
            dst = gather_at(core, 1 - parity, h, sub)
        else:
            src = wide_at(stream, h, sub)
            dst = gather_at(core, parity, h, sub)
        return remote(
            src, dst, wide_core_send.at[far, h, sub], wide_core_recv.at[far, h, sub], partner
        )

    def wide_core_arrival(far, h, sub):
        place = gather_at(other, 1 - parity if far else parity, h, sub)
        return remote(
            place, place, wide_core_send.at[far, h, sub], wide_core_recv.at[far, h, sub], partner
        )

    def wide_keep(far, h, sub):
        return pltpu.make_async_copy(
            far_at(h, sub) if far else wide_at(stream, h, sub),
            gather_at(core, 1 - parity if far else parity, h, sub),
            wide_local.at[far, h, sub],
        )

    def wide_product(block):
        wide_ref[block, :width, :] = dot(a_ref[...], b_ref[block], (0, 0))
        wide_ref[block, width:, :] = side_ref[block]

    def wide_start(k):
        wide_product((flip_xy, first[0], first[1], stream)[k])
        for sub in range(EARLY_SUBS):
            for h in range(2):
                if k == 0:
                    wide_one_copy(h, 1, sub).start()
                elif k == 1 + h:
                    wide_one_copy(h, 0, sub).start()

    def wide_more():
        for sub in range(EARLY_SUBS, SUBS):
            for h in range(2):
                for n in range(2):
                    wide_one_copy(h, 1 - n, sub).start()

    def wide_event_one(sub):
        at = slice(sub * sub_rows, (sub + 1) * sub_rows)
        for h in range(2):
            for n in range(2):
                wide_one_copy(h, n, sub).wait_recv()
            span = pl.ds(h * wide_half + sub * sub_rows, sub_rows)
            wide_ref[first[1 - h], span, :] += wide_one[h, 1, at, :]
            wide_two_copy(h, sub).start()
            wide_ref[stream, span, :] += wide_one[h, 0, at, :]

    def wide_event_two(sub):
        at = slice(sub * sub_rows, (sub + 1) * sub_rows)
        for h in range(2):
            wide_two_copy(h, sub).wait_recv()
            span = pl.ds(h * wide_half + sub * sub_rows, sub_rows)
            wide_ref[stream, span, :] += wide_two[h, at, :]
            wide_z_copy(h, sub).start()
            wide_core_copy(0, h, sub).start()
            wide_keep(0, h, sub).start()

    def wide_event_three(sub):
        for h in range(2):
            wide_z_copy(h, sub).wait_recv()
            wide_core_copy(1, h, sub).start()
            wide_keep(1, h, sub).start()

    share = width // 4

    def gain_part(which, block, product):
        at = slice(block * share, (block + 1) * share)
        weight = jnp.where(which == 0, wk_ref[at, :], wv_ref[at, :]).astype(F32)
        gain_ref[at, 0:1] += jnp.sum(product * weight, 1, keepdims=True)

    def token_product(block, which):
        at = slice(block * share, (block + 1) * share)
        return dot(tsort_ref[:, at], dkv_ref[which], (0, 0))

    def token_other():
        gain_ref[...] = jnp.zeros_like(gain_ref)
        for block in range(4):
            product = token_product(block, other)
            for h in range(2):
                send_ref[h, block] = product[h * kv_rows : (h + 1) * kv_rows]
            gain_part(other, block, product)
        for k, h, what in pairs:
            if what < 2:
                pair_copy(k, h, what).start()

    order = (flip_xy, first[0], first[1], stream)

    def pair_copy(k, h, what):
        block = order[k]
        src, at, size = (
            (send_ref.at[h, block], 0, kv_rows),
            (dwq_ref.at[block, other, h], kv_rows, q_rows),
            (small_ref.at[block], mix, 16),
        )[what]
        return remote(
            src,
            pair_ref.at[h, block, pl.ds(at, size)],
            pair_send.at[k, h, what],
            pair_recv.at[k, h, what],
            partner,
        )

    pairs = [(k, h, what) for k in range(4) for h in range(2) for what in range(3 - h)]

    def token_own():
        for block in range(4):
            product = token_product(block, core)
            for h in range(2):
                piece = product[h * kv_rows : (h + 1) * kv_rows]
                mine_ref[h, block, :kv_rows, :] = piece
                mine_ref[h, block, kv_rows:mix, :] = dwq_ref[block, core, h]
            gain_part(core, block, product)
        mine_ref[1, :, mix:, :] = jnp.zeros((4, 16, width), F32)
        small_ref[...] = jnp.zeros_like(small_ref)
        gain = jnp.broadcast_to(gain_ref[:, 0:1], gain_ref.shape).T[0:1, :] / row(gain_t_ref)
        for block in range(4):
            small_ref[block, 0:1, :] = vec_ref[0:1, block * width : (block + 1) * width] * here
            small_ref[block, 1:2, :] = dgain_q_ref[0:1, :]
            small_ref[block, 2:3, :] = vec_ref[2:3, :width] * here
            small_ref[block, 3:4, :] = vec_ref[1:2, :width] * here
            small_ref[block, 4:5, :] = gain
        for k in range(4):
            pair_copy(k, 0, 2).start()

    here = (chip == 0).astype(F32)

    token_step = 128

    def stage_copy(i):
        return pltpu.make_async_copy(
            stage_ref.at[i % 2],
            dtok_out.at[pl.ds(i * token_step, token_step)],
            stage_sem.at[i % 2],
        )

    def token_part(i):
        at = pl.ds(pl.multiple_of(i * token_step, token_step), token_step)
        target = lax.broadcasted_iota(jnp.int32, (token_step, rows), 1).astype(F32)
        pick = jnp.where(target == place_ref[at, 0:1], 1.0, 0.0).astype(BF16)
        dkey = dot(pick, dkv_ref[0]).astype(BF16)
        dval = dot(pick, dkv_ref[1]).astype(BF16)
        dnormed = dot(dkey, wk_ref[...], (1, 1)) + dot(dval, wv_ref[...], (1, 1))
        unit, inv = norm_parts(tok_ref[at, :].astype(F32))
        if i >= 2:
            stage_copy(i - 2).wait()
        stage_ref[i % 2] = norm_back(unit, inv, row(gain_t_ref), dnormed)
        stage_copy(i).start()

    def one_copy(h, n):
        block = (first[h], flip_xy)[n]
        return remote(
            mine_ref.at[h, block], one_ref.at[h, n], one_send.at[h, n], one_recv.at[h, n], near[h]
        )

    def two_copy(h):
        return remote(
            mine_ref.at[h, first[1 - h]], two_ref.at[h], two_send.at[h], two_recv.at[h], near[1 - h]
        )

    def pair_event():
        for k in range(4):
            block = order[k]
            for h in range(2):
                for what in range(3 - h):
                    pair_copy(k, h, what).wait_recv()
                mine_ref[h, block, :mix, :] += pair_ref[h, block, :mix, :]
                if h == 0:
                    mine_ref[h, block, mix:, :] = small_ref[block] + pair_ref[h, block, mix:, :]
                if k == 0:
                    one_copy(h, 1).start()
                elif k == 1 + h:
                    one_copy(h, 0).start()

    def one_event():
        for h in range(2):
            for n in range(2):
                one_copy(h, n).wait_recv()
            mine_ref[h, first[1 - h]] += one_ref[h, 1]
            two_copy(h).start()

    def two_event():
        for h in range(2):
            two_copy(h).wait_recv()
            total = mine_ref[h, stream] + one_ref[h, 0] + two_ref[h]
            for k in range(half_chunks):
                line_ref[lat_chunks + h * half_chunks + k] = total[k * ZROWS : (k + 1) * ZROWS]

    def right_copy(i):
        return remote(right_ref.at[i], right_ref.at[i], right_send.at[i], right_recv.at[i], right)

    def left_copy(i):
        return remote(left_ref.at[i], left_ref.at[i], left_send.at[i], left_recv.at[i], left)

    def back_copy(i):
        return remote(
            line_ref.at[i], dlat_out.at[core, i], back_send.at[i], back_recv.at[i], partner
        )

    def back_arrival(i):
        return remote(
            line_ref.at[i], dlat_out.at[other, i], back_send.at[i], back_recv.at[i], partner
        )

    def back_keep(i):
        return pltpu.make_async_copy(line_ref.at[i], dlat_out.at[core, i], back_local.at[i])

    def placed(t):
        late = t >= lat_chunks + GAP
        index = jnp.where(late, t - GAP, t)
        return index, (t >= 0) & (late | (t < lat_chunks)) & (index < all_chunks)

    def line_step(t):
        @pl.when(t < lat_chunks)
        def _():
            dpair_copy(t).wait_recv()
            line_ref[t] += dmine_ref[t]

        r, r_due = placed(t - LAG * chip)

        @pl.when(r_due)
        def _():
            @pl.when(has_left)
            def _():
                right_copy(r).wait_recv()
                right_ref[r] += line_ref[r]

            @pl.when(jnp.logical_not(has_left))
            def _():
                right_ref[r] = line_ref[r]

            @pl.when(has_right)
            def _():
                right_copy(r).start()

        u, u_due = placed(t - LAG * (chips - 1 - chip))

        @pl.when(u_due)
        def _():
            @pl.when(has_right)
            def _():
                left_copy(u).wait_recv()
                left_ref[u] += line_ref[u]

            @pl.when(jnp.logical_not(has_right))
            def _():
                left_ref[u] = line_ref[u]

            @pl.when(has_left)
            def _():
                left_copy(u).start()

        w, w_due = placed(t - LAG * jnp.maximum(chip, chips - 1 - chip))

        @pl.when(w_due)
        def _():
            line_ref[w] = right_ref[w] + left_ref[w] - line_ref[w]

            @pl.when(w < lat_chunks)
            def _():
                back_copy(w).start()
                back_keep(w).start()

    def spot(i):
        k = i - lat_chunks
        h = lax.div(k, half_chunks)
        return h, lax.rem(k, half_chunks)

    def by_half(h, pair):
        return jnp.where(h == 0, pair[0], pair[1])

    def block_of(h, k):
        return (stream, by_half(h, (flip_y, flip_x)), by_half(h, first), flip_xy)[k]

    def spread_src(i, k):
        h, c = spot(i)
        return line_ref.at[i] if k == 0 else spread_ref.at[k - 1, h, c]

    def spread_copy(i, k):
        h, c = spot(i)
        target = by_half(h, (flip_y, flip_x)) if k == 1 else by_half(h, first)
        return remote(
            spread_src(i, 1 if k == 3 else 0),
            spread_ref.at[k - 1, h, c],
            spread_send.at[k - 1, i - lat_chunks],
            spread_recv.at[k - 1, i - lat_chunks],
            (target, tok),
        )

    def share_copy(i, k):
        h, c = spot(i)
        return remote(
            spread_src(i, k),
            kv_out.at[core, block_of(h, k), h, c],
            share_send.at[k, i - lat_chunks],
            share_recv.at[k, i - lat_chunks],
            partner,
        )

    def share_arrival(i, k):
        h, c = spot(i)
        place = kv_out.at[other, block_of(h, k), h, c]
        return remote(
            place,
            place,
            share_send.at[k, i - lat_chunks],
            share_recv.at[k, i - lat_chunks],
            partner,
        )

    def kv_keep(i, k):
        h, c = spot(i)
        return pltpu.make_async_copy(
            spread_src(i, k),
            kv_out.at[core, block_of(h, k), h, c],
            keep_local.at[k, i - lat_chunks],
        )

    def spread_due(t):
        i, due = placed(t)
        i = jnp.maximum(i, lat_chunks)
        _, c = spot(i)
        return i, due & (t >= lat_chunks + GAP) & (c < kv_chunks)

    def spread_step(t):
        lag = LAG * jnp.maximum(chip, chips - 1 - chip)
        i, due = spread_due(t - lag)

        @pl.when(due)
        def _():
            spread_copy(i, 1).start()
            spread_copy(i, 2).start()
            share_copy(i, 0).start()
            kv_keep(i, 0).start()

        j, due_one = spread_due(t - lag - SPREAD_LAG)

        @pl.when(due_one)
        def _():
            spread_copy(j, 1).wait_recv()
            spread_copy(j, 3).start()
            share_copy(j, 1).start()
            kv_keep(j, 1).start()

        m, due_two = spread_due(t - lag - 2 * SPREAD_LAG)

        @pl.when(due_two)
        def _():
            for k in (2, 3):
                spread_copy(m, k).wait_recv()
                share_copy(m, k).start()
                kv_keep(m, k).start()

    def query_piece(h):
        return mine_ref.at[h, stream, pl.ds(kv_rows, q_rows)]

    def query_copy(h):
        return remote(
            query_piece(h),
            query_out.at[core, h],
            query_send.at[h],
            query_recv.at[h],
            partner,
        )

    def query_arrival(h):
        return remote(
            query_piece(h),
            query_out.at[other, h],
            query_send.at[h],
            query_recv.at[h],
            partner,
        )

    def query_keep(h):
        return pltpu.make_async_copy(query_piece(h), query_out.at[core, h], query_local.at[h])

    def query_event(h):
        flat = lat_chunks + h * half_chunks + kv_chunks
        for k in range(0, q_rows, 16):
            at = flat * ZROWS + k
            chunk, row = at // ZROWS, at % ZROWS
            mine_ref[h, stream, kv_rows + k : kv_rows + k + 16, :] = line_ref[
                chunk, row : row + 16, :
            ]
        query_copy(h).start()
        query_keep(h).start()
        if h == 0:
            at = flat * ZROWS + q_rows
            chunk, row = at // ZROWS, at % ZROWS
            small_out[...] = line_ref[chunk, row : row + 16, :]

    tail = LAG * (chips - 1)
    ready = lambda h: lat_chunks + GAP + (h + 1) * half_chunks - 1 + tail
    events = {}

    def at_tick(tick, run):
        events.setdefault(tick, []).append(run)

    parts = rows // token_step
    for i in range(parts):
        at_tick(TOKEN_TICKS[i % len(TOKEN_TICKS)], functools.partial(token_part, i))
    for k in range(4):
        at_tick(WIDE_START_TICKS[k], functools.partial(wide_start, k))
    at_tick(KV_TICKS[0], token_other)
    at_tick(KV_TICKS[1], token_own)
    at_tick(PAIR_TICK, pair_event)
    at_tick(MORE_TICK, wide_more)
    at_tick(ONE_TICK, one_event)
    at_tick(TWO_TICK, two_event)
    for sub in range(SUBS):
        at_tick(WIDE_ONE_TICKS[sub], functools.partial(wide_event_one, sub))
        at_tick(WIDE_TWO_TICKS[sub], functools.partial(wide_event_two, sub))
        if WIDE_THREE_TICKS[sub] >= 0:
            at_tick(WIDE_THREE_TICKS[sub], functools.partial(wide_event_three, sub))
    for copy in pulls:
        copy.wait()

    def step(t, carry):
        line_step(t)
        spread_step(t)
        for tick in sorted(events):

            @pl.when(t == tick)
            def _(tick=tick):
                for run in events[tick]:
                    run()

        return carry

    lax.fori_loop(0, ready(1) + 2 * SPREAD_LAG + 1, step, 0)
    for h in range(2):
        query_event(h)
    for sub in range(SUBS):
        if WIDE_THREE_TICKS[sub] < 0:
            wide_event_three(sub)

    def finish_lat(i, carry):
        dpair_copy(i).wait_send()
        back_copy(i).wait_send()
        back_arrival(i).wait_recv()
        back_keep(i).wait()
        return carry

    lax.fori_loop(0, lat_chunks, finish_lat, 0)

    def finish_line(i, carry):
        @pl.when(has_right)
        def _():
            right_copy(i).wait_send()

        @pl.when(has_left)
        def _():
            left_copy(i).wait_send()

        return carry

    lax.fori_loop(0, all_chunks, finish_line, 0)

    def finish_spread(n, carry):
        h = lax.div(n, kv_chunks)
        i = lat_chunks + h * half_chunks + lax.rem(n, kv_chunks)
        for k in range(4):
            if k:
                spread_copy(i, k).wait_send()
            share_copy(i, k).wait_send()
            share_arrival(i, k).wait_recv()
            kv_keep(i, k).wait()
        return carry

    lax.fori_loop(0, 2 * kv_chunks, finish_spread, 0)
    for i in range(parts - 2, parts):
        stage_copy(i).wait()
    for k, h, what in pairs:
        pair_copy(k, h, what).wait_send()
    for h in range(2):
        for n in range(2):
            one_copy(h, n).wait_send()
        two_copy(h).wait_send()
        query_copy(h).wait_send()
        query_arrival(h).wait_recv()
        query_keep(h).wait()
        for sub in range(SUBS):
            for n in range(2):
                wide_one_copy(h, n, sub).wait_send()
                wide_core_copy(n, h, sub).wait_send()
                wide_core_arrival(n, h, sub).wait_recv()
            wide_two_copy(h, sub).wait_send()
            wide_z_copy(h, sub).wait_send()
            wide_keep(0, h, sub).wait()
            wide_keep(1, h, sub).wait()


def gradients(
    dlat, a, b, side, dwq, vec, dgain_q, place, tokens, tsort, dkv, gain_t, wk, wv
):
    rows, width = tokens.shape
    half = dlat.shape[0] // 2
    lat_chunks = half // ZROWS
    wide_rows, wide_cols = a.shape[1] + side.shape[1], b.shape[2]
    share = width // 4
    kv_rows, q_rows = share // 2, share // 4
    block = kv_rows + q_rows + 16
    all_chunks = lat_chunks + 2 * block // ZROWS
    sds = jax.ShapeDtypeStruct
    dma = pltpu.SemaphoreType.DMA
    buf = lambda *shape: pltpu.VMEM(shape, F32)
    both = lambda *shape: [dma(shape), dma(shape)]
    return pl.pallas_call(
        gradient_kernel,
        name="gradients",
        out_shape=(
            sds((2, lat_chunks, ZROWS, width), F32),
            sds((2, 2, wide_rows, wide_cols), F32),
            sds((2, 4, 2, kv_rows // ZROWS, ZROWS, width), F32),
            sds((2, 2, q_rows, width), F32),
            sds((16, width), F32),
            sds((rows, width), F32),
        ),
        in_specs=[anywhere()] * 3
        + [vmem(), anywhere()]
        + [vmem()] * 3
        + [anywhere()] * 3
        + [vmem()] * 3,
        out_specs=(anywhere(),) * 4 + (vmem(), anywhere()),
        scratch_shapes=[
            buf(all_chunks, ZROWS, width),
            buf(all_chunks, ZROWS, width),
            buf(all_chunks, ZROWS, width),
            buf(lat_chunks, ZROWS, width),
            buf(4, wide_rows, wide_cols),
            buf(2, 2, wide_rows // 2, wide_cols),
            buf(2, wide_rows // 2, wide_cols),
            buf(2, 4, kv_rows, width),
            buf(2, 4, block, width),
            buf(2, 4, block, width),
            buf(2, 2, block, width),
            buf(2, block, width),
            buf(4, 16, width),
            buf(width, 128),
            buf(wide_rows, wide_cols),
            buf(3, 2, kv_rows // ZROWS, ZROWS, width),
            buf(2, 128, width),
            dma((2,)),
            pltpu.VMEM(a.shape, BF16),
            pltpu.VMEM(b.shape, BF16),
            buf(4, 2, 2, q_rows, width),
            pltpu.VMEM(tokens.shape, BF16),
            pltpu.VMEM(tsort.shape, BF16),
            pltpu.VMEM(dkv.shape, BF16),
            dma((7,)),
        ]
        + both(lat_chunks)
        + both(all_chunks)
        + both(all_chunks)
        + both(lat_chunks)
        + [dma((lat_chunks,))]
        + both(2, 2, SUBS)
        + both(2, SUBS)
        + both(2, SUBS)
        + both(2, 2, SUBS)
        + [dma((2, 2, SUBS))]
        + both(4, 2, 3)
        + both(2, 2)
        + both(2)
        + both(3, all_chunks - lat_chunks)
        + both(4, all_chunks - lat_chunks)
        + both(2)
        + [dma((2,)), dma((4, all_chunks - lat_chunks))],
        compiler_params=pltpu.CompilerParams(
            vmem_limit_bytes=VMEM_BYTES, collective_id=2, has_side_effects=True
        ),
    )(
        dlat.reshape(2, lat_chunks, ZROWS, width),
        a,
        b,
        side,
        dwq.reshape(4, 2, 2, q_rows, width),
        vec,
        dgain_q,
        place,
        tokens,
        tsort,
        dkv,
        gain_t,
        wk,
        wv,
    )


def closing_kernel(
    dlat_hbm,
    gather_hbm,
    kv_hbm,
    query_ref,
    small_ref,
    dtok_hbm,
    dlat_out,
    dtok_out,
    up_out,
    key_out,
    val_out,
    down_out,
    out_ref,
    wq_ref,
    gain_q_ref,
    gain_t_ref,
    gain_mlp_ref,
    bup_ref,
    bdn_ref,
    wide_ref,
    up_ref,
    dlat_ref,
    kv_ref,
    dtok_ref,
    down_ref,
    load_sems,
    store_sems,
):
    width = small_ref.shape[1]
    cols = wide_ref.shape[2]
    loads = [
        pltpu.make_async_copy(src, dst, load_sems.at[i])
        for i, (src, dst) in enumerate(
            (
                (gather_hbm.at[1], wide_ref),
                (gather_hbm.at[0], up_ref),
                (dlat_hbm, dlat_ref),
                (kv_hbm, kv_ref),
                (dtok_hbm, dtok_ref),
            )
        )
    ]
    for copy in loads:
        copy.start()
    stores = [
        pltpu.make_async_copy(src, dst, store_sems.at[i])
        for i, (src, dst) in enumerate(
            (
                (up_ref.at[0, pl.ds(0, width)], up_out.at[:, pl.ds(0, cols)]),
                (up_ref.at[1, pl.ds(0, width)], up_out.at[:, pl.ds(cols, cols)]),
                (dlat_ref, dlat_out),
                (kv_ref.at[0], key_out),
                (kv_ref.at[1], val_out),
                (dtok_ref, dtok_out),
                (down_ref, down_out),
            )
        )
    ]
    stream = lax.axis_index("stream")
    gain_t_ref[...] = small_ref[4]
    bup_ref[...] = small_ref[0]
    size = gain_q_ref.shape[0]
    for i, ref in ((1, gain_q_ref), (2, gain_mlp_ref), (3, bdn_ref)):
        line = small_ref[i : i + 1, :]
        piece = line[:, :size]
        for k in range(1, width // size):
            piece = jnp.where(stream == k, line[:, k * size : (k + 1) * size], piece)
        ref[...] = piece[0]
    wq_ref[...] = query_ref[...]
    loads[0].wait()
    for e in range(2):
        down_ref[e * cols : (e + 1) * cols, :] = wide_ref[e, :width, :].T
    stores[6].start()
    loads[1].wait()
    stores[0].start()
    stores[1].start()
    half = up_ref.shape[1] - width
    for e in range(2):
        out_ref[:half, e * cols : (e + 1) * cols] = up_ref[e, width:, :]
        out_ref[half:, e * cols : (e + 1) * cols] = wide_ref[e, width:, :]
    loads[2].wait()
    stores[2].start()
    loads[3].wait()
    stores[3].start()
    stores[4].start()
    loads[4].wait()
    stores[5].start()
    for copy in stores:
        copy.wait()


def closing(dlat, gather, kv, query, small, dtok):
    width = small.shape[1]
    wide_rows, cols = gather.shape[2:]
    share = query.shape[0]
    rows = dtok.shape[0]
    sds = lambda *shape: jax.ShapeDtypeStruct(shape, F32)
    return pl.pallas_call(
        closing_kernel,
        name="closing",
        out_shape=(
            sds(*dlat.shape),
            sds(rows, width),
            sds(width, 2 * cols),
            sds(width, width),
            sds(width, width),
            sds(2 * cols, width),
            sds(share, width),
            sds(share, width),
            sds(share),
            sds(width),
            sds(share),
            sds(2 * cols),
            sds(share),
        ),
        in_specs=[anywhere()] * 3 + [vmem()] * 2 + [anywhere()],
        out_specs=(anywhere(),) * 6 + (vmem(),) * 7,
        scratch_shapes=[
            pltpu.VMEM((2, wide_rows, cols), F32),
            pltpu.VMEM((2, wide_rows, cols), F32),
            pltpu.VMEM(dlat.shape, F32),
            pltpu.VMEM(kv.shape, F32),
            pltpu.VMEM(dtok.shape, F32),
            pltpu.VMEM((2 * cols, width), F32),
            pltpu.SemaphoreType.DMA((5,)),
            pltpu.SemaphoreType.DMA((7,)),
        ],
        compiler_params=pltpu.CompilerParams(vmem_limit_bytes=VMEM_BYTES),
    )(dlat, gather, kv, query, small, dtok)


def local(
    latents,
    tokens,
    token_sample,
    token_mask,
    drop_mask,
    gain_query,
    w_query,
    gain_token,
    w_key,
    w_value,
    w_out,
    gain_mlp,
    w_up,
    b_up,
    w_down,
    b_down,
    cotangent,
):
    samples, lat_rows, width = latents.shape
    part, keys, values, tsort, query, normed, place, bounds = attend_forward(
        token_sample, token_mask, tokens, latents, gain_query, w_query, gain_token, w_key, w_value
    )
    msg, result, dmid, a, b, side, vec = latent_block(
        part, drop_mask, latents, cotangent, w_out, gain_mlp, w_up, b_up, w_down, b_down
    )
    dkv, dlat, dgain_q, dwq, result = attend_backward(
        bounds, latents, keys, values, query, normed, msg, dmid, gain_query, w_query, result
    )
    dlat, gather, kv, dwq, small, d_tokens = gradients(
        dlat, a, b, side, dwq, vec, dgain_q, place, tokens, tsort, dkv, gain_token,
        w_key, w_value,
    )
    (
        d_latents,
        d_tokens,
        grad_up,
        grad_key,
        grad_value,
        grad_down,
        grad_out,
        grad_query,
        grad_gquery,
        grad_gtoken,
        grad_gmlp,
        grad_bup,
        grad_bdown,
    ) = closing(
        dlat.reshape(samples * lat_rows, width),
        gather,
        kv.reshape(2, width, width),
        dwq.reshape(-1, width),
        small,
        d_tokens,
    )
    return (
        result.reshape(latents.shape),
        d_latents.reshape(latents.shape),
        d_tokens,
        grad_gquery,
        grad_query.T,
        grad_gtoken,
        grad_key,
        grad_value,
        grad_out.T,
        grad_gmlp,
        grad_up,
        grad_bup,
        grad_down,
        grad_bdown,
    )


def solution(mesh):
    return jax.shard_map(
        local,
        mesh=mesh,
        in_specs=(
            P("stream", None, None),
            P(("stream", "tok"), None),
            P(("stream", "tok")),
            P(("stream", "tok")),
            P(),
            P(),
            P(),
            P(),
            P(),
            P(),
            P(),
            P(),
            P(),
            P(),
            P(),
            P(),
            P("stream", None, None),
        ),
        out_specs=(
            P("stream", None, None),
            P("stream", None, None),
            P(("stream", "tok"), None),
            P("stream"),
            P(None, "stream"),
            P(),
            P(),
            P(),
            P(None, "stream"),
            P("stream"),
            P(None, "stream"),
            P("stream"),
            P("stream", None),
            P("stream"),
        ),
        check_vma=False,
    )
```

```python
import functools

import jax
import jax.numpy as jnp
from jax import lax
from jax.experimental import pallas as pl
from jax.experimental.pallas import tpu as pltpu
from jax.sharding import PartitionSpec as P

HEADS = 12
HEAD_DIM = 64
PAIRS = HEADS // 2
PIECES = 4
PIECE_HEADS = HEADS // PIECES
NUM_ROWS = PIECE_HEADS * HEAD_DIM
PIECE_ROWS = NUM_ROWS + 16
MSG_ROWS = HEADS * HEAD_DIM + 32
BLOCK = 256
FWD_BLOCK = 128
PAD = 256
LAG = 2
GAP = 6
SUBS = 3
EARLY_SUBS = 1
SPREAD_LAG = 3
WIDE_START_TICKS = (1, 2, 2, 4)
KV_TICKS = (0, 3)
PAIR_TICK = 5
MORE_TICK = 21
ONE_TICK = 15
TWO_TICK = 20
WIDE_ONE_TICKS = (10, 27, 30)
WIDE_TWO_TICKS = (16, 32, 35)
WIDE_THREE_TICKS = (25, -1, -1)
TOKEN_TICKS = (6, 7, 8, 9, 11, 12, 13, 16)
NEG = -1e30
F32 = jnp.float32
BF16 = jnp.bfloat16
VMEM_BYTES = 56 * 1024 * 1024


def norm_parts(values):
    center = values - jnp.mean(values, -1, keepdims=True)
    spread = jnp.mean(center * center, -1, keepdims=True)
    inv = lax.rsqrt(spread + 1e-05)
    return center * inv, inv


def norm_back(unit, inv, gain, grad):
    scaled = grad * gain
    inner = scaled - jnp.mean(scaled, -1, keepdims=True)
    return inv * (inner - unit * jnp.mean(scaled * unit, -1, keepdims=True))


def dot(a, b, contract=(1, 0)):
    return lax.dot_general(
        a, b, (((contract[0],), (contract[1],)), ((), ())), preferred_element_type=F32
    )


def row(ref):
    return ref[...].reshape(1, ref.shape[0])


def piece_of(head):
    return head // PIECE_HEADS, head % PIECE_HEADS


def forward_kernel(
    sample_ref,
    mask_ref,
    tok_hbm,
    lat_hbm,
    gain_q_ref,
    wq_hbm,
    gain_t_ref,
    wk_hbm,
    wv_hbm,
    part_out,
    key_out,
    val_out,
    tsort_out,
    query_out,
    normed_out,
    place_ref,
    bounds_ref,
    tnorm_ref,
    pos_ref,
    top_ref,
    den_ref,
    num_ref,
    tok_ref,
    lat_ref,
    wq_ref,
    wk_ref,
    wv_ref,
    part_ref,
    key_ref,
    val_ref,
    tsort_ref,
    query_ref,
    normed_ref,
    load_sem,
    store_sem,
    sample_sem,
):
    loads = [
        pltpu.make_async_copy(src, dst, load_sem.at[i])
        for i, (src, dst) in enumerate(
            (
                (tok_hbm, tok_ref),
                (wk_hbm, wk_ref),
                (wv_hbm, wv_ref),
                (lat_hbm, lat_ref),
                (wq_hbm, wq_ref),
            )
        )
    ]
    for copy in loads:
        copy.start()
    stores = [
        pltpu.make_async_copy(src, dst, store_sem.at[i])
        for i, (src, dst) in enumerate(
            ((key_ref, key_out), (val_ref, val_out), (tsort_ref, tsort_out))
        )
    ]
    samples = part_ref.shape[0]

    def sample_stores(s):
        at = pl.ds(pl.multiple_of(s * 128, 128), 128)
        return [
            pltpu.make_async_copy(src, dst, sample_sem.at[i, s])
            for i, (src, dst) in enumerate(
                (
                    (part_ref.at[s], part_out.at[s]),
                    (query_ref.at[s], query_out.at[s]),
                    (normed_ref.at[at], normed_out.at[at]),
                )
            )
        ]

    rows = tok_ref.shape[0]
    width = tok_ref.shape[1]
    lat_rows = 128
    step = 256

    named = row(sample_ref) - lax.axis_index("stream") * samples
    ids = jnp.where(row(mask_ref) == 1, named, -1)
    lane = lax.broadcasted_iota(jnp.int32, (samples, rows), 1)
    member = ids == lax.broadcasted_iota(jnp.int32, (samples, rows), 0)
    ones = jnp.where(member, 1.0, 0.0)
    count = ones
    shift = 1
    while shift < rows:
        count = count + jnp.where(lane >= shift, pltpu.roll(count, shift, 1), 0.0)
        shift *= 2
    rank = count - ones
    begin = jnp.int32(0)
    pos = jnp.full((1, rows), -1.0, F32)
    for s in range(samples):
        total = jnp.sum(ones[s : s + 1]).astype(jnp.int32)
        bounds_ref[s] = begin
        bounds_ref[samples + s] = total
        pos = jnp.where(member[s : s + 1], rank[s : s + 1] + begin.astype(F32), pos)
        begin = begin + total
    pos_ref[...] = jnp.broadcast_to(pos, (8, rows))
    place_ref[...] = jnp.broadcast_to(pos, (128, rows)).T

    def token_norm(i, carry):
        at = pl.ds(pl.multiple_of(i * step, step), step)
        unit, _ = norm_parts(tok_ref[at, :].astype(F32))
        tnorm_ref[at, :] = (unit * row(gain_t_ref)).astype(BF16)
        return carry

    loads[0].wait()
    lax.fori_loop(0, rows // step, token_norm, 0)
    loads[1].wait()
    loads[2].wait()

    def token_sort(i, carry):
        at = pl.ds(pl.multiple_of(i * step, step), step)
        target = lax.broadcasted_iota(jnp.int32, (step, rows), 0) + i * step
        chosen = target.astype(F32) == pos_ref[0:1, :]
        pick = jnp.where(chosen, 1.0, 0.0).astype(BF16)
        tsort = dot(pick, tnorm_ref[...]).astype(BF16)
        tsort_ref[at, :] = tsort
        key_ref[at, :] = dot(tsort, wk_ref[...]).astype(BF16)
        val_ref[at, :] = dot(tsort, wv_ref[...]).astype(BF16)
        return carry

    lax.fori_loop(0, rows // step, token_sort, 0)
    key_ref[rows:, :] = jnp.zeros((PAD, width), BF16)
    val_ref[rows:, :] = jnp.zeros((PAD, width), BF16)
    for copy in stores:
        copy.start()
    loads[3].wait()
    loads[4].wait()

    def sample_step(s, carry):
        at = pl.ds(pl.multiple_of(s * lat_rows, lat_rows), lat_rows)
        unit, _ = norm_parts(lat_ref[at, :].astype(F32))
        normed = (unit * row(gain_q_ref)).astype(BF16)
        normed_ref[at, :] = normed
        query = dot(normed, wq_ref[...]) * 0.125
        turned = query.T.astype(BF16)
        blank = jnp.zeros((HEAD_DIM, lat_rows), BF16)
        for p in range(PAIRS):
            lo = 2 * p * HEAD_DIM
            query_ref[s, p, :HEAD_DIM, :lat_rows] = turned[lo : lo + HEAD_DIM]
            query_ref[s, p, :HEAD_DIM, lat_rows:] = blank
            query_ref[s, p, HEAD_DIM:, :lat_rows] = blank
            query_ref[s, p, HEAD_DIM:, lat_rows:] = turned[lo + HEAD_DIM : lo + 2 * HEAD_DIM]
        start = bounds_ref[s]
        total = bounds_ref[samples + s]
        base = lax.div(start, 16) * 16
        blocks = jnp.where(total > 0, lax.div(start + total - base + FWD_BLOCK - 1, FWD_BLOCK), 0)
        for piece in range(PIECES):
            part_ref[s, piece, NUM_ROWS:, :] = jnp.zeros((16, lat_rows), F32)
        num_ref[...] = jnp.zeros_like(num_ref)
        top_ref[...] = jnp.full_like(top_ref, NEG)
        den_ref[...] = jnp.zeros_like(den_ref)

        def block_step(b, carry):
            row = pl.multiple_of(base + b * FWD_BLOCK, 16)
            index = lax.broadcasted_iota(jnp.int32, (FWD_BLOCK, 2 * lat_rows), 0) + row
            inside = (index >= start) & (index < start + total)
            for p in range(PAIRS):
                cols = slice(p * 128, (p + 1) * 128)
                score = dot(key_ref[pl.ds(row, FWD_BLOCK), cols], query_ref[s, p])
                score = jnp.where(inside, score, NEG)
                old = top_ref[p : p + 1, :]
                new = jnp.maximum(old, jnp.max(score, 0, keepdims=True))
                fade = jnp.exp(old - new)
                weight = jnp.exp(score - new)
                top_ref[p : p + 1, :] = new
                den_ref[p : p + 1, :] = den_ref[p : p + 1, :] * fade + jnp.sum(
                    weight, 0, keepdims=True
                )
                both = dot(val_ref[pl.ds(row, FWD_BLOCK), cols], weight.astype(BF16), (0, 0))
                for half in range(2):
                    at_rows = slice(p * 128 + half * HEAD_DIM, p * 128 + (half + 1) * HEAD_DIM)
                    at_cols = slice(half * lat_rows, (half + 1) * lat_rows)
                    num_ref[at_rows, :] = (
                        num_ref[at_rows, :] * fade[:, at_cols]
                        + both[half * HEAD_DIM : (half + 1) * HEAD_DIM, at_cols]
                    )
            return carry

        lax.fori_loop(0, blocks, block_step, 0)
        for h in range(HEADS):
            piece, i = piece_of(h)
            p, half = h // 2, h % 2
            at_cols = slice(half * lat_rows, (half + 1) * lat_rows)
            part_ref[s, piece, i * HEAD_DIM : (i + 1) * HEAD_DIM, :] = num_ref[
                h * HEAD_DIM : (h + 1) * HEAD_DIM, :
            ]
            part_ref[s, piece, NUM_ROWS + i : NUM_ROWS + i + 1, :] = top_ref[p : p + 1, at_cols]
            part_ref[s, piece, NUM_ROWS + 8 + i : NUM_ROWS + 9 + i, :] = den_ref[
                p : p + 1, at_cols
            ]
        for copy in sample_stores(s):
            copy.start()
        return carry

    lax.fori_loop(0, samples, sample_step, 0)
    for copy in stores:
        copy.wait()

    def finish(s, carry):
        for copy in sample_stores(s):
            copy.wait()
        return carry

    lax.fori_loop(0, samples, finish, 0)


def vmem():
    return pl.BlockSpec(memory_space=pltpu.VMEM)


def anywhere():
    return pl.BlockSpec(memory_space=pl.ANY)


def smem():
    return pl.BlockSpec(memory_space=pltpu.SMEM)


def attend_forward(sample, mask, tokens, latents, gain_q, wq, gain_t, wk, wv):
    samples, lat_rows, width = latents.shape
    rows = tokens.shape[0]
    sds = jax.ShapeDtypeStruct
    return pl.pallas_call(
        forward_kernel,
        name="attend_forward",
        out_shape=(
            sds((samples, PIECES, PIECE_ROWS, lat_rows), F32),
            sds((rows + PAD, width), BF16),
            sds((rows + PAD, width), BF16),
            sds((rows, width), BF16),
            sds((samples, PAIRS, 128, 2 * lat_rows), BF16),
            sds((samples * lat_rows, width), BF16),
            sds((rows, 128), F32),
            sds((2 * samples,), jnp.int32),
        ),
        in_specs=[vmem()] * 2
        + [anywhere()] * 2
        + [vmem(), anywhere(), vmem()]
        + [anywhere()] * 2,
        out_specs=(anywhere(),) * 6 + (vmem(), smem()),
        scratch_shapes=[
            pltpu.VMEM((rows, width), BF16),
            pltpu.VMEM((8, rows), F32),
            pltpu.VMEM((8, 2 * lat_rows), F32),
            pltpu.VMEM((8, 2 * lat_rows), F32),
            pltpu.VMEM((width, lat_rows), F32),
            pltpu.VMEM((rows, width), BF16),
            pltpu.VMEM((samples * lat_rows, width), BF16),
            pltpu.VMEM((width, width), BF16),
            pltpu.VMEM((width, width), BF16),
            pltpu.VMEM((width, width), BF16),
            pltpu.VMEM((samples, PIECES, PIECE_ROWS, lat_rows), F32),
            pltpu.VMEM((rows + PAD, width), BF16),
            pltpu.VMEM((rows + PAD, width), BF16),
            pltpu.VMEM((rows, width), BF16),
            pltpu.VMEM((samples, PAIRS, 128, 2 * lat_rows), BF16),
            pltpu.VMEM((samples * lat_rows, width), BF16),
            pltpu.SemaphoreType.DMA((5,)),
            pltpu.SemaphoreType.DMA((3,)),
            pltpu.SemaphoreType.DMA((3, samples)),
        ],
        compiler_params=pltpu.CompilerParams(vmem_limit_bytes=VMEM_BYTES),
    )(
        sample,
        mask,
        tokens,
        latents.reshape(samples * lat_rows, width),
        gain_q,
        wq,
        gain_t,
        wk,
        wv,
    )


def backward_kernel(
    bounds_ref,
    lat_hbm,
    key_hbm,
    val_hbm,
    query_hbm,
    normed_hbm,
    msg_hbm,
    dmid_hbm,
    gain_q_ref,
    wq_hbm,
    res_hbm,
    dkv_out,
    dlat_out,
    dgain_ref,
    dwq_out,
    res_out,
    dk_ref,
    dv_ref,
    grad_ref,
    dquery_ref,
    turn_ref,
    stat_ref,
    res_ref,
    res_sems,
    lat_ref,
    key_ref,
    val_ref,
    query_ref,
    normed_ref,
    msg_ref,
    dmid_ref,
    wq_ref,
    dkv_ref,
    dlat_ref,
    dwq_ref,
    load_sem,
    sample_sem,
    dlat_sem,
    store_sem,
):
    samples = query_ref.shape[0]
    rows = dkv_ref.shape[1]
    lat_rows = 128
    step = 256
    width = dwq_ref.shape[0]
    for r in range(0, rows + PAD, step):
        dk_ref[r : r + step, :] = jnp.zeros((step, dk_ref.shape[1]), F32)
        dv_ref[r : r + step, :] = jnp.zeros((step, dv_ref.shape[1]), F32)
    loads = [
        pltpu.make_async_copy(src, dst, load_sem.at[i])
        for i, (src, dst) in enumerate(
            (
                (key_hbm, key_ref),
                (val_hbm, val_ref),
                (lat_hbm, lat_ref),
                (wq_hbm, wq_ref),
                (dmid_hbm, dmid_ref),
                (normed_hbm, normed_ref),
            )
        )
    ]

    def sample_loads(s):
        return [
            pltpu.make_async_copy(msg_hbm.at[s], msg_ref.at[s], sample_sem.at[0, s]),
            pltpu.make_async_copy(query_hbm.at[s], query_ref.at[s], sample_sem.at[1, s]),
        ]

    def dlat_store(s):
        at = pl.ds(pl.multiple_of(s * 128, 128), 128)
        return pltpu.make_async_copy(dlat_ref.at[at], dlat_out.at[at], dlat_sem.at[s])

    for copy in loads[:2] + sample_loads(0):
        copy.start()

    def start_sample(s, carry):
        for copy in sample_loads(s):
            copy.start()
        return carry

    for copy in loads[2:5]:
        copy.start()
    lax.fori_loop(1, query_ref.shape[0], start_sample, 0)
    loads[5].start()
    res_load = pltpu.make_async_copy(res_hbm, res_ref, res_sems.at[0])
    res_store = pltpu.make_async_copy(res_ref, res_out, res_sems.at[1])
    res_load.start()
    member = lax.axis_index("tok")
    grad_ref[...] = jnp.zeros_like(grad_ref)
    dgain_ref[...] = jnp.zeros_like(dgain_ref)

    loads[0].wait()
    loads[1].wait()

    def sample_step(s, carry):
        for copy in sample_loads(s):
            copy.wait()

        @pl.when(s == 0)
        def _():
            for copy in loads[2:5]:
                copy.wait()

        start = bounds_ref[s]
        total = bounds_ref[samples + s]
        base = lax.div(start, 16) * 16
        blocks = jnp.where(total > 0, lax.div(start + total - base + BLOCK - 1, BLOCK), 0)
        turn_ref[...] = jnp.zeros_like(turn_ref)
        for h in range(HEADS):
            p, half = h // 2, h % 2
            grad_ref[
                p,
                half * HEAD_DIM : (half + 1) * HEAD_DIM,
                half * lat_rows : (half + 1) * lat_rows,
            ] = msg_ref[s, h * HEAD_DIM : (h + 1) * HEAD_DIM, :].astype(BF16)

            stat_ref[p : p + 1, half * lat_rows : (half + 1) * lat_rows] = msg_ref[
                s, width + h : width + h + 1, :
            ]
            stat_ref[8 + p : 9 + p, half * lat_rows : (half + 1) * lat_rows] = msg_ref[
                s, width + 16 + h : width + 17 + h, :
            ]

        def block_step(b, carry):
            row = pl.multiple_of(base + b * BLOCK, 16)
            index = lax.broadcasted_iota(jnp.int32, (BLOCK, 2 * lat_rows), 0) + row
            inside = (index >= start) & (index < start + total)
            at = pl.ds(row, BLOCK)
            for p in range(PAIRS):
                cols = slice(p * 128, (p + 1) * 128)
                key = key_ref[at, cols]
                query = query_ref[s, p]
                grad = grad_ref[p]
                score = dot(key, query)
                weight = jnp.where(inside, jnp.exp(score - stat_ref[p : p + 1, :]), 0.0)
                dprob = dot(val_ref[at, cols], grad)
                dscore = (weight * (dprob - stat_ref[8 + p : 9 + p, :])).astype(BF16)
                dv_ref[at, cols] += dot(weight.astype(BF16), grad, (1, 1))
                dk_ref[at, cols] += dot(dscore, query, (1, 1))
                both = dot(key, dscore, (0, 0))
                for half in range(2):
                    turn_ref[
                        p * 128 + half * HEAD_DIM : p * 128 + (half + 1) * HEAD_DIM, :
                    ] += both[
                        half * HEAD_DIM : (half + 1) * HEAD_DIM,
                        half * lat_rows : (half + 1) * lat_rows,
                    ]
            return carry

        lax.fori_loop(0, blocks, block_step, 0)
        at = pl.ds(pl.multiple_of(s * lat_rows, lat_rows), lat_rows)
        dquery = (turn_ref[...].T * 0.125).astype(BF16)
        dquery_ref[at, :] = dquery
        unit, inv = norm_parts(lat_ref[at, :].astype(F32))
        dnormed = dot(dquery, wq_ref[...], (1, 1))
        dgain_ref[0:1, :] += jnp.sum(dnormed * unit, 0, keepdims=True)
        dlat = norm_back(unit, inv, row(gain_q_ref), dnormed)
        dlat_ref[at, :] = dlat
        j = s - lax.rem(member, 2) * (samples // 2)

        @pl.when((member < 2) & (j >= 0) & (j < samples // 2))
        def _():
            mine = pl.ds(pl.multiple_of(j * lat_rows, lat_rows), lat_rows)
            dlat_ref[at, :] = dlat + dmid_ref[mine, :]

        dlat_store(s).start()
        return carry

    lax.fori_loop(0, samples, sample_step, 0)
    res_load.wait()
    res_store.start()
    for r in range(0, rows, step):
        dkv_ref[0, r : r + step, :] = dk_ref[r : r + step, :].astype(BF16)
        dkv_ref[1, r : r + step, :] = dv_ref[r : r + step, :].astype(BF16)
    dkv_store = pltpu.make_async_copy(dkv_ref, dkv_out, store_sem.at[0])
    dkv_store.start()
    loads[5].wait()
    stores = []
    for c in range(0, width, 256):
        dwq_ref[c : c + 256, :] = dot(dquery_ref[:, c : c + 256], normed_ref[...], (0, 0))
        copy = pltpu.make_async_copy(
            dwq_ref.at[pl.ds(c, 256)], dwq_out.at[pl.ds(c, 256)], store_sem.at[1 + c // 256]
        )
        copy.start()
        stores.append(copy)
    res_store.wait()
    dkv_store.wait()
    for copy in stores:
        copy.wait()

    def finish(s, carry):
        dlat_store(s).wait()
        return carry

    lax.fori_loop(0, samples, finish, 0)


def attend_backward(bounds, latents, keys, values, query, normed, msg, dmid, gain_q, wq, result):
    samples, lat_rows, width = latents.shape
    rows = keys.shape[0] - PAD
    sds = jax.ShapeDtypeStruct
    return pl.pallas_call(
        backward_kernel,
        name="attend_backward",
        out_shape=(
            sds((2, rows, width), BF16),
            sds((samples * lat_rows, width), F32),
            sds((8, width), F32),
            sds((width, width), F32),
            sds(result.shape, BF16),
        ),
        in_specs=[smem()] + [anywhere()] * 7 + [vmem()] + [anywhere()] * 2,
        out_specs=(anywhere(),) * 2 + (vmem(),) + (anywhere(),) * 2,
        scratch_shapes=[
            pltpu.VMEM((rows + PAD, width), F32),
            pltpu.VMEM((rows + PAD, width), F32),
            pltpu.VMEM((PAIRS, 128, 2 * lat_rows), BF16),
            pltpu.VMEM((samples * lat_rows, width), BF16),
            pltpu.VMEM((width, lat_rows), F32),
            pltpu.VMEM((16, 2 * lat_rows), F32),
            pltpu.VMEM(result.shape, BF16),
            pltpu.SemaphoreType.DMA((2,)),
            pltpu.VMEM((samples * lat_rows, width), BF16),
            pltpu.VMEM((rows + PAD, width), BF16),
            pltpu.VMEM((rows + PAD, width), BF16),
            pltpu.VMEM(query.shape, BF16),
            pltpu.VMEM(normed.shape, BF16),
            pltpu.VMEM(msg.shape, F32),
            pltpu.VMEM(dmid.shape, F32),
            pltpu.VMEM(wq.shape, BF16),
            pltpu.VMEM((2, rows, width), BF16),
            pltpu.VMEM((samples * lat_rows, width), F32),
            pltpu.VMEM((width, width), F32),
            pltpu.SemaphoreType.DMA((6,)),
            pltpu.SemaphoreType.DMA((2, samples)),
            pltpu.SemaphoreType.DMA((samples,)),
            pltpu.SemaphoreType.DMA((1 + width // 256,)),
        ],
        compiler_params=pltpu.CompilerParams(vmem_limit_bytes=VMEM_BYTES),
    )(
        bounds,
        latents.reshape(samples * lat_rows, width),
        keys,
        values,
        query,
        normed,
        msg,
        dmid,
        gain_q,
        wq,
        result,
    )


MESH = pl.DeviceIdType.MESH


def merge(a_ref, b_ref, out_ref):
    a_tail, b_tail = a_ref[NUM_ROWS : NUM_ROWS + 8, :], b_ref[NUM_ROWS : NUM_ROWS + 8, :]
    top = jnp.maximum(a_tail, b_tail)
    a_fade, b_fade = jnp.exp(a_tail - top), jnp.exp(b_tail - top)
    den = a_ref[NUM_ROWS + 8 :, :] * a_fade + b_ref[NUM_ROWS + 8 :, :] * b_fade
    for i in range(PIECE_HEADS):
        at = slice(i * HEAD_DIM, (i + 1) * HEAD_DIM)
        out_ref[at, :] = (
            a_ref[at, :] * a_fade[i : i + 1, :] + b_ref[at, :] * b_fade[i : i + 1, :]
        )
    out_ref[NUM_ROWS : NUM_ROWS + 8, :] = top
    out_ref[NUM_ROWS + 8 :, :] = den


def gelu_parts(x):
    c = 0.7978845608028654
    square = x * x
    t = jnp.tanh(c * x * (1.0 + 0.044715 * square))
    half = 0.5 * (1.0 + t)
    slope = half + (0.5 * c) * x * (1.0 - t * t) * (1.0 + (3 * 0.044715) * square)
    return x * half, slope


def latent_kernel(
    part_hbm,
    drop_ref,
    lat_hbm,
    cot_hbm,
    wo_hbm,
    gain_ref,
    wup_hbm,
    bup_ref,
    wdn_hbm,
    bdn_ref,
    msg_out,
    res_all,
    dmid_out,
    a_out,
    b_out,
    side_ref,
    vec_ref,
    lat_ref,
    cot_ref,
    msg_ref,
    res_ref,
    dmid_ref,
    a_ref,
    b_ref,
    store_sem,
    wo_ref,
    wup_ref,
    wdn_ref,
    pair_ref,
    own_ref,
    right_in,
    right_out,
    left_in,
    left_out,
    res_out,
    res_in,
    att_t_ref,
    mid_ref,
    acc_ref,
    dacc_ref,
    hn_ref,
    dm_ref,
    da_ref,
    att_ref,
    hn_out,
    hn_in,
    half_out,
    half_in,
    side_all,
    side_in,
    hn_send,
    hn_recv,
    half_send,
    half_recv,
    side_send,
    side_recv,
    own_sem,
    weight_sem,
    pair_send,
    pair_recv,
    right_send,
    right_recv,
    left_send,
    left_recv,
    msg_send,
    msg_recv,
    res_send,
    res_recv,
):
    samples = msg_out.shape[0]
    half = samples // 2
    lat_rows = 128
    width = lat_ref.shape[1]
    chunks = half * PIECES
    stream = lax.axis_index("stream")
    tok = lax.axis_index("tok")
    chips = lax.axis_size("tok") // 2
    core = lax.rem(tok, 2)
    chip = lax.div(tok, 2)
    parity = lax.rem(chip, 2)
    other = 1 - core
    partner = (stream, tok + 1 - 2 * core)
    right = (stream, tok + 2)
    left = (stream, tok - 2)
    has_right = chip < chips - 1
    has_left = chip > 0
    on_first = core == 0

    barrier = pltpu.get_barrier_semaphore()
    pl.semaphore_signal(barrier, inc=1, device_id=partner, device_id_type=MESH)

    @pl.when(has_right)
    def _():
        pl.semaphore_signal(barrier, inc=1, device_id=right, device_id_type=MESH)

    @pl.when(has_left)
    def _():
        pl.semaphore_signal(barrier, inc=1, device_id=left, device_id_type=MESH)

    own_load = pltpu.make_async_copy(
        part_hbm.at[pl.ds(core * chunks, chunks)], own_ref, own_sem
    )
    own_load.start()
    weights = [
        pltpu.make_async_copy(src, dst, weight_sem.at[i])
        for i, (src, dst) in enumerate(
            (
                (lat_hbm, lat_ref),
                (cot_hbm, cot_ref),
                (wo_hbm, wo_ref),
                (wup_hbm, wup_ref),
                (wdn_hbm, wdn_ref),
            )
        )
    ]
    for copy in weights:
        copy.start()
    pl.semaphore_wait(
        barrier, 1 + has_right.astype(jnp.int32) + has_left.astype(jnp.int32)
    )

    def pair_copy(i):
        return pltpu.make_async_remote_copy(
            src_ref=part_hbm.at[(1 - core) * chunks + i],
            dst_ref=pair_ref.at[i],
            send_sem=pair_send.at[i],
            recv_sem=pair_recv.at[i],
            device_id=partner,
            device_id_type=MESH,
        )

    def right_copy(i):
        return pltpu.make_async_remote_copy(
            src_ref=right_out.at[i],
            dst_ref=right_in.at[i],
            send_sem=right_send.at[i],
            recv_sem=right_recv.at[i],
            device_id=right,
            device_id_type=MESH,
        )

    def left_copy(i):
        return pltpu.make_async_remote_copy(
            src_ref=left_out.at[i],
            dst_ref=left_in.at[i],
            send_sem=left_send.at[i],
            recv_sem=left_recv.at[i],
            device_id=left,
            device_id_type=MESH,
        )

    def stores(j, far):
        at = (other if far else core) * half + j
        rows = pl.ds(pl.multiple_of(at * lat_rows, lat_rows), lat_rows)
        mine = pl.ds(pl.multiple_of(j * lat_rows, lat_rows), lat_rows)
        pairs = [
            (res_ref.at[rows], res_all.at[rows]),
            (a_ref.at[rows], a_out.at[rows]),
            (b_ref.at[:, rows], b_out.at[:, rows]),
        ]
        if not far:
            pairs.append((msg_ref.at[j], msg_out.at[at]))
            pairs.append((dmid_ref.at[mine], dmid_out.at[mine]))
        return [
            pltpu.make_async_copy(src, dst, store_sem.at[far, i, j])
            for i, (src, dst) in enumerate(pairs)
        ]

    def msg_copy(j):
        at = core * half + j
        return pltpu.make_async_remote_copy(
            src_ref=msg_ref.at[j],
            dst_ref=msg_out.at[at],
            send_sem=msg_send.at[j],
            recv_sem=msg_recv.at[j],
            device_id=partner,
            device_id_type=MESH,
        )

    def msg_arrival(j):
        return pltpu.make_async_remote_copy(
            src_ref=msg_ref.at[j],
            dst_ref=msg_out.at[other * half + j],
            send_sem=msg_send.at[j],
            recv_sem=msg_recv.at[j],
            device_id=partner,
            device_id_type=MESH,
        )

    def res_copy(j):
        return pltpu.make_async_remote_copy(
            src_ref=res_out.at[j],
            dst_ref=res_in.at[j],
            send_sem=res_send.at[j],
            recv_sem=res_recv.at[j],
            device_id=partner,
            device_id_type=MESH,
        )

    def hn_copy(j):
        return pltpu.make_async_remote_copy(
            src_ref=hn_out.at[j],
            dst_ref=hn_in.at[j],
            send_sem=hn_send.at[j],
            recv_sem=hn_recv.at[j],
            device_id=partner,
            device_id_type=MESH,
        )

    def half_copy(i):
        return pltpu.make_async_remote_copy(
            src_ref=half_out.at[i],
            dst_ref=half_in.at[i],
            send_sem=half_send.at[i],
            recv_sem=half_recv.at[i],
            device_id=partner,
            device_id_type=MESH,
        )

    side_copy = pltpu.make_async_remote_copy(
        src_ref=side_all.at[:, 1 - core],
        dst_ref=side_in,
        send_sem=side_send,
        recv_sem=side_recv,
        device_id=partner,
        device_id_type=MESH,
    )

    def start_pair(i, carry):
        pair_copy(i).start()
        return carry

    lax.fori_loop(0, chunks, start_pair, 0)
    own_load.wait()

    drop = row(drop_ref).astype(F32)
    scale_all = drop * drop.shape[1] / jnp.sum(drop, 1, keepdims=True)
    drop_lane = lax.broadcasted_iota(jnp.int32, drop.shape, 1)
    vec_ref[...] = jnp.zeros_like(vec_ref)

    def take(j):
        at = other * half + j
        rows = pl.ds(pl.multiple_of(at * lat_rows, lat_rows), lat_rows)
        for q in range(PIECES):
            half_copy(j * PIECES + q).wait_recv()
            b_ref[q, rows, :] = half_in[j * PIECES + q].astype(BF16)
        res_copy(j).wait_recv()
        res_ref[rows, :] = res_in[j].astype(BF16)

        @pl.when(on_first)
        def _():
            hn_copy(j).wait_recv()
            a_ref[rows, :] = hn_in[j].astype(BF16)

        @pl.when(jnp.logical_not(on_first))
        def _():
            scale = jnp.sum(
                jnp.where(drop_lane == stream * samples + at, scale_all, 0.0), 1, keepdims=True
            )
            a_ref[rows, :] = (scale * cot_ref[rows, :].astype(F32)).astype(BF16)

        for copy in stores(j, 1):
            copy.start()

    def mlp(j, q):
        sample = core * half + j
        rows = pl.ds(pl.multiple_of(sample * lat_rows, lat_rows), lat_rows)
        mine = pl.ds(pl.multiple_of(j * lat_rows, lat_rows), lat_rows)
        scale = jnp.sum(
            jnp.where(drop_lane == stream * samples + sample, scale_all, 0.0), 1, keepdims=True
        )

        @pl.when(q == 0)
        def _():
            for h in range(HEADS):
                piece, i = piece_of(h)
                at = j * PIECES + piece
                den = own_ref[at, NUM_ROWS + 8 + i : NUM_ROWS + 9 + i, :]
                att_t_ref[h * HEAD_DIM : (h + 1) * HEAD_DIM, :] = own_ref[
                    at, i * HEAD_DIM : (i + 1) * HEAD_DIM, :
                ] * (1.0 / den)
            att = att_t_ref[...].T.astype(BF16)
            att_ref[mine, :] = jnp.where(parity == 0, att[:, : width // 2], att[:, width // 2 :])
            mid = lat_ref[rows, :].astype(F32) + scale * dot(att, wo_ref[...])
            mid_ref[...] = mid
            unit, _ = norm_parts(mid)
            hn = (unit * row(gain_ref)).astype(BF16)
            dm = (scale * cot_ref[rows, :].astype(F32)).astype(BF16)
            hn_ref[...] = hn
            dm_ref[...] = dm
            a_ref[rows, :] = jnp.where(on_first, hn, dm)

            @pl.when(jnp.logical_not(on_first))
            def _():
                hn_out[j] = hn.astype(F32)
                hn_copy(j).start()

            vec_ref[1:2, :width] += jnp.sum(dm.astype(F32), 0, keepdims=True)
            acc_ref[...] = jnp.broadcast_to(row(bdn_ref), acc_ref.shape)
            dacc_ref[...] = jnp.zeros_like(dacc_ref)

        span = wup_ref.shape[1] // PIECES
        cols = pl.ds(pl.multiple_of(q * span, 128), span)
        pre = dot(hn_ref[...], wup_ref[:, cols]) + bup_ref[cols].reshape(1, span)
        active, slope = gelu_parts(pre)
        hidden = active.astype(BF16)
        acc_ref[...] += dot(hidden, wdn_ref[cols, :])
        dpre = (slope * dot(dm_ref[...], wdn_ref[cols, :], (1, 1))).astype(BF16)
        piece = j * PIECES + q
        near_half = lambda x: jnp.where(parity == 0, x[:, : span // 2], x[:, span // 2 :])
        hidden_half, dpre_half = near_half(hidden), near_half(dpre)
        b_ref[q, rows, :] = jnp.where(on_first, dpre_half, hidden_half)
        half_out[piece] = jnp.where(on_first, hidden_half, dpre_half).astype(F32)
        half_copy(piece).start()
        vec_ref[0:1, cols] += jnp.sum(dpre.astype(F32), 0, keepdims=True)
        dacc_ref[...] += dot(dpre, wup_ref[:, cols], (1, 1))

        @pl.when(q == PIECES - 1)
        def _():
            mid = mid_ref[...]
            res = (mid + scale * acc_ref[...]).astype(BF16)
            res_ref[rows, :] = res
            res_out[j] = res.astype(F32)
            res_copy(j).start()
            unit, inv = norm_parts(mid)
            dhn = dacc_ref[...]
            vec_ref[2:3, :width] += jnp.sum(dhn * unit, 0, keepdims=True)
            dmid = cot_ref[rows, :].astype(F32) + norm_back(unit, inv, row(gain_ref), dhn)
            dmid_ref[mine, :] = dmid
            da = (scale * dmid).astype(BF16)
            da_ref[mine, :] = da
            datt_t = dot(wo_ref[...], da, (1, 1)).astype(BF16).astype(F32)
            msg_ref[j, width:, :] = jnp.zeros((MSG_ROWS - width, lat_rows), F32)
            for h in range(HEADS):
                piece, i = piece_of(h)
                at = j * PIECES + piece
                inverse = 1.0 / own_ref[at, NUM_ROWS + 8 + i : NUM_ROWS + 9 + i, :]
                span_h = slice(h * HEAD_DIM, (h + 1) * HEAD_DIM)
                one = datt_t[span_h]
                msg_ref[j, span_h, :] = (one * inverse).astype(BF16).astype(F32)
                delta = jnp.sum(one * att_t_ref[span_h, :], 0, keepdims=True) * inverse
                msg_ref[j, width + h : width + h + 1, :] = own_ref[
                    at, NUM_ROWS + i : NUM_ROWS + i + 1, :
                ]
                msg_ref[j, width + 16 + h : width + 17 + h, :] = delta
            msg_copy(j).start()
            for copy in stores(j, 0):
                copy.start()

            @pl.when(j > 0)
            def _():
                take(j - 1)

    def step(t, carry):
        @pl.when(t < chunks)
        def _():
            pair_copy(t).wait_recv()
            merge(own_ref.at[t], pair_ref.at[t], own_ref.at[t])

        r = t - LAG * chip

        @pl.when((r >= 0) & (r < chunks))
        def _():
            @pl.when(has_left)
            def _():
                right_copy(r).wait_recv()
                merge(own_ref.at[r], right_in.at[r], right_out.at[r])

            @pl.when(jnp.logical_not(has_left))
            def _():
                right_out[r] = own_ref[r]

            @pl.when(has_right)
            def _():
                right_copy(r).start()

        u = t - LAG * (chips - 1 - chip)

        @pl.when((u >= 0) & (u < chunks))
        def _():
            @pl.when(has_right)
            def _():
                left_copy(u).wait_recv()

            @pl.when(has_left)
            def _():
                @pl.when(has_right)
                def _():
                    merge(own_ref.at[u], left_in.at[u], left_out.at[u])

                @pl.when(jnp.logical_not(has_right))
                def _():
                    left_out[u] = own_ref[u]

                left_copy(u).start()

        w = t - LAG * jnp.maximum(chip, chips - 1 - chip)

        @pl.when((w >= 0) & (w < chunks))
        def _():
            @pl.when(has_right)
            def _():
                merge(right_out.at[w], left_in.at[w], own_ref.at[w])

            @pl.when(jnp.logical_not(has_right))
            def _():
                own_ref[w] = right_out[w]

        m = w - (PIECES - 1)

        @pl.when(m == 0)
        def _():
            for copy in weights:
                copy.wait()

        @pl.when((m >= 0) & (m < chunks))
        def _():
            mlp(lax.div(m, PIECES), lax.rem(m, PIECES))

        return carry

    lax.fori_loop(0, chunks + LAG * (chips - 1) + PIECES - 1, step, 0)

    share = width // 8
    for block in range(4):
        at = slice(block * 2 * share, (block + 1) * 2 * share)
        product = dot(da_ref[:, at], att_ref[...], (0, 0))
        side_all[block, 0] = product[:share]
        side_all[block, 1] = product[share:]
    side_copy.start()

    take(half - 1)

    def finish_chunk(i, carry):
        pair_copy(i).wait_send()
        half_copy(i).wait_send()

        @pl.when(has_right)
        def _():
            right_copy(i).wait_send()

        @pl.when(has_left)
        def _():
            left_copy(i).wait_send()

        return carry

    lax.fori_loop(0, chunks, finish_chunk, 0)

    def finish_sample(j, carry):
        @pl.when(jnp.logical_not(on_first))
        def _():
            hn_copy(j).wait_send()

        res_copy(j).wait_send()
        msg_copy(j).wait_send()
        msg_arrival(j).wait_recv()
        for copy in stores(j, 0) + stores(j, 1):
            copy.wait()
        return carry

    lax.fori_loop(0, half, finish_sample, 0)
    side_copy.wait()
    side_ref[...] = side_all[:, core] + side_in[...]


def latent_block(part, drop_mask, latents, cotangent, wo, gain, wup, bup, wdn, bdn):
    samples, lat_rows, width = latents.shape
    half = samples // 2
    chunks = half * PIECES
    hidden = wup.shape[1]
    sds = jax.ShapeDtypeStruct
    chunk = lambda: pltpu.VMEM((chunks, PIECE_ROWS, lat_rows), F32)
    dma = pltpu.SemaphoreType.DMA
    return pl.pallas_call(
        latent_kernel,
        name="latent_block",
        out_shape=(
            sds((samples, MSG_ROWS, lat_rows), F32),
            sds((samples * lat_rows, width), BF16),
            sds((half * lat_rows, width), F32),
            sds((samples * lat_rows, width), BF16),
            sds((PIECES, samples * lat_rows, hidden // PIECES // 2), BF16),
            sds((4, width // 8, width // 2), F32),
            sds((8, hidden), F32),
        ),
        in_specs=[
            anywhere(),
            vmem(),
            anywhere(),
            anywhere(),
            anywhere(),
            vmem(),
            anywhere(),
            vmem(),
            anywhere(),
            vmem(),
        ],
        out_specs=(anywhere(),) * 5 + (vmem(),) * 2,
        scratch_shapes=[
            pltpu.VMEM((samples * lat_rows, width), BF16),
            pltpu.VMEM((samples * lat_rows, width), BF16),
            pltpu.VMEM((half, MSG_ROWS, lat_rows), F32),
            pltpu.VMEM((samples * lat_rows, width), BF16),
            pltpu.VMEM((half * lat_rows, width), F32),
            pltpu.VMEM((samples * lat_rows, width), BF16),
            pltpu.VMEM((PIECES, samples * lat_rows, hidden // PIECES // 2), BF16),
            dma((2, 5, half)),
            pltpu.VMEM(wo.shape, BF16),
            pltpu.VMEM(wup.shape, BF16),
            pltpu.VMEM(wdn.shape, BF16),
            chunk(),
            chunk(),
            chunk(),
            chunk(),
            chunk(),
            chunk(),
            pltpu.VMEM((half, lat_rows, width), F32),
            pltpu.VMEM((half, lat_rows, width), F32),
            pltpu.VMEM((width, lat_rows), F32),
            pltpu.VMEM((lat_rows, width), F32),
            pltpu.VMEM((lat_rows, width), F32),
            pltpu.VMEM((lat_rows, width), F32),
            pltpu.VMEM((lat_rows, width), BF16),
            pltpu.VMEM((lat_rows, width), BF16),
            pltpu.VMEM((half * lat_rows, width), BF16),
            pltpu.VMEM((half * lat_rows, width // 2), BF16),
            pltpu.VMEM((half, lat_rows, width), F32),
            pltpu.VMEM((half, lat_rows, width), F32),
            pltpu.VMEM((chunks, lat_rows, hidden // PIECES // 2), F32),
            pltpu.VMEM((chunks, lat_rows, hidden // PIECES // 2), F32),
            pltpu.VMEM((4, 2, width // 8, width // 2), F32),
            pltpu.VMEM((4, width // 8, width // 2), F32),
            dma((half,)),
            dma((half,)),
            dma((chunks,)),
            dma((chunks,)),
            dma,
            dma,
            dma,
            dma((5,)),
            dma((chunks,)),
            dma((chunks,)),
            dma((chunks,)),
            dma((chunks,)),
            dma((chunks,)),
            dma((chunks,)),
            dma((half,)),
            dma((half,)),
            dma((half,)),
            dma((half,)),
        ],
        compiler_params=pltpu.CompilerParams(
            vmem_limit_bytes=VMEM_BYTES, collective_id=1, has_side_effects=True
        ),
    )(
        part.reshape(samples * PIECES, PIECE_ROWS, lat_rows),
        drop_mask,
        latents.reshape(samples * lat_rows, width),
        cotangent.reshape(samples * lat_rows, width),
        wo,
        gain,
        wup,
        bup,
        wdn,
        bdn,
    )


ZROWS = 32


def gradient_kernel(
    dlat_hbm,
    a_hbm,
    b_hbm,
    side_ref,
    dwq_hbm,
    vec_ref,
    dgain_q_ref,
    place_ref,
    tok_hbm,
    tsort_hbm,
    dkv_hbm,
    gain_t_ref,
    wk_ref,
    wv_ref,
    dlat_out,
    gather_out,
    kv_out,
    query_out,
    small_out,
    dtok_out,
    line_ref,
    right_ref,
    left_ref,
    dmine_ref,
    wide_ref,
    wide_one,
    wide_two,
    send_ref,
    mine_ref,
    pair_ref,
    one_ref,
    two_ref,
    small_ref,
    gain_ref,
    wide_far,
    spread_ref,
    stage_ref,
    stage_sem,
    a_ref,
    b_ref,
    dwq_ref,
    tok_ref,
    tsort_ref,
    dkv_ref,
    load_sem,
    dpair_send,
    dpair_recv,
    right_send,
    right_recv,
    left_send,
    left_recv,
    back_send,
    back_recv,
    back_local,
    wide_one_send,
    wide_one_recv,
    wide_two_send,
    wide_two_recv,
    wide_z_send,
    wide_z_recv,
    wide_core_send,
    wide_core_recv,
    wide_local,
    pair_send,
    pair_recv,
    one_send,
    one_recv,
    two_send,
    two_recv,
    spread_send,
    spread_recv,
    share_send,
    share_recv,
    query_send,
    query_recv,
    query_local,
    keep_local,
):
    rows, width = tok_ref.shape
    lat_chunks = dmine_ref.shape[0]
    all_chunks = line_ref.shape[0]
    kv_rows = send_ref.shape[2]
    q_rows = query_out.shape[2]
    mix = kv_rows + q_rows
    half_chunks = (all_chunks - lat_chunks) // 2
    kv_chunks = kv_rows // ZROWS
    wide_half = wide_ref.shape[1] // 2
    sub_rows = wide_half // SUBS

    stream = lax.axis_index("stream")
    tok = lax.axis_index("tok")
    chips = lax.axis_size("tok") // 2
    core = lax.rem(tok, 2)
    chip = lax.div(tok, 2)
    other = 1 - core
    parity = lax.rem(chip, 2)
    flip_x = stream + 1 - 2 * lax.rem(stream, 2)
    flip_y = lax.rem(stream + 2, 4)
    flip_xy = 3 - stream
    partner = (stream, tok + 1 - 2 * core)
    right = (stream, tok + 2)
    left = (stream, tok - 2)
    beside = (stream, tok + 2 - 4 * parity)
    near = ((flip_x, tok), (flip_y, tok))
    first = (flip_x, flip_y)
    has_right = chip < chips - 1
    has_left = chip > 0

    barrier = pltpu.get_barrier_semaphore()
    for target in (partner,) + near:
        pl.semaphore_signal(barrier, inc=1, device_id=target, device_id_type=MESH)

    @pl.when(has_right)
    def _():
        pl.semaphore_signal(barrier, inc=1, device_id=right, device_id_type=MESH)

    @pl.when(has_left)
    def _():
        pl.semaphore_signal(barrier, inc=1, device_id=left, device_id_type=MESH)

    def remote(src, dst, send, recv, target):
        return pltpu.make_async_remote_copy(
            src_ref=src,
            dst_ref=dst,
            send_sem=send,
            recv_sem=recv,
            device_id=target,
            device_id_type=MESH,
        )

    pulls = [
        pltpu.make_async_copy(src, dst, load_sem.at[i])
        for i, (src, dst) in enumerate(
            (
                (tsort_hbm, tsort_ref),
                (dkv_hbm, dkv_ref),
                (dlat_hbm.at[core], dmine_ref),
                (a_hbm, a_ref),
                (b_hbm, b_ref),
                (dwq_hbm, dwq_ref),
                (tok_hbm, tok_ref),
            )
        )
    ]
    for copy in pulls:
        copy.start()
    pl.semaphore_wait(barrier, 3 + has_right.astype(jnp.int32) + has_left.astype(jnp.int32))

    def dpair_copy(i):
        return remote(
            dlat_hbm.at[other, i], line_ref.at[i], dpair_send.at[i], dpair_recv.at[i], partner
        )

    def start_dpair(i, carry):
        dpair_copy(i).start()
        return carry

    lax.fori_loop(0, lat_chunks, start_dpair, 0)

    def wide_one_copy(h, n, sub):
        block = (first[h], flip_xy)[n]
        at = pl.ds(h * wide_half + sub * sub_rows, sub_rows)
        return remote(
            wide_ref.at[block, at],
            wide_one.at[h, n, pl.ds(sub * sub_rows, sub_rows)],
            wide_one_send.at[h, n, sub],
            wide_one_recv.at[h, n, sub],
            near[h],
        )

    def wide_at(block, h, sub):
        return wide_ref.at[block, pl.ds(h * wide_half + sub * sub_rows, sub_rows)]

    def wide_two_copy(h, sub):
        at = pl.ds(sub * sub_rows, sub_rows)
        return remote(
            wide_at(first[1 - h], h, sub),
            wide_two.at[h, at],
            wide_two_send.at[h, sub],
            wide_two_recv.at[h, sub],
            near[1 - h],
        )

    def gather_at(c, e, h, sub):
        return gather_out.at[c, e, pl.ds(h * wide_half + sub * sub_rows, sub_rows)]

    def far_at(h, sub):
        return wide_far.at[pl.ds(h * wide_half + sub * sub_rows, sub_rows)]

    def wide_z_copy(h, sub):
        return remote(
            wide_at(stream, h, sub),
            far_at(h, sub),
            wide_z_send.at[h, sub],
            wide_z_recv.at[h, sub],
            beside,
        )

    def wide_core_copy(far, h, sub):
        if far:
            src = far_at(h, sub)
            dst = gather_at(core, 1 - parity, h, sub)
        else:
            src = wide_at(stream, h, sub)
            dst = gather_at(core, parity, h, sub)
        return remote(
            src, dst, wide_core_send.at[far, h, sub], wide_core_recv.at[far, h, sub], partner
        )

    def wide_core_arrival(far, h, sub):
        place = gather_at(other, 1 - parity if far else parity, h, sub)
        return remote(
            place, place, wide_core_send.at[far, h, sub], wide_core_recv.at[far, h, sub], partner
        )

    def wide_keep(far, h, sub):
        return pltpu.make_async_copy(
            far_at(h, sub) if far else wide_at(stream, h, sub),
            gather_at(core, 1 - parity if far else parity, h, sub),
            wide_local.at[far, h, sub],
        )

    def wide_product(block):
        wide_ref[block, :width, :] = dot(a_ref[...], b_ref[block], (0, 0))
        wide_ref[block, width:, :] = side_ref[block]

    def wide_start(k):
        wide_product((flip_xy, first[0], first[1], stream)[k])
        for sub in range(EARLY_SUBS):
            for h in range(2):
                if k == 0:
                    wide_one_copy(h, 1, sub).start()
                elif k == 1 + h:
                    wide_one_copy(h, 0, sub).start()

    def wide_more():
        for sub in range(EARLY_SUBS, SUBS):
            for h in range(2):
                for n in range(2):
                    wide_one_copy(h, 1 - n, sub).start()

    def wide_event_one(sub):
        at = slice(sub * sub_rows, (sub + 1) * sub_rows)
        for h in range(2):
            for n in range(2):
                wide_one_copy(h, n, sub).wait_recv()
            span = pl.ds(h * wide_half + sub * sub_rows, sub_rows)
            wide_ref[first[1 - h], span, :] += wide_one[h, 1, at, :]
            wide_two_copy(h, sub).start()
            wide_ref[stream, span, :] += wide_one[h, 0, at, :]

    def wide_event_two(sub):
        at = slice(sub * sub_rows, (sub + 1) * sub_rows)
        for h in range(2):
            wide_two_copy(h, sub).wait_recv()
            span = pl.ds(h * wide_half + sub * sub_rows, sub_rows)
            wide_ref[stream, span, :] += wide_two[h, at, :]
            wide_z_copy(h, sub).start()
            wide_core_copy(0, h, sub).start()
            wide_keep(0, h, sub).start()

    def wide_event_three(sub):
        for h in range(2):
            wide_z_copy(h, sub).wait_recv()
            wide_core_copy(1, h, sub).start()
            wide_keep(1, h, sub).start()

    share = width // 4

    def gain_part(which, block, product):
        at = slice(block * share, (block + 1) * share)
        weight = jnp.where(which == 0, wk_ref[at, :], wv_ref[at, :]).astype(F32)
        gain_ref[at, 0:1] += jnp.sum(product * weight, 1, keepdims=True)

    def token_product(block, which):
        at = slice(block * share, (block + 1) * share)
        return dot(tsort_ref[:, at], dkv_ref[which], (0, 0))

    def token_other():
        gain_ref[...] = jnp.zeros_like(gain_ref)
        for block in range(4):
            product = token_product(block, other)
            for h in range(2):
                send_ref[h, block] = product[h * kv_rows : (h + 1) * kv_rows]
            gain_part(other, block, product)
        for k, h, what in pairs:
            if what < 2:
                pair_copy(k, h, what).start()

    order = (flip_xy, first[0], first[1], stream)

    def pair_copy(k, h, what):
        block = order[k]
        src, at, size = (
            (send_ref.at[h, block], 0, kv_rows),
            (dwq_ref.at[block, other, h], kv_rows, q_rows),
            (small_ref.at[block], mix, 16),
        )[what]
        return remote(
            src,
            pair_ref.at[h, block, pl.ds(at, size)],
            pair_send.at[k, h, what],
            pair_recv.at[k, h, what],
            partner,
        )

    pairs = [(k, h, what) for k in range(4) for h in range(2) for what in range(3 - h)]

    def token_own():
        for block in range(4):
            product = token_product(block, core)
            for h in range(2):
                piece = product[h * kv_rows : (h + 1) * kv_rows]
                mine_ref[h, block, :kv_rows, :] = piece
                mine_ref[h, block, kv_rows:mix, :] = dwq_ref[block, core, h]
            gain_part(core, block, product)
        mine_ref[1, :, mix:, :] = jnp.zeros((4, 16, width), F32)
        small_ref[...] = jnp.zeros_like(small_ref)
        gain = jnp.broadcast_to(gain_ref[:, 0:1], gain_ref.shape).T[0:1, :] / row(gain_t_ref)
        for block in range(4):
            small_ref[block, 0:1, :] = vec_ref[0:1, block * width : (block + 1) * width] * here
            small_ref[block, 1:2, :] = dgain_q_ref[0:1, :]
            small_ref[block, 2:3, :] = vec_ref[2:3, :width] * here
            small_ref[block, 3:4, :] = vec_ref[1:2, :width] * here
            small_ref[block, 4:5, :] = gain
        for k in range(4):
            pair_copy(k, 0, 2).start()

    here = (chip == 0).astype(F32)

    token_step = 128

    def stage_copy(i):
        return pltpu.make_async_copy(
            stage_ref.at[i % 2],
            dtok_out.at[pl.ds(i * token_step, token_step)],
            stage_sem.at[i % 2],
        )

    def token_part(i):
        at = pl.ds(pl.multiple_of(i * token_step, token_step), token_step)
        target = lax.broadcasted_iota(jnp.int32, (token_step, rows), 1).astype(F32)
        pick = jnp.where(target == place_ref[at, 0:1], 1.0, 0.0).astype(BF16)
        dkey = dot(pick, dkv_ref[0]).astype(BF16)
        dval = dot(pick, dkv_ref[1]).astype(BF16)
        dnormed = dot(dkey, wk_ref[...], (1, 1)) + dot(dval, wv_ref[...], (1, 1))
        unit, inv = norm_parts(tok_ref[at, :].astype(F32))
        if i >= 2:
            stage_copy(i - 2).wait()
        stage_ref[i % 2] = norm_back(unit, inv, row(gain_t_ref), dnormed)
        stage_copy(i).start()

    def one_copy(h, n):
        block = (first[h], flip_xy)[n]
        return remote(
            mine_ref.at[h, block], one_ref.at[h, n], one_send.at[h, n], one_recv.at[h, n], near[h]
        )

    def two_copy(h):
        return remote(
            mine_ref.at[h, first[1 - h]], two_ref.at[h], two_send.at[h], two_recv.at[h], near[1 - h]
        )

    def pair_event():
        for k in range(4):
            block = order[k]
            for h in range(2):
                for what in range(3 - h):
                    pair_copy(k, h, what).wait_recv()
                mine_ref[h, block, :mix, :] += pair_ref[h, block, :mix, :]
                if h == 0:
                    mine_ref[h, block, mix:, :] = small_ref[block] + pair_ref[h, block, mix:, :]
                if k == 0:
                    one_copy(h, 1).start()
                elif k == 1 + h:
                    one_copy(h, 0).start()

    def one_event():
        for h in range(2):
            for n in range(2):
                one_copy(h, n).wait_recv()
            mine_ref[h, first[1 - h]] += one_ref[h, 1]
            two_copy(h).start()

    def two_event():
        for h in range(2):
            two_copy(h).wait_recv()
            total = mine_ref[h, stream] + one_ref[h, 0] + two_ref[h]
            for k in range(half_chunks):
                line_ref[lat_chunks + h * half_chunks + k] = total[k * ZROWS : (k + 1) * ZROWS]

    def right_copy(i):
        return remote(right_ref.at[i], right_ref.at[i], right_send.at[i], right_recv.at[i], right)

    def left_copy(i):
        return remote(left_ref.at[i], left_ref.at[i], left_send.at[i], left_recv.at[i], left)

    def back_copy(i):
        return remote(
            line_ref.at[i], dlat_out.at[core, i], back_send.at[i], back_recv.at[i], partner
        )

    def back_arrival(i):
        return remote(
            line_ref.at[i], dlat_out.at[other, i], back_send.at[i], back_recv.at[i], partner
        )

    def back_keep(i):
        return pltpu.make_async_copy(line_ref.at[i], dlat_out.at[core, i], back_local.at[i])

    def placed(t):
        late = t >= lat_chunks + GAP
        index = jnp.where(late, t - GAP, t)
        return index, (t >= 0) & (late | (t < lat_chunks)) & (index < all_chunks)

    def line_step(t):
        @pl.when(t < lat_chunks)
        def _():
            dpair_copy(t).wait_recv()
            line_ref[t] += dmine_ref[t]

        r, r_due = placed(t - LAG * chip)

        @pl.when(r_due)
        def _():
            @pl.when(has_left)
            def _():
                right_copy(r).wait_recv()
                right_ref[r] += line_ref[r]

            @pl.when(jnp.logical_not(has_left))
            def _():
                right_ref[r] = line_ref[r]

            @pl.when(has_right)
            def _():
                right_copy(r).start()

        u, u_due = placed(t - LAG * (chips - 1 - chip))

        @pl.when(u_due)
        def _():
            @pl.when(has_right)
            def _():
                left_copy(u).wait_recv()
                left_ref[u] += line_ref[u]

            @pl.when(jnp.logical_not(has_right))
            def _():
                left_ref[u] = line_ref[u]

            @pl.when(has_left)
            def _():
                left_copy(u).start()

        w, w_due = placed(t - LAG * jnp.maximum(chip, chips - 1 - chip))

        @pl.when(w_due)
        def _():
            line_ref[w] = right_ref[w] + left_ref[w] - line_ref[w]

            @pl.when(w < lat_chunks)
            def _():
                back_copy(w).start()
                back_keep(w).start()

    def spot(i):
        k = i - lat_chunks
        h = lax.div(k, half_chunks)
        return h, lax.rem(k, half_chunks)

    def by_half(h, pair):
        return jnp.where(h == 0, pair[0], pair[1])

    def block_of(h, k):
        return (stream, by_half(h, (flip_y, flip_x)), by_half(h, first), flip_xy)[k]

    def spread_src(i, k):
        h, c = spot(i)
        return line_ref.at[i] if k == 0 else spread_ref.at[k - 1, h, c]

    def spread_copy(i, k):
        h, c = spot(i)
        target = by_half(h, (flip_y, flip_x)) if k == 1 else by_half(h, first)
        return remote(
            spread_src(i, 1 if k == 3 else 0),
            spread_ref.at[k - 1, h, c],
            spread_send.at[k - 1, i - lat_chunks],
            spread_recv.at[k - 1, i - lat_chunks],
            (target, tok),
        )

    def share_copy(i, k):
        h, c = spot(i)
        return remote(
            spread_src(i, k),
            kv_out.at[core, block_of(h, k), h, c],
            share_send.at[k, i - lat_chunks],
            share_recv.at[k, i - lat_chunks],
            partner,
        )

    def share_arrival(i, k):
        h, c = spot(i)
        place = kv_out.at[other, block_of(h, k), h, c]
        return remote(
            place,
            place,
            share_send.at[k, i - lat_chunks],
            share_recv.at[k, i - lat_chunks],
            partner,
        )

    def kv_keep(i, k):
        h, c = spot(i)
        return pltpu.make_async_copy(
            spread_src(i, k),
            kv_out.at[core, block_of(h, k), h, c],
            keep_local.at[k, i - lat_chunks],
        )

    def spread_due(t):
        i, due = placed(t)
        i = jnp.maximum(i, lat_chunks)
        _, c = spot(i)
        return i, due & (t >= lat_chunks + GAP) & (c < kv_chunks)

    def spread_step(t):
        lag = LAG * jnp.maximum(chip, chips - 1 - chip)
        i, due = spread_due(t - lag)

        @pl.when(due)
        def _():
            spread_copy(i, 1).start()
            spread_copy(i, 2).start()
            share_copy(i, 0).start()
            kv_keep(i, 0).start()

        j, due_one = spread_due(t - lag - SPREAD_LAG)

        @pl.when(due_one)
        def _():
            spread_copy(j, 1).wait_recv()
            spread_copy(j, 3).start()
            share_copy(j, 1).start()
            kv_keep(j, 1).start()

        m, due_two = spread_due(t - lag - 2 * SPREAD_LAG)

        @pl.when(due_two)
        def _():
            for k in (2, 3):
                spread_copy(m, k).wait_recv()
                share_copy(m, k).start()
                kv_keep(m, k).start()

    def query_piece(h):
        return mine_ref.at[h, stream, pl.ds(kv_rows, q_rows)]

    def query_copy(h):
        return remote(
            query_piece(h),
            query_out.at[core, h],
            query_send.at[h],
            query_recv.at[h],
            partner,
        )

    def query_arrival(h):
        return remote(
            query_piece(h),
            query_out.at[other, h],
            query_send.at[h],
            query_recv.at[h],
            partner,
        )

    def query_keep(h):
        return pltpu.make_async_copy(query_piece(h), query_out.at[core, h], query_local.at[h])

    def query_event(h):
        flat = lat_chunks + h * half_chunks + kv_chunks
        for k in range(0, q_rows, 16):
            at = flat * ZROWS + k
            chunk, row = at // ZROWS, at % ZROWS
            mine_ref[h, stream, kv_rows + k : kv_rows + k + 16, :] = line_ref[
                chunk, row : row + 16, :
            ]
        query_copy(h).start()
        query_keep(h).start()
        if h == 0:
            at = flat * ZROWS + q_rows
            chunk, row = at // ZROWS, at % ZROWS
            small_out[...] = line_ref[chunk, row : row + 16, :]

    tail = LAG * (chips - 1)
    ready = lambda h: lat_chunks + GAP + (h + 1) * half_chunks - 1 + tail
    events = {}

    def at_tick(tick, run):
        events.setdefault(tick, []).append(run)

    parts = rows // token_step
    for i in range(parts):
        at_tick(TOKEN_TICKS[i % len(TOKEN_TICKS)], functools.partial(token_part, i))
    for k in range(4):
        at_tick(WIDE_START_TICKS[k], functools.partial(wide_start, k))
    at_tick(KV_TICKS[0], token_other)
    at_tick(KV_TICKS[1], token_own)
    at_tick(PAIR_TICK, pair_event)
    at_tick(MORE_TICK, wide_more)
    at_tick(ONE_TICK, one_event)
    at_tick(TWO_TICK, two_event)
    for sub in range(SUBS):
        at_tick(WIDE_ONE_TICKS[sub], functools.partial(wide_event_one, sub))
        at_tick(WIDE_TWO_TICKS[sub], functools.partial(wide_event_two, sub))
        if WIDE_THREE_TICKS[sub] >= 0:
            at_tick(WIDE_THREE_TICKS[sub], functools.partial(wide_event_three, sub))
    for copy in pulls:
        copy.wait()

    def step(t, carry):
        line_step(t)
        spread_step(t)
        for tick in sorted(events):

            @pl.when(t == tick)
            def _(tick=tick):
                for run in events[tick]:
                    run()

        return carry

    lax.fori_loop(0, ready(1) + 2 * SPREAD_LAG + 1, step, 0)
    for h in range(2):
        query_event(h)
    for sub in range(SUBS):
        if WIDE_THREE_TICKS[sub] < 0:
            wide_event_three(sub)

    def finish_lat(i, carry):
        dpair_copy(i).wait_send()
        back_copy(i).wait_send()
        back_arrival(i).wait_recv()
        back_keep(i).wait()
        return carry

    lax.fori_loop(0, lat_chunks, finish_lat, 0)

    def finish_line(i, carry):
        @pl.when(has_right)
        def _():
            right_copy(i).wait_send()

        @pl.when(has_left)
        def _():
            left_copy(i).wait_send()

        return carry

    lax.fori_loop(0, all_chunks, finish_line, 0)

    def finish_spread(n, carry):
        h = lax.div(n, kv_chunks)
        i = lat_chunks + h * half_chunks + lax.rem(n, kv_chunks)
        for k in range(4):
            if k:
                spread_copy(i, k).wait_send()
            share_copy(i, k).wait_send()
            share_arrival(i, k).wait_recv()
            kv_keep(i, k).wait()
        return carry

    lax.fori_loop(0, 2 * kv_chunks, finish_spread, 0)
    for i in range(parts - 2, parts):
        stage_copy(i).wait()
    for k, h, what in pairs:
        pair_copy(k, h, what).wait_send()
    for h in range(2):
        for n in range(2):
            one_copy(h, n).wait_send()
        two_copy(h).wait_send()
        query_copy(h).wait_send()
        query_arrival(h).wait_recv()
        query_keep(h).wait()
        for sub in range(SUBS):
            for n in range(2):
                wide_one_copy(h, n, sub).wait_send()
                wide_core_copy(n, h, sub).wait_send()
                wide_core_arrival(n, h, sub).wait_recv()
            wide_two_copy(h, sub).wait_send()
            wide_z_copy(h, sub).wait_send()
            wide_keep(0, h, sub).wait()
            wide_keep(1, h, sub).wait()


def gradients(
    dlat, a, b, side, dwq, vec, dgain_q, place, tokens, tsort, dkv, gain_t, wk, wv
):
    rows, width = tokens.shape
    half = dlat.shape[0] // 2
    lat_chunks = half // ZROWS
    wide_rows, wide_cols = a.shape[1] + side.shape[1], b.shape[2]
    share = width // 4
    kv_rows, q_rows = share // 2, share // 4
    block = kv_rows + q_rows + 16
    all_chunks = lat_chunks + 2 * block // ZROWS
    sds = jax.ShapeDtypeStruct
    dma = pltpu.SemaphoreType.DMA
    buf = lambda *shape: pltpu.VMEM(shape, F32)
    both = lambda *shape: [dma(shape), dma(shape)]
    return pl.pallas_call(
        gradient_kernel,
        name="gradients",
        out_shape=(
            sds((2, lat_chunks, ZROWS, width), F32),
            sds((2, 2, wide_rows, wide_cols), F32),
            sds((2, 4, 2, kv_rows // ZROWS, ZROWS, width), F32),
            sds((2, 2, q_rows, width), F32),
            sds((16, width), F32),
            sds((rows, width), F32),
        ),
        in_specs=[anywhere()] * 3
        + [vmem(), anywhere()]
        + [vmem()] * 3
        + [anywhere()] * 3
        + [vmem()] * 3,
        out_specs=(anywhere(),) * 4 + (vmem(), anywhere()),
        scratch_shapes=[
            buf(all_chunks, ZROWS, width),
            buf(all_chunks, ZROWS, width),
            buf(all_chunks, ZROWS, width),
            buf(lat_chunks, ZROWS, width),
            buf(4, wide_rows, wide_cols),
            buf(2, 2, wide_rows // 2, wide_cols),
            buf(2, wide_rows // 2, wide_cols),
            buf(2, 4, kv_rows, width),
            buf(2, 4, block, width),
            buf(2, 4, block, width),
            buf(2, 2, block, width),
            buf(2, block, width),
            buf(4, 16, width),
            buf(width, 128),
            buf(wide_rows, wide_cols),
            buf(3, 2, kv_rows // ZROWS, ZROWS, width),
            buf(2, 128, width),
            dma((2,)),
            pltpu.VMEM(a.shape, BF16),
            pltpu.VMEM(b.shape, BF16),
            buf(4, 2, 2, q_rows, width),
            pltpu.VMEM(tokens.shape, BF16),
            pltpu.VMEM(tsort.shape, BF16),
            pltpu.VMEM(dkv.shape, BF16),
            dma((7,)),
        ]
        + both(lat_chunks)
        + both(all_chunks)
        + both(all_chunks)
        + both(lat_chunks)
        + [dma((lat_chunks,))]
        + both(2, 2, SUBS)
        + both(2, SUBS)
        + both(2, SUBS)
        + both(2, 2, SUBS)
        + [dma((2, 2, SUBS))]
        + both(4, 2, 3)
        + both(2, 2)
        + both(2)
        + both(3, all_chunks - lat_chunks)
        + both(4, all_chunks - lat_chunks)
        + both(2)
        + [dma((2,)), dma((4, all_chunks - lat_chunks))],
        compiler_params=pltpu.CompilerParams(
            vmem_limit_bytes=VMEM_BYTES, collective_id=2, has_side_effects=True
        ),
    )(
        dlat.reshape(2, lat_chunks, ZROWS, width),
        a,
        b,
        side,
        dwq.reshape(4, 2, 2, q_rows, width),
        vec,
        dgain_q,
        place,
        tokens,
        tsort,
        dkv,
        gain_t,
        wk,
        wv,
    )


def closing_kernel(
    dlat_hbm,
    gather_hbm,
    kv_hbm,
    query_ref,
    small_ref,
    dtok_hbm,
    dlat_out,
    dtok_out,
    up_out,
    key_out,
    val_out,
    down_out,
    out_ref,
    wq_ref,
    gain_q_ref,
    gain_t_ref,
    gain_mlp_ref,
    bup_ref,
    bdn_ref,
    wide_ref,
    up_ref,
    dlat_ref,
    kv_ref,
    dtok_ref,
    down_ref,
    load_sems,
    store_sems,
):
    width = small_ref.shape[1]
    cols = wide_ref.shape[2]
    loads = [
        pltpu.make_async_copy(src, dst, load_sems.at[i])
        for i, (src, dst) in enumerate(
            (
                (gather_hbm.at[1], wide_ref),
                (gather_hbm.at[0], up_ref),
                (dlat_hbm, dlat_ref),
                (kv_hbm, kv_ref),
                (dtok_hbm, dtok_ref),
            )
        )
    ]
    for copy in loads:
        copy.start()
    stores = [
        pltpu.make_async_copy(src, dst, store_sems.at[i])
        for i, (src, dst) in enumerate(
            (
                (up_ref.at[0, pl.ds(0, width)], up_out.at[:, pl.ds(0, cols)]),
                (up_ref.at[1, pl.ds(0, width)], up_out.at[:, pl.ds(cols, cols)]),
                (dlat_ref, dlat_out),
                (kv_ref.at[0], key_out),
                (kv_ref.at[1], val_out),
                (dtok_ref, dtok_out),
                (down_ref, down_out),
            )
        )
    ]
    stream = lax.axis_index("stream")
    gain_t_ref[...] = small_ref[4]
    bup_ref[...] = small_ref[0]
    size = gain_q_ref.shape[0]
    for i, ref in ((1, gain_q_ref), (2, gain_mlp_ref), (3, bdn_ref)):
        line = small_ref[i : i + 1, :]
        piece = line[:, :size]
        for k in range(1, width // size):
            piece = jnp.where(stream == k, line[:, k * size : (k + 1) * size], piece)
        ref[...] = piece[0]
    wq_ref[...] = query_ref[...]
    loads[0].wait()
    for e in range(2):
        down_ref[e * cols : (e + 1) * cols, :] = wide_ref[e, :width, :].T
    stores[6].start()
    loads[1].wait()
    stores[0].start()
    stores[1].start()
    half = up_ref.shape[1] - width
    for e in range(2):
        out_ref[:half, e * cols : (e + 1) * cols] = up_ref[e, width:, :]
        out_ref[half:, e * cols : (e + 1) * cols] = wide_ref[e, width:, :]
    loads[2].wait()
    stores[2].start()
    loads[3].wait()
    stores[3].start()
    stores[4].start()
    loads[4].wait()
    stores[5].start()
    for copy in stores:
        copy.wait()


def closing(dlat, gather, kv, query, small, dtok):
    width = small.shape[1]
    wide_rows, cols = gather.shape[2:]
    share = query.shape[0]
    rows = dtok.shape[0]
    sds = lambda *shape: jax.ShapeDtypeStruct(shape, F32)
    return pl.pallas_call(
        closing_kernel,
        name="closing",
        out_shape=(
            sds(*dlat.shape),
            sds(rows, width),
            sds(width, 2 * cols),
            sds(width, width),
            sds(width, width),
            sds(2 * cols, width),
            sds(share, width),
            sds(share, width),
            sds(share),
            sds(width),
            sds(share),
            sds(2 * cols),
            sds(share),
        ),
        in_specs=[anywhere()] * 3 + [vmem()] * 2 + [anywhere()],
        out_specs=(anywhere(),) * 6 + (vmem(),) * 7,
        scratch_shapes=[
            pltpu.VMEM((2, wide_rows, cols), F32),
            pltpu.VMEM((2, wide_rows, cols), F32),
            pltpu.VMEM(dlat.shape, F32),
            pltpu.VMEM(kv.shape, F32),
            pltpu.VMEM(dtok.shape, F32),
            pltpu.VMEM((2 * cols, width), F32),
            pltpu.SemaphoreType.DMA((5,)),
            pltpu.SemaphoreType.DMA((7,)),
        ],
        compiler_params=pltpu.CompilerParams(vmem_limit_bytes=VMEM_BYTES),
    )(dlat, gather, kv, query, small, dtok)


def local(
    latents,
    tokens,
    token_sample,
    token_mask,
    drop_mask,
    gain_query,
    w_query,
    gain_token,
    w_key,
    w_value,
    w_out,
    gain_mlp,
    w_up,
    b_up,
    w_down,
    b_down,
    cotangent,
):
    samples, lat_rows, width = latents.shape
    part, keys, values, tsort, query, normed, place, bounds = attend_forward(
        token_sample, token_mask, tokens, latents, gain_query, w_query, gain_token, w_key, w_value
    )
    msg, result, dmid, a, b, side, vec = latent_block(
        part, drop_mask, latents, cotangent, w_out, gain_mlp, w_up, b_up, w_down, b_down
    )
    dkv, dlat, dgain_q, dwq, result = attend_backward(
        bounds, latents, keys, values, query, normed, msg, dmid, gain_query, w_query, result
    )
    dlat, gather, kv, dwq, small, d_tokens = gradients(
        dlat, a, b, side, dwq, vec, dgain_q, place, tokens, tsort, dkv, gain_token,
        w_key, w_value,
    )
    (
        d_latents,
        d_tokens,
        grad_up,
        grad_key,
        grad_value,
        grad_down,
        grad_out,
        grad_query,
        grad_gquery,
        grad_gtoken,
        grad_gmlp,
        grad_bup,
        grad_bdown,
    ) = closing(
        dlat.reshape(samples * lat_rows, width),
        gather,
        kv.reshape(2, width, width),
        dwq.reshape(-1, width),
        small,
        d_tokens,
    )
    return (
        result.reshape(latents.shape),
        d_latents.reshape(latents.shape),
        d_tokens,
        grad_gquery,
        grad_query.T,
        grad_gtoken,
        grad_key,
        grad_value,
        grad_out.T,
        grad_gmlp,
        grad_up,
        grad_bup,
        grad_down,
        grad_bdown,
    )


def solution(mesh):
    return jax.shard_map(
        local,
        mesh=mesh,
        in_specs=(
            P("stream", None, None),
            P(("stream", "tok"), None),
            P(("stream", "tok")),
            P(("stream", "tok")),
            P(),
            P(),
            P(),
            P(),
            P(),
            P(),
            P(),
            P(),
            P(),
            P(),
            P(),
            P(),
            P("stream", None, None),
        ),
        out_specs=(
            P("stream", None, None),
            P("stream", None, None),
            P(("stream", "tok"), None),
            P("stream"),
            P(None, "stream"),
            P(),
            P(),
            P(),
            P(None, "stream"),
            P("stream"),
            P(None, "stream"),
            P("stream"),
            P("stream", None),
            P("stream"),
        ),
        check_vma=False,
    )
```

```python
import functools

import jax
import jax.numpy as jnp
from jax import lax
from jax.experimental import pallas as pl
from jax.experimental.pallas import tpu as pltpu
from jax.sharding import PartitionSpec as P

HEADS = 12
HEAD_DIM = 64
PAIRS = HEADS // 2
PIECES = 4
PIECE_HEADS = HEADS // PIECES
NUM_ROWS = PIECE_HEADS * HEAD_DIM
PIECE_ROWS = NUM_ROWS + 16
MSG_ROWS = HEADS * HEAD_DIM + 32
BLOCK = 256
FWD_BLOCK = 128
PAD = 256
LAG = 2
ZROWS = 32
LINE_LAG = 2
GAP = 6
SUBS = 3
EARLY_SUBS = 1
SPREAD_LAG = 4
WIDE_START_TICKS = (1, 2, 2, 4)
KV_TICKS = (0, 3)
PAIR_TICK = 5
MORE_TICK = 16
ONE_TICK = 15
TWO_TICK = 20
WIDE_ONE_TICKS = (10, 27, 30)
WIDE_TWO_TICKS = (16, 32, 35)
WIDE_THREE_TICKS = (25, -1, -1)
LAT_TICKS = (0, 4, 8)
TOKEN_TICKS = (6, 7, 8, 9, 11, 12, 13, 16)
NEG = -1e30
F32 = jnp.float32
BF16 = jnp.bfloat16
VMEM_BYTES = 60 * 1024 * 1024


def norm_parts(values):
    center = values - jnp.mean(values, -1, keepdims=True)
    spread = jnp.mean(center * center, -1, keepdims=True)
    inv = lax.rsqrt(spread + 1e-05)
    return center * inv, inv


def norm_back(unit, inv, gain, grad):
    scaled = grad * gain
    inner = scaled - jnp.mean(scaled, -1, keepdims=True)
    return inv * (inner - unit * jnp.mean(scaled * unit, -1, keepdims=True))


def dot(a, b, contract=(1, 0)):
    return lax.dot_general(
        a, b, (((contract[0],), (contract[1],)), ((), ())), preferred_element_type=F32
    )


def row(ref):
    return ref[...].reshape(1, ref.shape[0])


def piece_of(head):
    return head // PIECE_HEADS, head % PIECE_HEADS


def forward_kernel(
    sample_ref,
    mask_ref,
    tok_hbm,
    lat_hbm,
    gain_q_ref,
    wq_hbm,
    gain_t_ref,
    wk_hbm,
    wv_hbm,
    part_out,
    key_out,
    val_out,
    tsort_out,
    query_out,
    normed_out,
    place_ref,
    bounds_ref,
    tnorm_ref,
    pos_ref,
    top_ref,
    den_ref,
    num_ref,
    tok_ref,
    lat_ref,
    wq_ref,
    wk_ref,
    wv_ref,
    part_ref,
    key_ref,
    val_ref,
    tsort_ref,
    query_ref,
    normed_ref,
    load_sem,
    store_sem,
    sample_sem,
):
    loads = [
        pltpu.make_async_copy(src, dst, load_sem.at[i])
        for i, (src, dst) in enumerate(
            (
                (tok_hbm, tok_ref),
                (wk_hbm, wk_ref),
                (wv_hbm, wv_ref),
                (lat_hbm, lat_ref),
                (wq_hbm, wq_ref),
            )
        )
    ]
    for n in (0, 3, 4, 1, 2):
        loads[n].start()
    stores = [
        pltpu.make_async_copy(src, dst, store_sem.at[i])
        for i, (src, dst) in enumerate(
            ((key_ref, key_out), (val_ref, val_out), (tsort_ref, tsort_out))
        )
    ]
    samples = part_ref.shape[0]

    def sample_stores(s):
        at = pl.ds(pl.multiple_of(s * 128, 128), 128)
        return [
            pltpu.make_async_copy(src, dst, sample_sem.at[i, s])
            for i, (src, dst) in enumerate(
                (
                    (part_ref.at[s], part_out.at[s]),
                    (query_ref.at[s], query_out.at[s]),
                    (normed_ref.at[at], normed_out.at[at]),
                )
            )
        ]

    rows = tok_ref.shape[0]
    width = tok_ref.shape[1]
    lat_rows = 128
    step = 256

    named = row(sample_ref) - lax.axis_index("stream") * samples
    ids = jnp.where(row(mask_ref) == 1, named, -1)
    lane = lax.broadcasted_iota(jnp.int32, (samples, rows), 1)
    member = ids == lax.broadcasted_iota(jnp.int32, (samples, rows), 0)
    ones = jnp.where(member, 1.0, 0.0)
    count = ones
    shift = 1
    while shift < rows:
        count = count + jnp.where(lane >= shift, pltpu.roll(count, shift, 1), 0.0)
        shift *= 2
    rank = count - ones
    begin = jnp.int32(0)
    pos = jnp.full((1, rows), -1.0, F32)
    for s in range(samples):
        total = jnp.sum(ones[s : s + 1]).astype(jnp.int32)
        bounds_ref[s] = begin
        bounds_ref[samples + s] = total
        pos = jnp.where(member[s : s + 1], rank[s : s + 1] + begin.astype(F32), pos)
        begin = begin + total
    pos_ref[...] = jnp.broadcast_to(pos, (8, rows))
    place_ref[...] = jnp.broadcast_to(pos, (128, rows)).T

    def token_norm(i, carry):
        at = pl.ds(pl.multiple_of(i * step, step), step)
        unit, _ = norm_parts(tok_ref[at, :].astype(F32))
        tnorm_ref[at, :] = (unit * row(gain_t_ref)).astype(BF16)
        return carry

    def lat_norm(i, carry):
        at = pl.ds(pl.multiple_of(i * step, step), step)
        unit, _ = norm_parts(lat_ref[at, :].astype(F32))
        normed = (unit * row(gain_q_ref)).astype(BF16)
        normed_ref[at, :] = normed
        turned = (dot(normed, wq_ref[...]) * 0.125).T.astype(BF16)
        blank = jnp.zeros((HEAD_DIM, lat_rows), BF16)
        for n in range(step // lat_rows):
            s = i * (step // lat_rows) + n
            span = slice(n * lat_rows, (n + 1) * lat_rows)
            for p in range(PAIRS):
                lo = 2 * p * HEAD_DIM
                mid, hi = lo + HEAD_DIM, lo + 2 * HEAD_DIM
                query_ref[s, p, :HEAD_DIM, :lat_rows] = turned[lo:mid, span]
                query_ref[s, p, :HEAD_DIM, lat_rows:] = blank
                query_ref[s, p, HEAD_DIM:, :lat_rows] = blank
                query_ref[s, p, HEAD_DIM:, lat_rows:] = turned[mid:hi, span]
        return carry

    def both_norm(i, carry):
        return token_norm(i, lat_norm(i, carry))

    loads[0].wait()
    loads[3].wait()
    loads[4].wait()
    if rows == samples * lat_rows:
        lax.fori_loop(0, rows // step, both_norm, 0)
    else:
        lax.fori_loop(0, rows // step, token_norm, 0)
        lax.fori_loop(0, samples * lat_rows // step, lat_norm, 0)
    loads[1].wait()
    loads[2].wait()

    def token_sort(i, carry):
        at = pl.ds(pl.multiple_of(i * step, step), step)
        target = lax.broadcasted_iota(jnp.int32, (step, rows), 0) + i * step
        chosen = target.astype(F32) == pos_ref[0:1, :]
        pick = jnp.where(chosen, 1.0, 0.0).astype(BF16)
        tsort = dot(pick, tnorm_ref[...]).astype(BF16)
        tsort_ref[at, :] = tsort
        key_ref[at, :] = dot(tsort, wk_ref[...]).astype(BF16)
        val_ref[at, :] = dot(tsort, wv_ref[...]).astype(BF16)
        return carry

    lax.fori_loop(0, rows // step, token_sort, 0)
    key_ref[rows:, :] = jnp.zeros((PAD, width), BF16)
    val_ref[rows:, :] = jnp.zeros((PAD, width), BF16)
    for copy in stores:
        copy.start()

    def sample_step(s, carry):
        start = bounds_ref[s]
        total = bounds_ref[samples + s]
        base = lax.div(start, 16) * 16
        blocks = jnp.where(total > 0, lax.div(start + total - base + FWD_BLOCK - 1, FWD_BLOCK), 0)
        for piece in range(PIECES):
            part_ref[s, piece, NUM_ROWS:, :] = jnp.zeros((16, lat_rows), F32)
        num_ref[...] = jnp.zeros_like(num_ref)
        top_ref[...] = jnp.full_like(top_ref, NEG)
        den_ref[...] = jnp.zeros_like(den_ref)

        def block_step(b, carry):
            row = pl.multiple_of(base + b * FWD_BLOCK, 16)
            index = lax.broadcasted_iota(jnp.int32, (FWD_BLOCK, 2 * lat_rows), 0) + row
            inside = (index >= start) & (index < start + total)
            for p in range(PAIRS):
                cols = slice(p * 128, (p + 1) * 128)
                score = dot(key_ref[pl.ds(row, FWD_BLOCK), cols], query_ref[s, p])
                score = jnp.where(inside, score, NEG)
                old = top_ref[p : p + 1, :]
                new = jnp.maximum(old, jnp.max(score, 0, keepdims=True))
                fade = jnp.exp(old - new)
                weight = jnp.exp(score - new)
                top_ref[p : p + 1, :] = new
                den_ref[p : p + 1, :] = den_ref[p : p + 1, :] * fade + jnp.sum(
                    weight, 0, keepdims=True
                )
                both = dot(val_ref[pl.ds(row, FWD_BLOCK), cols], weight.astype(BF16), (0, 0))
                for half in range(2):
                    at_rows = slice(p * 128 + half * HEAD_DIM, p * 128 + (half + 1) * HEAD_DIM)
                    at_cols = slice(half * lat_rows, (half + 1) * lat_rows)
                    num_ref[at_rows, :] = (
                        num_ref[at_rows, :] * fade[:, at_cols]
                        + both[half * HEAD_DIM : (half + 1) * HEAD_DIM, at_cols]
                    )
            return carry

        lax.fori_loop(0, blocks, block_step, 0)
        for h in range(HEADS):
            piece, i = piece_of(h)
            p, half = h // 2, h % 2
            at_cols = slice(half * lat_rows, (half + 1) * lat_rows)
            part_ref[s, piece, i * HEAD_DIM : (i + 1) * HEAD_DIM, :] = num_ref[
                h * HEAD_DIM : (h + 1) * HEAD_DIM, :
            ]
            part_ref[s, piece, NUM_ROWS + i : NUM_ROWS + i + 1, :] = top_ref[p : p + 1, at_cols]
            part_ref[s, piece, NUM_ROWS + 8 + i : NUM_ROWS + 9 + i, :] = den_ref[
                p : p + 1, at_cols
            ]
        for copy in sample_stores(s):
            copy.start()
        return carry

    lax.fori_loop(0, samples, sample_step, 0)
    for copy in stores:
        copy.wait()

    def finish(s, carry):
        for copy in sample_stores(s):
            copy.wait()
        return carry

    lax.fori_loop(0, samples, finish, 0)


def vmem():
    return pl.BlockSpec(memory_space=pltpu.VMEM)


def anywhere():
    return pl.BlockSpec(memory_space=pl.ANY)


def smem():
    return pl.BlockSpec(memory_space=pltpu.SMEM)


def attend_forward(sample, mask, tokens, latents, gain_q, wq, gain_t, wk, wv):
    samples, lat_rows, width = latents.shape
    rows = tokens.shape[0]
    sds = jax.ShapeDtypeStruct
    return pl.pallas_call(
        forward_kernel,
        name="attend_forward",
        out_shape=(
            sds((samples, PIECES, PIECE_ROWS, lat_rows), F32),
            sds((rows + PAD, width), BF16),
            sds((rows + PAD, width), BF16),
            sds((rows, width), BF16),
            sds((samples, PAIRS, 128, 2 * lat_rows), BF16),
            sds((samples * lat_rows, width), BF16),
            sds((rows, 128), F32),
            sds((2 * samples,), jnp.int32),
        ),
        in_specs=[vmem()] * 2
        + [anywhere()] * 2
        + [vmem(), anywhere(), vmem()]
        + [anywhere()] * 2,
        out_specs=(anywhere(),) * 6 + (vmem(), smem()),
        scratch_shapes=[
            pltpu.VMEM((rows, width), BF16),
            pltpu.VMEM((8, rows), F32),
            pltpu.VMEM((8, 2 * lat_rows), F32),
            pltpu.VMEM((8, 2 * lat_rows), F32),
            pltpu.VMEM((width, lat_rows), F32),
            pltpu.VMEM((rows, width), BF16),
            pltpu.VMEM((samples * lat_rows, width), BF16),
            pltpu.VMEM((width, width), BF16),
            pltpu.VMEM((width, width), BF16),
            pltpu.VMEM((width, width), BF16),
            pltpu.VMEM((samples, PIECES, PIECE_ROWS, lat_rows), F32),
            pltpu.VMEM((rows + PAD, width), BF16),
            pltpu.VMEM((rows + PAD, width), BF16),
            pltpu.VMEM((rows, width), BF16),
            pltpu.VMEM((samples, PAIRS, 128, 2 * lat_rows), BF16),
            pltpu.VMEM((samples * lat_rows, width), BF16),
            pltpu.SemaphoreType.DMA((5,)),
            pltpu.SemaphoreType.DMA((3,)),
            pltpu.SemaphoreType.DMA((3, samples)),
        ],
        compiler_params=pltpu.CompilerParams(vmem_limit_bytes=VMEM_BYTES),
    )(
        sample,
        mask,
        tokens,
        latents.reshape(samples * lat_rows, width),
        gain_q,
        wq,
        gain_t,
        wk,
        wv,
    )


def backward_kernel(
    bounds_ref,
    key_hbm,
    val_hbm,
    query_hbm,
    normed_hbm,
    msg_hbm,
    gain_q_ref,
    wq_hbm,
    res_hbm,
    dkv_out,
    dquery_out,
    dgain_ref,
    dwq_out,
    res_out,
    dk_ref,
    dv_ref,
    grad_ref,
    dquery_ref,
    turn_ref,
    stat_ref,
    res_ref,
    res_sems,
    key_ref,
    val_ref,
    query_ref,
    normed_ref,
    msg_ref,
    wq_ref,
    dkv_ref,
    dwq_ref,
    load_sem,
    sample_sem,
    dlat_sem,
    store_sem,
):
    samples = query_ref.shape[0]
    rows = dkv_ref.shape[1]
    lat_rows = 128
    step = 256
    width = dwq_ref.shape[0]
    for r in range(0, rows + PAD, step):
        dk_ref[r : r + step, :] = jnp.zeros((step, dk_ref.shape[1]), F32)
        dv_ref[r : r + step, :] = jnp.zeros((step, dv_ref.shape[1]), F32)
    loads = [
        pltpu.make_async_copy(src, dst, load_sem.at[i])
        for i, (src, dst) in enumerate(
            (
                (key_hbm, key_ref),
                (val_hbm, val_ref),
                (wq_hbm, wq_ref),
                (normed_hbm, normed_ref),
            )
        )
    ]

    def sample_loads(s):
        return [
            pltpu.make_async_copy(msg_hbm.at[s], msg_ref.at[s], sample_sem.at[0, s]),
            pltpu.make_async_copy(query_hbm.at[s], query_ref.at[s], sample_sem.at[1, s]),
        ]

    def dquery_store(s):
        at = pl.ds(pl.multiple_of(s * 128, 128), 128)
        return pltpu.make_async_copy(dquery_ref.at[at], dquery_out.at[at], dlat_sem.at[s])

    for copy in loads[:2] + sample_loads(0):
        copy.start()

    def start_sample(s, carry):
        for copy in sample_loads(s):
            copy.start()
        return carry

    lax.fori_loop(1, query_ref.shape[0], start_sample, 0)
    loads[2].start()
    loads[3].start()
    res_load = pltpu.make_async_copy(res_hbm, res_ref, res_sems.at[0])
    res_store = pltpu.make_async_copy(res_ref, res_out, res_sems.at[1])
    res_load.start()
    grad_ref[...] = jnp.zeros_like(grad_ref)
    dgain_ref[...] = jnp.zeros_like(dgain_ref)

    loads[0].wait()
    loads[1].wait()

    def sample_step(s, carry):
        for copy in sample_loads(s):
            copy.wait()
        start = bounds_ref[s]
        total = bounds_ref[samples + s]
        base = lax.div(start, 16) * 16
        blocks = jnp.where(total > 0, lax.div(start + total - base + BLOCK - 1, BLOCK), 0)
        turn_ref[...] = jnp.zeros_like(turn_ref)
        for h in range(HEADS):
            p, half = h // 2, h % 2
            grad_ref[
                p,
                half * HEAD_DIM : (half + 1) * HEAD_DIM,
                half * lat_rows : (half + 1) * lat_rows,
            ] = msg_ref[s, h * HEAD_DIM : (h + 1) * HEAD_DIM, :].astype(BF16)

            stat_ref[p : p + 1, half * lat_rows : (half + 1) * lat_rows] = msg_ref[
                s, width + h : width + h + 1, :
            ]
            stat_ref[8 + p : 9 + p, half * lat_rows : (half + 1) * lat_rows] = msg_ref[
                s, width + 16 + h : width + 17 + h, :
            ]

        def block_step(b, carry):
            row = pl.multiple_of(base + b * BLOCK, 16)
            index = lax.broadcasted_iota(jnp.int32, (BLOCK, 2 * lat_rows), 0) + row
            inside = (index >= start) & (index < start + total)
            at = pl.ds(row, BLOCK)
            for p in range(PAIRS):
                cols = slice(p * 128, (p + 1) * 128)
                key = key_ref[at, cols]
                query = query_ref[s, p]
                grad = grad_ref[p]
                score = dot(key, query)
                weight = jnp.where(inside, jnp.exp(score - stat_ref[p : p + 1, :]), 0.0)
                dprob = dot(val_ref[at, cols], grad)
                dscore = (weight * (dprob - stat_ref[8 + p : 9 + p, :])).astype(BF16)
                dv_ref[at, cols] += dot(weight.astype(BF16), grad, (1, 1))
                dk_ref[at, cols] += dot(dscore, query, (1, 1))
                both = dot(key, dscore, (0, 0))
                for half in range(2):
                    turn_ref[
                        p * 128 + half * HEAD_DIM : p * 128 + (half + 1) * HEAD_DIM, :
                    ] += both[
                        half * HEAD_DIM : (half + 1) * HEAD_DIM,
                        half * lat_rows : (half + 1) * lat_rows,
                    ]
            return carry

        lax.fori_loop(0, blocks, block_step, 0)
        at = pl.ds(pl.multiple_of(s * lat_rows, lat_rows), lat_rows)
        dquery = (turn_ref[...].T * 0.125).astype(BF16)
        dquery_ref[at, :] = dquery
        dquery_store(s).start()
        return carry

    lax.fori_loop(0, samples, sample_step, 0)
    res_load.wait()
    res_store.start()
    for r in range(0, rows, step):
        dkv_ref[0, r : r + step, :] = dk_ref[r : r + step, :].astype(BF16)
        dkv_ref[1, r : r + step, :] = dv_ref[r : r + step, :].astype(BF16)
    dkv_store = pltpu.make_async_copy(dkv_ref, dkv_out, store_sem.at[0])
    dkv_store.start()
    loads[2].wait()
    loads[3].wait()
    gain = jnp.zeros((1, width), F32)
    stores = []
    for c in range(0, width, 256):
        dwq_ref[c : c + 256, :] = dot(dquery_ref[:, c : c + 256], normed_ref[...], (0, 0))
        copy = pltpu.make_async_copy(
            dwq_ref.at[pl.ds(c, 256)], dwq_out.at[pl.ds(c, 256)], store_sem.at[1 + c // 256]
        )
        copy.start()
        stores.append(copy)
        weight = wq_ref[:, c : c + 256].astype(F32).T
        gain += jnp.sum(weight * dwq_ref[c : c + 256, :], 0, keepdims=True)
    dgain_ref[0:1, :] = gain / row(gain_q_ref)
    res_store.wait()
    dkv_store.wait()
    for copy in stores:
        copy.wait()

    def finish(s, carry):
        dquery_store(s).wait()
        return carry

    lax.fori_loop(0, samples, finish, 0)


def attend_backward(bounds, keys, values, query, normed, msg, gain_q, wq, result):
    samples, _, lat_rows = msg.shape
    width = wq.shape[0]
    rows = keys.shape[0] - PAD
    sds = jax.ShapeDtypeStruct
    return pl.pallas_call(
        backward_kernel,
        name="attend_backward",
        out_shape=(
            sds((2, rows, width), BF16),
            sds((samples * lat_rows, width), BF16),
            sds((8, width), F32),
            sds((width, width), F32),
            sds(result.shape, BF16),
        ),
        in_specs=[smem()] + [anywhere()] * 5 + [vmem()] + [anywhere()] * 2,
        out_specs=(anywhere(),) * 2 + (vmem(),) + (anywhere(),) * 2,
        scratch_shapes=[
            pltpu.VMEM((rows + PAD, width), F32),
            pltpu.VMEM((rows + PAD, width), F32),
            pltpu.VMEM((PAIRS, 128, 2 * lat_rows), BF16),
            pltpu.VMEM((samples * lat_rows, width), BF16),
            pltpu.VMEM((width, lat_rows), F32),
            pltpu.VMEM((16, 2 * lat_rows), F32),
            pltpu.VMEM(result.shape, BF16),
            pltpu.SemaphoreType.DMA((2,)),
            pltpu.VMEM((rows + PAD, width), BF16),
            pltpu.VMEM((rows + PAD, width), BF16),
            pltpu.VMEM(query.shape, BF16),
            pltpu.VMEM(normed.shape, BF16),
            pltpu.VMEM(msg.shape, F32),
            pltpu.VMEM(wq.shape, BF16),
            pltpu.VMEM((2, rows, width), BF16),
            pltpu.VMEM((width, width), F32),
            pltpu.SemaphoreType.DMA((4,)),
            pltpu.SemaphoreType.DMA((2, samples)),
            pltpu.SemaphoreType.DMA((samples,)),
            pltpu.SemaphoreType.DMA((1 + width // 256,)),
        ],
        compiler_params=pltpu.CompilerParams(vmem_limit_bytes=VMEM_BYTES),
    )(
        bounds,
        keys,
        values,
        query,
        normed,
        msg,
        gain_q,
        wq,
        result,
    )


MESH = pl.DeviceIdType.MESH


def merge(a_ref, b_ref, out_ref):
    a_tail, b_tail = a_ref[NUM_ROWS : NUM_ROWS + 8, :], b_ref[NUM_ROWS : NUM_ROWS + 8, :]
    top = jnp.maximum(a_tail, b_tail)
    a_fade, b_fade = jnp.exp(a_tail - top), jnp.exp(b_tail - top)
    den = a_ref[NUM_ROWS + 8 :, :] * a_fade + b_ref[NUM_ROWS + 8 :, :] * b_fade
    for i in range(PIECE_HEADS):
        at = slice(i * HEAD_DIM, (i + 1) * HEAD_DIM)
        out_ref[at, :] = (
            a_ref[at, :] * a_fade[i : i + 1, :] + b_ref[at, :] * b_fade[i : i + 1, :]
        )
    out_ref[NUM_ROWS : NUM_ROWS + 8, :] = top
    out_ref[NUM_ROWS + 8 :, :] = den


def gelu_parts(x):
    c = 0.7978845608028654
    square = x * x
    t = jnp.tanh(c * x * (1.0 + 0.044715 * square))
    half = 0.5 * (1.0 + t)
    slope = half + (0.5 * c) * x * (1.0 - t * t) * (1.0 + (3 * 0.044715) * square)
    return x * half, slope


def latent_kernel(
    part_hbm,
    drop_ref,
    lat_hbm,
    cot_hbm,
    wo_hbm,
    gain_ref,
    wup_hbm,
    bup_ref,
    wdn_hbm,
    bdn_ref,
    msg_out,
    res_all,
    dmid_out,
    a_out,
    b_out,
    side_ref,
    vec_ref,
    lat_ref,
    cot_ref,
    msg_ref,
    res_ref,
    dmid_ref,
    a_ref,
    b_ref,
    store_sem,
    wo_ref,
    wup_ref,
    wdn_ref,
    pair_ref,
    own_ref,
    right_in,
    right_out,
    left_in,
    left_out,
    res_out,
    res_in,
    att_t_ref,
    mid_ref,
    acc_ref,
    dacc_ref,
    hn_ref,
    dm_ref,
    da_ref,
    att_ref,
    hn_out,
    hn_in,
    half_out,
    half_in,
    side_all,
    side_in,
    hn_send,
    hn_recv,
    half_send,
    half_recv,
    side_send,
    side_recv,
    own_sem,
    weight_sem,
    pair_send,
    pair_recv,
    right_send,
    right_recv,
    left_send,
    left_recv,
    msg_send,
    msg_recv,
    res_send,
    res_recv,
):
    samples = msg_out.shape[0]
    half = samples // 2
    lat_rows = 128
    width = lat_ref.shape[1]
    chunks = half * PIECES
    stream = lax.axis_index("stream")
    tok = lax.axis_index("tok")
    chips = lax.axis_size("tok") // 2
    core = lax.rem(tok, 2)
    chip = lax.div(tok, 2)
    parity = lax.rem(chip, 2)
    other = 1 - core
    partner = (stream, tok + 1 - 2 * core)
    right = (stream, tok + 2)
    left = (stream, tok - 2)
    has_right = chip < chips - 1
    has_left = chip > 0
    on_first = core == 0

    barrier = pltpu.get_barrier_semaphore()
    pl.semaphore_signal(barrier, inc=1, device_id=partner, device_id_type=MESH)

    @pl.when(has_right)
    def _():
        pl.semaphore_signal(barrier, inc=1, device_id=right, device_id_type=MESH)

    @pl.when(has_left)
    def _():
        pl.semaphore_signal(barrier, inc=1, device_id=left, device_id_type=MESH)

    own_load = pltpu.make_async_copy(
        part_hbm.at[pl.ds(core * chunks, chunks)], own_ref, own_sem
    )
    own_load.start()
    weights = [
        pltpu.make_async_copy(src, dst, weight_sem.at[i])
        for i, (src, dst) in enumerate(
            (
                (lat_hbm, lat_ref),
                (cot_hbm, cot_ref),
                (wo_hbm, wo_ref),
                (wup_hbm, wup_ref),
                (wdn_hbm, wdn_ref),
            )
        )
    ]
    for copy in weights:
        copy.start()
    pl.semaphore_wait(
        barrier, 1 + has_right.astype(jnp.int32) + has_left.astype(jnp.int32)
    )

    def pair_copy(i):
        return pltpu.make_async_remote_copy(
            src_ref=part_hbm.at[(1 - core) * chunks + i],
            dst_ref=pair_ref.at[i],
            send_sem=pair_send.at[i],
            recv_sem=pair_recv.at[i],
            device_id=partner,
            device_id_type=MESH,
        )

    def right_copy(i):
        return pltpu.make_async_remote_copy(
            src_ref=right_out.at[i],
            dst_ref=right_in.at[i],
            send_sem=right_send.at[i],
            recv_sem=right_recv.at[i],
            device_id=right,
            device_id_type=MESH,
        )

    def left_copy(i):
        return pltpu.make_async_remote_copy(
            src_ref=left_out.at[i],
            dst_ref=left_in.at[i],
            send_sem=left_send.at[i],
            recv_sem=left_recv.at[i],
            device_id=left,
            device_id_type=MESH,
        )

    def stores(j, far):
        at = (other if far else core) * half + j
        rows = pl.ds(pl.multiple_of(at * lat_rows, lat_rows), lat_rows)
        mine = pl.ds(pl.multiple_of(j * lat_rows, lat_rows), lat_rows)
        pairs = [
            (res_ref.at[rows], res_all.at[rows]),
            (a_ref.at[rows], a_out.at[rows]),
            (b_ref.at[:, rows], b_out.at[:, rows]),
        ]
        if not far:
            pairs.append((msg_ref.at[j], msg_out.at[at]))
            pairs.append((dmid_ref.at[mine], dmid_out.at[mine]))
        return [
            pltpu.make_async_copy(src, dst, store_sem.at[far, i, j])
            for i, (src, dst) in enumerate(pairs)
        ]

    def msg_copy(j):
        at = core * half + j
        return pltpu.make_async_remote_copy(
            src_ref=msg_ref.at[j],
            dst_ref=msg_out.at[at],
            send_sem=msg_send.at[j],
            recv_sem=msg_recv.at[j],
            device_id=partner,
            device_id_type=MESH,
        )

    def msg_arrival(j):
        return pltpu.make_async_remote_copy(
            src_ref=msg_ref.at[j],
            dst_ref=msg_out.at[other * half + j],
            send_sem=msg_send.at[j],
            recv_sem=msg_recv.at[j],
            device_id=partner,
            device_id_type=MESH,
        )

    def res_copy(j):
        return pltpu.make_async_remote_copy(
            src_ref=res_out.at[j],
            dst_ref=res_in.at[j],
            send_sem=res_send.at[j],
            recv_sem=res_recv.at[j],
            device_id=partner,
            device_id_type=MESH,
        )

    def hn_copy(j):
        return pltpu.make_async_remote_copy(
            src_ref=hn_out.at[j],
            dst_ref=hn_in.at[j],
            send_sem=hn_send.at[j],
            recv_sem=hn_recv.at[j],
            device_id=partner,
            device_id_type=MESH,
        )

    def half_copy(i):
        return pltpu.make_async_remote_copy(
            src_ref=half_out.at[i],
            dst_ref=half_in.at[i],
            send_sem=half_send.at[i],
            recv_sem=half_recv.at[i],
            device_id=partner,
            device_id_type=MESH,
        )

    side_copy = pltpu.make_async_remote_copy(
        src_ref=side_all.at[:, 1 - core],
        dst_ref=side_in,
        send_sem=side_send,
        recv_sem=side_recv,
        device_id=partner,
        device_id_type=MESH,
    )

    def start_pair(i, carry):
        pair_copy(i).start()
        return carry

    lax.fori_loop(0, chunks, start_pair, 0)
    own_load.wait()

    drop = row(drop_ref).astype(F32)
    scale_all = drop * drop.shape[1] / jnp.sum(drop, 1, keepdims=True)
    drop_lane = lax.broadcasted_iota(jnp.int32, drop.shape, 1)
    vec_ref[...] = jnp.zeros_like(vec_ref)

    def take(j):
        at = other * half + j
        rows = pl.ds(pl.multiple_of(at * lat_rows, lat_rows), lat_rows)
        for q in range(PIECES):
            half_copy(j * PIECES + q).wait_recv()
            b_ref[q, rows, :] = half_in[j * PIECES + q].astype(BF16)
        res_copy(j).wait_recv()
        res_ref[rows, :] = res_in[j].astype(BF16)

        @pl.when(on_first)
        def _():
            hn_copy(j).wait_recv()
            a_ref[rows, :] = hn_in[j].astype(BF16)

        @pl.when(jnp.logical_not(on_first))
        def _():
            scale = jnp.sum(
                jnp.where(drop_lane == stream * samples + at, scale_all, 0.0), 1, keepdims=True
            )
            a_ref[rows, :] = (scale * cot_ref[rows, :].astype(F32)).astype(BF16)

        for copy in stores(j, 1):
            copy.start()

    def mlp(j, q):
        sample = core * half + j
        rows = pl.ds(pl.multiple_of(sample * lat_rows, lat_rows), lat_rows)
        mine = pl.ds(pl.multiple_of(j * lat_rows, lat_rows), lat_rows)
        scale = jnp.sum(
            jnp.where(drop_lane == stream * samples + sample, scale_all, 0.0), 1, keepdims=True
        )

        @pl.when(q == 0)
        def _():
            for h in range(HEADS):
                piece, i = piece_of(h)
                at = j * PIECES + piece
                den = own_ref[at, NUM_ROWS + 8 + i : NUM_ROWS + 9 + i, :]
                att_t_ref[h * HEAD_DIM : (h + 1) * HEAD_DIM, :] = own_ref[
                    at, i * HEAD_DIM : (i + 1) * HEAD_DIM, :
                ] * (1.0 / den)
            att = att_t_ref[...].T.astype(BF16)
            att_ref[mine, :] = jnp.where(parity == 0, att[:, : width // 2], att[:, width // 2 :])
            mid = lat_ref[rows, :].astype(F32) + scale * dot(att, wo_ref[...])
            mid_ref[...] = mid
            unit, _ = norm_parts(mid)
            hn = (unit * row(gain_ref)).astype(BF16)
            dm = (scale * cot_ref[rows, :].astype(F32)).astype(BF16)
            hn_ref[...] = hn
            dm_ref[...] = dm
            a_ref[rows, :] = jnp.where(on_first, hn, dm)

            @pl.when(jnp.logical_not(on_first))
            def _():
                hn_out[j] = hn.astype(F32)
                hn_copy(j).start()

            vec_ref[1:2, :width] += jnp.sum(dm.astype(F32), 0, keepdims=True)
            acc_ref[...] = jnp.broadcast_to(row(bdn_ref), acc_ref.shape)
            dacc_ref[...] = jnp.zeros_like(dacc_ref)

        span = wup_ref.shape[1] // PIECES
        cols = pl.ds(pl.multiple_of(q * span, 128), span)
        pre = dot(hn_ref[...], wup_ref[:, cols]) + bup_ref[cols].reshape(1, span)
        active, slope = gelu_parts(pre)
        hidden = active.astype(BF16)
        acc_ref[...] += dot(hidden, wdn_ref[cols, :])
        dpre = (slope * dot(dm_ref[...], wdn_ref[cols, :], (1, 1))).astype(BF16)
        piece = j * PIECES + q
        near_half = lambda x: jnp.where(parity == 0, x[:, : span // 2], x[:, span // 2 :])
        hidden_half, dpre_half = near_half(hidden), near_half(dpre)
        b_ref[q, rows, :] = jnp.where(on_first, dpre_half, hidden_half)
        half_out[piece] = jnp.where(on_first, hidden_half, dpre_half).astype(F32)
        half_copy(piece).start()
        vec_ref[0:1, cols] += jnp.sum(dpre.astype(F32), 0, keepdims=True)
        dacc_ref[...] += dot(dpre, wup_ref[:, cols], (1, 1))

        @pl.when(q == PIECES - 1)
        def _():
            mid = mid_ref[...]
            res = (mid + scale * acc_ref[...]).astype(BF16)
            res_ref[rows, :] = res
            res_out[j] = res.astype(F32)
            res_copy(j).start()
            unit, inv = norm_parts(mid)
            dhn = dacc_ref[...]
            vec_ref[2:3, :width] += jnp.sum(dhn * unit, 0, keepdims=True)
            dmid = cot_ref[rows, :].astype(F32) + norm_back(unit, inv, row(gain_ref), dhn)
            dmid_ref[mine, :] = dmid
            da = (scale * dmid).astype(BF16)
            da_ref[mine, :] = da
            datt_t = dot(wo_ref[...], da, (1, 1)).astype(BF16).astype(F32)
            msg_ref[j, width:, :] = jnp.zeros((MSG_ROWS - width, lat_rows), F32)
            for h in range(HEADS):
                piece, i = piece_of(h)
                at = j * PIECES + piece
                inverse = 1.0 / own_ref[at, NUM_ROWS + 8 + i : NUM_ROWS + 9 + i, :]
                span_h = slice(h * HEAD_DIM, (h + 1) * HEAD_DIM)
                one = datt_t[span_h]
                msg_ref[j, span_h, :] = (one * inverse).astype(BF16).astype(F32)
                delta = jnp.sum(one * att_t_ref[span_h, :], 0, keepdims=True) * inverse
                msg_ref[j, width + h : width + h + 1, :] = own_ref[
                    at, NUM_ROWS + i : NUM_ROWS + i + 1, :
                ]
                msg_ref[j, width + 16 + h : width + 17 + h, :] = delta
            msg_copy(j).start()
            for copy in stores(j, 0):
                copy.start()

            @pl.when(j > 0)
            def _():
                take(j - 1)

    def step(t, carry):
        @pl.when(t < chunks)
        def _():
            pair_copy(t).wait_recv()
            merge(own_ref.at[t], pair_ref.at[t], own_ref.at[t])

        r = t - LAG * chip

        @pl.when((r >= 0) & (r < chunks))
        def _():
            @pl.when(has_left)
            def _():
                right_copy(r).wait_recv()
                merge(own_ref.at[r], right_in.at[r], right_out.at[r])

            @pl.when(jnp.logical_not(has_left))
            def _():
                right_out[r] = own_ref[r]

            @pl.when(has_right)
            def _():
                right_copy(r).start()

        u = t - LAG * (chips - 1 - chip)

        @pl.when((u >= 0) & (u < chunks))
        def _():
            @pl.when(has_right)
            def _():
                left_copy(u).wait_recv()

            @pl.when(has_left)
            def _():
                @pl.when(has_right)
                def _():
                    merge(own_ref.at[u], left_in.at[u], left_out.at[u])

                @pl.when(jnp.logical_not(has_right))
                def _():
                    left_out[u] = own_ref[u]

                left_copy(u).start()

        w = t - LAG * jnp.maximum(chip, chips - 1 - chip)

        @pl.when((w >= 0) & (w < chunks))
        def _():
            @pl.when(has_right)
            def _():
                merge(right_out.at[w], left_in.at[w], own_ref.at[w])

            @pl.when(jnp.logical_not(has_right))
            def _():
                own_ref[w] = right_out[w]

        m = w - (PIECES - 1)

        @pl.when(m == 0)
        def _():
            for copy in weights:
                copy.wait()

        @pl.when((m >= 0) & (m < chunks))
        def _():
            mlp(lax.div(m, PIECES), lax.rem(m, PIECES))

        return carry

    lax.fori_loop(0, chunks + LAG * (chips - 1) + PIECES - 1, step, 0)

    share = width // 8
    for block in range(4):
        at = slice(block * 2 * share, (block + 1) * 2 * share)
        product = dot(da_ref[:, at], att_ref[...], (0, 0))
        side_all[block, 0] = product[:share]
        side_all[block, 1] = product[share:]
    side_copy.start()

    take(half - 1)

    def finish_chunk(i, carry):
        pair_copy(i).wait_send()
        half_copy(i).wait_send()

        @pl.when(has_right)
        def _():
            right_copy(i).wait_send()

        @pl.when(has_left)
        def _():
            left_copy(i).wait_send()

        return carry

    lax.fori_loop(0, chunks, finish_chunk, 0)

    def finish_sample(j, carry):
        @pl.when(jnp.logical_not(on_first))
        def _():
            hn_copy(j).wait_send()

        res_copy(j).wait_send()
        msg_copy(j).wait_send()
        msg_arrival(j).wait_recv()
        for copy in stores(j, 0) + stores(j, 1):
            copy.wait()
        return carry

    lax.fori_loop(0, half, finish_sample, 0)
    side_copy.wait()
    side_ref[...] = side_all[:, core] + side_in[...]


def latent_block(part, drop_mask, latents, cotangent, wo, gain, wup, bup, wdn, bdn):
    samples, lat_rows, width = latents.shape
    half = samples // 2
    chunks = half * PIECES
    hidden = wup.shape[1]
    sds = jax.ShapeDtypeStruct
    chunk = lambda: pltpu.VMEM((chunks, PIECE_ROWS, lat_rows), F32)
    dma = pltpu.SemaphoreType.DMA
    return pl.pallas_call(
        latent_kernel,
        name="latent_block",
        out_shape=(
            sds((samples, MSG_ROWS, lat_rows), F32),
            sds((samples * lat_rows, width), BF16),
            sds((half * lat_rows, width), F32),
            sds((samples * lat_rows, width), BF16),
            sds((PIECES, samples * lat_rows, hidden // PIECES // 2), BF16),
            sds((4, width // 8, width // 2), F32),
            sds((8, hidden), F32),
        ),
        in_specs=[
            anywhere(),
            vmem(),
            anywhere(),
            anywhere(),
            anywhere(),
            vmem(),
            anywhere(),
            vmem(),
            anywhere(),
            vmem(),
        ],
        out_specs=(anywhere(),) * 5 + (vmem(),) * 2,
        scratch_shapes=[
            pltpu.VMEM((samples * lat_rows, width), BF16),
            pltpu.VMEM((samples * lat_rows, width), BF16),
            pltpu.VMEM((half, MSG_ROWS, lat_rows), F32),
            pltpu.VMEM((samples * lat_rows, width), BF16),
            pltpu.VMEM((half * lat_rows, width), F32),
            pltpu.VMEM((samples * lat_rows, width), BF16),
            pltpu.VMEM((PIECES, samples * lat_rows, hidden // PIECES // 2), BF16),
            dma((2, 5, half)),
            pltpu.VMEM(wo.shape, BF16),
            pltpu.VMEM(wup.shape, BF16),
            pltpu.VMEM(wdn.shape, BF16),
            chunk(),
            chunk(),
            chunk(),
            chunk(),
            chunk(),
            chunk(),
            pltpu.VMEM((half, lat_rows, width), F32),
            pltpu.VMEM((half, lat_rows, width), F32),
            pltpu.VMEM((width, lat_rows), F32),
            pltpu.VMEM((lat_rows, width), F32),
            pltpu.VMEM((lat_rows, width), F32),
            pltpu.VMEM((lat_rows, width), F32),
            pltpu.VMEM((lat_rows, width), BF16),
            pltpu.VMEM((lat_rows, width), BF16),
            pltpu.VMEM((half * lat_rows, width), BF16),
            pltpu.VMEM((half * lat_rows, width // 2), BF16),
            pltpu.VMEM((half, lat_rows, width), F32),
            pltpu.VMEM((half, lat_rows, width), F32),
            pltpu.VMEM((chunks, lat_rows, hidden // PIECES // 2), F32),
            pltpu.VMEM((chunks, lat_rows, hidden // PIECES // 2), F32),
            pltpu.VMEM((4, 2, width // 8, width // 2), F32),
            pltpu.VMEM((4, width // 8, width // 2), F32),
            dma((half,)),
            dma((half,)),
            dma((chunks,)),
            dma((chunks,)),
            dma,
            dma,
            dma,
            dma((5,)),
            dma((chunks,)),
            dma((chunks,)),
            dma((chunks,)),
            dma((chunks,)),
            dma((chunks,)),
            dma((chunks,)),
            dma((half,)),
            dma((half,)),
            dma((half,)),
            dma((half,)),
        ],
        compiler_params=pltpu.CompilerParams(
            vmem_limit_bytes=VMEM_BYTES, collective_id=1, has_side_effects=True
        ),
    )(
        part.reshape(samples * PIECES, PIECE_ROWS, lat_rows),
        drop_mask,
        latents.reshape(samples * lat_rows, width),
        cotangent.reshape(samples * lat_rows, width),
        wo,
        gain,
        wup,
        bup,
        wdn,
        bdn,
    )


def gradient_kernel(
    dquery_hbm,
    dmid_hbm,
    lat_hbm,
    gain_q_ref,
    wq_hbm,
    a_hbm,
    b_hbm,
    side_ref,
    dwq_hbm,
    vec_ref,
    dgain_q_ref,
    place_ref,
    tok_hbm,
    tsort_hbm,
    dkv_hbm,
    gain_t_ref,
    wk_ref,
    wv_ref,
    dlat_out,
    gather_out,
    kv_out,
    query_out,
    small_out,
    dtok_out,
    line_ref,
    right_ref,
    left_ref,
    dmine_ref,
    wide_ref,
    wide_one,
    wide_two,
    send_ref,
    mine_ref,
    pair_ref,
    one_ref,
    two_ref,
    small_ref,
    gain_ref,
    wide_far,
    spread_ref,
    stage_ref,
    stage_sem,
    dsend_ref,
    dquery_ref,
    lat_ref,
    wq_ref,
    a_ref,
    b_ref,
    dwq_ref,
    tok_ref,
    tsort_ref,
    dkv_ref,
    load_sem,
    dpair_send,
    dpair_recv,
    right_send,
    right_recv,
    left_send,
    left_recv,
    back_send,
    back_recv,
    back_local,
    wide_one_send,
    wide_one_recv,
    wide_two_send,
    wide_two_recv,
    wide_z_send,
    wide_z_recv,
    wide_core_send,
    wide_core_recv,
    wide_local,
    pair_send,
    pair_recv,
    one_send,
    one_recv,
    two_send,
    two_recv,
    spread_send,
    spread_recv,
    share_send,
    share_recv,
    query_send,
    query_recv,
    query_local,
    keep_local,
):
    rows, width = tok_ref.shape
    lat_chunks = dmine_ref.shape[0]
    all_chunks = line_ref.shape[0]
    kv_rows = send_ref.shape[2]
    q_rows = query_out.shape[2]
    mix = kv_rows + q_rows
    half_chunks = (all_chunks - lat_chunks) // 2
    kv_chunks = kv_rows // ZROWS
    wide_half = wide_ref.shape[1] // 2
    sub_rows = wide_half // SUBS

    stream = lax.axis_index("stream")
    tok = lax.axis_index("tok")
    chips = lax.axis_size("tok") // 2
    core = lax.rem(tok, 2)
    chip = lax.div(tok, 2)
    other = 1 - core
    parity = lax.rem(chip, 2)
    flip_x = stream + 1 - 2 * lax.rem(stream, 2)
    flip_y = lax.rem(stream + 2, 4)
    flip_xy = 3 - stream
    partner = (stream, tok + 1 - 2 * core)
    right = (stream, tok + 2)
    left = (stream, tok - 2)
    beside = (stream, tok + 2 - 4 * parity)
    near = ((flip_x, tok), (flip_y, tok))
    first = (flip_x, flip_y)
    has_right = chip < chips - 1
    has_left = chip > 0
    here = (chip == 0).astype(F32)

    barrier = pltpu.get_barrier_semaphore()
    for target in (partner,) + near:
        pl.semaphore_signal(barrier, inc=1, device_id=target, device_id_type=MESH)

    @pl.when(has_right)
    def _():
        pl.semaphore_signal(barrier, inc=1, device_id=right, device_id_type=MESH)

    @pl.when(has_left)
    def _():
        pl.semaphore_signal(barrier, inc=1, device_id=left, device_id_type=MESH)

    def remote(src, dst, send, recv, target):
        return pltpu.make_async_remote_copy(
            src_ref=src,
            dst_ref=dst,
            send_sem=send,
            recv_sem=recv,
            device_id=target,
            device_id_type=MESH,
        )

    pulls = [
        pltpu.make_async_copy(src, dst, load_sem.at[i])
        for i, (src, dst) in enumerate(
            (
                (tsort_hbm, tsort_ref),
                (dkv_hbm, dkv_ref),
                (dmid_hbm, dmine_ref),
                (a_hbm, a_ref),
                (b_hbm, b_ref),
                (dwq_hbm, dwq_ref),
                (tok_hbm, tok_ref),
                (dquery_hbm, dquery_ref),
                (lat_hbm, lat_ref),
                (wq_hbm, wq_ref),
            )
        )
    ]
    for n in (7, 8, 9, 2, 0, 1, 5, 3, 4, 6):
        pulls[n].start()
    pl.semaphore_wait(barrier, 3 + has_right.astype(jnp.int32) + has_left.astype(jnp.int32))

    def dpair_copy(i):
        return remote(
            dsend_ref.at[i], line_ref.at[i], dpair_send.at[i], dpair_recv.at[i], partner
        )

    lat_rows = 128
    per_sample = lat_rows // ZROWS

    def lat_gradient(which, j):
        sample = which * (lat_chunks // per_sample) + j
        at = pl.ds(pl.multiple_of(sample * lat_rows, lat_rows), lat_rows)
        unit, inv = norm_parts(lat_ref[at, :].astype(F32))
        dnormed = dot(dquery_ref[at, :], wq_ref[...], (1, 1))
        return norm_back(unit, inv, row(gain_q_ref), dnormed)

    def lat_event(j):
        grad = lat_gradient(other, j)
        for c in range(per_sample):
            dsend_ref[j * per_sample + c] = grad[c * ZROWS : (c + 1) * ZROWS]
            dpair_copy(j * per_sample + c).start()
        grad = lat_gradient(core, j)
        for c in range(per_sample):
            i = j * per_sample + c
            dmine_ref[i] = grad[c * ZROWS : (c + 1) * ZROWS] + dmine_ref[i] * here

    def wide_one_copy(h, n, sub):
        block = (first[h], flip_xy)[n]
        at = pl.ds(h * wide_half + sub * sub_rows, sub_rows)
        return remote(
            wide_ref.at[block, at],
            wide_one.at[h, n, pl.ds(sub * sub_rows, sub_rows)],
            wide_one_send.at[h, n, sub],
            wide_one_recv.at[h, n, sub],
            near[h],
        )

    def wide_at(block, h, sub):
        return wide_ref.at[block, pl.ds(h * wide_half + sub * sub_rows, sub_rows)]

    def wide_two_copy(h, sub):
        at = pl.ds(sub * sub_rows, sub_rows)
        return remote(
            wide_at(first[1 - h], h, sub),
            wide_two.at[h, at],
            wide_two_send.at[h, sub],
            wide_two_recv.at[h, sub],
            near[1 - h],
        )

    def gather_at(c, e, h, sub):
        return gather_out.at[c, e, pl.ds(h * wide_half + sub * sub_rows, sub_rows)]

    def far_at(h, sub):
        return wide_far.at[pl.ds(h * wide_half + sub * sub_rows, sub_rows)]

    def wide_z_copy(h, sub):
        return remote(
            wide_at(stream, h, sub),
            far_at(h, sub),
            wide_z_send.at[h, sub],
            wide_z_recv.at[h, sub],
            beside,
        )

    def wide_core_copy(far, h, sub):
        if far:
            src = far_at(h, sub)
            dst = gather_at(core, 1 - parity, h, sub)
        else:
            src = wide_at(stream, h, sub)
            dst = gather_at(core, parity, h, sub)
        return remote(
            src, dst, wide_core_send.at[far, h, sub], wide_core_recv.at[far, h, sub], partner
        )

    def wide_core_arrival(far, h, sub):
        place = gather_at(other, 1 - parity if far else parity, h, sub)
        return remote(
            place, place, wide_core_send.at[far, h, sub], wide_core_recv.at[far, h, sub], partner
        )

    def wide_keep(far, h, sub):
        return pltpu.make_async_copy(
            far_at(h, sub) if far else wide_at(stream, h, sub),
            gather_at(core, 1 - parity if far else parity, h, sub),
            wide_local.at[far, h, sub],
        )

    def wide_product(block):
        wide_ref[block, :width, :] = dot(a_ref[...], b_ref[block], (0, 0))
        wide_ref[block, width:, :] = side_ref[block]

    def wide_start(k):
        if k == 0:
            pulls[3].wait()
            pulls[4].wait()
        wide_product((flip_xy, first[0], first[1], stream)[k])
        for sub in range(EARLY_SUBS):
            for h in range(2):
                if k == 0:
                    wide_one_copy(h, 1, sub).start()
                elif k == 1 + h:
                    wide_one_copy(h, 0, sub).start()

    def wide_more():
        for sub in range(EARLY_SUBS, SUBS):
            for h in range(2):
                for n in range(2):
                    wide_one_copy(h, 1 - n, sub).start()

    def wide_event_one(sub):
        at = slice(sub * sub_rows, (sub + 1) * sub_rows)
        for h in range(2):
            for n in range(2):
                wide_one_copy(h, n, sub).wait_recv()
            span = pl.ds(h * wide_half + sub * sub_rows, sub_rows)
            wide_ref[first[1 - h], span, :] += wide_one[h, 1, at, :]
            wide_two_copy(h, sub).start()
            wide_ref[stream, span, :] += wide_one[h, 0, at, :]

    def wide_event_two(sub):
        at = slice(sub * sub_rows, (sub + 1) * sub_rows)
        for h in range(2):
            wide_two_copy(h, sub).wait_recv()
            span = pl.ds(h * wide_half + sub * sub_rows, sub_rows)
            wide_ref[stream, span, :] += wide_two[h, at, :]
            wide_z_copy(h, sub).start()
            wide_core_copy(0, h, sub).start()
            wide_keep(0, h, sub).start()

    def wide_event_three(sub):
        for h in range(2):
            wide_z_copy(h, sub).wait_recv()
            wide_core_copy(1, h, sub).start()
            wide_keep(1, h, sub).start()

    share = width // 4

    def gain_part(which, block, product):
        at = slice(block * share, (block + 1) * share)
        weight = jnp.where(which == 0, wk_ref[at, :], wv_ref[at, :]).astype(F32)
        gain_ref[at, 0:1] += jnp.sum(product * weight, 1, keepdims=True)

    def token_product(block, which):
        at = slice(block * share, (block + 1) * share)
        return dot(tsort_ref[:, at], dkv_ref[which], (0, 0))

    def token_other():
        for n in (0, 1, 5):
            pulls[n].wait()
        gain_ref[...] = jnp.zeros_like(gain_ref)
        for block in range(4):
            product = token_product(block, other)
            for h in range(2):
                send_ref[h, block] = product[h * kv_rows : (h + 1) * kv_rows]
            gain_part(other, block, product)
        for k, h, what in pairs:
            if what < 2:
                pair_copy(k, h, what).start()

    order = (flip_xy, first[0], first[1], stream)

    def pair_copy(k, h, what):
        block = order[k]
        src, at, size = (
            (send_ref.at[h, block], 0, kv_rows),
            (dwq_ref.at[block, other, h], kv_rows, q_rows),
            (small_ref.at[block], mix, 16),
        )[what]
        return remote(
            src,
            pair_ref.at[h, block, pl.ds(at, size)],
            pair_send.at[k, h, what],
            pair_recv.at[k, h, what],
            partner,
        )

    pairs = [(k, h, what) for k in range(4) for h in range(2) for what in range(3 - h)]

    def token_own():
        for block in range(4):
            product = token_product(block, core)
            for h in range(2):
                piece = product[h * kv_rows : (h + 1) * kv_rows]
                mine_ref[h, block, :kv_rows, :] = piece
                mine_ref[h, block, kv_rows:mix, :] = dwq_ref[block, core, h]
            gain_part(core, block, product)
        mine_ref[1, :, mix:, :] = jnp.zeros((4, 16, width), F32)
        small_ref[...] = jnp.zeros_like(small_ref)
        gain = jnp.broadcast_to(gain_ref[:, 0:1], gain_ref.shape).T[0:1, :] / row(gain_t_ref)
        for block in range(4):
            small_ref[block, 0:1, :] = vec_ref[0:1, block * width : (block + 1) * width] * here
            small_ref[block, 1:2, :] = dgain_q_ref[0:1, :]
            small_ref[block, 2:3, :] = vec_ref[2:3, :width] * here
            small_ref[block, 3:4, :] = vec_ref[1:2, :width] * here
            small_ref[block, 4:5, :] = gain
        for k in range(4):
            pair_copy(k, 0, 2).start()

    token_step = 128

    def stage_copy(i):
        return pltpu.make_async_copy(
            stage_ref.at[i % 2],
            dtok_out.at[pl.ds(i * token_step, token_step)],
            stage_sem.at[i % 2],
        )

    def token_part(i):
        if i == 0:
            pulls[6].wait()
        at = pl.ds(pl.multiple_of(i * token_step, token_step), token_step)
        target = lax.broadcasted_iota(jnp.int32, (token_step, rows), 1).astype(F32)
        pick = jnp.where(target == place_ref[at, 0:1], 1.0, 0.0).astype(BF16)
        dkey = dot(pick, dkv_ref[0]).astype(BF16)
        dval = dot(pick, dkv_ref[1]).astype(BF16)
        dnormed = dot(dkey, wk_ref[...], (1, 1)) + dot(dval, wv_ref[...], (1, 1))
        unit, inv = norm_parts(tok_ref[at, :].astype(F32))
        if i >= 2:
            stage_copy(i - 2).wait()
        stage_ref[i % 2] = norm_back(unit, inv, row(gain_t_ref), dnormed)
        stage_copy(i).start()

    def one_copy(h, n):
        block = (first[h], flip_xy)[n]
        return remote(
            mine_ref.at[h, block], one_ref.at[h, n], one_send.at[h, n], one_recv.at[h, n], near[h]
        )

    def two_copy(h):
        return remote(
            mine_ref.at[h, first[1 - h]], two_ref.at[h], two_send.at[h], two_recv.at[h], near[1 - h]
        )

    def pair_event():
        for k in range(4):
            block = order[k]
            for h in range(2):
                for what in range(3 - h):
                    pair_copy(k, h, what).wait_recv()
                mine_ref[h, block, :mix, :] += pair_ref[h, block, :mix, :]
                if h == 0:
                    mine_ref[h, block, mix:, :] = small_ref[block] + pair_ref[h, block, mix:, :]
                if k == 0:
                    one_copy(h, 1).start()
                elif k == 1 + h:
                    one_copy(h, 0).start()

    def one_event():
        for h in range(2):
            for n in range(2):
                one_copy(h, n).wait_recv()
            mine_ref[h, first[1 - h]] += one_ref[h, 1]
            two_copy(h).start()

    def two_event():
        for h in range(2):
            two_copy(h).wait_recv()
            total = mine_ref[h, stream] + one_ref[h, 0] + two_ref[h]
            for k in range(half_chunks):
                line_ref[lat_chunks + h * half_chunks + k] = total[k * ZROWS : (k + 1) * ZROWS]

    def right_copy(i):
        return remote(right_ref.at[i], right_ref.at[i], right_send.at[i], right_recv.at[i], right)

    def left_copy(i):
        return remote(left_ref.at[i], left_ref.at[i], left_send.at[i], left_recv.at[i], left)

    def back_copy(i):
        return remote(
            line_ref.at[i], dlat_out.at[core, i], back_send.at[i], back_recv.at[i], partner
        )

    def back_arrival(i):
        return remote(
            line_ref.at[i], dlat_out.at[other, i], back_send.at[i], back_recv.at[i], partner
        )

    def back_keep(i):
        return pltpu.make_async_copy(line_ref.at[i], dlat_out.at[core, i], back_local.at[i])

    def placed(t):
        late = t >= lat_chunks + GAP
        index = jnp.where(late, t - GAP, t)
        return index, (t >= 0) & (late | (t < lat_chunks)) & (index < all_chunks)

    def line_step(t):
        @pl.when(t < lat_chunks)
        def _():
            dpair_copy(t).wait_recv()
            line_ref[t] += dmine_ref[t]

        r, r_due = placed(t - LINE_LAG * chip)

        @pl.when(r_due)
        def _():
            @pl.when(has_left)
            def _():
                right_copy(r).wait_recv()
                right_ref[r] += line_ref[r]

            @pl.when(jnp.logical_not(has_left))
            def _():
                right_ref[r] = line_ref[r]

            @pl.when(has_right)
            def _():
                right_copy(r).start()

        u, u_due = placed(t - LINE_LAG * (chips - 1 - chip))

        @pl.when(u_due)
        def _():
            @pl.when(has_right)
            def _():
                left_copy(u).wait_recv()
                left_ref[u] += line_ref[u]

            @pl.when(jnp.logical_not(has_right))
            def _():
                left_ref[u] = line_ref[u]

            @pl.when(has_left)
            def _():
                left_copy(u).start()

        w, w_due = placed(t - LINE_LAG * jnp.maximum(chip, chips - 1 - chip))

        @pl.when(w_due)
        def _():
            line_ref[w] = right_ref[w] + left_ref[w] - line_ref[w]

            @pl.when(w < lat_chunks)
            def _():
                back_copy(w).start()
                back_keep(w).start()

    def spot(i):
        k = i - lat_chunks
        h = lax.div(k, half_chunks)
        return h, lax.rem(k, half_chunks)

    def by_half(h, pair):
        return jnp.where(h == 0, pair[0], pair[1])

    def block_of(h, k):
        return (stream, by_half(h, (flip_y, flip_x)), by_half(h, first), flip_xy)[k]

    def spread_src(i, k):
        h, c = spot(i)
        return line_ref.at[i] if k == 0 else spread_ref.at[k - 1, h, c]

    def spread_copy(i, k):
        h, c = spot(i)
        target = by_half(h, (flip_y, flip_x)) if k == 1 else by_half(h, first)
        return remote(
            spread_src(i, 1 if k == 3 else 0),
            spread_ref.at[k - 1, h, c],
            spread_send.at[k - 1, i - lat_chunks],
            spread_recv.at[k - 1, i - lat_chunks],
            (target, tok),
        )

    def share_copy(i, k):
        h, c = spot(i)
        return remote(
            spread_src(i, k),
            kv_out.at[core, block_of(h, k), h, c],
            share_send.at[k, i - lat_chunks],
            share_recv.at[k, i - lat_chunks],
            partner,
        )

    def share_arrival(i, k):
        h, c = spot(i)
        place = kv_out.at[other, block_of(h, k), h, c]
        return remote(
            place,
            place,
            share_send.at[k, i - lat_chunks],
            share_recv.at[k, i - lat_chunks],
            partner,
        )

    def kv_keep(i, k):
        h, c = spot(i)
        return pltpu.make_async_copy(
            spread_src(i, k),
            kv_out.at[core, block_of(h, k), h, c],
            keep_local.at[k, i - lat_chunks],
        )

    def spread_due(t):
        i, due = placed(t)
        i = jnp.maximum(i, lat_chunks)
        _, c = spot(i)
        return i, due & (t >= lat_chunks + GAP) & (c < kv_chunks)

    def spread_step(t):
        lag = LINE_LAG * jnp.maximum(chip, chips - 1 - chip)
        i, due = spread_due(t - lag)

        @pl.when(due)
        def _():
            spread_copy(i, 1).start()
            spread_copy(i, 2).start()
            share_copy(i, 0).start()
            kv_keep(i, 0).start()

        j, due_one = spread_due(t - lag - SPREAD_LAG)

        @pl.when(due_one)
        def _():
            spread_copy(j, 1).wait_recv()
            spread_copy(j, 3).start()
            share_copy(j, 1).start()
            kv_keep(j, 1).start()

        m, due_two = spread_due(t - lag - 2 * SPREAD_LAG)

        @pl.when(due_two)
        def _():
            for k in (2, 3):
                spread_copy(m, k).wait_recv()
                share_copy(m, k).start()
                kv_keep(m, k).start()

    def query_piece(h):
        return mine_ref.at[h, stream, pl.ds(kv_rows, q_rows)]

    def query_copy(h):
        return remote(
            query_piece(h),
            query_out.at[core, h],
            query_send.at[h],
            query_recv.at[h],
            partner,
        )

    def query_arrival(h):
        return remote(
            query_piece(h),
            query_out.at[other, h],
            query_send.at[h],
            query_recv.at[h],
            partner,
        )

    def query_keep(h):
        return pltpu.make_async_copy(query_piece(h), query_out.at[core, h], query_local.at[h])

    def query_event(h):
        flat = lat_chunks + h * half_chunks + kv_chunks
        for k in range(0, q_rows, 16):
            at = flat * ZROWS + k
            chunk, row = at // ZROWS, at % ZROWS
            mine_ref[h, stream, kv_rows + k : kv_rows + k + 16, :] = line_ref[
                chunk, row : row + 16, :
            ]
        query_copy(h).start()
        query_keep(h).start()
        if h == 0:
            at = flat * ZROWS + q_rows
            chunk, row = at // ZROWS, at % ZROWS
            small_out[...] = line_ref[chunk, row : row + 16, :]

    tail = LINE_LAG * (chips - 1)
    ready = lambda h: lat_chunks + GAP + (h + 1) * half_chunks - 1 + tail
    events = {}

    def at_tick(tick, run):
        events.setdefault(tick, []).append(run)

    parts = rows // token_step
    for i in range(parts):
        at_tick(TOKEN_TICKS[i % len(TOKEN_TICKS)], functools.partial(token_part, i))
    for k in range(4):
        at_tick(WIDE_START_TICKS[k], functools.partial(wide_start, k))
    at_tick(KV_TICKS[0], token_other)
    at_tick(KV_TICKS[1], token_own)
    at_tick(PAIR_TICK, pair_event)
    at_tick(MORE_TICK, wide_more)
    at_tick(ONE_TICK, one_event)
    at_tick(TWO_TICK, two_event)
    for sub in range(SUBS):
        at_tick(WIDE_ONE_TICKS[sub], functools.partial(wide_event_one, sub))
        at_tick(WIDE_TWO_TICKS[sub], functools.partial(wide_event_two, sub))
        if WIDE_THREE_TICKS[sub] >= 0:
            at_tick(WIDE_THREE_TICKS[sub], functools.partial(wide_event_three, sub))
    for n in (7, 8, 9, 2):
        pulls[n].wait()
    lat_event(0)
    for j in range(1, lat_chunks // per_sample):
        at_tick(LAT_TICKS[j - 1], functools.partial(lat_event, j))

    def step(t, carry):
        line_step(t)
        spread_step(t)
        for tick in sorted(events):

            @pl.when(t == tick)
            def _(tick=tick):
                for run in events[tick]:
                    run()

        return carry

    lax.fori_loop(0, ready(1) + 2 * SPREAD_LAG + 1, step, 0)
    for h in range(2):
        query_event(h)
    for sub in range(SUBS):
        if WIDE_THREE_TICKS[sub] < 0:
            wide_event_three(sub)

    def finish_lat(i, carry):
        dpair_copy(i).wait_send()
        back_copy(i).wait_send()
        back_arrival(i).wait_recv()
        back_keep(i).wait()
        return carry

    lax.fori_loop(0, lat_chunks, finish_lat, 0)

    def finish_line(i, carry):
        @pl.when(has_right)
        def _():
            right_copy(i).wait_send()

        @pl.when(has_left)
        def _():
            left_copy(i).wait_send()

        return carry

    lax.fori_loop(0, all_chunks, finish_line, 0)

    def finish_spread(n, carry):
        h = lax.div(n, kv_chunks)
        i = lat_chunks + h * half_chunks + lax.rem(n, kv_chunks)
        for k in range(4):
            if k:
                spread_copy(i, k).wait_send()
            share_copy(i, k).wait_send()
            share_arrival(i, k).wait_recv()
            kv_keep(i, k).wait()
        return carry

    lax.fori_loop(0, 2 * kv_chunks, finish_spread, 0)
    for i in range(parts - 2, parts):
        stage_copy(i).wait()
    for k, h, what in pairs:
        pair_copy(k, h, what).wait_send()
    for h in range(2):
        for n in range(2):
            one_copy(h, n).wait_send()
        two_copy(h).wait_send()
        query_copy(h).wait_send()
        query_arrival(h).wait_recv()
        query_keep(h).wait()
        for sub in range(SUBS):
            for n in range(2):
                wide_one_copy(h, n, sub).wait_send()
                wide_core_copy(n, h, sub).wait_send()
                wide_core_arrival(n, h, sub).wait_recv()
            wide_two_copy(h, sub).wait_send()
            wide_z_copy(h, sub).wait_send()
            wide_keep(0, h, sub).wait()
            wide_keep(1, h, sub).wait()


def gradients(
    dquery, dmid, latents, gain_q, wq, a, b, side, dwq, vec, dgain_q, place, tokens, tsort, dkv,
    gain_t, wk, wv,
):
    rows, width = tokens.shape
    half = dquery.shape[0] // 2
    lat_chunks = half // ZROWS
    wide_rows, wide_cols = a.shape[1] + side.shape[1], b.shape[2]
    share = width // 4
    kv_rows, q_rows = share // 2, share // 4
    block = kv_rows + q_rows + 16
    all_chunks = lat_chunks + 2 * block // ZROWS
    sds = jax.ShapeDtypeStruct
    dma = pltpu.SemaphoreType.DMA
    buf = lambda *shape: pltpu.VMEM(shape, F32)
    both = lambda *shape: [dma(shape), dma(shape)]
    return pl.pallas_call(
        gradient_kernel,
        name="gradients",
        out_shape=(
            sds((2, lat_chunks, ZROWS, width), F32),
            sds((2, 2, wide_rows, wide_cols), F32),
            sds((2, 4, 2, kv_rows // ZROWS, ZROWS, width), F32),
            sds((2, 2, q_rows, width), F32),
            sds((16, width), F32),
            sds((rows, width), F32),
        ),
        in_specs=[anywhere()] * 3
        + [vmem()]
        + [anywhere()] * 3
        + [vmem(), anywhere()]
        + [vmem()] * 3
        + [anywhere()] * 3
        + [vmem()] * 3,
        out_specs=(anywhere(),) * 4 + (vmem(), anywhere()),
        scratch_shapes=[
            buf(all_chunks, ZROWS, width),
            buf(all_chunks, ZROWS, width),
            buf(all_chunks, ZROWS, width),
            buf(lat_chunks, ZROWS, width),
            buf(4, wide_rows, wide_cols),
            buf(2, 2, wide_rows // 2, wide_cols),
            buf(2, wide_rows // 2, wide_cols),
            buf(2, 4, kv_rows, width),
            buf(2, 4, block, width),
            buf(2, 4, block, width),
            buf(2, 2, block, width),
            buf(2, block, width),
            buf(4, 16, width),
            buf(width, 128),
            buf(wide_rows, wide_cols),
            buf(3, 2, kv_rows // ZROWS, ZROWS, width),
            buf(2, 128, width),
            dma((2,)),
            buf(lat_chunks, ZROWS, width),
            pltpu.VMEM(dquery.shape, BF16),
            pltpu.VMEM(dquery.shape, BF16),
            pltpu.VMEM(wq.shape, BF16),
            pltpu.VMEM(a.shape, BF16),
            pltpu.VMEM(b.shape, BF16),
            buf(4, 2, 2, q_rows, width),
            pltpu.VMEM(tokens.shape, BF16),
            pltpu.VMEM(tsort.shape, BF16),
            pltpu.VMEM(dkv.shape, BF16),
            dma((10,)),
        ]
        + both(lat_chunks)
        + both(all_chunks)
        + both(all_chunks)
        + both(lat_chunks)
        + [dma((lat_chunks,))]
        + both(2, 2, SUBS)
        + both(2, SUBS)
        + both(2, SUBS)
        + both(2, 2, SUBS)
        + [dma((2, 2, SUBS))]
        + both(4, 2, 3)
        + both(2, 2)
        + both(2)
        + both(3, all_chunks - lat_chunks)
        + both(4, all_chunks - lat_chunks)
        + both(2)
        + [dma((2,)), dma((4, all_chunks - lat_chunks))],
        compiler_params=pltpu.CompilerParams(
            vmem_limit_bytes=VMEM_BYTES, collective_id=2, has_side_effects=True
        ),
    )(
        dquery,
        dmid.reshape(lat_chunks, ZROWS, width),
        latents.reshape(2 * half, width),
        gain_q,
        wq,
        a,
        b,
        side,
        dwq.reshape(4, 2, 2, q_rows, width),
        vec,
        dgain_q,
        place,
        tokens,
        tsort,
        dkv,
        gain_t,
        wk,
        wv,
    )


def closing_kernel(
    dlat_hbm,
    gather_hbm,
    kv_hbm,
    query_ref,
    small_ref,
    dtok_hbm,
    dlat_out,
    dtok_out,
    up_out,
    key_out,
    val_out,
    down_out,
    out_ref,
    wq_ref,
    gain_q_ref,
    gain_t_ref,
    gain_mlp_ref,
    bup_ref,
    bdn_ref,
    wide_ref,
    up_ref,
    dlat_ref,
    kv_ref,
    dtok_ref,
    down_ref,
    load_sems,
    store_sems,
):
    width = small_ref.shape[1]
    cols = wide_ref.shape[2]
    loads = [
        pltpu.make_async_copy(src, dst, load_sems.at[i])
        for i, (src, dst) in enumerate(
            (
                (gather_hbm.at[1], wide_ref),
                (gather_hbm.at[0], up_ref),
                (dlat_hbm, dlat_ref),
                (kv_hbm, kv_ref),
                (dtok_hbm, dtok_ref),
            )
        )
    ]
    for copy in loads:
        copy.start()
    stores = [
        pltpu.make_async_copy(src, dst, store_sems.at[i])
        for i, (src, dst) in enumerate(
            (
                (up_ref.at[0, pl.ds(0, width)], up_out.at[:, pl.ds(0, cols)]),
                (up_ref.at[1, pl.ds(0, width)], up_out.at[:, pl.ds(cols, cols)]),
                (dlat_ref, dlat_out),
                (kv_ref.at[0], key_out),
                (kv_ref.at[1], val_out),
                (dtok_ref, dtok_out),
                (down_ref, down_out),
            )
        )
    ]
    stream = lax.axis_index("stream")
    gain_t_ref[...] = small_ref[4]
    bup_ref[...] = small_ref[0]
    size = gain_q_ref.shape[0]
    for i, ref in ((1, gain_q_ref), (2, gain_mlp_ref), (3, bdn_ref)):
        line = small_ref[i : i + 1, :]
        piece = line[:, :size]
        for k in range(1, width // size):
            piece = jnp.where(stream == k, line[:, k * size : (k + 1) * size], piece)
        ref[...] = piece[0]
    wq_ref[...] = query_ref[...]
    loads[0].wait()
    for e in range(2):
        down_ref[e * cols : (e + 1) * cols, :] = wide_ref[e, :width, :].T
    stores[6].start()
    loads[1].wait()
    stores[0].start()
    stores[1].start()
    half = up_ref.shape[1] - width
    for e in range(2):
        out_ref[:half, e * cols : (e + 1) * cols] = up_ref[e, width:, :]
        out_ref[half:, e * cols : (e + 1) * cols] = wide_ref[e, width:, :]
    loads[2].wait()
    stores[2].start()
    loads[3].wait()
    stores[3].start()
    stores[4].start()
    loads[4].wait()
    stores[5].start()
    for copy in stores:
        copy.wait()


def closing(dlat, gather, kv, query, small, dtok):
    width = small.shape[1]
    wide_rows, cols = gather.shape[2:]
    share = query.shape[0]
    rows = dtok.shape[0]
    sds = lambda *shape: jax.ShapeDtypeStruct(shape, F32)
    return pl.pallas_call(
        closing_kernel,
        name="closing",
        out_shape=(
            sds(*dlat.shape),
            sds(rows, width),
            sds(width, 2 * cols),
            sds(width, width),
            sds(width, width),
            sds(2 * cols, width),
            sds(share, width),
            sds(share, width),
            sds(share),
            sds(width),
            sds(share),
            sds(2 * cols),
            sds(share),
        ),
        in_specs=[anywhere()] * 3 + [vmem()] * 2 + [anywhere()],
        out_specs=(anywhere(),) * 6 + (vmem(),) * 7,
        scratch_shapes=[
            pltpu.VMEM((2, wide_rows, cols), F32),
            pltpu.VMEM((2, wide_rows, cols), F32),
            pltpu.VMEM(dlat.shape, F32),
            pltpu.VMEM(kv.shape, F32),
            pltpu.VMEM(dtok.shape, F32),
            pltpu.VMEM((2 * cols, width), F32),
            pltpu.SemaphoreType.DMA((5,)),
            pltpu.SemaphoreType.DMA((7,)),
        ],
        compiler_params=pltpu.CompilerParams(vmem_limit_bytes=VMEM_BYTES),
    )(dlat, gather, kv, query, small, dtok)


def local(
    latents,
    tokens,
    token_sample,
    token_mask,
    drop_mask,
    gain_query,
    w_query,
    gain_token,
    w_key,
    w_value,
    w_out,
    gain_mlp,
    w_up,
    b_up,
    w_down,
    b_down,
    cotangent,
):
    samples, lat_rows, width = latents.shape
    part, keys, values, tsort, query, normed, place, bounds = attend_forward(
        token_sample, token_mask, tokens, latents, gain_query, w_query, gain_token, w_key, w_value
    )
    msg, result, dmid, a, b, side, vec = latent_block(
        part, drop_mask, latents, cotangent, w_out, gain_mlp, w_up, b_up, w_down, b_down
    )
    dkv, dquery, dgain_q, dwq, result = attend_backward(
        bounds, keys, values, query, normed, msg, gain_query, w_query, result
    )
    dlat, gather, kv, dwq, small, d_tokens = gradients(
        dquery, dmid, latents, gain_query, w_query, a, b, side, dwq, vec, dgain_q, place, tokens,
        tsort, dkv, gain_token,
        w_key, w_value,
    )
    (
        d_latents,
        d_tokens,
        grad_up,
        grad_key,
        grad_value,
        grad_down,
        grad_out,
        grad_query,
        grad_gquery,
        grad_gtoken,
        grad_gmlp,
        grad_bup,
        grad_bdown,
    ) = closing(
        dlat.reshape(samples * lat_rows, width),
        gather,
        kv.reshape(2, width, width),
        dwq.reshape(-1, width),
        small,
        d_tokens,
    )
    return (
        result.reshape(latents.shape),
        d_latents.reshape(latents.shape),
        d_tokens,
        grad_gquery,
        grad_query.T,
        grad_gtoken,
        grad_key,
        grad_value,
        grad_out.T,
        grad_gmlp,
        grad_up,
        grad_bup,
        grad_down,
        grad_bdown,
    )


def solution(mesh):
    return jax.shard_map(
        local,
        mesh=mesh,
        in_specs=(
            P("stream", None, None),
            P(("stream", "tok"), None),
            P(("stream", "tok")),
            P(("stream", "tok")),
            P(),
            P(),
            P(),
            P(),
            P(),
            P(),
            P(),
            P(),
            P(),
            P(),
            P(),
            P(),
            P("stream", None, None),
        ),
        out_specs=(
            P("stream", None, None),
            P("stream", None, None),
            P(("stream", "tok"), None),
            P("stream"),
            P(None, "stream"),
            P(),
            P(),
            P(),
            P(None, "stream"),
            P("stream"),
            P(None, "stream"),
            P("stream"),
            P("stream", None),
            P("stream"),
        ),
        check_vma=False,
    )
```

```python
import functools

import jax
import jax.numpy as jnp
from jax import lax
from jax.experimental import pallas as pl
from jax.experimental.pallas import tpu as pltpu
from jax.sharding import PartitionSpec as P

HEADS = 12
HEAD_DIM = 64
PAIRS = HEADS // 2
PIECES = 4
PIECE_HEADS = HEADS // PIECES
NUM_ROWS = PIECE_HEADS * HEAD_DIM
PIECE_ROWS = NUM_ROWS + 16
MSG_ROWS = HEADS * HEAD_DIM + 32
BLOCK = 256
FWD_BLOCK = 128
PAD = 256
LAG = 2
ZROWS = 32
LINE_LAG = 2
GAP = 6
SUBS = 3
EARLY_SUBS = 1
SPREAD_LAG = 5
WIDE_START_TICKS = (1, 2, 2, 4)
KV_TICKS = (0, 3)
PAIR_TICK = 5
MORE_TICK = 20
ONE_TICK = 15
TWO_TICK = 20
WIDE_ONE_TICKS = (10, 27, 30)
WIDE_TWO_TICKS = (16, 32, 35)
WIDE_THREE_TICKS = (25, -1, -1)
LAT_TICKS = (0, 4, 8)
TOKEN_TICKS = (22, 23, 24, 25, 26, 27, 28, 29)
NEG = -1e30
F32 = jnp.float32
BF16 = jnp.bfloat16
VMEM_BYTES = 60 * 1024 * 1024


def norm_parts(values):
    center = values - jnp.mean(values, -1, keepdims=True)
    spread = jnp.mean(center * center, -1, keepdims=True)
    inv = lax.rsqrt(spread + 1e-05)
    return center * inv, inv


def norm_back(unit, inv, gain, grad):
    scaled = grad * gain
    inner = scaled - jnp.mean(scaled, -1, keepdims=True)
    return inv * (inner - unit * jnp.mean(scaled * unit, -1, keepdims=True))


def dot(a, b, contract=(1, 0)):
    return lax.dot_general(
        a, b, (((contract[0],), (contract[1],)), ((), ())), preferred_element_type=F32
    )


def row(ref):
    return ref[...].reshape(1, ref.shape[0])


def piece_of(head):
    return head // PIECE_HEADS, head % PIECE_HEADS


def forward_kernel(
    sample_ref,
    mask_ref,
    tok_hbm,
    lat_hbm,
    gain_q_ref,
    wq_hbm,
    gain_t_ref,
    wk_hbm,
    wv_hbm,
    part_out,
    key_out,
    val_out,
    tsort_out,
    query_out,
    normed_out,
    place_ref,
    bounds_ref,
    tnorm_ref,
    pos_ref,
    top_ref,
    den_ref,
    num_ref,
    tok_ref,
    lat_ref,
    wq_ref,
    wk_ref,
    wv_ref,
    part_ref,
    key_ref,
    val_ref,
    tsort_ref,
    query_ref,
    normed_ref,
    load_sem,
    store_sem,
    sample_sem,
):
    loads = [
        pltpu.make_async_copy(src, dst, load_sem.at[i])
        for i, (src, dst) in enumerate(
            (
                (tok_hbm, tok_ref),
                (wk_hbm, wk_ref),
                (wv_hbm, wv_ref),
                (lat_hbm, lat_ref),
                (wq_hbm, wq_ref),
            )
        )
    ]
    for n in (0, 3, 4, 1, 2):
        loads[n].start()
    stores = [
        pltpu.make_async_copy(src, dst, store_sem.at[i])
        for i, (src, dst) in enumerate(
            ((key_ref, key_out), (val_ref, val_out), (tsort_ref, tsort_out))
        )
    ]
    samples = part_ref.shape[0]

    def sample_stores(s):
        at = pl.ds(pl.multiple_of(s * 128, 128), 128)
        return [
            pltpu.make_async_copy(src, dst, sample_sem.at[i, s])
            for i, (src, dst) in enumerate(
                (
                    (part_ref.at[s], part_out.at[s]),
                    (query_ref.at[s], query_out.at[s]),
                    (normed_ref.at[at], normed_out.at[at]),
                )
            )
        ]

    rows = tok_ref.shape[0]
    width = tok_ref.shape[1]
    lat_rows = 128
    step = 256

    named = row(sample_ref) - lax.axis_index("stream") * samples
    ids = jnp.where(row(mask_ref) == 1, named, -1)
    lane = lax.broadcasted_iota(jnp.int32, (samples, rows), 1)
    member = ids == lax.broadcasted_iota(jnp.int32, (samples, rows), 0)
    ones = jnp.where(member, 1.0, 0.0)
    count = ones
    shift = 1
    while shift < rows:
        count = count + jnp.where(lane >= shift, pltpu.roll(count, shift, 1), 0.0)
        shift *= 2
    rank = count - ones
    begin = jnp.int32(0)
    pos = jnp.full((1, rows), -1.0, F32)
    for s in range(samples):
        total = jnp.sum(ones[s : s + 1]).astype(jnp.int32)
        bounds_ref[s] = begin
        bounds_ref[samples + s] = total
        pos = jnp.where(member[s : s + 1], rank[s : s + 1] + begin.astype(F32), pos)
        begin = begin + total
    pos_ref[...] = jnp.broadcast_to(pos, (8, rows))
    place_ref[...] = jnp.broadcast_to(pos, (128, rows)).T

    def token_norm(i, carry):
        at = pl.ds(pl.multiple_of(i * step, step), step)
        unit, _ = norm_parts(tok_ref[at, :].astype(F32))
        tnorm_ref[at, :] = (unit * row(gain_t_ref)).astype(BF16)
        return carry

    def lat_norm(i, carry):
        at = pl.ds(pl.multiple_of(i * step, step), step)
        unit, _ = norm_parts(lat_ref[at, :].astype(F32))
        normed = (unit * row(gain_q_ref)).astype(BF16)
        normed_ref[at, :] = normed
        turned = (dot(normed, wq_ref[...]) * 0.125).T.astype(BF16)
        blank = jnp.zeros((HEAD_DIM, lat_rows), BF16)
        for n in range(step // lat_rows):
            s = i * (step // lat_rows) + n
            span = slice(n * lat_rows, (n + 1) * lat_rows)
            for p in range(PAIRS):
                lo = 2 * p * HEAD_DIM
                mid, hi = lo + HEAD_DIM, lo + 2 * HEAD_DIM
                query_ref[s, p, :HEAD_DIM, :lat_rows] = turned[lo:mid, span]
                query_ref[s, p, :HEAD_DIM, lat_rows:] = blank
                query_ref[s, p, HEAD_DIM:, :lat_rows] = blank
                query_ref[s, p, HEAD_DIM:, lat_rows:] = turned[mid:hi, span]
        return carry

    def both_norm(i, carry):
        return token_norm(i, lat_norm(i, carry))

    loads[0].wait()
    loads[3].wait()
    loads[4].wait()
    if rows == samples * lat_rows:
        lax.fori_loop(0, rows // step, both_norm, 0)
    else:
        lax.fori_loop(0, rows // step, token_norm, 0)
        lax.fori_loop(0, samples * lat_rows // step, lat_norm, 0)
    loads[1].wait()
    loads[2].wait()

    def token_sort(i, carry):
        at = pl.ds(pl.multiple_of(i * step, step), step)
        target = lax.broadcasted_iota(jnp.int32, (step, rows), 0) + i * step
        chosen = target.astype(F32) == pos_ref[0:1, :]
        pick = jnp.where(chosen, 1.0, 0.0).astype(BF16)
        tsort = dot(pick, tnorm_ref[...]).astype(BF16)
        tsort_ref[at, :] = tsort
        key_ref[at, :] = dot(tsort, wk_ref[...]).astype(BF16)
        val_ref[at, :] = dot(tsort, wv_ref[...]).astype(BF16)
        return carry

    lax.fori_loop(0, rows // step, token_sort, 0)
    key_ref[rows:, :] = jnp.zeros((PAD, width), BF16)
    val_ref[rows:, :] = jnp.zeros((PAD, width), BF16)
    for copy in stores:
        copy.start()

    def sample_step(s, carry):
        start = bounds_ref[s]
        total = bounds_ref[samples + s]
        base = lax.div(start, 16) * 16
        blocks = jnp.where(total > 0, lax.div(start + total - base + FWD_BLOCK - 1, FWD_BLOCK), 0)
        for piece in range(PIECES):
            part_ref[s, piece, NUM_ROWS:, :] = jnp.zeros((16, lat_rows), F32)
        num_ref[...] = jnp.zeros_like(num_ref)
        top_ref[...] = jnp.full_like(top_ref, NEG)
        den_ref[...] = jnp.zeros_like(den_ref)

        def block_step(b, carry):
            row = pl.multiple_of(base + b * FWD_BLOCK, 16)
            index = lax.broadcasted_iota(jnp.int32, (FWD_BLOCK, 2 * lat_rows), 0) + row
            inside = (index >= start) & (index < start + total)
            for p in range(PAIRS):
                cols = slice(p * 128, (p + 1) * 128)
                score = dot(key_ref[pl.ds(row, FWD_BLOCK), cols], query_ref[s, p])
                score = jnp.where(inside, score, NEG)
                old = top_ref[p : p + 1, :]
                new = jnp.maximum(old, jnp.max(score, 0, keepdims=True))
                fade = jnp.exp(old - new)
                weight = jnp.exp(score - new)
                top_ref[p : p + 1, :] = new
                den_ref[p : p + 1, :] = den_ref[p : p + 1, :] * fade + jnp.sum(
                    weight, 0, keepdims=True
                )
                both = dot(val_ref[pl.ds(row, FWD_BLOCK), cols], weight.astype(BF16), (0, 0))
                for half in range(2):
                    at_rows = slice(p * 128 + half * HEAD_DIM, p * 128 + (half + 1) * HEAD_DIM)
                    at_cols = slice(half * lat_rows, (half + 1) * lat_rows)
                    num_ref[at_rows, :] = (
                        num_ref[at_rows, :] * fade[:, at_cols]
                        + both[half * HEAD_DIM : (half + 1) * HEAD_DIM, at_cols]
                    )
            return carry

        lax.fori_loop(0, blocks, block_step, 0)
        for h in range(HEADS):
            piece, i = piece_of(h)
            p, half = h // 2, h % 2
            at_cols = slice(half * lat_rows, (half + 1) * lat_rows)
            part_ref[s, piece, i * HEAD_DIM : (i + 1) * HEAD_DIM, :] = num_ref[
                h * HEAD_DIM : (h + 1) * HEAD_DIM, :
            ]
            part_ref[s, piece, NUM_ROWS + i : NUM_ROWS + i + 1, :] = top_ref[p : p + 1, at_cols]
            part_ref[s, piece, NUM_ROWS + 8 + i : NUM_ROWS + 9 + i, :] = den_ref[
                p : p + 1, at_cols
            ]
        for copy in sample_stores(s):
            copy.start()
        return carry

    lax.fori_loop(0, samples, sample_step, 0)
    for copy in stores:
        copy.wait()

    def finish(s, carry):
        for copy in sample_stores(s):
            copy.wait()
        return carry

    lax.fori_loop(0, samples, finish, 0)


def vmem():
    return pl.BlockSpec(memory_space=pltpu.VMEM)


def anywhere():
    return pl.BlockSpec(memory_space=pl.ANY)


def smem():
    return pl.BlockSpec(memory_space=pltpu.SMEM)


def attend_forward(sample, mask, tokens, latents, gain_q, wq, gain_t, wk, wv):
    samples, lat_rows, width = latents.shape
    rows = tokens.shape[0]
    sds = jax.ShapeDtypeStruct
    return pl.pallas_call(
        forward_kernel,
        name="attend_forward",
        out_shape=(
            sds((samples, PIECES, PIECE_ROWS, lat_rows), F32),
            sds((rows + PAD, width), BF16),
            sds((rows + PAD, width), BF16),
            sds((rows, width), BF16),
            sds((samples, PAIRS, 128, 2 * lat_rows), BF16),
            sds((samples * lat_rows, width), BF16),
            sds((rows, 128), F32),
            sds((2 * samples,), jnp.int32),
        ),
        in_specs=[vmem()] * 2
        + [anywhere()] * 2
        + [vmem(), anywhere(), vmem()]
        + [anywhere()] * 2,
        out_specs=(anywhere(),) * 6 + (vmem(), smem()),
        scratch_shapes=[
            pltpu.VMEM((rows, width), BF16),
            pltpu.VMEM((8, rows), F32),
            pltpu.VMEM((8, 2 * lat_rows), F32),
            pltpu.VMEM((8, 2 * lat_rows), F32),
            pltpu.VMEM((width, lat_rows), F32),
            pltpu.VMEM((rows, width), BF16),
            pltpu.VMEM((samples * lat_rows, width), BF16),
            pltpu.VMEM((width, width), BF16),
            pltpu.VMEM((width, width), BF16),
            pltpu.VMEM((width, width), BF16),
            pltpu.VMEM((samples, PIECES, PIECE_ROWS, lat_rows), F32),
            pltpu.VMEM((rows + PAD, width), BF16),
            pltpu.VMEM((rows + PAD, width), BF16),
            pltpu.VMEM((rows, width), BF16),
            pltpu.VMEM((samples, PAIRS, 128, 2 * lat_rows), BF16),
            pltpu.VMEM((samples * lat_rows, width), BF16),
            pltpu.SemaphoreType.DMA((5,)),
            pltpu.SemaphoreType.DMA((3,)),
            pltpu.SemaphoreType.DMA((3, samples)),
        ],
        compiler_params=pltpu.CompilerParams(vmem_limit_bytes=VMEM_BYTES),
    )(
        sample,
        mask,
        tokens,
        latents.reshape(samples * lat_rows, width),
        gain_q,
        wq,
        gain_t,
        wk,
        wv,
    )


def backward_kernel(
    bounds_ref,
    key_hbm,
    val_hbm,
    query_hbm,
    normed_hbm,
    msg_hbm,
    gain_q_ref,
    wq_hbm,
    res_hbm,
    dkv_out,
    dquery_out,
    dgain_ref,
    dwq_out,
    res_out,
    dk_ref,
    dv_ref,
    grad_ref,
    dquery_ref,
    turn_ref,
    stat_ref,
    res_ref,
    res_sems,
    key_ref,
    val_ref,
    query_ref,
    normed_ref,
    msg_ref,
    wq_ref,
    dkv_ref,
    dwq_ref,
    load_sem,
    sample_sem,
    dlat_sem,
    store_sem,
):
    samples = query_ref.shape[0]
    rows = dkv_ref.shape[1]
    lat_rows = 128
    step = 256
    width = dwq_ref.shape[0]
    for r in range(0, rows + PAD, step):
        dk_ref[r : r + step, :] = jnp.zeros((step, dk_ref.shape[1]), F32)
        dv_ref[r : r + step, :] = jnp.zeros((step, dv_ref.shape[1]), F32)
    loads = [
        pltpu.make_async_copy(src, dst, load_sem.at[i])
        for i, (src, dst) in enumerate(
            (
                (key_hbm, key_ref),
                (val_hbm, val_ref),
                (wq_hbm, wq_ref),
                (normed_hbm, normed_ref),
            )
        )
    ]

    def sample_loads(s):
        return [
            pltpu.make_async_copy(msg_hbm.at[s], msg_ref.at[s], sample_sem.at[0, s]),
            pltpu.make_async_copy(query_hbm.at[s], query_ref.at[s], sample_sem.at[1, s]),
        ]

    def dquery_store(s):
        at = pl.ds(pl.multiple_of(s * 128, 128), 128)
        return pltpu.make_async_copy(dquery_ref.at[at], dquery_out.at[at], dlat_sem.at[s])

    for copy in loads[:2] + sample_loads(0):
        copy.start()

    def start_sample(s, carry):
        for copy in sample_loads(s):
            copy.start()
        return carry

    lax.fori_loop(1, query_ref.shape[0], start_sample, 0)
    loads[2].start()
    loads[3].start()
    res_load = pltpu.make_async_copy(res_hbm, res_ref, res_sems.at[0])
    res_store = pltpu.make_async_copy(res_ref, res_out, res_sems.at[1])
    res_load.start()
    grad_ref[...] = jnp.zeros_like(grad_ref)
    dgain_ref[...] = jnp.zeros_like(dgain_ref)

    loads[0].wait()
    loads[1].wait()

    def sample_step(s, carry):
        for copy in sample_loads(s):
            copy.wait()
        start = bounds_ref[s]
        total = bounds_ref[samples + s]
        base = lax.div(start, 16) * 16
        blocks = jnp.where(total > 0, lax.div(start + total - base + BLOCK - 1, BLOCK), 0)
        turn_ref[...] = jnp.zeros_like(turn_ref)
        for h in range(HEADS):
            p, half = h // 2, h % 2
            grad_ref[
                p,
                half * HEAD_DIM : (half + 1) * HEAD_DIM,
                half * lat_rows : (half + 1) * lat_rows,
            ] = msg_ref[s, h * HEAD_DIM : (h + 1) * HEAD_DIM, :].astype(BF16)

            stat_ref[p : p + 1, half * lat_rows : (half + 1) * lat_rows] = msg_ref[
                s, width + h : width + h + 1, :
            ]
            stat_ref[8 + p : 9 + p, half * lat_rows : (half + 1) * lat_rows] = msg_ref[
                s, width + 16 + h : width + 17 + h, :
            ]

        def block_step(b, carry):
            row = pl.multiple_of(base + b * BLOCK, 16)
            index = lax.broadcasted_iota(jnp.int32, (BLOCK, 2 * lat_rows), 0) + row
            inside = (index >= start) & (index < start + total)
            at = pl.ds(row, BLOCK)
            for p in range(PAIRS):
                cols = slice(p * 128, (p + 1) * 128)
                key = key_ref[at, cols]
                query = query_ref[s, p]
                grad = grad_ref[p]
                score = dot(key, query)
                weight = jnp.where(inside, jnp.exp(score - stat_ref[p : p + 1, :]), 0.0)
                dprob = dot(val_ref[at, cols], grad)
                dscore = (weight * (dprob - stat_ref[8 + p : 9 + p, :])).astype(BF16)
                dv_ref[at, cols] += dot(weight.astype(BF16), grad, (1, 1))
                dk_ref[at, cols] += dot(dscore, query, (1, 1))
                both = dot(key, dscore, (0, 0))
                for half in range(2):
                    turn_ref[
                        p * 128 + half * HEAD_DIM : p * 128 + (half + 1) * HEAD_DIM, :
                    ] += both[
                        half * HEAD_DIM : (half + 1) * HEAD_DIM,
                        half * lat_rows : (half + 1) * lat_rows,
                    ]
            return carry

        lax.fori_loop(0, blocks, block_step, 0)
        at = pl.ds(pl.multiple_of(s * lat_rows, lat_rows), lat_rows)
        dquery = (turn_ref[...].T * 0.125).astype(BF16)
        dquery_ref[at, :] = dquery
        dquery_store(s).start()
        return carry

    lax.fori_loop(0, samples, sample_step, 0)
    res_load.wait()
    res_store.start()
    for r in range(0, rows, step):
        dkv_ref[0, r : r + step, :] = dk_ref[r : r + step, :].astype(BF16)
        dkv_ref[1, r : r + step, :] = dv_ref[r : r + step, :].astype(BF16)
    dkv_store = pltpu.make_async_copy(dkv_ref, dkv_out, store_sem.at[0])
    dkv_store.start()
    loads[2].wait()
    loads[3].wait()
    gain = jnp.zeros((1, width), F32)
    stores = []
    for c in range(0, width, 256):
        dwq_ref[c : c + 256, :] = dot(dquery_ref[:, c : c + 256], normed_ref[...], (0, 0))
        copy = pltpu.make_async_copy(
            dwq_ref.at[pl.ds(c, 256)], dwq_out.at[pl.ds(c, 256)], store_sem.at[1 + c // 256]
        )
        copy.start()
        stores.append(copy)
        weight = wq_ref[:, c : c + 256].astype(F32).T
        gain += jnp.sum(weight * dwq_ref[c : c + 256, :], 0, keepdims=True)
    dgain_ref[0:1, :] = gain / row(gain_q_ref)
    res_store.wait()
    dkv_store.wait()
    for copy in stores:
        copy.wait()

    def finish(s, carry):
        dquery_store(s).wait()
        return carry

    lax.fori_loop(0, samples, finish, 0)


def attend_backward(bounds, keys, values, query, normed, msg, gain_q, wq, result):
    samples, _, lat_rows = msg.shape
    width = wq.shape[0]
    rows = keys.shape[0] - PAD
    sds = jax.ShapeDtypeStruct
    return pl.pallas_call(
        backward_kernel,
        name="attend_backward",
        out_shape=(
            sds((2, rows, width), BF16),
            sds((samples * lat_rows, width), BF16),
            sds((8, width), F32),
            sds((width, width), F32),
            sds(result.shape, BF16),
        ),
        in_specs=[smem()] + [anywhere()] * 5 + [vmem()] + [anywhere()] * 2,
        out_specs=(anywhere(),) * 2 + (vmem(),) + (anywhere(),) * 2,
        scratch_shapes=[
            pltpu.VMEM((rows + PAD, width), F32),
            pltpu.VMEM((rows + PAD, width), F32),
            pltpu.VMEM((PAIRS, 128, 2 * lat_rows), BF16),
            pltpu.VMEM((samples * lat_rows, width), BF16),
            pltpu.VMEM((width, lat_rows), F32),
            pltpu.VMEM((16, 2 * lat_rows), F32),
            pltpu.VMEM(result.shape, BF16),
            pltpu.SemaphoreType.DMA((2,)),
            pltpu.VMEM((rows + PAD, width), BF16),
            pltpu.VMEM((rows + PAD, width), BF16),
            pltpu.VMEM(query.shape, BF16),
            pltpu.VMEM(normed.shape, BF16),
            pltpu.VMEM(msg.shape, F32),
            pltpu.VMEM(wq.shape, BF16),
            pltpu.VMEM((2, rows, width), BF16),
            pltpu.VMEM((width, width), F32),
            pltpu.SemaphoreType.DMA((4,)),
            pltpu.SemaphoreType.DMA((2, samples)),
            pltpu.SemaphoreType.DMA((samples,)),
            pltpu.SemaphoreType.DMA((1 + width // 256,)),
        ],
        compiler_params=pltpu.CompilerParams(vmem_limit_bytes=VMEM_BYTES),
    )(
        bounds,
        keys,
        values,
        query,
        normed,
        msg,
        gain_q,
        wq,
        result,
    )


MESH = pl.DeviceIdType.MESH


def merge(a_ref, b_ref, out_ref):
    a_tail, b_tail = a_ref[NUM_ROWS : NUM_ROWS + 8, :], b_ref[NUM_ROWS : NUM_ROWS + 8, :]
    top = jnp.maximum(a_tail, b_tail)
    a_fade, b_fade = jnp.exp(a_tail - top), jnp.exp(b_tail - top)
    den = a_ref[NUM_ROWS + 8 :, :] * a_fade + b_ref[NUM_ROWS + 8 :, :] * b_fade
    for i in range(PIECE_HEADS):
        at = slice(i * HEAD_DIM, (i + 1) * HEAD_DIM)
        out_ref[at, :] = (
            a_ref[at, :] * a_fade[i : i + 1, :] + b_ref[at, :] * b_fade[i : i + 1, :]
        )
    out_ref[NUM_ROWS : NUM_ROWS + 8, :] = top
    out_ref[NUM_ROWS + 8 :, :] = den


def gelu_parts(x):
    c = 0.7978845608028654
    square = x * x
    t = jnp.tanh(c * x * (1.0 + 0.044715 * square))
    half = 0.5 * (1.0 + t)
    slope = half + (0.5 * c) * x * (1.0 - t * t) * (1.0 + (3 * 0.044715) * square)
    return x * half, slope


def latent_kernel(
    part_hbm,
    drop_ref,
    lat_hbm,
    cot_hbm,
    wo_hbm,
    gain_ref,
    wup_hbm,
    bup_ref,
    wdn_hbm,
    bdn_ref,
    msg_out,
    res_all,
    dmid_out,
    a_out,
    b_out,
    side_ref,
    vec_ref,
    lat_ref,
    cot_ref,
    msg_ref,
    res_ref,
    dmid_ref,
    a_ref,
    b_ref,
    store_sem,
    wo_ref,
    wup_ref,
    wdn_ref,
    pair_ref,
    own_ref,
    right_in,
    right_out,
    left_in,
    left_out,
    res_out,
    res_in,
    att_t_ref,
    mid_ref,
    acc_ref,
    dacc_ref,
    hn_ref,
    dm_ref,
    da_ref,
    att_ref,
    hn_out,
    hn_in,
    half_out,
    half_in,
    side_all,
    side_in,
    hn_send,
    hn_recv,
    half_send,
    half_recv,
    side_send,
    side_recv,
    own_sem,
    weight_sem,
    pair_send,
    pair_recv,
    right_send,
    right_recv,
    left_send,
    left_recv,
    msg_send,
    msg_recv,
    res_send,
    res_recv,
):
    samples = msg_out.shape[0]
    half = samples // 2
    lat_rows = 128
    width = lat_ref.shape[1]
    chunks = half * PIECES
    stream = lax.axis_index("stream")
    tok = lax.axis_index("tok")
    chips = lax.axis_size("tok") // 2
    core = lax.rem(tok, 2)
    chip = lax.div(tok, 2)
    parity = lax.rem(chip, 2)
    other = 1 - core
    partner = (stream, tok + 1 - 2 * core)
    right = (stream, tok + 2)
    left = (stream, tok - 2)
    has_right = chip < chips - 1
    has_left = chip > 0
    on_first = core == 0

    barrier = pltpu.get_barrier_semaphore()
    pl.semaphore_signal(barrier, inc=1, device_id=partner, device_id_type=MESH)

    @pl.when(has_right)
    def _():
        pl.semaphore_signal(barrier, inc=1, device_id=right, device_id_type=MESH)

    @pl.when(has_left)
    def _():
        pl.semaphore_signal(barrier, inc=1, device_id=left, device_id_type=MESH)

    own_load = pltpu.make_async_copy(
        part_hbm.at[pl.ds(core * chunks, chunks)], own_ref, own_sem
    )
    own_load.start()
    weights = [
        pltpu.make_async_copy(src, dst, weight_sem.at[i])
        for i, (src, dst) in enumerate(
            (
                (lat_hbm, lat_ref),
                (cot_hbm, cot_ref),
                (wo_hbm, wo_ref),
                (wup_hbm, wup_ref),
                (wdn_hbm, wdn_ref),
            )
        )
    ]
    for copy in weights:
        copy.start()
    pl.semaphore_wait(
        barrier, 1 + has_right.astype(jnp.int32) + has_left.astype(jnp.int32)
    )

    def pair_copy(i):
        return pltpu.make_async_remote_copy(
            src_ref=part_hbm.at[(1 - core) * chunks + i],
            dst_ref=pair_ref.at[i],
            send_sem=pair_send.at[i],
            recv_sem=pair_recv.at[i],
            device_id=partner,
            device_id_type=MESH,
        )

    def right_copy(i):
        return pltpu.make_async_remote_copy(
            src_ref=right_out.at[i],
            dst_ref=right_in.at[i],
            send_sem=right_send.at[i],
            recv_sem=right_recv.at[i],
            device_id=right,
            device_id_type=MESH,
        )

    def left_copy(i):
        return pltpu.make_async_remote_copy(
            src_ref=left_out.at[i],
            dst_ref=left_in.at[i],
            send_sem=left_send.at[i],
            recv_sem=left_recv.at[i],
            device_id=left,
            device_id_type=MESH,
        )

    def stores(j, far):
        at = (other if far else core) * half + j
        rows = pl.ds(pl.multiple_of(at * lat_rows, lat_rows), lat_rows)
        mine = pl.ds(pl.multiple_of(j * lat_rows, lat_rows), lat_rows)
        pairs = [
            (res_ref.at[rows], res_all.at[rows]),
            (a_ref.at[rows], a_out.at[rows]),
            (b_ref.at[:, rows], b_out.at[:, rows]),
        ]
        if not far:
            pairs.append((msg_ref.at[j], msg_out.at[at]))
            pairs.append((dmid_ref.at[mine], dmid_out.at[mine]))
        return [
            pltpu.make_async_copy(src, dst, store_sem.at[far, i, j])
            for i, (src, dst) in enumerate(pairs)
        ]

    def msg_copy(j):
        at = core * half + j
        return pltpu.make_async_remote_copy(
            src_ref=msg_ref.at[j],
            dst_ref=msg_out.at[at],
            send_sem=msg_send.at[j],
            recv_sem=msg_recv.at[j],
            device_id=partner,
            device_id_type=MESH,
        )

    def msg_arrival(j):
        return pltpu.make_async_remote_copy(
            src_ref=msg_ref.at[j],
            dst_ref=msg_out.at[other * half + j],
            send_sem=msg_send.at[j],
            recv_sem=msg_recv.at[j],
            device_id=partner,
            device_id_type=MESH,
        )

    def res_copy(j):
        return pltpu.make_async_remote_copy(
            src_ref=res_out.at[j],
            dst_ref=res_in.at[j],
            send_sem=res_send.at[j],
            recv_sem=res_recv.at[j],
            device_id=partner,
            device_id_type=MESH,
        )

    def hn_copy(j):
        return pltpu.make_async_remote_copy(
            src_ref=hn_out.at[j],
            dst_ref=hn_in.at[j],
            send_sem=hn_send.at[j],
            recv_sem=hn_recv.at[j],
            device_id=partner,
            device_id_type=MESH,
        )

    def half_copy(i):
        return pltpu.make_async_remote_copy(
            src_ref=half_out.at[i],
            dst_ref=half_in.at[i],
            send_sem=half_send.at[i],
            recv_sem=half_recv.at[i],
            device_id=partner,
            device_id_type=MESH,
        )

    side_copy = pltpu.make_async_remote_copy(
        src_ref=side_all.at[:, 1 - core],
        dst_ref=side_in,
        send_sem=side_send,
        recv_sem=side_recv,
        device_id=partner,
        device_id_type=MESH,
    )

    def start_pair(i, carry):
        pair_copy(i).start()
        return carry

    lax.fori_loop(0, chunks, start_pair, 0)
    own_load.wait()

    drop = row(drop_ref).astype(F32)
    scale_all = drop * drop.shape[1] / jnp.sum(drop, 1, keepdims=True)
    drop_lane = lax.broadcasted_iota(jnp.int32, drop.shape, 1)
    vec_ref[...] = jnp.zeros_like(vec_ref)

    def take(j):
        at = other * half + j
        rows = pl.ds(pl.multiple_of(at * lat_rows, lat_rows), lat_rows)
        for q in range(PIECES):
            half_copy(j * PIECES + q).wait_recv()
            b_ref[q, rows, :] = half_in[j * PIECES + q].astype(BF16)
        res_copy(j).wait_recv()
        res_ref[rows, :] = res_in[j].astype(BF16)

        @pl.when(on_first)
        def _():
            hn_copy(j).wait_recv()
            a_ref[rows, :] = hn_in[j].astype(BF16)

        @pl.when(jnp.logical_not(on_first))
        def _():
            scale = jnp.sum(
                jnp.where(drop_lane == stream * samples + at, scale_all, 0.0), 1, keepdims=True
            )
            a_ref[rows, :] = (scale * cot_ref[rows, :].astype(F32)).astype(BF16)

        for copy in stores(j, 1):
            copy.start()

    def mlp(j, q):
        sample = core * half + j
        rows = pl.ds(pl.multiple_of(sample * lat_rows, lat_rows), lat_rows)
        mine = pl.ds(pl.multiple_of(j * lat_rows, lat_rows), lat_rows)
        scale = jnp.sum(
            jnp.where(drop_lane == stream * samples + sample, scale_all, 0.0), 1, keepdims=True
        )

        @pl.when(q == 0)
        def _():
            for h in range(HEADS):
                piece, i = piece_of(h)
                at = j * PIECES + piece
                den = own_ref[at, NUM_ROWS + 8 + i : NUM_ROWS + 9 + i, :]
                att_t_ref[h * HEAD_DIM : (h + 1) * HEAD_DIM, :] = own_ref[
                    at, i * HEAD_DIM : (i + 1) * HEAD_DIM, :
                ] * (1.0 / den)
            att = att_t_ref[...].T.astype(BF16)
            att_ref[mine, :] = jnp.where(parity == 0, att[:, : width // 2], att[:, width // 2 :])
            mid = lat_ref[rows, :].astype(F32) + scale * dot(att, wo_ref[...])
            mid_ref[...] = mid
            unit, _ = norm_parts(mid)
            hn = (unit * row(gain_ref)).astype(BF16)
            dm = (scale * cot_ref[rows, :].astype(F32)).astype(BF16)
            hn_ref[...] = hn
            dm_ref[...] = dm
            a_ref[rows, :] = jnp.where(on_first, hn, dm)

            @pl.when(jnp.logical_not(on_first))
            def _():
                hn_out[j] = hn.astype(F32)
                hn_copy(j).start()

            vec_ref[1:2, :width] += jnp.sum(dm.astype(F32), 0, keepdims=True)
            acc_ref[...] = jnp.broadcast_to(row(bdn_ref), acc_ref.shape)
            dacc_ref[...] = jnp.zeros_like(dacc_ref)

        span = wup_ref.shape[1] // PIECES
        cols = pl.ds(pl.multiple_of(q * span, 128), span)
        pre = dot(hn_ref[...], wup_ref[:, cols]) + bup_ref[cols].reshape(1, span)
        active, slope = gelu_parts(pre)
        hidden = active.astype(BF16)
        acc_ref[...] += dot(hidden, wdn_ref[cols, :])
        dpre = (slope * dot(dm_ref[...], wdn_ref[cols, :], (1, 1))).astype(BF16)
        piece = j * PIECES + q
        near_half = lambda x: jnp.where(parity == 0, x[:, : span // 2], x[:, span // 2 :])
        hidden_half, dpre_half = near_half(hidden), near_half(dpre)
        b_ref[q, rows, :] = jnp.where(on_first, dpre_half, hidden_half)
        half_out[piece] = jnp.where(on_first, hidden_half, dpre_half).astype(F32)
        half_copy(piece).start()
        vec_ref[0:1, cols] += jnp.sum(dpre.astype(F32), 0, keepdims=True)
        dacc_ref[...] += dot(dpre, wup_ref[:, cols], (1, 1))

        @pl.when(q == PIECES - 1)
        def _():
            mid = mid_ref[...]
            res = (mid + scale * acc_ref[...]).astype(BF16)
            res_ref[rows, :] = res
            res_out[j] = res.astype(F32)
            res_copy(j).start()
            unit, inv = norm_parts(mid)
            dhn = dacc_ref[...]
            vec_ref[2:3, :width] += jnp.sum(dhn * unit, 0, keepdims=True)
            dmid = cot_ref[rows, :].astype(F32) + norm_back(unit, inv, row(gain_ref), dhn)
            dmid_ref[mine, :] = dmid
            da = (scale * dmid).astype(BF16)
            da_ref[mine, :] = da
            datt_t = dot(wo_ref[...], da, (1, 1)).astype(BF16).astype(F32)
            msg_ref[j, width:, :] = jnp.zeros((MSG_ROWS - width, lat_rows), F32)
            for h in range(HEADS):
                piece, i = piece_of(h)
                at = j * PIECES + piece
                inverse = 1.0 / own_ref[at, NUM_ROWS + 8 + i : NUM_ROWS + 9 + i, :]
                span_h = slice(h * HEAD_DIM, (h + 1) * HEAD_DIM)
                one = datt_t[span_h]
                msg_ref[j, span_h, :] = (one * inverse).astype(BF16).astype(F32)
                delta = jnp.sum(one * att_t_ref[span_h, :], 0, keepdims=True) * inverse
                msg_ref[j, width + h : width + h + 1, :] = own_ref[
                    at, NUM_ROWS + i : NUM_ROWS + i + 1, :
                ]
                msg_ref[j, width + 16 + h : width + 17 + h, :] = delta
            msg_copy(j).start()
            for copy in stores(j, 0):
                copy.start()

            @pl.when(j > 0)
            def _():
                take(j - 1)

    def step(t, carry):
        @pl.when(t < chunks)
        def _():
            pair_copy(t).wait_recv()
            merge(own_ref.at[t], pair_ref.at[t], own_ref.at[t])

        r = t - LAG * chip

        @pl.when((r >= 0) & (r < chunks))
        def _():
            @pl.when(has_left)
            def _():
                right_copy(r).wait_recv()
                merge(own_ref.at[r], right_in.at[r], right_out.at[r])

            @pl.when(jnp.logical_not(has_left))
            def _():
                right_out[r] = own_ref[r]

            @pl.when(has_right)
            def _():
                right_copy(r).start()

        u = t - LAG * (chips - 1 - chip)

        @pl.when((u >= 0) & (u < chunks))
        def _():
            @pl.when(has_right)
            def _():
                left_copy(u).wait_recv()

            @pl.when(has_left)
            def _():
                @pl.when(has_right)
                def _():
                    merge(own_ref.at[u], left_in.at[u], left_out.at[u])

                @pl.when(jnp.logical_not(has_right))
                def _():
                    left_out[u] = own_ref[u]

                left_copy(u).start()

        w = t - LAG * jnp.maximum(chip, chips - 1 - chip)

        @pl.when((w >= 0) & (w < chunks))
        def _():
            @pl.when(has_right)
            def _():
                merge(right_out.at[w], left_in.at[w], own_ref.at[w])

            @pl.when(jnp.logical_not(has_right))
            def _():
                own_ref[w] = right_out[w]

        m = w - (PIECES - 1)

        @pl.when(m == 0)
        def _():
            for copy in weights:
                copy.wait()

        @pl.when((m >= 0) & (m < chunks))
        def _():
            mlp(lax.div(m, PIECES), lax.rem(m, PIECES))

        return carry

    lax.fori_loop(0, chunks + LAG * (chips - 1) + PIECES - 1, step, 0)

    share = width // 8
    for block in range(4):
        at = slice(block * 2 * share, (block + 1) * 2 * share)
        product = dot(da_ref[:, at], att_ref[...], (0, 0))
        side_all[block, 0] = product[:share]
        side_all[block, 1] = product[share:]
    side_copy.start()

    take(half - 1)

    def finish_chunk(i, carry):
        pair_copy(i).wait_send()
        half_copy(i).wait_send()

        @pl.when(has_right)
        def _():
            right_copy(i).wait_send()

        @pl.when(has_left)
        def _():
            left_copy(i).wait_send()

        return carry

    lax.fori_loop(0, chunks, finish_chunk, 0)

    def finish_sample(j, carry):
        @pl.when(jnp.logical_not(on_first))
        def _():
            hn_copy(j).wait_send()

        res_copy(j).wait_send()
        msg_copy(j).wait_send()
        msg_arrival(j).wait_recv()
        for copy in stores(j, 0) + stores(j, 1):
            copy.wait()
        return carry

    lax.fori_loop(0, half, finish_sample, 0)
    side_copy.wait()
    side_ref[...] = side_all[:, core] + side_in[...]


def latent_block(part, drop_mask, latents, cotangent, wo, gain, wup, bup, wdn, bdn):
    samples, lat_rows, width = latents.shape
    half = samples // 2
    chunks = half * PIECES
    hidden = wup.shape[1]
    sds = jax.ShapeDtypeStruct
    chunk = lambda: pltpu.VMEM((chunks, PIECE_ROWS, lat_rows), F32)
    dma = pltpu.SemaphoreType.DMA
    return pl.pallas_call(
        latent_kernel,
        name="latent_block",
        out_shape=(
            sds((samples, MSG_ROWS, lat_rows), F32),
            sds((samples * lat_rows, width), BF16),
            sds((half * lat_rows, width), F32),
            sds((samples * lat_rows, width), BF16),
            sds((PIECES, samples * lat_rows, hidden // PIECES // 2), BF16),
            sds((4, width // 8, width // 2), F32),
            sds((8, hidden), F32),
        ),
        in_specs=[
            anywhere(),
            vmem(),
            anywhere(),
            anywhere(),
            anywhere(),
            vmem(),
            anywhere(),
            vmem(),
            anywhere(),
            vmem(),
        ],
        out_specs=(anywhere(),) * 5 + (vmem(),) * 2,
        scratch_shapes=[
            pltpu.VMEM((samples * lat_rows, width), BF16),
            pltpu.VMEM((samples * lat_rows, width), BF16),
            pltpu.VMEM((half, MSG_ROWS, lat_rows), F32),
            pltpu.VMEM((samples * lat_rows, width), BF16),
            pltpu.VMEM((half * lat_rows, width), F32),
            pltpu.VMEM((samples * lat_rows, width), BF16),
            pltpu.VMEM((PIECES, samples * lat_rows, hidden // PIECES // 2), BF16),
            dma((2, 5, half)),
            pltpu.VMEM(wo.shape, BF16),
            pltpu.VMEM(wup.shape, BF16),
            pltpu.VMEM(wdn.shape, BF16),
            chunk(),
            chunk(),
            chunk(),
            chunk(),
            chunk(),
            chunk(),
            pltpu.VMEM((half, lat_rows, width), F32),
            pltpu.VMEM((half, lat_rows, width), F32),
            pltpu.VMEM((width, lat_rows), F32),
            pltpu.VMEM((lat_rows, width), F32),
            pltpu.VMEM((lat_rows, width), F32),
            pltpu.VMEM((lat_rows, width), F32),
            pltpu.VMEM((lat_rows, width), BF16),
            pltpu.VMEM((lat_rows, width), BF16),
            pltpu.VMEM((half * lat_rows, width), BF16),
            pltpu.VMEM((half * lat_rows, width // 2), BF16),
            pltpu.VMEM((half, lat_rows, width), F32),
            pltpu.VMEM((half, lat_rows, width), F32),
            pltpu.VMEM((chunks, lat_rows, hidden // PIECES // 2), F32),
            pltpu.VMEM((chunks, lat_rows, hidden // PIECES // 2), F32),
            pltpu.VMEM((4, 2, width // 8, width // 2), F32),
            pltpu.VMEM((4, width // 8, width // 2), F32),
            dma((half,)),
            dma((half,)),
            dma((chunks,)),
            dma((chunks,)),
            dma,
            dma,
            dma,
            dma((5,)),
            dma((chunks,)),
            dma((chunks,)),
            dma((chunks,)),
            dma((chunks,)),
            dma((chunks,)),
            dma((chunks,)),
            dma((half,)),
            dma((half,)),
            dma((half,)),
            dma((half,)),
        ],
        compiler_params=pltpu.CompilerParams(
            vmem_limit_bytes=VMEM_BYTES, collective_id=1, has_side_effects=True
        ),
    )(
        part.reshape(samples * PIECES, PIECE_ROWS, lat_rows),
        drop_mask,
        latents.reshape(samples * lat_rows, width),
        cotangent.reshape(samples * lat_rows, width),
        wo,
        gain,
        wup,
        bup,
        wdn,
        bdn,
    )


def gradient_kernel(
    dquery_hbm,
    dmid_hbm,
    lat_hbm,
    gain_q_ref,
    wq_hbm,
    a_hbm,
    b_hbm,
    side_ref,
    dwq_hbm,
    vec_ref,
    dgain_q_ref,
    place_ref,
    tok_hbm,
    tsort_hbm,
    dkv_hbm,
    gain_t_ref,
    wk_ref,
    wv_ref,
    dlat_out,
    gather_out,
    kv_out,
    query_out,
    small_out,
    dtok_out,
    line_ref,
    right_ref,
    left_ref,
    dmine_ref,
    wide_ref,
    wide_one,
    wide_two,
    send_ref,
    mine_ref,
    pair_ref,
    one_ref,
    two_ref,
    small_ref,
    gain_ref,
    wide_far,
    spread_ref,
    stage_ref,
    stage_sem,
    dsend_ref,
    dquery_ref,
    lat_ref,
    wq_ref,
    a_ref,
    b_ref,
    dwq_ref,
    tok_ref,
    tsort_ref,
    dkv_ref,
    load_sem,
    dpair_send,
    dpair_recv,
    right_send,
    right_recv,
    left_send,
    left_recv,
    back_send,
    back_recv,
    back_local,
    wide_one_send,
    wide_one_recv,
    wide_two_send,
    wide_two_recv,
    wide_z_send,
    wide_z_recv,
    wide_core_send,
    wide_core_recv,
    wide_local,
    pair_send,
    pair_recv,
    one_send,
    one_recv,
    two_send,
    two_recv,
    spread_send,
    spread_recv,
    share_send,
    share_recv,
    query_send,
    query_recv,
    query_local,
    keep_local,
):
    rows, width = tok_ref.shape
    lat_chunks = dmine_ref.shape[0]
    all_chunks = line_ref.shape[0]
    kv_rows = send_ref.shape[2]
    q_rows = query_out.shape[2]
    mix = kv_rows + q_rows
    half_chunks = (all_chunks - lat_chunks) // 2
    kv_chunks = kv_rows // ZROWS
    wide_half = wide_ref.shape[1] // 2
    sub_rows = wide_half // SUBS

    stream = lax.axis_index("stream")
    tok = lax.axis_index("tok")
    chips = lax.axis_size("tok") // 2
    core = lax.rem(tok, 2)
    chip = lax.div(tok, 2)
    other = 1 - core
    parity = lax.rem(chip, 2)
    flip_x = stream + 1 - 2 * lax.rem(stream, 2)
    flip_y = lax.rem(stream + 2, 4)
    flip_xy = 3 - stream
    partner = (stream, tok + 1 - 2 * core)
    right = (stream, tok + 2)
    left = (stream, tok - 2)
    beside = (stream, tok + 2 - 4 * parity)
    near = ((flip_x, tok), (flip_y, tok))
    first = (flip_x, flip_y)
    has_right = chip < chips - 1
    has_left = chip > 0
    here = (chip == 0).astype(F32)

    barrier = pltpu.get_barrier_semaphore()
    for target in (partner,) + near:
        pl.semaphore_signal(barrier, inc=1, device_id=target, device_id_type=MESH)

    @pl.when(has_right)
    def _():
        pl.semaphore_signal(barrier, inc=1, device_id=right, device_id_type=MESH)

    @pl.when(has_left)
    def _():
        pl.semaphore_signal(barrier, inc=1, device_id=left, device_id_type=MESH)

    def remote(src, dst, send, recv, target):
        return pltpu.make_async_remote_copy(
            src_ref=src,
            dst_ref=dst,
            send_sem=send,
            recv_sem=recv,
            device_id=target,
            device_id_type=MESH,
        )

    pulls = [
        pltpu.make_async_copy(src, dst, load_sem.at[i])
        for i, (src, dst) in enumerate(
            (
                (tsort_hbm, tsort_ref),
                (dkv_hbm, dkv_ref),
                (dmid_hbm, dmine_ref),
                (a_hbm, a_ref),
                (b_hbm, b_ref),
                (dwq_hbm, dwq_ref),
                (tok_hbm, tok_ref),
                (dquery_hbm, dquery_ref),
                (lat_hbm, lat_ref),
                (wq_hbm, wq_ref),
            )
        )
    ]
    for n in (7, 8, 9, 2, 0, 1, 5, 3, 4, 6):
        pulls[n].start()
    pl.semaphore_wait(barrier, 3 + has_right.astype(jnp.int32) + has_left.astype(jnp.int32))

    def dpair_copy(i):
        return remote(
            dsend_ref.at[i], line_ref.at[i], dpair_send.at[i], dpair_recv.at[i], partner
        )

    lat_rows = 128
    per_sample = lat_rows // ZROWS

    def lat_gradient(which, j):
        sample = which * (lat_chunks // per_sample) + j
        at = pl.ds(pl.multiple_of(sample * lat_rows, lat_rows), lat_rows)
        unit, inv = norm_parts(lat_ref[at, :].astype(F32))
        dnormed = dot(dquery_ref[at, :], wq_ref[...], (1, 1))
        return norm_back(unit, inv, row(gain_q_ref), dnormed)

    def lat_event(j):
        grad = lat_gradient(other, j)
        for c in range(per_sample):
            dsend_ref[j * per_sample + c] = grad[c * ZROWS : (c + 1) * ZROWS]
            dpair_copy(j * per_sample + c).start()
        grad = lat_gradient(core, j)
        for c in range(per_sample):
            i = j * per_sample + c
            dmine_ref[i] = grad[c * ZROWS : (c + 1) * ZROWS] + dmine_ref[i] * here

    def wide_one_copy(h, n, sub):
        block = (first[h], flip_xy)[n]
        at = pl.ds(h * wide_half + sub * sub_rows, sub_rows)
        return remote(
            wide_ref.at[block, at],
            wide_one.at[h, n, pl.ds(sub * sub_rows, sub_rows)],
            wide_one_send.at[h, n, sub],
            wide_one_recv.at[h, n, sub],
            near[h],
        )

    def wide_at(block, h, sub):
        return wide_ref.at[block, pl.ds(h * wide_half + sub * sub_rows, sub_rows)]

    def wide_two_copy(h, sub):
        at = pl.ds(sub * sub_rows, sub_rows)
        return remote(
            wide_at(first[1 - h], h, sub),
            wide_two.at[h, at],
            wide_two_send.at[h, sub],
            wide_two_recv.at[h, sub],
            near[1 - h],
        )

    def gather_at(c, e, h, sub):
        return gather_out.at[c, e, pl.ds(h * wide_half + sub * sub_rows, sub_rows)]

    def far_at(h, sub):
        return wide_far.at[pl.ds(h * wide_half + sub * sub_rows, sub_rows)]

    def wide_z_copy(h, sub):
        return remote(
            wide_at(stream, h, sub),
            far_at(h, sub),
            wide_z_send.at[h, sub],
            wide_z_recv.at[h, sub],
            beside,
        )

    def wide_core_copy(far, h, sub):
        if far:
            src = far_at(h, sub)
            dst = gather_at(core, 1 - parity, h, sub)
        else:
            src = wide_at(stream, h, sub)
            dst = gather_at(core, parity, h, sub)
        return remote(
            src, dst, wide_core_send.at[far, h, sub], wide_core_recv.at[far, h, sub], partner
        )

    def wide_core_arrival(far, h, sub):
        place = gather_at(other, 1 - parity if far else parity, h, sub)
        return remote(
            place, place, wide_core_send.at[far, h, sub], wide_core_recv.at[far, h, sub], partner
        )

    def wide_keep(far, h, sub):
        return pltpu.make_async_copy(
            far_at(h, sub) if far else wide_at(stream, h, sub),
            gather_at(core, 1 - parity if far else parity, h, sub),
            wide_local.at[far, h, sub],
        )

    def wide_product(block):
        wide_ref[block, :width, :] = dot(a_ref[...], b_ref[block], (0, 0))
        wide_ref[block, width:, :] = side_ref[block]

    def wide_start(k):
        if k == 0:
            pulls[3].wait()
            pulls[4].wait()
        wide_product((flip_xy, first[0], first[1], stream)[k])
        for sub in range(EARLY_SUBS):
            for h in range(2):
                if k == 0:
                    wide_one_copy(h, 1, sub).start()
                elif k == 1 + h:
                    wide_one_copy(h, 0, sub).start()

    def wide_more():
        for sub in range(EARLY_SUBS, SUBS):
            for h in range(2):
                for n in range(2):
                    wide_one_copy(h, 1 - n, sub).start()

    def wide_event_one(sub):
        at = slice(sub * sub_rows, (sub + 1) * sub_rows)
        for h in range(2):
            for n in range(2):
                wide_one_copy(h, n, sub).wait_recv()
            span = pl.ds(h * wide_half + sub * sub_rows, sub_rows)
            wide_ref[first[1 - h], span, :] += wide_one[h, 1, at, :]
            wide_two_copy(h, sub).start()
            wide_ref[stream, span, :] += wide_one[h, 0, at, :]

    def wide_event_two(sub):
        at = slice(sub * sub_rows, (sub + 1) * sub_rows)
        for h in range(2):
            wide_two_copy(h, sub).wait_recv()
            span = pl.ds(h * wide_half + sub * sub_rows, sub_rows)
            wide_ref[stream, span, :] += wide_two[h, at, :]
            wide_z_copy(h, sub).start()
            wide_core_copy(0, h, sub).start()
            wide_keep(0, h, sub).start()

    def wide_event_three(sub):
        for h in range(2):
            wide_z_copy(h, sub).wait_recv()
            wide_core_copy(1, h, sub).start()
            wide_keep(1, h, sub).start()

    share = width // 4

    def gain_part(which, block, product):
        at = slice(block * share, (block + 1) * share)
        weight = jnp.where(which == 0, wk_ref[at, :], wv_ref[at, :]).astype(F32)
        gain_ref[at, 0:1] += jnp.sum(product * weight, 1, keepdims=True)

    def token_product(block, which):
        at = slice(block * share, (block + 1) * share)
        return dot(tsort_ref[:, at], dkv_ref[which], (0, 0))

    def token_other():
        for n in (0, 1, 5):
            pulls[n].wait()
        gain_ref[...] = jnp.zeros_like(gain_ref)
        for block in range(4):
            product = token_product(block, other)
            for h in range(2):
                send_ref[h, block] = product[h * kv_rows : (h + 1) * kv_rows]
            gain_part(other, block, product)
        for k, h, what in pairs:
            if what < 2:
                pair_copy(k, h, what).start()

    order = (flip_xy, first[0], first[1], stream)

    def pair_copy(k, h, what):
        block = order[k]
        src, at, size = (
            (send_ref.at[h, block], 0, kv_rows),
            (dwq_ref.at[block, other, h], kv_rows, q_rows),
            (small_ref.at[block], mix, 16),
        )[what]
        return remote(
            src,
            pair_ref.at[h, block, pl.ds(at, size)],
            pair_send.at[k, h, what],
            pair_recv.at[k, h, what],
            partner,
        )

    pairs = [(k, h, what) for k in range(4) for h in range(2) for what in range(3 - h)]

    def token_own():
        for block in range(4):
            product = token_product(block, core)
            for h in range(2):
                piece = product[h * kv_rows : (h + 1) * kv_rows]
                mine_ref[h, block, :kv_rows, :] = piece
                mine_ref[h, block, kv_rows:mix, :] = dwq_ref[block, core, h]
            gain_part(core, block, product)
        mine_ref[1, :, mix:, :] = jnp.zeros((4, 16, width), F32)
        small_ref[...] = jnp.zeros_like(small_ref)
        gain = jnp.broadcast_to(gain_ref[:, 0:1], gain_ref.shape).T[0:1, :] / row(gain_t_ref)
        for block in range(4):
            small_ref[block, 0:1, :] = vec_ref[0:1, block * width : (block + 1) * width] * here
            small_ref[block, 1:2, :] = dgain_q_ref[0:1, :]
            small_ref[block, 2:3, :] = vec_ref[2:3, :width] * here
            small_ref[block, 3:4, :] = vec_ref[1:2, :width] * here
            small_ref[block, 4:5, :] = gain
        for k in range(4):
            pair_copy(k, 0, 2).start()

    token_step = 128

    def stage_copy(i):
        return pltpu.make_async_copy(
            stage_ref.at[i % 2],
            dtok_out.at[pl.ds(i * token_step, token_step)],
            stage_sem.at[i % 2],
        )

    def token_part(i):
        if i == 0:
            pulls[6].wait()
        at = pl.ds(pl.multiple_of(i * token_step, token_step), token_step)
        target = lax.broadcasted_iota(jnp.int32, (token_step, rows), 1).astype(F32)
        pick = jnp.where(target == place_ref[at, 0:1], 1.0, 0.0).astype(BF16)
        dkey = dot(pick, dkv_ref[0]).astype(BF16)
        dval = dot(pick, dkv_ref[1]).astype(BF16)
        dnormed = dot(dkey, wk_ref[...], (1, 1)) + dot(dval, wv_ref[...], (1, 1))
        unit, inv = norm_parts(tok_ref[at, :].astype(F32))
        if i >= 2:
            stage_copy(i - 2).wait()
        stage_ref[i % 2] = norm_back(unit, inv, row(gain_t_ref), dnormed)
        stage_copy(i).start()

    def one_copy(h, n):
        block = (first[h], flip_xy)[n]
        return remote(
            mine_ref.at[h, block], one_ref.at[h, n], one_send.at[h, n], one_recv.at[h, n], near[h]
        )

    def two_copy(h):
        return remote(
            mine_ref.at[h, first[1 - h]], two_ref.at[h], two_send.at[h], two_recv.at[h], near[1 - h]
        )

    def pair_event():
        for k in range(4):
            block = order[k]
            for h in range(2):
                for what in range(3 - h):
                    pair_copy(k, h, what).wait_recv()
                mine_ref[h, block, :mix, :] += pair_ref[h, block, :mix, :]
                if h == 0:
                    mine_ref[h, block, mix:, :] = small_ref[block] + pair_ref[h, block, mix:, :]
                if k == 0:
                    one_copy(h, 1).start()
                elif k == 1 + h:
                    one_copy(h, 0).start()

    def one_event():
        for h in range(2):
            for n in range(2):
                one_copy(h, n).wait_recv()
            mine_ref[h, first[1 - h]] += one_ref[h, 1]
            two_copy(h).start()

    def two_event():
        for h in range(2):
            two_copy(h).wait_recv()
            total = mine_ref[h, stream] + one_ref[h, 0] + two_ref[h]
            for k in range(half_chunks):
                line_ref[lat_chunks + h * half_chunks + k] = total[k * ZROWS : (k + 1) * ZROWS]

    def right_copy(i):
        return remote(right_ref.at[i], right_ref.at[i], right_send.at[i], right_recv.at[i], right)

    def left_copy(i):
        return remote(left_ref.at[i], left_ref.at[i], left_send.at[i], left_recv.at[i], left)

    def back_copy(i):
        return remote(
            line_ref.at[i], dlat_out.at[core, i], back_send.at[i], back_recv.at[i], partner
        )

    def back_arrival(i):
        return remote(
            line_ref.at[i], dlat_out.at[other, i], back_send.at[i], back_recv.at[i], partner
        )

    def back_keep(i):
        return pltpu.make_async_copy(line_ref.at[i], dlat_out.at[core, i], back_local.at[i])

    def placed(t):
        late = t >= lat_chunks + GAP
        index = jnp.where(late, t - GAP, t)
        return index, (t >= 0) & (late | (t < lat_chunks)) & (index < all_chunks)

    def line_step(t):
        @pl.when(t < lat_chunks)
        def _():
            dpair_copy(t).wait_recv()
            line_ref[t] += dmine_ref[t]

        r, r_due = placed(t - LINE_LAG * chip)

        @pl.when(r_due)
        def _():
            @pl.when(has_left)
            def _():
                right_copy(r).wait_recv()
                right_ref[r] += line_ref[r]

            @pl.when(jnp.logical_not(has_left))
            def _():
                right_ref[r] = line_ref[r]

            @pl.when(has_right)
            def _():
                right_copy(r).start()

        u, u_due = placed(t - LINE_LAG * (chips - 1 - chip))

        @pl.when(u_due)
        def _():
            @pl.when(has_right)
            def _():
                left_copy(u).wait_recv()
                left_ref[u] += line_ref[u]

            @pl.when(jnp.logical_not(has_right))
            def _():
                left_ref[u] = line_ref[u]

            @pl.when(has_left)
            def _():
                left_copy(u).start()

        w, w_due = placed(t - LINE_LAG * jnp.maximum(chip, chips - 1 - chip))

        @pl.when(w_due)
        def _():
            line_ref[w] = right_ref[w] + left_ref[w] - line_ref[w]

            @pl.when(w < lat_chunks)
            def _():
                back_copy(w).start()
                back_keep(w).start()

    def spot(i):
        k = i - lat_chunks
        h = lax.div(k, half_chunks)
        return h, lax.rem(k, half_chunks)

    def by_half(h, pair):
        return jnp.where(h == 0, pair[0], pair[1])

    def block_of(h, k):
        return (stream, by_half(h, (flip_y, flip_x)), by_half(h, first), flip_xy)[k]

    def spread_src(i, k):
        h, c = spot(i)
        return line_ref.at[i] if k == 0 else spread_ref.at[k - 1, h, c]

    def spread_copy(i, k):
        h, c = spot(i)
        target = by_half(h, (flip_y, flip_x)) if k == 1 else by_half(h, first)
        return remote(
            spread_src(i, 1 if k == 3 else 0),
            spread_ref.at[k - 1, h, c],
            spread_send.at[k - 1, i - lat_chunks],
            spread_recv.at[k - 1, i - lat_chunks],
            (target, tok),
        )

    def share_copy(i, k):
        h, c = spot(i)
        return remote(
            spread_src(i, k),
            kv_out.at[core, block_of(h, k), h, c],
            share_send.at[k, i - lat_chunks],
            share_recv.at[k, i - lat_chunks],
            partner,
        )

    def share_arrival(i, k):
        h, c = spot(i)
        place = kv_out.at[other, block_of(h, k), h, c]
        return remote(
            place,
            place,
            share_send.at[k, i - lat_chunks],
            share_recv.at[k, i - lat_chunks],
            partner,
        )

    def kv_keep(i, k):
        h, c = spot(i)
        return pltpu.make_async_copy(
            spread_src(i, k),
            kv_out.at[core, block_of(h, k), h, c],
            keep_local.at[k, i - lat_chunks],
        )

    def spread_due(t):
        i, due = placed(t)
        i = jnp.maximum(i, lat_chunks)
        _, c = spot(i)
        return i, due & (t >= lat_chunks + GAP) & (c < kv_chunks)

    def spread_step(t):
        lag = LINE_LAG * jnp.maximum(chip, chips - 1 - chip)
        i, due = spread_due(t - lag)

        @pl.when(due)
        def _():
            spread_copy(i, 1).start()
            spread_copy(i, 2).start()
            share_copy(i, 0).start()
            kv_keep(i, 0).start()

        j, due_one = spread_due(t - lag - SPREAD_LAG)

        @pl.when(due_one)
        def _():
            spread_copy(j, 1).wait_recv()
            spread_copy(j, 3).start()
            share_copy(j, 1).start()
            kv_keep(j, 1).start()

        m, due_two = spread_due(t - lag - 2 * SPREAD_LAG)

        @pl.when(due_two)
        def _():
            for k in (2, 3):
                spread_copy(m, k).wait_recv()
                share_copy(m, k).start()
                kv_keep(m, k).start()

    def query_piece(h):
        return mine_ref.at[h, stream, pl.ds(kv_rows, q_rows)]

    def query_copy(h):
        return remote(
            query_piece(h),
            query_out.at[core, h],
            query_send.at[h],
            query_recv.at[h],
            partner,
        )

    def query_arrival(h):
        return remote(
            query_piece(h),
            query_out.at[other, h],
            query_send.at[h],
            query_recv.at[h],
            partner,
        )

    def query_keep(h):
        return pltpu.make_async_copy(query_piece(h), query_out.at[core, h], query_local.at[h])

    def query_event(h):
        flat = lat_chunks + h * half_chunks + kv_chunks
        for k in range(0, q_rows, 16):
            at = flat * ZROWS + k
            chunk, row = at // ZROWS, at % ZROWS
            mine_ref[h, stream, kv_rows + k : kv_rows + k + 16, :] = line_ref[
                chunk, row : row + 16, :
            ]
        query_copy(h).start()
        query_keep(h).start()
        if h == 0:
            at = flat * ZROWS + q_rows
            chunk, row = at // ZROWS, at % ZROWS
            small_out[...] = line_ref[chunk, row : row + 16, :]

    tail = LINE_LAG * (chips - 1)
    ready = lambda h: lat_chunks + GAP + (h + 1) * half_chunks - 1 + tail
    events = {}

    def at_tick(tick, run):
        events.setdefault(tick, []).append(run)

    parts = rows // token_step
    for i in range(parts):
        at_tick(TOKEN_TICKS[i % len(TOKEN_TICKS)], functools.partial(token_part, i))
    for k in range(4):
        at_tick(WIDE_START_TICKS[k], functools.partial(wide_start, k))
    at_tick(KV_TICKS[0], token_other)
    at_tick(KV_TICKS[1], token_own)
    at_tick(PAIR_TICK, pair_event)
    at_tick(MORE_TICK, wide_more)
    at_tick(ONE_TICK, one_event)
    at_tick(TWO_TICK, two_event)
    for sub in range(SUBS):
        at_tick(WIDE_ONE_TICKS[sub], functools.partial(wide_event_one, sub))
        at_tick(WIDE_TWO_TICKS[sub], functools.partial(wide_event_two, sub))
        if WIDE_THREE_TICKS[sub] >= 0:
            at_tick(WIDE_THREE_TICKS[sub], functools.partial(wide_event_three, sub))
    for n in (7, 8, 9, 2):
        pulls[n].wait()
    lat_event(0)
    for j in range(1, lat_chunks // per_sample):
        at_tick(LAT_TICKS[j - 1], functools.partial(lat_event, j))

    def step(t, carry):
        line_step(t)
        spread_step(t)
        for tick in sorted(events):

            @pl.when(t == tick)
            def _(tick=tick):
                for run in events[tick]:
                    run()

        return carry

    lax.fori_loop(0, ready(1) + 2 * SPREAD_LAG + 1, step, 0)
    for h in range(2):
        query_event(h)
    for sub in range(SUBS):
        if WIDE_THREE_TICKS[sub] < 0:
            wide_event_three(sub)

    def finish_lat(i, carry):
        dpair_copy(i).wait_send()
        back_copy(i).wait_send()
        back_arrival(i).wait_recv()
        back_keep(i).wait()
        return carry

    lax.fori_loop(0, lat_chunks, finish_lat, 0)

    def finish_line(i, carry):
        @pl.when(has_right)
        def _():
            right_copy(i).wait_send()

        @pl.when(has_left)
        def _():
            left_copy(i).wait_send()

        return carry

    lax.fori_loop(0, all_chunks, finish_line, 0)

    def finish_spread(n, carry):
        h = lax.div(n, kv_chunks)
        i = lat_chunks + h * half_chunks + lax.rem(n, kv_chunks)
        for k in range(4):
            if k:
                spread_copy(i, k).wait_send()
            share_copy(i, k).wait_send()
            share_arrival(i, k).wait_recv()
            kv_keep(i, k).wait()
        return carry

    lax.fori_loop(0, 2 * kv_chunks, finish_spread, 0)
    for i in range(parts - 2, parts):
        stage_copy(i).wait()
    for k, h, what in pairs:
        pair_copy(k, h, what).wait_send()
    for h in range(2):
        for n in range(2):
            one_copy(h, n).wait_send()
        two_copy(h).wait_send()
        query_copy(h).wait_send()
        query_arrival(h).wait_recv()
        query_keep(h).wait()
        for sub in range(SUBS):
            for n in range(2):
                wide_one_copy(h, n, sub).wait_send()
                wide_core_copy(n, h, sub).wait_send()
                wide_core_arrival(n, h, sub).wait_recv()
            wide_two_copy(h, sub).wait_send()
            wide_z_copy(h, sub).wait_send()
            wide_keep(0, h, sub).wait()
            wide_keep(1, h, sub).wait()


def gradients(
    dquery, dmid, latents, gain_q, wq, a, b, side, dwq, vec, dgain_q, place, tokens, tsort, dkv,
    gain_t, wk, wv,
):
    rows, width = tokens.shape
    half = dquery.shape[0] // 2
    lat_chunks = half // ZROWS
    wide_rows, wide_cols = a.shape[1] + side.shape[1], b.shape[2]
    share = width // 4
    kv_rows, q_rows = share // 2, share // 4
    block = kv_rows + q_rows + 16
    all_chunks = lat_chunks + 2 * block // ZROWS
    sds = jax.ShapeDtypeStruct
    dma = pltpu.SemaphoreType.DMA
    buf = lambda *shape: pltpu.VMEM(shape, F32)
    both = lambda *shape: [dma(shape), dma(shape)]
    return pl.pallas_call(
        gradient_kernel,
        name="gradients",
        out_shape=(
            sds((2, lat_chunks, ZROWS, width), F32),
            sds((2, 2, wide_rows, wide_cols), F32),
            sds((2, 4, 2, kv_rows // ZROWS, ZROWS, width), F32),
            sds((2, 2, q_rows, width), F32),
            sds((16, width), F32),
            sds((rows, width), F32),
        ),
        in_specs=[anywhere()] * 3
        + [vmem()]
        + [anywhere()] * 3
        + [vmem(), anywhere()]
        + [vmem()] * 3
        + [anywhere()] * 3
        + [vmem()] * 3,
        out_specs=(anywhere(),) * 4 + (vmem(), anywhere()),
        scratch_shapes=[
            buf(all_chunks, ZROWS, width),
            buf(all_chunks, ZROWS, width),
            buf(all_chunks, ZROWS, width),
            buf(lat_chunks, ZROWS, width),
            buf(4, wide_rows, wide_cols),
            buf(2, 2, wide_rows // 2, wide_cols),
            buf(2, wide_rows // 2, wide_cols),
            buf(2, 4, kv_rows, width),
            buf(2, 4, block, width),
            buf(2, 4, block, width),
            buf(2, 2, block, width),
            buf(2, block, width),
            buf(4, 16, width),
            buf(width, 128),
            buf(wide_rows, wide_cols),
            buf(3, 2, kv_rows // ZROWS, ZROWS, width),
            buf(2, 128, width),
            dma((2,)),
            buf(lat_chunks, ZROWS, width),
            pltpu.VMEM(dquery.shape, BF16),
            pltpu.VMEM(dquery.shape, BF16),
            pltpu.VMEM(wq.shape, BF16),
            pltpu.VMEM(a.shape, BF16),
            pltpu.VMEM(b.shape, BF16),
            buf(4, 2, 2, q_rows, width),
            pltpu.VMEM(tokens.shape, BF16),
            pltpu.VMEM(tsort.shape, BF16),
            pltpu.VMEM(dkv.shape, BF16),
            dma((10,)),
        ]
        + both(lat_chunks)
        + both(all_chunks)
        + both(all_chunks)
        + both(lat_chunks)
        + [dma((lat_chunks,))]
        + both(2, 2, SUBS)
        + both(2, SUBS)
        + both(2, SUBS)
        + both(2, 2, SUBS)
        + [dma((2, 2, SUBS))]
        + both(4, 2, 3)
        + both(2, 2)
        + both(2)
        + both(3, all_chunks - lat_chunks)
        + both(4, all_chunks - lat_chunks)
        + both(2)
        + [dma((2,)), dma((4, all_chunks - lat_chunks))],
        compiler_params=pltpu.CompilerParams(
            vmem_limit_bytes=VMEM_BYTES, collective_id=2, has_side_effects=True
        ),
    )(
        dquery,
        dmid.reshape(lat_chunks, ZROWS, width),
        latents.reshape(2 * half, width),
        gain_q,
        wq,
        a,
        b,
        side,
        dwq.reshape(4, 2, 2, q_rows, width),
        vec,
        dgain_q,
        place,
        tokens,
        tsort,
        dkv,
        gain_t,
        wk,
        wv,
    )


def closing_kernel(
    dlat_hbm,
    gather_hbm,
    kv_hbm,
    query_ref,
    small_ref,
    dtok_hbm,
    dlat_out,
    dtok_out,
    up_out,
    key_out,
    val_out,
    down_out,
    out_ref,
    wq_ref,
    gain_q_ref,
    gain_t_ref,
    gain_mlp_ref,
    bup_ref,
    bdn_ref,
    wide_ref,
    up_ref,
    dlat_ref,
    kv_ref,
    dtok_ref,
    down_ref,
    load_sems,
    store_sems,
):
    width = small_ref.shape[1]
    cols = wide_ref.shape[2]
    loads = [
        pltpu.make_async_copy(src, dst, load_sems.at[i])
        for i, (src, dst) in enumerate(
            (
                (gather_hbm.at[1], wide_ref),
                (gather_hbm.at[0], up_ref),
                (dlat_hbm, dlat_ref),
                (kv_hbm, kv_ref),
                (dtok_hbm, dtok_ref),
            )
        )
    ]
    for copy in loads:
        copy.start()
    stores = [
        pltpu.make_async_copy(src, dst, store_sems.at[i])
        for i, (src, dst) in enumerate(
            (
                (up_ref.at[0, pl.ds(0, width)], up_out.at[:, pl.ds(0, cols)]),
                (up_ref.at[1, pl.ds(0, width)], up_out.at[:, pl.ds(cols, cols)]),
                (dlat_ref, dlat_out),
                (kv_ref.at[0], key_out),
                (kv_ref.at[1], val_out),
                (dtok_ref, dtok_out),
                (down_ref, down_out),
            )
        )
    ]
    stream = lax.axis_index("stream")
    gain_t_ref[...] = small_ref[4]
    bup_ref[...] = small_ref[0]
    size = gain_q_ref.shape[0]
    for i, ref in ((1, gain_q_ref), (2, gain_mlp_ref), (3, bdn_ref)):
        line = small_ref[i : i + 1, :]
        piece = line[:, :size]
        for k in range(1, width // size):
            piece = jnp.where(stream == k, line[:, k * size : (k + 1) * size], piece)
        ref[...] = piece[0]
    wq_ref[...] = query_ref[...]
    loads[0].wait()
    for e in range(2):
        down_ref[e * cols : (e + 1) * cols, :] = wide_ref[e, :width, :].T
    stores[6].start()
    loads[1].wait()
    stores[0].start()
    stores[1].start()
    half = up_ref.shape[1] - width
    for e in range(2):
        out_ref[:half, e * cols : (e + 1) * cols] = up_ref[e, width:, :]
        out_ref[half:, e * cols : (e + 1) * cols] = wide_ref[e, width:, :]
    loads[2].wait()
    stores[2].start()
    loads[3].wait()
    stores[3].start()
    stores[4].start()
    loads[4].wait()
    stores[5].start()
    for copy in stores:
        copy.wait()


def closing(dlat, gather, kv, query, small, dtok):
    width = small.shape[1]
    wide_rows, cols = gather.shape[2:]
    share = query.shape[0]
    rows = dtok.shape[0]
    sds = lambda *shape: jax.ShapeDtypeStruct(shape, F32)
    return pl.pallas_call(
        closing_kernel,
        name="closing",
        out_shape=(
            sds(*dlat.shape),
            sds(rows, width),
            sds(width, 2 * cols),
            sds(width, width),
            sds(width, width),
            sds(2 * cols, width),
            sds(share, width),
            sds(share, width),
            sds(share),
            sds(width),
            sds(share),
            sds(2 * cols),
            sds(share),
        ),
        in_specs=[anywhere()] * 3 + [vmem()] * 2 + [anywhere()],
        out_specs=(anywhere(),) * 6 + (vmem(),) * 7,
        scratch_shapes=[
            pltpu.VMEM((2, wide_rows, cols), F32),
            pltpu.VMEM((2, wide_rows, cols), F32),
            pltpu.VMEM(dlat.shape, F32),
            pltpu.VMEM(kv.shape, F32),
            pltpu.VMEM(dtok.shape, F32),
            pltpu.VMEM((2 * cols, width), F32),
            pltpu.SemaphoreType.DMA((5,)),
            pltpu.SemaphoreType.DMA((7,)),
        ],
        compiler_params=pltpu.CompilerParams(vmem_limit_bytes=VMEM_BYTES),
    )(dlat, gather, kv, query, small, dtok)


def local(
    latents,
    tokens,
    token_sample,
    token_mask,
    drop_mask,
    gain_query,
    w_query,
    gain_token,
    w_key,
    w_value,
    w_out,
    gain_mlp,
    w_up,
    b_up,
    w_down,
    b_down,
    cotangent,
):
    samples, lat_rows, width = latents.shape
    part, keys, values, tsort, query, normed, place, bounds = attend_forward(
        token_sample, token_mask, tokens, latents, gain_query, w_query, gain_token, w_key, w_value
    )
    msg, result, dmid, a, b, side, vec = latent_block(
        part, drop_mask, latents, cotangent, w_out, gain_mlp, w_up, b_up, w_down, b_down
    )
    dkv, dquery, dgain_q, dwq, result = attend_backward(
        bounds, keys, values, query, normed, msg, gain_query, w_query, result
    )
    dlat, gather, kv, dwq, small, d_tokens = gradients(
        dquery, dmid, latents, gain_query, w_query, a, b, side, dwq, vec, dgain_q, place, tokens,
        tsort, dkv, gain_token,
        w_key, w_value,
    )
    (
        d_latents,
        d_tokens,
        grad_up,
        grad_key,
        grad_value,
        grad_down,
        grad_out,
        grad_query,
        grad_gquery,
        grad_gtoken,
        grad_gmlp,
        grad_bup,
        grad_bdown,
    ) = closing(
        dlat.reshape(samples * lat_rows, width),
        gather,
        kv.reshape(2, width, width),
        dwq.reshape(-1, width),
        small,
        d_tokens,
    )
    return (
        result.reshape(latents.shape),
        d_latents.reshape(latents.shape),
        d_tokens,
        grad_gquery,
        grad_query.T,
        grad_gtoken,
        grad_key,
        grad_value,
        grad_out.T,
        grad_gmlp,
        grad_up,
        grad_bup,
        grad_down,
        grad_bdown,
    )


def solution(mesh):
    return jax.shard_map(
        local,
        mesh=mesh,
        in_specs=(
            P("stream", None, None),
            P(("stream", "tok"), None),
            P(("stream", "tok")),
            P(("stream", "tok")),
            P(),
            P(),
            P(),
            P(),
            P(),
            P(),
            P(),
            P(),
            P(),
            P(),
            P(),
            P(),
            P("stream", None, None),
        ),
        out_specs=(
            P("stream", None, None),
            P("stream", None, None),
            P(("stream", "tok"), None),
            P("stream"),
            P(None, "stream"),
            P(),
            P(),
            P(),
            P(None, "stream"),
            P("stream"),
            P(None, "stream"),
            P("stream"),
            P("stream", None),
            P("stream"),
        ),
        check_vma=False,
    )
```

```python
import functools

import jax
import jax.numpy as jnp
from jax import lax
from jax.experimental import pallas as pl
from jax.experimental.pallas import tpu as pltpu
from jax.sharding import PartitionSpec as P

HEADS = 12
HEAD_DIM = 64
PAIRS = HEADS // 2
PIECES = 4
PIECE_HEADS = HEADS // PIECES
NUM_ROWS = PIECE_HEADS * HEAD_DIM
PIECE_ROWS = NUM_ROWS + 16
MSG_ROWS = HEADS * HEAD_DIM + 32
BLOCK = 256
FWD_BLOCK = 128
PAD = 256
LAG = 2
ZROWS = 32
LINE_LAG = 2
GAP = 6
SUBS = 3
EARLY_SUBS = 1
SPREAD_LAG = 5
WIDE_START_TICKS = (1, 2, 2, 4)
KV_TICKS = (0, 3)
PAIR_TICK = 5
MORE_TICK = 20
ONE_TICK = 15
TWO_TICK = 20
WIDE_ONE_TICKS = (10, 27, 30)
WIDE_TWO_TICKS = (16, 32, 35)
WIDE_THREE_TICKS = (25, -1, -1)
LAT_TICKS = (0, 4, 8)
TOKEN_TICKS = (22, 23, 24, 25, 26, 27, 28, 29)
NEG = -1e30
F32 = jnp.float32
BF16 = jnp.bfloat16
VMEM_BYTES = 60 * 1024 * 1024


def norm_parts(values):
    center = values - jnp.mean(values, -1, keepdims=True)
    spread = jnp.mean(center * center, -1, keepdims=True)
    inv = lax.rsqrt(spread + 1e-05)
    return center * inv, inv


def norm_back(unit, inv, gain, grad):
    scaled = grad * gain
    inner = scaled - jnp.mean(scaled, -1, keepdims=True)
    return inv * (inner - unit * jnp.mean(scaled * unit, -1, keepdims=True))


def dot(a, b, contract=(1, 0)):
    return lax.dot_general(
        a, b, (((contract[0],), (contract[1],)), ((), ())), preferred_element_type=F32
    )


def row(ref):
    return ref[...].reshape(1, ref.shape[0])


def piece_of(head):
    return head // PIECE_HEADS, head % PIECE_HEADS


def forward_kernel(
    sample_ref,
    mask_ref,
    tok_hbm,
    lat_hbm,
    gain_q_ref,
    wq_hbm,
    gain_t_ref,
    wk_hbm,
    wv_hbm,
    part_out,
    key_out,
    val_out,
    tsort_out,
    query_out,
    normed_out,
    place_ref,
    bounds_ref,
    tnorm_ref,
    pos_ref,
    top_ref,
    den_ref,
    num_ref,
    tok_ref,
    lat_ref,
    wq_ref,
    wk_ref,
    wv_ref,
    part_ref,
    key_ref,
    val_ref,
    tsort_ref,
    query_ref,
    normed_ref,
    load_sem,
    store_sem,
    sample_sem,
):
    loads = [
        pltpu.make_async_copy(src, dst, load_sem.at[i])
        for i, (src, dst) in enumerate(
            (
                (tok_hbm, tok_ref),
                (wk_hbm, wk_ref),
                (wv_hbm, wv_ref),
                (lat_hbm, lat_ref),
                (wq_hbm, wq_ref),
            )
        )
    ]
    for n in (0, 3, 4, 1, 2):
        loads[n].start()
    stores = [
        pltpu.make_async_copy(src, dst, store_sem.at[i])
        for i, (src, dst) in enumerate(
            ((key_ref, key_out), (val_ref, val_out), (tsort_ref, tsort_out))
        )
    ]
    samples = part_ref.shape[0]

    def sample_stores(s):
        at = pl.ds(pl.multiple_of(s * 128, 128), 128)
        return [
            pltpu.make_async_copy(src, dst, sample_sem.at[i, s])
            for i, (src, dst) in enumerate(
                (
                    (part_ref.at[s], part_out.at[s]),
                    (query_ref.at[s], query_out.at[s]),
                    (normed_ref.at[at], normed_out.at[at]),
                )
            )
        ]

    rows = tok_ref.shape[0]
    width = tok_ref.shape[1]
    lat_rows = 128
    step = 256

    named = row(sample_ref) - lax.axis_index("stream") * samples
    ids = jnp.where(row(mask_ref) == 1, named, -1)
    lane = lax.broadcasted_iota(jnp.int32, (samples, rows), 1)
    member = ids == lax.broadcasted_iota(jnp.int32, (samples, rows), 0)
    ones = jnp.where(member, 1.0, 0.0)
    count = ones
    shift = 1
    while shift < rows:
        count = count + jnp.where(lane >= shift, pltpu.roll(count, shift, 1), 0.0)
        shift *= 2
    rank = count - ones
    begin = jnp.int32(0)
    pos = jnp.full((1, rows), -1.0, F32)
    for s in range(samples):
        total = jnp.sum(ones[s : s + 1]).astype(jnp.int32)
        bounds_ref[s] = begin
        bounds_ref[samples + s] = total
        pos = jnp.where(member[s : s + 1], rank[s : s + 1] + begin.astype(F32), pos)
        begin = begin + total
    pos_ref[...] = jnp.broadcast_to(pos, (8, rows))
    place_ref[...] = jnp.broadcast_to(pos, (128, rows)).T

    def token_norm(i, carry):
        at = pl.ds(pl.multiple_of(i * step, step), step)
        unit, _ = norm_parts(tok_ref[at, :].astype(F32))
        tnorm_ref[at, :] = (unit * row(gain_t_ref)).astype(BF16)
        return carry

    def lat_norm(i, carry):
        at = pl.ds(pl.multiple_of(i * step, step), step)
        unit, _ = norm_parts(lat_ref[at, :].astype(F32))
        normed = (unit * row(gain_q_ref)).astype(BF16)
        normed_ref[at, :] = normed
        turned = (dot(normed, wq_ref[...]) * 0.125).T.astype(BF16)
        blank = jnp.zeros((HEAD_DIM, lat_rows), BF16)
        for n in range(step // lat_rows):
            s = i * (step // lat_rows) + n
            span = slice(n * lat_rows, (n + 1) * lat_rows)
            for p in range(PAIRS):
                lo = 2 * p * HEAD_DIM
                mid, hi = lo + HEAD_DIM, lo + 2 * HEAD_DIM
                query_ref[s, p, :HEAD_DIM, :lat_rows] = turned[lo:mid, span]
                query_ref[s, p, :HEAD_DIM, lat_rows:] = blank
                query_ref[s, p, HEAD_DIM:, :lat_rows] = blank
                query_ref[s, p, HEAD_DIM:, lat_rows:] = turned[mid:hi, span]
        return carry

    def both_norm(i, carry):
        return token_norm(i, lat_norm(i, carry))

    loads[0].wait()
    loads[3].wait()
    loads[4].wait()
    if rows == samples * lat_rows:
        lax.fori_loop(0, rows // step, both_norm, 0)
    else:
        lax.fori_loop(0, rows // step, token_norm, 0)
        lax.fori_loop(0, samples * lat_rows // step, lat_norm, 0)
    loads[1].wait()
    loads[2].wait()

    def token_sort(i, carry):
        at = pl.ds(pl.multiple_of(i * step, step), step)
        target = lax.broadcasted_iota(jnp.int32, (step, rows), 0) + i * step
        chosen = target.astype(F32) == pos_ref[0:1, :]
        pick = jnp.where(chosen, 1.0, 0.0).astype(BF16)
        tsort = dot(pick, tnorm_ref[...]).astype(BF16)
        tsort_ref[at, :] = tsort
        key_ref[at, :] = dot(tsort, wk_ref[...]).astype(BF16)
        val_ref[at, :] = dot(tsort, wv_ref[...]).astype(BF16)
        return carry

    lax.fori_loop(0, rows // step, token_sort, 0)
    key_ref[rows:, :] = jnp.zeros((PAD, width), BF16)
    val_ref[rows:, :] = jnp.zeros((PAD, width), BF16)
    for copy in stores:
        copy.start()

    def sample_step(s, carry):
        start = bounds_ref[s]
        total = bounds_ref[samples + s]
        base = lax.div(start, 16) * 16
        blocks = jnp.where(total > 0, lax.div(start + total - base + FWD_BLOCK - 1, FWD_BLOCK), 0)
        for piece in range(PIECES):
            part_ref[s, piece, NUM_ROWS:, :] = jnp.zeros((16, lat_rows), F32)
        num_ref[...] = jnp.zeros_like(num_ref)
        top_ref[...] = jnp.full_like(top_ref, NEG)
        den_ref[...] = jnp.zeros_like(den_ref)

        def block_step(b, carry):
            row = pl.multiple_of(base + b * FWD_BLOCK, 16)
            index = lax.broadcasted_iota(jnp.int32, (FWD_BLOCK, 2 * lat_rows), 0) + row
            inside = (index >= start) & (index < start + total)
            for p in range(PAIRS):
                cols = slice(p * 128, (p + 1) * 128)
                score = dot(key_ref[pl.ds(row, FWD_BLOCK), cols], query_ref[s, p])
                score = jnp.where(inside, score, NEG)
                old = top_ref[p : p + 1, :]
                new = jnp.maximum(old, jnp.max(score, 0, keepdims=True))
                fade = jnp.exp(old - new)
                weight = jnp.exp(score - new)
                top_ref[p : p + 1, :] = new
                den_ref[p : p + 1, :] = den_ref[p : p + 1, :] * fade + jnp.sum(
                    weight, 0, keepdims=True
                )
                both = dot(val_ref[pl.ds(row, FWD_BLOCK), cols], weight.astype(BF16), (0, 0))
                for half in range(2):
                    at_rows = slice(p * 128 + half * HEAD_DIM, p * 128 + (half + 1) * HEAD_DIM)
                    at_cols = slice(half * lat_rows, (half + 1) * lat_rows)
                    num_ref[at_rows, :] = (
                        num_ref[at_rows, :] * fade[:, at_cols]
                        + both[half * HEAD_DIM : (half + 1) * HEAD_DIM, at_cols]
                    )
            return carry

        lax.fori_loop(0, blocks, block_step, 0)
        for h in range(HEADS):
            piece, i = piece_of(h)
            p, half = h // 2, h % 2
            at_cols = slice(half * lat_rows, (half + 1) * lat_rows)
            part_ref[s, piece, i * HEAD_DIM : (i + 1) * HEAD_DIM, :] = num_ref[
                h * HEAD_DIM : (h + 1) * HEAD_DIM, :
            ]
            part_ref[s, piece, NUM_ROWS + i : NUM_ROWS + i + 1, :] = top_ref[p : p + 1, at_cols]
            part_ref[s, piece, NUM_ROWS + 8 + i : NUM_ROWS + 9 + i, :] = den_ref[
                p : p + 1, at_cols
            ]
        for copy in sample_stores(s):
            copy.start()
        return carry

    lax.fori_loop(0, samples, sample_step, 0)
    for copy in stores:
        copy.wait()

    def finish(s, carry):
        for copy in sample_stores(s):
            copy.wait()
        return carry

    lax.fori_loop(0, samples, finish, 0)


def vmem():
    return pl.BlockSpec(memory_space=pltpu.VMEM)


def anywhere():
    return pl.BlockSpec(memory_space=pl.ANY)


def smem():
    return pl.BlockSpec(memory_space=pltpu.SMEM)


def attend_forward(sample, mask, tokens, latents, gain_q, wq, gain_t, wk, wv):
    samples, lat_rows, width = latents.shape
    rows = tokens.shape[0]
    sds = jax.ShapeDtypeStruct
    return pl.pallas_call(
        forward_kernel,
        name="attend_forward",
        out_shape=(
            sds((samples, PIECES, PIECE_ROWS, lat_rows), F32),
            sds((rows + PAD, width), BF16),
            sds((rows + PAD, width), BF16),
            sds((rows, width), BF16),
            sds((samples, PAIRS, 128, 2 * lat_rows), BF16),
            sds((samples * lat_rows, width), BF16),
            sds((rows, 128), F32),
            sds((2 * samples,), jnp.int32),
        ),
        in_specs=[vmem()] * 2
        + [anywhere()] * 2
        + [vmem(), anywhere(), vmem()]
        + [anywhere()] * 2,
        out_specs=(anywhere(),) * 6 + (vmem(), smem()),
        scratch_shapes=[
            pltpu.VMEM((rows, width), BF16),
            pltpu.VMEM((8, rows), F32),
            pltpu.VMEM((8, 2 * lat_rows), F32),
            pltpu.VMEM((8, 2 * lat_rows), F32),
            pltpu.VMEM((width, lat_rows), F32),
            pltpu.VMEM((rows, width), BF16),
            pltpu.VMEM((samples * lat_rows, width), BF16),
            pltpu.VMEM((width, width), BF16),
            pltpu.VMEM((width, width), BF16),
            pltpu.VMEM((width, width), BF16),
            pltpu.VMEM((samples, PIECES, PIECE_ROWS, lat_rows), F32),
            pltpu.VMEM((rows + PAD, width), BF16),
            pltpu.VMEM((rows + PAD, width), BF16),
            pltpu.VMEM((rows, width), BF16),
            pltpu.VMEM((samples, PAIRS, 128, 2 * lat_rows), BF16),
            pltpu.VMEM((samples * lat_rows, width), BF16),
            pltpu.SemaphoreType.DMA((5,)),
            pltpu.SemaphoreType.DMA((3,)),
            pltpu.SemaphoreType.DMA((3, samples)),
        ],
        compiler_params=pltpu.CompilerParams(vmem_limit_bytes=VMEM_BYTES),
    )(
        sample,
        mask,
        tokens,
        latents.reshape(samples * lat_rows, width),
        gain_q,
        wq,
        gain_t,
        wk,
        wv,
    )


def backward_kernel(
    bounds_ref,
    key_hbm,
    val_hbm,
    query_hbm,
    normed_hbm,
    msg_hbm,
    gain_q_ref,
    wq_hbm,
    res_hbm,
    dkv_out,
    dquery_out,
    dgain_ref,
    dwq_out,
    res_out,
    dk_ref,
    dv_ref,
    grad_ref,
    dquery_ref,
    turn_ref,
    stat_ref,
    res_ref,
    res_sems,
    key_ref,
    val_ref,
    query_ref,
    normed_ref,
    msg_ref,
    wq_ref,
    dkv_ref,
    dwq_ref,
    load_sem,
    sample_sem,
    dlat_sem,
    store_sem,
):
    samples = query_ref.shape[0]
    rows = dkv_ref.shape[1]
    lat_rows = 128
    step = 256
    width = dwq_ref.shape[0]
    for r in range(0, rows + PAD, step):
        dk_ref[r : r + step, :] = jnp.zeros((step, dk_ref.shape[1]), F32)
        dv_ref[r : r + step, :] = jnp.zeros((step, dv_ref.shape[1]), F32)
    loads = [
        pltpu.make_async_copy(src, dst, load_sem.at[i])
        for i, (src, dst) in enumerate(
            (
                (key_hbm, key_ref),
                (val_hbm, val_ref),
                (wq_hbm, wq_ref),
                (normed_hbm, normed_ref),
            )
        )
    ]

    def sample_loads(s):
        return [
            pltpu.make_async_copy(msg_hbm.at[s], msg_ref.at[s], sample_sem.at[0, s]),
            pltpu.make_async_copy(query_hbm.at[s], query_ref.at[s], sample_sem.at[1, s]),
        ]

    def dquery_store(s):
        at = pl.ds(pl.multiple_of(s * 128, 128), 128)
        return pltpu.make_async_copy(dquery_ref.at[at], dquery_out.at[at], dlat_sem.at[s])

    for copy in loads[:2] + sample_loads(0):
        copy.start()

    def start_sample(s, carry):
        for copy in sample_loads(s):
            copy.start()
        return carry

    lax.fori_loop(1, query_ref.shape[0], start_sample, 0)
    loads[2].start()
    loads[3].start()
    res_load = pltpu.make_async_copy(res_hbm, res_ref, res_sems.at[0])
    res_store = pltpu.make_async_copy(res_ref, res_out, res_sems.at[1])
    res_load.start()
    grad_ref[...] = jnp.zeros_like(grad_ref)
    dgain_ref[...] = jnp.zeros_like(dgain_ref)

    loads[0].wait()
    loads[1].wait()

    def sample_step(s, carry):
        for copy in sample_loads(s):
            copy.wait()
        start = bounds_ref[s]
        total = bounds_ref[samples + s]
        base = lax.div(start, 16) * 16
        blocks = jnp.where(total > 0, lax.div(start + total - base + BLOCK - 1, BLOCK), 0)
        turn_ref[...] = jnp.zeros_like(turn_ref)
        for h in range(HEADS):
            p, half = h // 2, h % 2
            grad_ref[
                p,
                half * HEAD_DIM : (half + 1) * HEAD_DIM,
                half * lat_rows : (half + 1) * lat_rows,
            ] = msg_ref[s, h * HEAD_DIM : (h + 1) * HEAD_DIM, :].astype(BF16)

            stat_ref[p : p + 1, half * lat_rows : (half + 1) * lat_rows] = msg_ref[
                s, width + h : width + h + 1, :
            ]
            stat_ref[8 + p : 9 + p, half * lat_rows : (half + 1) * lat_rows] = msg_ref[
                s, width + 16 + h : width + 17 + h, :
            ]

        def block_step(b, carry):
            row = pl.multiple_of(base + b * BLOCK, 16)
            index = lax.broadcasted_iota(jnp.int32, (BLOCK, 2 * lat_rows), 0) + row
            inside = (index >= start) & (index < start + total)
            at = pl.ds(row, BLOCK)
            for p in range(PAIRS):
                cols = slice(p * 128, (p + 1) * 128)
                key = key_ref[at, cols]
                query = query_ref[s, p]
                grad = grad_ref[p]
                score = dot(key, query)
                weight = jnp.where(inside, jnp.exp(score - stat_ref[p : p + 1, :]), 0.0)
                dprob = dot(val_ref[at, cols], grad)
                dscore = (weight * (dprob - stat_ref[8 + p : 9 + p, :])).astype(BF16)
                dv_ref[at, cols] += dot(weight.astype(BF16), grad, (1, 1))
                dk_ref[at, cols] += dot(dscore, query, (1, 1))
                both = dot(key, dscore, (0, 0))
                for half in range(2):
                    turn_ref[
                        p * 128 + half * HEAD_DIM : p * 128 + (half + 1) * HEAD_DIM, :
                    ] += both[
                        half * HEAD_DIM : (half + 1) * HEAD_DIM,
                        half * lat_rows : (half + 1) * lat_rows,
                    ]
            return carry

        lax.fori_loop(0, blocks, block_step, 0)
        at = pl.ds(pl.multiple_of(s * lat_rows, lat_rows), lat_rows)
        dquery = (turn_ref[...].T * 0.125).astype(BF16)
        dquery_ref[at, :] = dquery
        dquery_store(s).start()
        return carry

    lax.fori_loop(0, samples, sample_step, 0)
    res_load.wait()
    res_store.start()
    for r in range(0, rows, step):
        dkv_ref[0, r : r + step, :] = dk_ref[r : r + step, :].astype(BF16)
        dkv_ref[1, r : r + step, :] = dv_ref[r : r + step, :].astype(BF16)
    dkv_store = pltpu.make_async_copy(dkv_ref, dkv_out, store_sem.at[0])
    dkv_store.start()
    loads[2].wait()
    loads[3].wait()
    gain = jnp.zeros((1, width), F32)
    stores = []
    for c in range(0, width, 256):
        dwq_ref[c : c + 256, :] = dot(dquery_ref[:, c : c + 256], normed_ref[...], (0, 0))
        copy = pltpu.make_async_copy(
            dwq_ref.at[pl.ds(c, 256)], dwq_out.at[pl.ds(c, 256)], store_sem.at[1 + c // 256]
        )
        copy.start()
        stores.append(copy)
        weight = wq_ref[:, c : c + 256].astype(F32).T
        gain += jnp.sum(weight * dwq_ref[c : c + 256, :], 0, keepdims=True)
    dgain_ref[0:1, :] = gain / row(gain_q_ref)
    res_store.wait()
    dkv_store.wait()
    for copy in stores:
        copy.wait()

    def finish(s, carry):
        dquery_store(s).wait()
        return carry

    lax.fori_loop(0, samples, finish, 0)


def attend_backward(bounds, keys, values, query, normed, msg, gain_q, wq, result):
    samples, _, lat_rows = msg.shape
    width = wq.shape[0]
    rows = keys.shape[0] - PAD
    sds = jax.ShapeDtypeStruct
    return pl.pallas_call(
        backward_kernel,
        name="attend_backward",
        out_shape=(
            sds((2, rows, width), BF16),
            sds((samples * lat_rows, width), BF16),
            sds((8, width), F32),
            sds((width, width), F32),
            sds(result.shape, BF16),
        ),
        in_specs=[smem()] + [anywhere()] * 5 + [vmem()] + [anywhere()] * 2,
        out_specs=(anywhere(),) * 2 + (vmem(),) + (anywhere(),) * 2,
        scratch_shapes=[
            pltpu.VMEM((rows + PAD, width), F32),
            pltpu.VMEM((rows + PAD, width), F32),
            pltpu.VMEM((PAIRS, 128, 2 * lat_rows), BF16),
            pltpu.VMEM((samples * lat_rows, width), BF16),
            pltpu.VMEM((width, lat_rows), F32),
            pltpu.VMEM((16, 2 * lat_rows), F32),
            pltpu.VMEM(result.shape, BF16),
            pltpu.SemaphoreType.DMA((2,)),
            pltpu.VMEM((rows + PAD, width), BF16),
            pltpu.VMEM((rows + PAD, width), BF16),
            pltpu.VMEM(query.shape, BF16),
            pltpu.VMEM(normed.shape, BF16),
            pltpu.VMEM(msg.shape, F32),
            pltpu.VMEM(wq.shape, BF16),
            pltpu.VMEM((2, rows, width), BF16),
            pltpu.VMEM((width, width), F32),
            pltpu.SemaphoreType.DMA((4,)),
            pltpu.SemaphoreType.DMA((2, samples)),
            pltpu.SemaphoreType.DMA((samples,)),
            pltpu.SemaphoreType.DMA((1 + width // 256,)),
        ],
        compiler_params=pltpu.CompilerParams(vmem_limit_bytes=VMEM_BYTES),
    )(
        bounds,
        keys,
        values,
        query,
        normed,
        msg,
        gain_q,
        wq,
        result,
    )


MESH = pl.DeviceIdType.MESH


def merge(a_ref, b_ref, out_ref):
    a_tail, b_tail = a_ref[NUM_ROWS : NUM_ROWS + 8, :], b_ref[NUM_ROWS : NUM_ROWS + 8, :]
    top = jnp.maximum(a_tail, b_tail)
    a_fade, b_fade = jnp.exp(a_tail - top), jnp.exp(b_tail - top)
    den = a_ref[NUM_ROWS + 8 :, :] * a_fade + b_ref[NUM_ROWS + 8 :, :] * b_fade
    for i in range(PIECE_HEADS):
        at = slice(i * HEAD_DIM, (i + 1) * HEAD_DIM)
        out_ref[at, :] = (
            a_ref[at, :] * a_fade[i : i + 1, :] + b_ref[at, :] * b_fade[i : i + 1, :]
        )
    out_ref[NUM_ROWS : NUM_ROWS + 8, :] = top
    out_ref[NUM_ROWS + 8 :, :] = den


def gelu_parts(x):
    c = 0.7978845608028654
    square = x * x
    t = jnp.tanh(c * x * (1.0 + 0.044715 * square))
    half = 0.5 * (1.0 + t)
    slope = half + (0.5 * c) * x * (1.0 - t * t) * (1.0 + (3 * 0.044715) * square)
    return x * half, slope


def latent_kernel(
    part_hbm,
    drop_ref,
    lat_hbm,
    cot_hbm,
    wo_hbm,
    gain_ref,
    wup_hbm,
    bup_ref,
    wdn_hbm,
    bdn_ref,
    msg_out,
    res_all,
    dmid_out,
    a_out,
    b_out,
    side_ref,
    vec_ref,
    lat_ref,
    cot_ref,
    msg_ref,
    res_ref,
    dmid_ref,
    a_ref,
    b_ref,
    store_sem,
    wo_ref,
    wup_ref,
    wdn_ref,
    pair_ref,
    own_ref,
    right_in,
    right_out,
    left_in,
    left_out,
    res_out,
    res_in,
    att_t_ref,
    mid_ref,
    acc_ref,
    dacc_ref,
    hn_ref,
    dm_ref,
    da_ref,
    att_ref,
    hn_out,
    hn_in,
    half_out,
    half_in,
    side_all,
    side_in,
    hn_send,
    hn_recv,
    half_send,
    half_recv,
    side_send,
    side_recv,
    own_sem,
    weight_sem,
    pair_send,
    pair_recv,
    right_send,
    right_recv,
    left_send,
    left_recv,
    msg_send,
    msg_recv,
    res_send,
    res_recv,
):
    samples = msg_out.shape[0]
    half = samples // 2
    lat_rows = 128
    width = lat_ref.shape[1]
    chunks = half * PIECES
    stream = lax.axis_index("stream")
    tok = lax.axis_index("tok")
    chips = lax.axis_size("tok") // 2
    core = lax.rem(tok, 2)
    chip = lax.div(tok, 2)
    parity = lax.rem(chip, 2)
    other = 1 - core
    partner = (stream, tok + 1 - 2 * core)
    right = (stream, tok + 2)
    left = (stream, tok - 2)
    has_right = chip < chips - 1
    has_left = chip > 0
    on_first = core == 0

    barrier = pltpu.get_barrier_semaphore()
    pl.semaphore_signal(barrier, inc=1, device_id=partner, device_id_type=MESH)

    @pl.when(has_right)
    def _():
        pl.semaphore_signal(barrier, inc=1, device_id=right, device_id_type=MESH)

    @pl.when(has_left)
    def _():
        pl.semaphore_signal(barrier, inc=1, device_id=left, device_id_type=MESH)

    own_load = pltpu.make_async_copy(
        part_hbm.at[pl.ds(core * chunks, chunks)], own_ref, own_sem
    )
    own_load.start()
    weights = [
        pltpu.make_async_copy(src, dst, weight_sem.at[i])
        for i, (src, dst) in enumerate(
            (
                (lat_hbm, lat_ref),
                (cot_hbm, cot_ref),
                (wo_hbm, wo_ref),
                (wup_hbm, wup_ref),
                (wdn_hbm, wdn_ref),
            )
        )
    ]
    for copy in weights:
        copy.start()
    pl.semaphore_wait(
        barrier, 1 + has_right.astype(jnp.int32) + has_left.astype(jnp.int32)
    )

    def pair_copy(i):
        return pltpu.make_async_remote_copy(
            src_ref=part_hbm.at[(1 - core) * chunks + i],
            dst_ref=pair_ref.at[i],
            send_sem=pair_send.at[i],
            recv_sem=pair_recv.at[i],
            device_id=partner,
            device_id_type=MESH,
        )

    def right_copy(i):
        return pltpu.make_async_remote_copy(
            src_ref=right_out.at[i],
            dst_ref=right_in.at[i],
            send_sem=right_send.at[i],
            recv_sem=right_recv.at[i],
            device_id=right,
            device_id_type=MESH,
        )

    def left_copy(i):
        return pltpu.make_async_remote_copy(
            src_ref=left_out.at[i],
            dst_ref=left_in.at[i],
            send_sem=left_send.at[i],
            recv_sem=left_recv.at[i],
            device_id=left,
            device_id_type=MESH,
        )

    def stores(j, far):
        at = (other if far else core) * half + j
        rows = pl.ds(pl.multiple_of(at * lat_rows, lat_rows), lat_rows)
        mine = pl.ds(pl.multiple_of(j * lat_rows, lat_rows), lat_rows)
        pairs = [
            (res_ref.at[rows], res_all.at[rows]),
            (a_ref.at[rows], a_out.at[rows]),
            (b_ref.at[:, rows], b_out.at[:, rows]),
        ]
        if not far:
            pairs.append((msg_ref.at[j], msg_out.at[at]))
            pairs.append((dmid_ref.at[mine], dmid_out.at[mine]))
        return [
            pltpu.make_async_copy(src, dst, store_sem.at[far, i, j])
            for i, (src, dst) in enumerate(pairs)
        ]

    def msg_copy(j):
        at = core * half + j
        return pltpu.make_async_remote_copy(
            src_ref=msg_ref.at[j],
            dst_ref=msg_out.at[at],
            send_sem=msg_send.at[j],
            recv_sem=msg_recv.at[j],
            device_id=partner,
            device_id_type=MESH,
        )

    def msg_arrival(j):
        return pltpu.make_async_remote_copy(
            src_ref=msg_ref.at[j],
            dst_ref=msg_out.at[other * half + j],
            send_sem=msg_send.at[j],
            recv_sem=msg_recv.at[j],
            device_id=partner,
            device_id_type=MESH,
        )

    def res_copy(j):
        return pltpu.make_async_remote_copy(
            src_ref=res_out.at[j],
            dst_ref=res_in.at[j],
            send_sem=res_send.at[j],
            recv_sem=res_recv.at[j],
            device_id=partner,
            device_id_type=MESH,
        )

    def hn_copy(j):
        return pltpu.make_async_remote_copy(
            src_ref=hn_out.at[j],
            dst_ref=hn_in.at[j],
            send_sem=hn_send.at[j],
            recv_sem=hn_recv.at[j],
            device_id=partner,
            device_id_type=MESH,
        )

    def half_copy(i):
        return pltpu.make_async_remote_copy(
            src_ref=half_out.at[i],
            dst_ref=half_in.at[i],
            send_sem=half_send.at[i],
            recv_sem=half_recv.at[i],
            device_id=partner,
            device_id_type=MESH,
        )

    side_copy = pltpu.make_async_remote_copy(
        src_ref=side_all.at[:, 1 - core],
        dst_ref=side_in,
        send_sem=side_send,
        recv_sem=side_recv,
        device_id=partner,
        device_id_type=MESH,
    )

    def start_pair(i, carry):
        pair_copy(i).start()
        return carry

    lax.fori_loop(0, chunks, start_pair, 0)
    own_load.wait()

    drop = row(drop_ref).astype(F32)
    scale_all = drop * drop.shape[1] / jnp.sum(drop, 1, keepdims=True)
    drop_lane = lax.broadcasted_iota(jnp.int32, drop.shape, 1)
    vec_ref[...] = jnp.zeros_like(vec_ref)

    def take(j):
        at = other * half + j
        rows = pl.ds(pl.multiple_of(at * lat_rows, lat_rows), lat_rows)
        for q in range(PIECES):
            half_copy(j * PIECES + q).wait_recv()
            b_ref[q, rows, :] = half_in[j * PIECES + q].astype(BF16)
        res_copy(j).wait_recv()
        res_ref[rows, :] = res_in[j].astype(BF16)

        @pl.when(on_first)
        def _():
            hn_copy(j).wait_recv()
            a_ref[rows, :] = hn_in[j].astype(BF16)

        @pl.when(jnp.logical_not(on_first))
        def _():
            scale = jnp.sum(
                jnp.where(drop_lane == stream * samples + at, scale_all, 0.0), 1, keepdims=True
            )
            a_ref[rows, :] = (scale * cot_ref[rows, :].astype(F32)).astype(BF16)

        for copy in stores(j, 1):
            copy.start()

    def mlp(j, q):
        sample = core * half + j
        rows = pl.ds(pl.multiple_of(sample * lat_rows, lat_rows), lat_rows)
        mine = pl.ds(pl.multiple_of(j * lat_rows, lat_rows), lat_rows)
        scale = jnp.sum(
            jnp.where(drop_lane == stream * samples + sample, scale_all, 0.0), 1, keepdims=True
        )

        @pl.when(q == 0)
        def _():
            for h in range(HEADS):
                piece, i = piece_of(h)
                at = j * PIECES + piece
                den = own_ref[at, NUM_ROWS + 8 + i : NUM_ROWS + 9 + i, :]
                att_t_ref[h * HEAD_DIM : (h + 1) * HEAD_DIM, :] = own_ref[
                    at, i * HEAD_DIM : (i + 1) * HEAD_DIM, :
                ] * (1.0 / den)
            att = att_t_ref[...].T.astype(BF16)
            att_ref[mine, :] = jnp.where(parity == 0, att[:, : width // 2], att[:, width // 2 :])
            mid = lat_ref[rows, :].astype(F32) + scale * dot(att, wo_ref[...])
            mid_ref[...] = mid
            unit, _ = norm_parts(mid)
            hn = (unit * row(gain_ref)).astype(BF16)
            dm = (scale * cot_ref[rows, :].astype(F32)).astype(BF16)
            hn_ref[...] = hn
            dm_ref[...] = dm
            a_ref[rows, :] = jnp.where(on_first, hn, dm)

            @pl.when(jnp.logical_not(on_first))
            def _():
                hn_out[j] = hn.astype(F32)
                hn_copy(j).start()

            vec_ref[1:2, :width] += jnp.sum(dm.astype(F32), 0, keepdims=True)
            acc_ref[...] = jnp.broadcast_to(row(bdn_ref), acc_ref.shape)
            dacc_ref[...] = jnp.zeros_like(dacc_ref)

        span = wup_ref.shape[1] // PIECES
        cols = pl.ds(pl.multiple_of(q * span, 128), span)
        pre = dot(hn_ref[...], wup_ref[:, cols]) + bup_ref[cols].reshape(1, span)
        active, slope = gelu_parts(pre)
        hidden = active.astype(BF16)
        acc_ref[...] += dot(hidden, wdn_ref[cols, :])
        dpre = (slope * dot(dm_ref[...], wdn_ref[cols, :], (1, 1))).astype(BF16)
        piece = j * PIECES + q
        near_half = lambda x: jnp.where(parity == 0, x[:, : span // 2], x[:, span // 2 :])
        hidden_half, dpre_half = near_half(hidden), near_half(dpre)
        b_ref[q, rows, :] = jnp.where(on_first, dpre_half, hidden_half)
        half_out[piece] = jnp.where(on_first, hidden_half, dpre_half).astype(F32)
        half_copy(piece).start()
        vec_ref[0:1, cols] += jnp.sum(dpre.astype(F32), 0, keepdims=True)
        dacc_ref[...] += dot(dpre, wup_ref[:, cols], (1, 1))

        @pl.when(q == PIECES - 1)
        def _():
            mid = mid_ref[...]
            res = (mid + scale * acc_ref[...]).astype(BF16)
            res_ref[rows, :] = res
            res_out[j] = res.astype(F32)
            res_copy(j).start()
            unit, inv = norm_parts(mid)
            dhn = dacc_ref[...]
            vec_ref[2:3, :width] += jnp.sum(dhn * unit, 0, keepdims=True)
            dmid = cot_ref[rows, :].astype(F32) + norm_back(unit, inv, row(gain_ref), dhn)
            dmid_ref[mine, :] = dmid
            da = (scale * dmid).astype(BF16)
            da_ref[mine, :] = da
            datt_t = dot(wo_ref[...], da, (1, 1)).astype(BF16).astype(F32)
            msg_ref[j, width:, :] = jnp.zeros((MSG_ROWS - width, lat_rows), F32)
            for h in range(HEADS):
                piece, i = piece_of(h)
                at = j * PIECES + piece
                inverse = 1.0 / own_ref[at, NUM_ROWS + 8 + i : NUM_ROWS + 9 + i, :]
                span_h = slice(h * HEAD_DIM, (h + 1) * HEAD_DIM)
                one = datt_t[span_h]
                msg_ref[j, span_h, :] = (one * inverse).astype(BF16).astype(F32)
                delta = jnp.sum(one * att_t_ref[span_h, :], 0, keepdims=True) * inverse
                msg_ref[j, width + h : width + h + 1, :] = own_ref[
                    at, NUM_ROWS + i : NUM_ROWS + i + 1, :
                ]
                msg_ref[j, width + 16 + h : width + 17 + h, :] = delta
            msg_copy(j).start()
            for copy in stores(j, 0):
                copy.start()

            @pl.when(j > 0)
            def _():
                take(j - 1)

    def step(t, carry):
        @pl.when(t < chunks)
        def _():
            pair_copy(t).wait_recv()
            merge(own_ref.at[t], pair_ref.at[t], own_ref.at[t])

        r = t - LAG * chip

        @pl.when((r >= 0) & (r < chunks))
        def _():
            @pl.when(has_left)
            def _():
                right_copy(r).wait_recv()
                merge(own_ref.at[r], right_in.at[r], right_out.at[r])

            @pl.when(jnp.logical_not(has_left))
            def _():
                right_out[r] = own_ref[r]

            @pl.when(has_right)
            def _():
                right_copy(r).start()

        u = t - LAG * (chips - 1 - chip)

        @pl.when((u >= 0) & (u < chunks))
        def _():
            @pl.when(has_right)
            def _():
                left_copy(u).wait_recv()

            @pl.when(has_left)
            def _():
                @pl.when(has_right)
                def _():
                    merge(own_ref.at[u], left_in.at[u], left_out.at[u])

                @pl.when(jnp.logical_not(has_right))
                def _():
                    left_out[u] = own_ref[u]

                left_copy(u).start()

        w = t - LAG * jnp.maximum(chip, chips - 1 - chip)

        @pl.when((w >= 0) & (w < chunks))
        def _():
            @pl.when(has_right)
            def _():
                merge(right_out.at[w], left_in.at[w], own_ref.at[w])

            @pl.when(jnp.logical_not(has_right))
            def _():
                own_ref[w] = right_out[w]

        m = w - (PIECES - 1)

        @pl.when(m == 0)
        def _():
            for copy in weights:
                copy.wait()

        @pl.when((m >= 0) & (m < chunks))
        def _():
            mlp(lax.div(m, PIECES), lax.rem(m, PIECES))

        return carry

    lax.fori_loop(0, chunks + LAG * (chips - 1) + PIECES - 1, step, 0)

    share = width // 8
    for block in range(4):
        at = slice(block * 2 * share, (block + 1) * 2 * share)
        product = dot(da_ref[:, at], att_ref[...], (0, 0))
        side_all[block, 0] = product[:share]
        side_all[block, 1] = product[share:]
    side_copy.start()

    take(half - 1)

    def finish_chunk(i, carry):
        pair_copy(i).wait_send()
        half_copy(i).wait_send()

        @pl.when(has_right)
        def _():
            right_copy(i).wait_send()

        @pl.when(has_left)
        def _():
            left_copy(i).wait_send()

        return carry

    lax.fori_loop(0, chunks, finish_chunk, 0)

    def finish_sample(j, carry):
        @pl.when(jnp.logical_not(on_first))
        def _():
            hn_copy(j).wait_send()

        res_copy(j).wait_send()
        msg_copy(j).wait_send()
        msg_arrival(j).wait_recv()
        for copy in stores(j, 0) + stores(j, 1):
            copy.wait()
        return carry

    lax.fori_loop(0, half, finish_sample, 0)
    side_copy.wait()
    side_ref[...] = side_all[:, core] + side_in[...]


def latent_block(part, drop_mask, latents, cotangent, wo, gain, wup, bup, wdn, bdn):
    samples, lat_rows, width = latents.shape
    half = samples // 2
    chunks = half * PIECES
    hidden = wup.shape[1]
    sds = jax.ShapeDtypeStruct
    chunk = lambda: pltpu.VMEM((chunks, PIECE_ROWS, lat_rows), F32)
    dma = pltpu.SemaphoreType.DMA
    return pl.pallas_call(
        latent_kernel,
        name="latent_block",
        out_shape=(
            sds((samples, MSG_ROWS, lat_rows), F32),
            sds((samples * lat_rows, width), BF16),
            sds((half * lat_rows, width), F32),
            sds((samples * lat_rows, width), BF16),
            sds((PIECES, samples * lat_rows, hidden // PIECES // 2), BF16),
            sds((4, width // 8, width // 2), F32),
            sds((8, hidden), F32),
        ),
        in_specs=[
            anywhere(),
            vmem(),
            anywhere(),
            anywhere(),
            anywhere(),
            vmem(),
            anywhere(),
            vmem(),
            anywhere(),
            vmem(),
        ],
        out_specs=(anywhere(),) * 5 + (vmem(),) * 2,
        scratch_shapes=[
            pltpu.VMEM((samples * lat_rows, width), BF16),
            pltpu.VMEM((samples * lat_rows, width), BF16),
            pltpu.VMEM((half, MSG_ROWS, lat_rows), F32),
            pltpu.VMEM((samples * lat_rows, width), BF16),
            pltpu.VMEM((half * lat_rows, width), F32),
            pltpu.VMEM((samples * lat_rows, width), BF16),
            pltpu.VMEM((PIECES, samples * lat_rows, hidden // PIECES // 2), BF16),
            dma((2, 5, half)),
            pltpu.VMEM(wo.shape, BF16),
            pltpu.VMEM(wup.shape, BF16),
            pltpu.VMEM(wdn.shape, BF16),
            chunk(),
            chunk(),
            chunk(),
            chunk(),
            chunk(),
            chunk(),
            pltpu.VMEM((half, lat_rows, width), F32),
            pltpu.VMEM((half, lat_rows, width), F32),
            pltpu.VMEM((width, lat_rows), F32),
            pltpu.VMEM((lat_rows, width), F32),
            pltpu.VMEM((lat_rows, width), F32),
            pltpu.VMEM((lat_rows, width), F32),
            pltpu.VMEM((lat_rows, width), BF16),
            pltpu.VMEM((lat_rows, width), BF16),
            pltpu.VMEM((half * lat_rows, width), BF16),
            pltpu.VMEM((half * lat_rows, width // 2), BF16),
            pltpu.VMEM((half, lat_rows, width), F32),
            pltpu.VMEM((half, lat_rows, width), F32),
            pltpu.VMEM((chunks, lat_rows, hidden // PIECES // 2), F32),
            pltpu.VMEM((chunks, lat_rows, hidden // PIECES // 2), F32),
            pltpu.VMEM((4, 2, width // 8, width // 2), F32),
            pltpu.VMEM((4, width // 8, width // 2), F32),
            dma((half,)),
            dma((half,)),
            dma((chunks,)),
            dma((chunks,)),
            dma,
            dma,
            dma,
            dma((5,)),
            dma((chunks,)),
            dma((chunks,)),
            dma((chunks,)),
            dma((chunks,)),
            dma((chunks,)),
            dma((chunks,)),
            dma((half,)),
            dma((half,)),
            dma((half,)),
            dma((half,)),
        ],
        compiler_params=pltpu.CompilerParams(
            vmem_limit_bytes=VMEM_BYTES, collective_id=1, has_side_effects=True
        ),
    )(
        part.reshape(samples * PIECES, PIECE_ROWS, lat_rows),
        drop_mask,
        latents.reshape(samples * lat_rows, width),
        cotangent.reshape(samples * lat_rows, width),
        wo,
        gain,
        wup,
        bup,
        wdn,
        bdn,
    )


def gradient_kernel(
    dquery_hbm,
    dmid_hbm,
    lat_hbm,
    gain_q_ref,
    wq_hbm,
    a_hbm,
    b_hbm,
    side_ref,
    dwq_hbm,
    vec_ref,
    dgain_q_ref,
    place_ref,
    tok_hbm,
    tsort_hbm,
    dkv_hbm,
    gain_t_ref,
    wk_ref,
    wv_ref,
    dlat_out,
    gather_out,
    kv_out,
    query_out,
    small_out,
    dtok_out,
    line_ref,
    right_ref,
    left_ref,
    dmine_ref,
    wide_ref,
    wide_one,
    wide_two,
    send_ref,
    mine_ref,
    pair_ref,
    one_ref,
    two_ref,
    small_ref,
    gain_ref,
    wide_far,
    spread_ref,
    stage_ref,
    stage_sem,
    dsend_ref,
    dquery_ref,
    lat_ref,
    wq_ref,
    a_ref,
    b_ref,
    dwq_ref,
    tok_ref,
    tsort_ref,
    dkv_ref,
    load_sem,
    dpair_send,
    dpair_recv,
    right_send,
    right_recv,
    left_send,
    left_recv,
    back_send,
    back_recv,
    back_local,
    wide_one_send,
    wide_one_recv,
    wide_two_send,
    wide_two_recv,
    wide_z_send,
    wide_z_recv,
    wide_core_send,
    wide_core_recv,
    wide_local,
    pair_send,
    pair_recv,
    one_send,
    one_recv,
    two_send,
    two_recv,
    spread_send,
    spread_recv,
    share_send,
    share_recv,
    query_send,
    query_recv,
    query_local,
    keep_local,
):
    rows, width = tok_ref.shape
    lat_chunks = dmine_ref.shape[0]
    all_chunks = line_ref.shape[0]
    kv_rows = send_ref.shape[2]
    q_rows = query_out.shape[2]
    mix = kv_rows + q_rows
    half_chunks = (all_chunks - lat_chunks) // 2
    kv_chunks = kv_rows // ZROWS
    wide_half = wide_ref.shape[1] // 2
    sub_rows = wide_half // SUBS

    stream = lax.axis_index("stream")
    tok = lax.axis_index("tok")
    chips = lax.axis_size("tok") // 2
    core = lax.rem(tok, 2)
    chip = lax.div(tok, 2)
    other = 1 - core
    parity = lax.rem(chip, 2)
    flip_x = stream + 1 - 2 * lax.rem(stream, 2)
    flip_y = lax.rem(stream + 2, 4)
    flip_xy = 3 - stream
    partner = (stream, tok + 1 - 2 * core)
    right = (stream, tok + 2)
    left = (stream, tok - 2)
    beside = (stream, tok + 2 - 4 * parity)
    near = ((flip_x, tok), (flip_y, tok))
    first = (flip_x, flip_y)
    has_right = chip < chips - 1
    has_left = chip > 0
    here = (chip == 0).astype(F32)

    barrier = pltpu.get_barrier_semaphore()
    for target in (partner,) + near:
        pl.semaphore_signal(barrier, inc=1, device_id=target, device_id_type=MESH)

    @pl.when(has_right)
    def _():
        pl.semaphore_signal(barrier, inc=1, device_id=right, device_id_type=MESH)

    @pl.when(has_left)
    def _():
        pl.semaphore_signal(barrier, inc=1, device_id=left, device_id_type=MESH)

    def remote(src, dst, send, recv, target):
        return pltpu.make_async_remote_copy(
            src_ref=src,
            dst_ref=dst,
            send_sem=send,
            recv_sem=recv,
            device_id=target,
            device_id_type=MESH,
        )

    pulls = [
        pltpu.make_async_copy(src, dst, load_sem.at[i])
        for i, (src, dst) in enumerate(
            (
                (tsort_hbm, tsort_ref),
                (dkv_hbm, dkv_ref),
                (dmid_hbm, dmine_ref),
                (a_hbm, a_ref),
                (b_hbm, b_ref),
                (dwq_hbm, dwq_ref),
                (tok_hbm, tok_ref),
                (dquery_hbm, dquery_ref),
                (lat_hbm, lat_ref),
                (wq_hbm, wq_ref),
            )
        )
    ]
    for n in (7, 8, 9, 2, 0, 1, 5, 3, 4, 6):
        pulls[n].start()
    pl.semaphore_wait(barrier, 3 + has_right.astype(jnp.int32) + has_left.astype(jnp.int32))

    def dpair_copy(i):
        return remote(
            dsend_ref.at[i], line_ref.at[i], dpair_send.at[i], dpair_recv.at[i], partner
        )

    lat_rows = 128
    per_sample = lat_rows // ZROWS

    def lat_gradient(which, j):
        sample = which * (lat_chunks // per_sample) + j
        at = pl.ds(pl.multiple_of(sample * lat_rows, lat_rows), lat_rows)
        unit, inv = norm_parts(lat_ref[at, :].astype(F32))
        dnormed = dot(dquery_ref[at, :], wq_ref[...], (1, 1))
        return norm_back(unit, inv, row(gain_q_ref), dnormed)

    def lat_event(j):
        grad = lat_gradient(other, j)
        for c in range(per_sample):
            dsend_ref[j * per_sample + c] = grad[c * ZROWS : (c + 1) * ZROWS]
            dpair_copy(j * per_sample + c).start()
        grad = lat_gradient(core, j)
        for c in range(per_sample):
            i = j * per_sample + c
            dmine_ref[i] = grad[c * ZROWS : (c + 1) * ZROWS] + dmine_ref[i] * here

    def wide_one_copy(h, n, sub):
        block = (first[h], flip_xy)[n]
        at = pl.ds(h * wide_half + sub * sub_rows, sub_rows)
        return remote(
            wide_ref.at[block, at],
            wide_one.at[h, n, pl.ds(sub * sub_rows, sub_rows)],
            wide_one_send.at[h, n, sub],
            wide_one_recv.at[h, n, sub],
            near[h],
        )

    def wide_at(block, h, sub):
        return wide_ref.at[block, pl.ds(h * wide_half + sub * sub_rows, sub_rows)]

    def wide_two_copy(h, sub):
        at = pl.ds(sub * sub_rows, sub_rows)
        return remote(
            wide_at(first[1 - h], h, sub),
            wide_two.at[h, at],
            wide_two_send.at[h, sub],
            wide_two_recv.at[h, sub],
            near[1 - h],
        )

    def gather_at(c, e, h, sub):
        return gather_out.at[c, e, pl.ds(h * wide_half + sub * sub_rows, sub_rows)]

    def far_at(h, sub):
        return wide_far.at[pl.ds(h * wide_half + sub * sub_rows, sub_rows)]

    def wide_z_copy(h, sub):
        return remote(
            wide_at(stream, h, sub),
            far_at(h, sub),
            wide_z_send.at[h, sub],
            wide_z_recv.at[h, sub],
            beside,
        )

    def wide_core_copy(far, h, sub):
        if far:
            src = far_at(h, sub)
            dst = gather_at(core, 1 - parity, h, sub)
        else:
            src = wide_at(stream, h, sub)
            dst = gather_at(core, parity, h, sub)
        return remote(
            src, dst, wide_core_send.at[far, h, sub], wide_core_recv.at[far, h, sub], partner
        )

    def wide_core_arrival(far, h, sub):
        place = gather_at(other, 1 - parity if far else parity, h, sub)
        return remote(
            place, place, wide_core_send.at[far, h, sub], wide_core_recv.at[far, h, sub], partner
        )

    def wide_keep(far, h, sub):
        return pltpu.make_async_copy(
            far_at(h, sub) if far else wide_at(stream, h, sub),
            gather_at(core, 1 - parity if far else parity, h, sub),
            wide_local.at[far, h, sub],
        )

    def wide_product(block):
        wide_ref[block, :width, :] = dot(a_ref[...], b_ref[block], (0, 0))
        wide_ref[block, width:, :] = side_ref[block]

    def wide_start(k):
        if k == 0:
            pulls[3].wait()
            pulls[4].wait()
        wide_product((flip_xy, first[0], first[1], stream)[k])
        for sub in range(EARLY_SUBS):
            for h in range(2):
                if k == 0:
                    wide_one_copy(h, 1, sub).start()
                elif k == 1 + h:
                    wide_one_copy(h, 0, sub).start()

    def wide_more():
        for sub in range(EARLY_SUBS, SUBS):
            for h in range(2):
                for n in range(2):
                    wide_one_copy(h, 1 - n, sub).start()

    def wide_event_one(sub):
        at = slice(sub * sub_rows, (sub + 1) * sub_rows)
        for h in range(2):
            for n in range(2):
                wide_one_copy(h, n, sub).wait_recv()
            span = pl.ds(h * wide_half + sub * sub_rows, sub_rows)
            wide_ref[first[1 - h], span, :] += wide_one[h, 1, at, :]
            wide_two_copy(h, sub).start()
            wide_ref[stream, span, :] += wide_one[h, 0, at, :]

    def wide_event_two(sub):
        at = slice(sub * sub_rows, (sub + 1) * sub_rows)
        for h in range(2):
            wide_two_copy(h, sub).wait_recv()
            span = pl.ds(h * wide_half + sub * sub_rows, sub_rows)
            wide_ref[stream, span, :] += wide_two[h, at, :]
            wide_z_copy(h, sub).start()
            wide_core_copy(0, h, sub).start()
            wide_keep(0, h, sub).start()

    def wide_event_three(sub):
        for h in range(2):
            wide_z_copy(h, sub).wait_recv()
            wide_core_copy(1, h, sub).start()
            wide_keep(1, h, sub).start()

    share = width // 4

    def gain_part(which, block, product):
        at = slice(block * share, (block + 1) * share)
        weight = jnp.where(which == 0, wk_ref[at, :], wv_ref[at, :]).astype(F32)
        gain_ref[at, 0:1] += jnp.sum(product * weight, 1, keepdims=True)

    def token_product(block, which):
        at = slice(block * share, (block + 1) * share)
        return dot(tsort_ref[:, at], dkv_ref[which], (0, 0))

    def token_other():
        for n in (0, 1, 5):
            pulls[n].wait()
        gain_ref[...] = jnp.zeros_like(gain_ref)
        for block in range(4):
            product = token_product(block, other)
            for h in range(2):
                send_ref[h, block] = product[h * kv_rows : (h + 1) * kv_rows]
            gain_part(other, block, product)
        for k, h, what in pairs:
            if what < 2:
                pair_copy(k, h, what).start()

    order = (flip_xy, first[0], first[1], stream)

    def pair_copy(k, h, what):
        block = order[k]
        src, at, size = (
            (send_ref.at[h, block], 0, kv_rows),
            (dwq_ref.at[block, other, h], kv_rows, q_rows),
            (small_ref.at[block], mix, 16),
        )[what]
        return remote(
            src,
            pair_ref.at[h, block, pl.ds(at, size)],
            pair_send.at[k, h, what],
            pair_recv.at[k, h, what],
            partner,
        )

    pairs = [(k, h, what) for k in range(4) for h in range(2) for what in range(3 - h)]

    def token_own():
        for block in range(4):
            product = token_product(block, core)
            for h in range(2):
                piece = product[h * kv_rows : (h + 1) * kv_rows]
                mine_ref[h, block, :kv_rows, :] = piece
                mine_ref[h, block, kv_rows:mix, :] = dwq_ref[block, core, h]
            gain_part(core, block, product)
        mine_ref[1, :, mix:, :] = jnp.zeros((4, 16, width), F32)
        small_ref[...] = jnp.zeros_like(small_ref)
        gain = jnp.broadcast_to(gain_ref[:, 0:1], gain_ref.shape).T[0:1, :] / row(gain_t_ref)
        for block in range(4):
            small_ref[block, 0:1, :] = vec_ref[0:1, block * width : (block + 1) * width] * here
            small_ref[block, 1:2, :] = dgain_q_ref[0:1, :]
            small_ref[block, 2:3, :] = vec_ref[2:3, :width] * here
            small_ref[block, 3:4, :] = vec_ref[1:2, :width] * here
            small_ref[block, 4:5, :] = gain
        for k in range(4):
            pair_copy(k, 0, 2).start()

    token_step = 128

    def stage_copy(i):
        return pltpu.make_async_copy(
            stage_ref.at[i % 2],
            dtok_out.at[pl.ds(i * token_step, token_step)],
            stage_sem.at[i % 2],
        )

    def token_part(i):
        if i == 0:
            pulls[6].wait()
        at = pl.ds(pl.multiple_of(i * token_step, token_step), token_step)
        target = lax.broadcasted_iota(jnp.int32, (token_step, rows), 1).astype(F32)
        pick = jnp.where(target == place_ref[at, 0:1], 1.0, 0.0).astype(BF16)
        dkey = dot(pick, dkv_ref[0]).astype(BF16)
        dval = dot(pick, dkv_ref[1]).astype(BF16)
        dnormed = dot(dkey, wk_ref[...], (1, 1)) + dot(dval, wv_ref[...], (1, 1))
        unit, inv = norm_parts(tok_ref[at, :].astype(F32))
        if i >= 2:
            stage_copy(i - 2).wait()
        stage_ref[i % 2] = norm_back(unit, inv, row(gain_t_ref), dnormed)
        stage_copy(i).start()

    def one_copy(h, n):
        block = (first[h], flip_xy)[n]
        return remote(
            mine_ref.at[h, block], one_ref.at[h, n], one_send.at[h, n], one_recv.at[h, n], near[h]
        )

    def two_copy(h):
        return remote(
            mine_ref.at[h, first[1 - h]], two_ref.at[h], two_send.at[h], two_recv.at[h], near[1 - h]
        )

    def pair_event():
        for k in range(4):
            block = order[k]
            for h in range(2):
                for what in range(3 - h):
                    pair_copy(k, h, what).wait_recv()
                mine_ref[h, block, :mix, :] += pair_ref[h, block, :mix, :]
                if h == 0:
                    mine_ref[h, block, mix:, :] = small_ref[block] + pair_ref[h, block, mix:, :]
                if k == 0:
                    one_copy(h, 1).start()
                elif k == 1 + h:
                    one_copy(h, 0).start()

    def one_event():
        for h in range(2):
            for n in range(2):
                one_copy(h, n).wait_recv()
            mine_ref[h, first[1 - h]] += one_ref[h, 1]
            two_copy(h).start()

    def two_event():
        for h in range(2):
            two_copy(h).wait_recv()
            total = mine_ref[h, stream] + one_ref[h, 0] + two_ref[h]
            for k in range(half_chunks):
                line_ref[lat_chunks + h * half_chunks + k] = total[k * ZROWS : (k + 1) * ZROWS]

    def right_copy(i):
        return remote(right_ref.at[i], right_ref.at[i], right_send.at[i], right_recv.at[i], right)

    def left_copy(i):
        return remote(left_ref.at[i], left_ref.at[i], left_send.at[i], left_recv.at[i], left)

    def back_copy(i):
        return remote(
            line_ref.at[i], dlat_out.at[core, i], back_send.at[i], back_recv.at[i], partner
        )

    def back_arrival(i):
        return remote(
            line_ref.at[i], dlat_out.at[other, i], back_send.at[i], back_recv.at[i], partner
        )

    def back_keep(i):
        return pltpu.make_async_copy(line_ref.at[i], dlat_out.at[core, i], back_local.at[i])

    def placed(t):
        late = t >= lat_chunks + GAP
        index = jnp.where(late, t - GAP, t)
        return index, (t >= 0) & (late | (t < lat_chunks)) & (index < all_chunks)

    def line_step(t):
        @pl.when(t < lat_chunks)
        def _():
            dpair_copy(t).wait_recv()
            line_ref[t] += dmine_ref[t]

        r, r_due = placed(t - LINE_LAG * chip)

        @pl.when(r_due)
        def _():
            @pl.when(has_left)
            def _():
                right_copy(r).wait_recv()
                right_ref[r] += line_ref[r]

            @pl.when(jnp.logical_not(has_left))
            def _():
                right_ref[r] = line_ref[r]

            @pl.when(has_right)
            def _():
                right_copy(r).start()

        u, u_due = placed(t - LINE_LAG * (chips - 1 - chip))

        @pl.when(u_due)
        def _():
            @pl.when(has_right)
            def _():
                left_copy(u).wait_recv()
                left_ref[u] += line_ref[u]

            @pl.when(jnp.logical_not(has_right))
            def _():
                left_ref[u] = line_ref[u]

            @pl.when(has_left)
            def _():
                left_copy(u).start()

        w, w_due = placed(t - LINE_LAG * jnp.maximum(chip, chips - 1 - chip))

        @pl.when(w_due)
        def _():
            line_ref[w] = right_ref[w] + left_ref[w] - line_ref[w]

            @pl.when(w < lat_chunks)
            def _():
                back_copy(w).start()
                back_keep(w).start()

    def spot(i):
        k = i - lat_chunks
        h = lax.div(k, half_chunks)
        return h, lax.rem(k, half_chunks)

    def by_half(h, pair):
        return jnp.where(h == 0, pair[0], pair[1])

    def block_of(h, k):
        return (stream, by_half(h, (flip_y, flip_x)), by_half(h, first), flip_xy)[k]

    def spread_src(i, k):
        h, c = spot(i)
        return line_ref.at[i] if k == 0 else spread_ref.at[k - 1, h, c]

    def spread_copy(i, k):
        h, c = spot(i)
        target = by_half(h, (flip_y, flip_x)) if k == 1 else by_half(h, first)
        return remote(
            spread_src(i, 1 if k == 3 else 0),
            spread_ref.at[k - 1, h, c],
            spread_send.at[k - 1, i - lat_chunks],
            spread_recv.at[k - 1, i - lat_chunks],
            (target, tok),
        )

    def share_copy(i, k):
        h, c = spot(i)
        return remote(
            spread_src(i, k),
            kv_out.at[core, block_of(h, k), h, c],
            share_send.at[k, i - lat_chunks],
            share_recv.at[k, i - lat_chunks],
            partner,
        )

    def share_arrival(i, k):
        h, c = spot(i)
        place = kv_out.at[other, block_of(h, k), h, c]
        return remote(
            place,
            place,
            share_send.at[k, i - lat_chunks],
            share_recv.at[k, i - lat_chunks],
            partner,
        )

    def kv_keep(i, k):
        h, c = spot(i)
        return pltpu.make_async_copy(
            spread_src(i, k),
            kv_out.at[core, block_of(h, k), h, c],
            keep_local.at[k, i - lat_chunks],
        )

    def spread_due(t):
        i, due = placed(t)
        i = jnp.maximum(i, lat_chunks)
        _, c = spot(i)
        return i, due & (t >= lat_chunks + GAP) & (c < kv_chunks)

    def spread_step(t):
        lag = LINE_LAG * jnp.maximum(chip, chips - 1 - chip)
        i, due = spread_due(t - lag)

        @pl.when(due)
        def _():
            spread_copy(i, 1).start()
            spread_copy(i, 2).start()
            share_copy(i, 0).start()
            kv_keep(i, 0).start()

        j, due_one = spread_due(t - lag - SPREAD_LAG)

        @pl.when(due_one)
        def _():
            spread_copy(j, 1).wait_recv()
            spread_copy(j, 3).start()
            share_copy(j, 1).start()
            kv_keep(j, 1).start()

        m, due_two = spread_due(t - lag - 2 * SPREAD_LAG)

        @pl.when(due_two)
        def _():
            for k in (2, 3):
                spread_copy(m, k).wait_recv()
                share_copy(m, k).start()
                kv_keep(m, k).start()

    def query_piece(h):
        return mine_ref.at[h, stream, pl.ds(kv_rows, q_rows)]

    def query_copy(h):
        return remote(
            query_piece(h),
            query_out.at[core, h],
            query_send.at[h],
            query_recv.at[h],
            partner,
        )

    def query_arrival(h):
        return remote(
            query_piece(h),
            query_out.at[other, h],
            query_send.at[h],
            query_recv.at[h],
            partner,
        )

    def query_keep(h):
        return pltpu.make_async_copy(query_piece(h), query_out.at[core, h], query_local.at[h])

    def query_event(h):
        flat = lat_chunks + h * half_chunks + kv_chunks
        for k in range(0, q_rows, 16):
            at = flat * ZROWS + k
            chunk, row = at // ZROWS, at % ZROWS
            mine_ref[h, stream, kv_rows + k : kv_rows + k + 16, :] = line_ref[
                chunk, row : row + 16, :
            ]
        query_copy(h).start()
        query_keep(h).start()
        if h == 0:
            at = flat * ZROWS + q_rows
            chunk, row = at // ZROWS, at % ZROWS
            small_out[...] = line_ref[chunk, row : row + 16, :]

    tail = LINE_LAG * (chips - 1)
    ready = lambda h: lat_chunks + GAP + (h + 1) * half_chunks - 1 + tail
    events = {}

    def at_tick(tick, run):
        events.setdefault(tick, []).append(run)

    parts = rows // token_step
    for i in range(parts):
        at_tick(TOKEN_TICKS[i % len(TOKEN_TICKS)], functools.partial(token_part, i))
    for k in range(4):
        at_tick(WIDE_START_TICKS[k], functools.partial(wide_start, k))
    at_tick(KV_TICKS[0], token_other)
    at_tick(KV_TICKS[1], token_own)
    at_tick(PAIR_TICK, pair_event)
    at_tick(MORE_TICK, wide_more)
    at_tick(ONE_TICK, one_event)
    at_tick(TWO_TICK, two_event)
    for sub in range(SUBS):
        at_tick(WIDE_ONE_TICKS[sub], functools.partial(wide_event_one, sub))
        at_tick(WIDE_TWO_TICKS[sub], functools.partial(wide_event_two, sub))
        if WIDE_THREE_TICKS[sub] >= 0:
            at_tick(WIDE_THREE_TICKS[sub], functools.partial(wide_event_three, sub))
    for n in (7, 8, 9, 2):
        pulls[n].wait()
    lat_event(0)
    for j in range(1, lat_chunks // per_sample):
        at_tick(LAT_TICKS[j - 1], functools.partial(lat_event, j))

    def step(t, carry):
        line_step(t)
        spread_step(t)
        for tick in sorted(events):

            @pl.when(t == tick)
            def _(tick=tick):
                for run in events[tick]:
                    run()

        return carry

    lax.fori_loop(0, ready(1) + 2 * SPREAD_LAG + 1, step, 0)
    for h in range(2):
        query_event(h)
    for sub in range(SUBS):
        if WIDE_THREE_TICKS[sub] < 0:
            wide_event_three(sub)

    def finish_lat(i, carry):
        dpair_copy(i).wait_send()
        back_copy(i).wait_send()
        back_arrival(i).wait_recv()
        back_keep(i).wait()
        return carry

    lax.fori_loop(0, lat_chunks, finish_lat, 0)

    def finish_line(i, carry):
        @pl.when(has_right)
        def _():
            right_copy(i).wait_send()

        @pl.when(has_left)
        def _():
            left_copy(i).wait_send()

        return carry

    lax.fori_loop(0, all_chunks, finish_line, 0)

    def finish_spread(n, carry):
        h = lax.div(n, kv_chunks)
        i = lat_chunks + h * half_chunks + lax.rem(n, kv_chunks)
        for k in range(4):
            if k:
                spread_copy(i, k).wait_send()
            share_copy(i, k).wait_send()
            share_arrival(i, k).wait_recv()
            kv_keep(i, k).wait()
        return carry

    lax.fori_loop(0, 2 * kv_chunks, finish_spread, 0)
    for i in range(parts - 2, parts):
        stage_copy(i).wait()
    for k, h, what in pairs:
        pair_copy(k, h, what).wait_send()
    for h in range(2):
        for n in range(2):
            one_copy(h, n).wait_send()
        two_copy(h).wait_send()
        query_copy(h).wait_send()
        query_arrival(h).wait_recv()
        query_keep(h).wait()
        for sub in range(SUBS):
            for n in range(2):
                wide_one_copy(h, n, sub).wait_send()
                wide_core_copy(n, h, sub).wait_send()
                wide_core_arrival(n, h, sub).wait_recv()
            wide_two_copy(h, sub).wait_send()
            wide_z_copy(h, sub).wait_send()
            wide_keep(0, h, sub).wait()
            wide_keep(1, h, sub).wait()


def gradients(
    dquery, dmid, latents, gain_q, wq, a, b, side, dwq, vec, dgain_q, place, tokens, tsort, dkv,
    gain_t, wk, wv,
):
    rows, width = tokens.shape
    half = dquery.shape[0] // 2
    lat_chunks = half // ZROWS
    wide_rows, wide_cols = a.shape[1] + side.shape[1], b.shape[2]
    share = width // 4
    kv_rows, q_rows = share // 2, share // 4
    block = kv_rows + q_rows + 16
    all_chunks = lat_chunks + 2 * block // ZROWS
    sds = jax.ShapeDtypeStruct
    dma = pltpu.SemaphoreType.DMA
    buf = lambda *shape: pltpu.VMEM(shape, F32)
    both = lambda *shape: [dma(shape), dma(shape)]
    return pl.pallas_call(
        gradient_kernel,
        name="gradients",
        out_shape=(
            sds((2, lat_chunks, ZROWS, width), F32),
            sds((2, 2, wide_rows, wide_cols), F32),
            sds((2, 4, 2, kv_rows // ZROWS, ZROWS, width), F32),
            sds((2, 2, q_rows, width), F32),
            sds((16, width), F32),
            sds((rows, width), F32),
        ),
        in_specs=[anywhere()] * 3
        + [vmem()]
        + [anywhere()] * 3
        + [vmem(), anywhere()]
        + [vmem()] * 3
        + [anywhere()] * 3
        + [vmem()] * 3,
        out_specs=(anywhere(),) * 4 + (vmem(), anywhere()),
        scratch_shapes=[
            buf(all_chunks, ZROWS, width),
            buf(all_chunks, ZROWS, width),
            buf(all_chunks, ZROWS, width),
            buf(lat_chunks, ZROWS, width),
            buf(4, wide_rows, wide_cols),
            buf(2, 2, wide_rows // 2, wide_cols),
            buf(2, wide_rows // 2, wide_cols),
            buf(2, 4, kv_rows, width),
            buf(2, 4, block, width),
            buf(2, 4, block, width),
            buf(2, 2, block, width),
            buf(2, block, width),
            buf(4, 16, width),
            buf(width, 128),
            buf(wide_rows, wide_cols),
            buf(3, 2, kv_rows // ZROWS, ZROWS, width),
            buf(2, 128, width),
            dma((2,)),
            buf(lat_chunks, ZROWS, width),
            pltpu.VMEM(dquery.shape, BF16),
            pltpu.VMEM(dquery.shape, BF16),
            pltpu.VMEM(wq.shape, BF16),
            pltpu.VMEM(a.shape, BF16),
            pltpu.VMEM(b.shape, BF16),
            buf(4, 2, 2, q_rows, width),
            pltpu.VMEM(tokens.shape, BF16),
            pltpu.VMEM(tsort.shape, BF16),
            pltpu.VMEM(dkv.shape, BF16),
            dma((10,)),
        ]
        + both(lat_chunks)
        + both(all_chunks)
        + both(all_chunks)
        + both(lat_chunks)
        + [dma((lat_chunks,))]
        + both(2, 2, SUBS)
        + both(2, SUBS)
        + both(2, SUBS)
        + both(2, 2, SUBS)
        + [dma((2, 2, SUBS))]
        + both(4, 2, 3)
        + both(2, 2)
        + both(2)
        + both(3, all_chunks - lat_chunks)
        + both(4, all_chunks - lat_chunks)
        + both(2)
        + [dma((2,)), dma((4, all_chunks - lat_chunks))],
        compiler_params=pltpu.CompilerParams(
            vmem_limit_bytes=VMEM_BYTES, collective_id=2, has_side_effects=True
        ),
    )(
        dquery,
        dmid.reshape(lat_chunks, ZROWS, width),
        latents.reshape(2 * half, width),
        gain_q,
        wq,
        a,
        b,
        side,
        dwq.reshape(4, 2, 2, q_rows, width),
        vec,
        dgain_q,
        place,
        tokens,
        tsort,
        dkv,
        gain_t,
        wk,
        wv,
    )


def closing_kernel(
    dlat_hbm,
    gather_hbm,
    kv_hbm,
    query_ref,
    small_ref,
    dtok_hbm,
    dlat_out,
    dtok_out,
    up_out,
    key_out,
    val_out,
    down_out,
    out_ref,
    wq_ref,
    gain_q_ref,
    gain_t_ref,
    gain_mlp_ref,
    bup_ref,
    bdn_ref,
    wide_ref,
    up_ref,
    dlat_ref,
    kv_ref,
    dtok_ref,
    down_ref,
    load_sems,
    store_sems,
):
    width = small_ref.shape[1]
    cols = wide_ref.shape[2]
    wide_load = pltpu.make_async_copy(gather_hbm.at[1], wide_ref, load_sems.at[0])
    up_load = pltpu.make_async_copy(gather_hbm.at[0], up_ref, load_sems.at[1])
    up_stores = [
        pltpu.make_async_copy(
            up_ref.at[e, pl.ds(0, width)], up_out.at[:, pl.ds(e * cols, cols)], store_sems.at[e]
        )
        for e in range(2)
    ]
    down_stores = [
        pltpu.make_async_copy(
            down_ref.at[pl.ds(e * cols, cols)],
            down_out.at[pl.ds(e * cols, cols)],
            store_sems.at[2 + e],
        )
        for e in range(2)
    ]
    moves = []
    for src, mid, dst in (
        (kv_hbm.at[0], kv_ref.at[0], key_out),
        (kv_hbm.at[1], kv_ref.at[1], val_out),
        (dlat_hbm, dlat_ref, dlat_out),
        (dtok_hbm, dtok_ref, dtok_out),
    ):
        span = mid.shape[0] // 4
        for n in range(4):
            at = pl.ds(n * span, span)
            k = len(moves)
            moves.append(
                (
                    pltpu.make_async_copy(src.at[at], mid.at[at], load_sems.at[2 + k]),
                    pltpu.make_async_copy(mid.at[at], dst.at[at], store_sems.at[4 + k]),
                )
            )
    wide_load.start()
    for load, _ in moves:
        load.start()
    up_load.start()
    stream = lax.axis_index("stream")
    gain_t_ref[...] = small_ref[4]
    bup_ref[...] = small_ref[0]
    size = gain_q_ref.shape[0]
    for i, ref in ((1, gain_q_ref), (2, gain_mlp_ref), (3, bdn_ref)):
        line = small_ref[i : i + 1, :]
        piece = line[:, :size]
        for k in range(1, width // size):
            piece = jnp.where(stream == k, line[:, k * size : (k + 1) * size], piece)
        ref[...] = piece[0]
    wq_ref[...] = query_ref[...]
    wide_load.wait()
    for e in range(2):
        down_ref[e * cols : (e + 1) * cols, :] = wide_ref[e, :width, :].T
        down_stores[e].start()
        for load, store in moves[2 * e : 2 * e + 2]:
            load.wait()
            store.start()
    for load, store in moves[4:]:
        load.wait()
        store.start()
    up_load.wait()
    half = up_ref.shape[1] - width
    for e in range(2):
        up_stores[e].start()
        out_ref[:half, e * cols : (e + 1) * cols] = up_ref[e, width:, :]
        out_ref[half:, e * cols : (e + 1) * cols] = wide_ref[e, width:, :]
    for copy in up_stores + down_stores:
        copy.wait()
    for _, store in moves:
        store.wait()


def closing(dlat, gather, kv, query, small, dtok):
    width = small.shape[1]
    wide_rows, cols = gather.shape[2:]
    share = query.shape[0]
    rows = dtok.shape[0]
    sds = lambda *shape: jax.ShapeDtypeStruct(shape, F32)
    return pl.pallas_call(
        closing_kernel,
        name="closing",
        out_shape=(
            sds(*dlat.shape),
            sds(rows, width),
            sds(width, 2 * cols),
            sds(width, width),
            sds(width, width),
            sds(2 * cols, width),
            sds(share, width),
            sds(share, width),
            sds(share),
            sds(width),
            sds(share),
            sds(2 * cols),
            sds(share),
        ),
        in_specs=[anywhere()] * 3 + [vmem()] * 2 + [anywhere()],
        out_specs=(anywhere(),) * 6 + (vmem(),) * 7,
        scratch_shapes=[
            pltpu.VMEM((2, wide_rows, cols), F32),
            pltpu.VMEM((2, wide_rows, cols), F32),
            pltpu.VMEM(dlat.shape, F32),
            pltpu.VMEM(kv.shape, F32),
            pltpu.VMEM(dtok.shape, F32),
            pltpu.VMEM((2 * cols, width), F32),
            pltpu.SemaphoreType.DMA((18,)),
            pltpu.SemaphoreType.DMA((20,)),
        ],
        compiler_params=pltpu.CompilerParams(vmem_limit_bytes=VMEM_BYTES),
    )(dlat, gather, kv, query, small, dtok)


def local(
    latents,
    tokens,
    token_sample,
    token_mask,
    drop_mask,
    gain_query,
    w_query,
    gain_token,
    w_key,
    w_value,
    w_out,
    gain_mlp,
    w_up,
    b_up,
    w_down,
    b_down,
    cotangent,
):
    samples, lat_rows, width = latents.shape
    part, keys, values, tsort, query, normed, place, bounds = attend_forward(
        token_sample, token_mask, tokens, latents, gain_query, w_query, gain_token, w_key, w_value
    )
    msg, result, dmid, a, b, side, vec = latent_block(
        part, drop_mask, latents, cotangent, w_out, gain_mlp, w_up, b_up, w_down, b_down
    )
    dkv, dquery, dgain_q, dwq, result = attend_backward(
        bounds, keys, values, query, normed, msg, gain_query, w_query, result
    )
    dlat, gather, kv, dwq, small, d_tokens = gradients(
        dquery, dmid, latents, gain_query, w_query, a, b, side, dwq, vec, dgain_q, place, tokens,
        tsort, dkv, gain_token,
        w_key, w_value,
    )
    (
        d_latents,
        d_tokens,
        grad_up,
        grad_key,
        grad_value,
        grad_down,
        grad_out,
        grad_query,
        grad_gquery,
        grad_gtoken,
        grad_gmlp,
        grad_bup,
        grad_bdown,
    ) = closing(
        dlat.reshape(samples * lat_rows, width),
        gather,
        kv.reshape(2, width, width),
        dwq.reshape(-1, width),
        small,
        d_tokens,
    )
    return (
        result.reshape(latents.shape),
        d_latents.reshape(latents.shape),
        d_tokens,
        grad_gquery,
        grad_query.T,
        grad_gtoken,
        grad_key,
        grad_value,
        grad_out.T,
        grad_gmlp,
        grad_up,
        grad_bup,
        grad_down,
        grad_bdown,
    )


def solution(mesh):
    return jax.shard_map(
        local,
        mesh=mesh,
        in_specs=(
            P("stream", None, None),
            P(("stream", "tok"), None),
            P(("stream", "tok")),
            P(("stream", "tok")),
            P(),
            P(),
            P(),
            P(),
            P(),
            P(),
            P(),
            P(),
            P(),
            P(),
            P(),
            P(),
            P("stream", None, None),
        ),
        out_specs=(
            P("stream", None, None),
            P("stream", None, None),
            P(("stream", "tok"), None),
            P("stream"),
            P(None, "stream"),
            P(),
            P(),
            P(),
            P(None, "stream"),
            P("stream"),
            P(None, "stream"),
            P("stream"),
            P("stream", None),
            P("stream"),
        ),
        check_vma=False,
    )
```
